32 devices in a mesh: row: 8 (over y, x, core), col: 4 (over z).
Axes of the slice: x: 2, y: 2, z: 4, core: 2. Of those that a mesh axis runs over, the one named last changes fastest.
Arguments:
- tokens: bfloat16 [8192, 2048], P('row', 'col'), may hold values from -6 to 6
- cotangent: bfloat16 [8192, 2048], P('row', 'col'), may hold values from -6 to 6
- segments: int32 [8192], P('row'), may hold values from 0 to 20, never falling along the last dimension, each value on 1 to 800 neighbouring positions
- w_query: bfloat16 [2048, 2048], P('row', 'col'), may hold values from -0.125 to 0.125
- w_key: bfloat16 [2048, 2048], P('row', 'col'), may hold values from -0.125 to 0.125
- w_value: bfloat16 [2048, 2048], P('row', 'col'), may hold values from -0.125 to 0.125
- w_out: bfloat16 [2048, 2048], P('col', 'row'), may hold values from -1 to 1
- w_gate: bfloat16 [2048, 8192], P('row', 'col'), may hold values from -0.125 to 0.125
- w_up: bfloat16 [2048, 8192], P('row', 'col'), may hold values from -0.125 to 0.125
- w_down: bfloat16 [8192, 2048], P('col', 'row'), may hold values from -0.0625 to 0.0625
Outputs:
- output: bfloat16 [8192, 2048], P('row', 'col')
- grad_tokens: bfloat16 [8192, 2048], P('row', 'col')
- grad_query: float32 [2048, 2048], P('row', 'col')
- grad_key: float32 [2048, 2048], P('row', 'col')
- grad_value: float32 [2048, 2048], P('row', 'col')
- grad_out: float32 [2048, 2048], P('col', 'row')
- grad_gate: float32 [2048, 8192], P('row', 'col')
- grad_up: float32 [2048, 8192], P('row', 'col')
- grad_down: float32 [8192, 2048], P('col', 'row')
The draws below stay inside these ranges and needn't reach their ends.
Inputs may be any that keep to these rules, and one draw needn't show every extreme that they name: `segments`: segment numbers never fall along the tokens; each segment covers 1 to 800 tokens, one exactly that many.
All inputs are finite; a program needn't handle non-finite values.
Results may differ from the reference program's by a relative error of at most 0.018.
Values may be sent and summed in bfloat16 or wider, within the bound.
A program may use at most 256 MiB of HBM per device.

```python
import math
import jax
import jax.numpy as jnp
import numpy as np
from jax import lax

D = 2048
FF = 8192
HEADS = 16
HEAD_DIM = 128
SEQ = 1024
TOKENS = 8192
SEG_MOST = 800
SEG_COUNT = 21


def strengthened(values, key, source, target, blocks, factor):
    owner, partner = [(jnp.arange(values.shape[position]) // (values.shape[position] // blocks)).reshape([-1 if axis == position else 1 for axis in range(values.ndim)]) for position in (source, target)]
    chosen = jax.random.permutation(key, blocks)[partner]
    strong = (owner == chosen) | (owner == (partner + blocks // 2) % blocks)
    return jnp.where(strong, factor * values, values)


def block_scale(stream_key, shape, cuts, least, top_value):
    def one(axis_at, blocks):
        steps = jax.random.uniform(jax.random.fold_in(jax.random.fold_in(stream_key, 6), axis_at), (blocks,), jnp.float32, least / len(cuts), top_value / len(cuts))
        return jnp.repeat(jnp.exp(steps), shape[axis_at] // blocks).reshape((-1,) + (1,) * (len(shape) - axis_at - 1))

    factor_of = one(*cuts[0])
    for cut in cuts[1:]:
        factor_of = factor_of * one(*cut)
    return factor_of


def length_profile(number_of, total, limit, lean):
    weights = [(1 << 20) // math.isqrt(standing ** lean) + 1 for standing in range(2, number_of + 1)]
    spare, holding = total - limit - (number_of - 1), [1] * (number_of - 1)
    while spare > 0:
        free = [i for i in range(number_of - 1) if holding[i] < limit]
        pool, left = sum([weights[i] for i in free]), spare
        for i in free:
            more = min(limit - holding[i], max(1, left * weights[i] // pool), spare)
            holding[i] = holding[i] + more
            spare = spare - more
    return np.array([limit] + holding)


def ragged_sizes(own_key, number_of, total, limit, lean):
    if number_of == 2:
        one = jax.random.randint(own_key, (), max(1, total - limit), min(limit, total - 1) + 1)
        return jnp.stack([one, total - one])
    sizes = jnp.asarray(length_profile(number_of, total, limit, lean), jnp.int32)
    pairs = (number_of - 1) // 2
    giver, taker = sizes[1:1 + 2 * pairs:2], sizes[2:2 + 2 * pairs:2]
    margin = jnp.minimum(giver - 1, limit - taker)
    moved = jax.random.randint(jax.random.fold_in(own_key, 1), (pairs,), 0, 1 << 20) % (margin + 1)
    sizes = sizes.at[1:1 + 2 * pairs:2].set(giver - moved).at[2:2 + 2 * pairs:2].set(taker + moved)
    return sizes[jax.random.permutation(jax.random.fold_in(own_key, 2), number_of)]


def gaussian(rng, extent, scale, most, cuts=(), kind=jnp.bfloat16):
    entries = jax.random.normal(rng, extent, jnp.float32) * scale
    if len(cuts) > 0:
        entries = block_scale(rng, extent, cuts, -0.22, 0.18) * entries
    return jnp.clip(entries, min=-most, max=most).astype(kind)


def gaussian_with(rng, dims, deviation, most, cuts, heavy, held_as=jnp.bfloat16):
    values = deviation * jax.random.normal(rng, dims, jnp.float32)
    if cuts:
        values = values * block_scale(rng, dims, cuts, -0.22, 0.18)
    return jnp.clip(strengthened(values, jax.random.fold_in(rng, 3), *heavy), -most, most).astype(held_as)


def setup_inputs(seed: int = 0) -> dict:
    arg_keys = jax.random.split(jax.random.key(seed), 11)
    return {
        "tokens": gaussian(arg_keys[0], (TOKENS, D), 1.0, 6.0, ((0, 8), (1, 4))),
        "cotangent": gaussian_with(arg_keys[1], (TOKENS, D), 1.0, 6.0, ((0, 8), (1, 4)), (0, 1, 8, 2.0)),
        "segments": jnp.searchsorted(jnp.cumsum(ragged_sizes(arg_keys[2], SEG_COUNT, TOKENS, SEG_MOST, 1)), jnp.arange(TOKENS), side="right").astype(jnp.int32),
        "w_query": gaussian(arg_keys[3], (D, D), D ** -0.5, 0.125, ((0, 8), (1, 4))),
        "w_key": gaussian(arg_keys[4], (D, D), D ** -0.5, 0.125, ((0, 8), (1, 4))),
        "w_value": gaussian(arg_keys[5], (D, D), D ** -0.5, 0.125, ((0, 8), (1, 4))),
        "w_out": gaussian(arg_keys[6], (D, D), (D // 64) ** -0.5, 1.0, ((0, 4), (1, 8))),
        "w_gate": gaussian(arg_keys[7], (D, FF), D ** -0.5, 0.125, ((0, 8), (1, 4))),
        "w_up": gaussian(arg_keys[8], (D, FF), D ** -0.5, 0.125, ((0, 8), (1, 4))),
        "w_down": gaussian(arg_keys[9], (FF, D), FF ** -0.5, 0.0625, ((0, 4), (1, 8))),
    }


@jax.custom_vjp
def low(v):
    return lax.optimization_barrier(v.astype(jnp.bfloat16)).astype(jnp.float32)

@jax.custom_vjp
def low_back(v):
    return v

def low_keep(v):
    return (low(v), None)

def low_pass(kept, grad):
    return (grad,)

def back_keep(v):
    return (v, None)

def back_low(kept, grad):
    return (low(grad),)
low.defvjp(low_keep, low_pass)
low_back.defvjp(back_keep, back_low)
EPSILON = 1e-05
MASKED = -1e+30

def matmul_high(left, right):
    return jnp.dot(left, right, precision=lax.Precision.HIGHEST, preferred_element_type=jnp.float32)

def layer_norm(values):
    centre = lax.optimization_barrier(jnp.mean(values, axis=-1, keepdims=True))
    spread = lax.optimization_barrier(jnp.mean(values * values, axis=-1, keepdims=True)) - centre * centre
    return (values - centre) * lax.rsqrt(spread + EPSILON)

def allowed_of(segment_ids):
    places = jnp.arange(segment_ids.shape[0], dtype=jnp.int32)
    causal = places[None, :] <= places[:, None]
    return (segment_ids[:, None] == segment_ids[None, :]) & causal

def count_seen(segment_ids):
    return lax.optimization_barrier(jnp.sum(allowed_of(segment_ids).astype(jnp.int32), axis=1)) - 1

def rope_tables(positions):
    halfway = HEAD_DIM // 2
    inverse = 10000.0 ** (-(jnp.arange(halfway, dtype=jnp.float32) * 2.0 / HEAD_DIM))
    angles = positions.astype(jnp.float32)[:, None] * inverse[None, :]
    return (jnp.cos(angles)[:, None, :], jnp.sin(angles)[:, None, :])

def rotate(values, cos_table, sin_table):
    shaped = values.reshape(values.shape[0], -1, HEAD_DIM)
    halfway = HEAD_DIM // 2
    first_half = shaped[..., :halfway]
    second_half = shaped[..., halfway:]
    turned = jnp.concatenate([first_half * cos_table - second_half * sin_table, second_half * cos_table + first_half * sin_table], axis=-1)
    return turned.reshape(values.shape)

def attend_sequence(blocks_in):
    query_seq, key_seq, value_seq, segment_ids = blocks_in
    allowed = allowed_of(segment_ids)
    score_scale = HEAD_DIM ** (-0.5)
    scores = low_back(jnp.einsum('qhd,khd->hqk', query_seq, key_seq, precision=lax.Precision.HIGHEST) * score_scale)
    scores = jnp.where(allowed[None], scores, MASKED)
    row_peak = lax.optimization_barrier(jnp.max(scores, axis=-1, keepdims=True))
    exponent = jnp.exp(scores - row_peak)
    probs = exponent / lax.optimization_barrier(jnp.sum(exponent, axis=-1, keepdims=True))
    weights = low(probs)
    return jnp.einsum('hqk,khd->qhd', weights, value_seq, precision=lax.Precision.HIGHEST)

def reference(tokens, cotangent, segments, w_query, w_key, w_value, w_out, w_gate, w_up, w_down):
    segment_rows = segments.reshape(-1, SEQ)
    positions = lax.map(count_seen, segment_rows).reshape(-1)
    cos_table, sin_table = rope_tables(positions)
    shaped = (TOKENS // SEQ, SEQ, HEADS, HEAD_DIM)

    def forward(inputs, query_w, key_w, value_w, out_w, gate_w, up_w, down_w):
        act_one = low(layer_norm(inputs))
        query = low_back(matmul_high(act_one, query_w))
        keys = low_back(matmul_high(act_one, key_w))
        values = low_back(matmul_high(act_one, value_w))
        query_r = low(rotate(query, cos_table, sin_table))
        key_r = low(rotate(keys, cos_table, sin_table))
        value_r = low(values)
        attended = lax.map(jax.checkpoint(attend_sequence), (query_r.reshape(shaped), key_r.reshape(shaped), value_r.reshape(shaped), segment_rows))
        attended = low(low_back(attended.reshape(TOKENS, D)))
        resid = inputs + low_back(matmul_high(attended, out_w))
        act_two = low(layer_norm(resid))
        gate = low_back(matmul_high(act_two, gate_w))
        upward = low_back(matmul_high(act_two, up_w))
        hidden = low(jax.nn.silu(gate) * upward)
        return resid + matmul_high(hidden, down_w)
    floats = [a.astype(jnp.float32) for a in (tokens, w_query, w_key, w_value, w_out, w_gate, w_up, w_down)]
    result, pull = jax.vjp(forward, *floats)
    grads = pull(cotangent.astype(jnp.float32))
    return (result.astype(jnp.bfloat16), grads[0].astype(jnp.bfloat16), grads[1], grads[2], grads[3], grads[4], grads[5], grads[6], grads[7])
```

```python
import functools

import jax
import jax.numpy as jnp
from jax import lax
from jax.experimental import pallas as pl
from jax.experimental.pallas import tpu as pltpu
from jax.sharding import PartitionSpec as P

HEAD_DIM = 128
HALF = HEAD_DIM // 2
SEQ = 1024
EPSILON = 1e-05
MASKED = -1e30
SCALE = HEAD_DIM ** (-0.5)
BF = jnp.bfloat16
F32 = jnp.float32
MIB = 1 << 20
ANY = pl.BlockSpec(memory_space=pl.ANY)


def dot_nn(left, right):
    return jnp.dot(left, right, preferred_element_type=F32)


def dot_tn(left, right):
    return lax.dot_general(left, right, (((0,), (0,)), ((), ())), preferred_element_type=F32)


def dot_nt(left, right):
    return lax.dot_general(left, right, (((1,), (1,)), ((), ())), preferred_element_type=F32)


def struct(shape, dtype):
    return jax.ShapeDtypeStruct(shape, dtype)


def params(mib=60):
    return pltpu.CompilerParams(vmem_limit_bytes=mib * MIB)


def cost(flops, moved):
    return pl.CostEstimate(flops=int(flops), bytes_accessed=int(moved), transcendentals=0)


def count_seen(segment_ids):
    places = jnp.arange(segment_ids.shape[0], dtype=jnp.int32)
    causal = places[None, :] <= places[:, None]
    allowed = (segment_ids[:, None] == segment_ids[None, :]) & causal
    return jnp.sum(allowed.astype(jnp.int32), axis=1) - 1


def rope_tables(segments):
    positions = jax.vmap(count_seen)(segments.reshape(-1, SEQ)).reshape(-1)
    inverse = 10000.0 ** (-(jnp.arange(HALF, dtype=F32) * 2.0 / HEAD_DIM))
    angles = positions.astype(F32)[:, None] * inverse[None, :]
    cosine, sine = jnp.cos(angles), jnp.sin(angles)
    return jnp.concatenate([cosine, cosine], 1), jnp.concatenate([-sine, sine], 1)


def turn(values, cos_table, sin_table):
    return values * cos_table + pltpu.roll(values, HALF, 1) * sin_table


def norm_rows(x):
    centre = jnp.mean(x, axis=-1, keepdims=True)
    spread = jnp.mean(x * x, axis=-1, keepdims=True) - centre * centre
    inverse = lax.rsqrt(spread + EPSILON)
    return centre, inverse


def qkv_kernel(C, place, *refs):
    pieces = refs[:C]
    w_ref, cos_ref, sin_ref, x_ref, a_ref, q_ref, k_ref, v_ref, mu_ref, r_ref = refs[C:]
    width = pieces[0].shape[1]
    me = place[0]
    for k in range(C):
        owner = lax.rem(me - k + C, C)
        x_ref[:, pl.ds(pl.multiple_of(owner * width, width), width)] = pieces[k][...]
    x = x_ref[...].astype(F32)
    centre, inverse = norm_rows(x)
    a = ((x - centre) * inverse).astype(BF)
    a_ref[...] = a
    mu_ref[...] = centre
    r_ref[...] = inverse
    cosine, sine = cos_ref[...], sin_ref[...]
    for index, out in enumerate((q_ref, k_ref, v_ref)):
        product = dot_nn(a, w_ref[:, index * width : (index + 1) * width])
        if index == 2:
            out[...] = product.astype(BF)
            continue
        for start in range(0, width, HEAD_DIM):
            part = product[:, start : start + HEAD_DIM]
            out[:, start : start + HEAD_DIM] = turn(part, cosine, sine).astype(BF)


def norm_and_project(place, pieces, w_qkv, cos_table, sin_table):
    C = len(pieces)
    T, width = pieces[0].shape
    D = width * C
    bt = 256
    rows = lambda n: pl.BlockSpec((bt, n), lambda i, p: (i, 0))
    return pl.pallas_call(
        functools.partial(qkv_kernel, C),
        grid_spec=pltpu.PrefetchScalarGridSpec(
            num_scalar_prefetch=1,
            grid=(T // bt,),
            in_specs=[rows(width)] * C
            + [
                pl.BlockSpec(w_qkv.shape, lambda i, p: (0, 0), pipeline_mode=pl.Buffered(1)),
                rows(HEAD_DIM),
                rows(HEAD_DIM),
            ],
            out_specs=[rows(D), rows(D), rows(width), rows(width), rows(width), rows(1), rows(1)],
        ),
        out_shape=[
            struct((T, D), BF),
            struct((T, D), BF),
            struct((T, width), BF),
            struct((T, width), BF),
            struct((T, width), BF),
            struct((T, 1), F32),
            struct((T, 1), F32),
        ],
        compiler_params=params(),
        cost_estimate=cost(2 * T * D * 3 * width, 14 * MIB),
        name="norm_and_project",
    )(place, *pieces, w_qkv, cos_table, sin_table)


def allowed_block(seg_key, seg_query, first_query):
    shape = (seg_key.shape[0], seg_query.shape[1])
    keys = lax.broadcasted_iota(jnp.int32, shape, 0)
    queries = lax.broadcasted_iota(jnp.int32, shape, 1) + first_query
    return (seg_key == seg_query) & (keys <= queries)


def attend_kernel(bq, q_ref, k_ref, v_ref, segk_ref, segq_ref, o_ref, log_ref):
    length = q_ref.shape[0]
    for start in range(0, length, bq):
        stop = start + bq
        scores = dot_nt(k_ref[:stop], q_ref[start:stop]) * SCALE
        allowed = allowed_block(segk_ref[:stop], segq_ref[0, :, start:stop], start)
        scores = jnp.where(allowed, scores, MASKED)
        peak = jnp.max(scores, axis=0, keepdims=True)
        exponent = jnp.exp(scores - peak)
        total = jnp.sum(exponent, axis=0, keepdims=True)
        weights = (exponent * (1.0 / total)).astype(BF)
        o_ref[start:stop] = dot_tn(v_ref[:stop], weights).T.astype(BF)
        log_ref[0, 0, :, start:stop] = peak + jnp.log(total)


def attend(q, k, v, seg_column, seg_row):
    T, width = q.shape
    heads, sequences = width // HEAD_DIM, T // SEQ
    one = pl.BlockSpec((SEQ, HEAD_DIM), lambda s, h: (s, h))
    return pl.pallas_call(
        functools.partial(attend_kernel, 256),
        grid=(sequences, heads),
        in_specs=[
            one,
            one,
            one,
            pl.BlockSpec((SEQ, 1), lambda s, h: (s, 0)),
            pl.BlockSpec((1, 1, SEQ), lambda s, h: (s, 0, 0)),
        ],
        out_specs=[one, pl.BlockSpec((1, 1, 1, SEQ), lambda s, h: (s, h, 0, 0))],
        out_shape=[struct((T, width), BF), struct((sequences, heads, 1, SEQ), F32)],
        compiler_params=params(),
        cost_estimate=cost(4 * T * SEQ * width, 5 * MIB),
        name="attend",
    )(q, k, v, seg_column, seg_row)


def attend_back_kernel(
    bq, q_ref, k_ref, v_ref, do_ref, log_ref, segk_ref, segq_ref, cos_ref, sin_ref, dq_ref, dk_ref, dv_ref, dk_sum, dv_sum
):
    length = q_ref.shape[0]
    dk_sum[...] = jnp.zeros_like(dk_sum)
    dv_sum[...] = jnp.zeros_like(dv_sum)
    for start in range(0, length, bq):
        stop = start + bq
        keys, queries, grads = k_ref[:stop], q_ref[start:stop], do_ref[start:stop]
        scores = dot_nt(keys, queries) * SCALE
        allowed = allowed_block(segk_ref[:stop], segq_ref[0, :, start:stop], start)
        scores = jnp.where(allowed, scores, MASKED)
        probs = jnp.exp(scores - log_ref[0, 0, :, start:stop])
        dv_sum[:stop] += dot_nn(probs.astype(BF), grads)
        grad_probs = dot_nt(v_ref[:stop], grads)
        inner = jnp.sum(probs * grad_probs, axis=0, keepdims=True)
        grad_scores = (probs * (grad_probs - inner)).astype(BF)
        dk_sum[:stop] += dot_nn(grad_scores, queries)
        grad_query = dot_tn(keys, grad_scores).T * SCALE
        dq_ref[start:stop] = turn(grad_query, cos_ref[start:stop], -sin_ref[start:stop]).astype(BF)
    dk_ref[...] = turn(dk_sum[...] * SCALE, cos_ref[...], -sin_ref[...]).astype(BF)
    dv_ref[...] = dv_sum[...].astype(BF)


def attend_back(q, k, v, do, log_total, seg_column, seg_row, cos_table, sin_table):
    T, width = q.shape
    heads, sequences = width // HEAD_DIM, T // SEQ
    one = pl.BlockSpec((SEQ, HEAD_DIM), lambda s, h: (s, h))
    table = pl.BlockSpec((SEQ, HEAD_DIM), lambda s, h: (s, 0))
    return pl.pallas_call(
        functools.partial(attend_back_kernel, 256),
        grid=(sequences, heads),
        in_specs=[
            one,
            one,
            one,
            one,
            pl.BlockSpec((1, 1, 1, SEQ), lambda s, h: (s, h, 0, 0)),
            pl.BlockSpec((SEQ, 1), lambda s, h: (s, 0)),
            pl.BlockSpec((1, 1, SEQ), lambda s, h: (s, 0, 0)),
            table,
            table,
        ],
        out_specs=[one, one, one],
        out_shape=[struct((T, width), BF)] * 3,
        scratch_shapes=[pltpu.VMEM((SEQ, HEAD_DIM), F32), pltpu.VMEM((SEQ, HEAD_DIM), F32)],
        compiler_params=params(),
        cost_estimate=cost(10 * T * SEQ * width, 9 * MIB),
        name="attend_back",
    )(q, k, v, do, log_total, seg_column, seg_row, cos_table, sin_table)


def out_kernel(C, place, *refs):
    pieces = refs[:C]
    w_ref, x_ref, o_ref, h_ref, b_ref, mu_ref, r_ref = refs[C:]
    width = pieces[0].shape[1]
    blocks, part = w_ref.shape[0], w_ref.shape[2]
    me = place[0]
    for k in range(C):
        owner = lax.rem(me - k + C, C)
        o_ref[:, pl.ds(pl.multiple_of(owner * width, width), width)] = pieces[k][...]
    heads = o_ref[...]
    for n in range(blocks):
        columns = slice(n * part, (n + 1) * part)
        h_ref[:, columns] = x_ref[:, columns].astype(F32) + dot_nn(heads, w_ref[n])
    h = h_ref[...]
    centre, inverse = norm_rows(h)
    b_ref[...] = ((h - centre) * inverse).astype(BF)
    mu_ref[...] = centre
    r_ref[...] = inverse


def project_and_norm(place, pieces, w_out, x_full):
    C = len(pieces)
    T, D = x_full.shape
    width = D // C
    bt = 256
    rows = lambda n: pl.BlockSpec((bt, n), lambda i, p: (i, 0))
    return pl.pallas_call(
        functools.partial(out_kernel, C),
        grid_spec=pltpu.PrefetchScalarGridSpec(
            num_scalar_prefetch=1,
            grid=(T // bt,),
            in_specs=[rows(width)] * C
            + [pl.BlockSpec(w_out.shape, lambda i, p: (0, 0, 0), pipeline_mode=pl.Buffered(1)), rows(D)],
            out_specs=[rows(D), rows(D), rows(D), rows(1), rows(1)],
        ),
        out_shape=[
            struct((T, D), BF),
            struct((T, D), F32),
            struct((T, D), BF),
            struct((T, 1), F32),
            struct((T, 1), F32),
        ],
        compiler_params=params(),
        cost_estimate=cost(2 * T * D * D, 32 * MIB),
        name="project_and_norm",
    )(place, *pieces, w_out, x_full)


def hidden_kernel(b_ref, dy_ref, wg_ref, wu_ref, wd_ref, hm_ref, dg_ref, du_ref):
    b = b_ref[...]
    gate = dot_nn(b, wg_ref[...])
    upward = dot_nn(b, wu_ref[...])
    grad_hidden = dot_nn(dy_ref[...], wd_ref[...])
    sigmoid = jax.nn.sigmoid(gate)
    silu = gate * sigmoid
    hm_ref[...] = (silu * upward).astype(BF)
    dg_ref[...] = (grad_hidden * upward * sigmoid * (1.0 + gate * (1.0 - sigmoid))).astype(BF)
    du_ref[...] = (grad_hidden * silu).astype(BF)


def hidden_units(b, dy, w_gate, w_up, w_down):
    T, D = b.shape
    F = w_gate.shape[1]
    bt, bf = 512, 512
    left = pl.BlockSpec((bt, D), lambda j, i: (i, 0))
    right = pl.BlockSpec((D, bf), lambda j, i: (0, j))
    out = pl.BlockSpec((bt, bf), lambda j, i: (i, j))
    return pl.pallas_call(
        hidden_kernel,
        grid=(F // bf, T // bt),
        in_specs=[left, left, right, right, right],
        out_specs=[out, out, out],
        out_shape=[struct((T, F), BF)] * 3,
        compiler_params=params(),
        cost_estimate=cost(6 * T * D * F, 60 * MIB),
        name="hidden_units",
    )(b, dy, w_gate, w_up, w_down)


def sum_nt_kernel(pairs, *refs):
    total = dot_nt(refs[0][...], refs[pairs][...])
    for k in range(1, pairs):
        total += dot_nt(refs[k][...], refs[pairs + k][...])
    refs[-1][...] = total.astype(refs[-1].dtype)


def sum_nt(lefts, rights, name):
    T = lefts[0].shape[0]
    N = rights[0].shape[0]
    bt, bn = 512, 512
    deep = sum(left.shape[1] for left in lefts)
    return pl.pallas_call(
        functools.partial(sum_nt_kernel, len(lefts)),
        grid=(N // bn, T // bt),
        in_specs=[pl.BlockSpec((bt, left.shape[1]), lambda j, i: (i, 0)) for left in lefts]
        + [pl.BlockSpec((bn, right.shape[1]), lambda j, i: (j, 0)) for right in rights],
        out_specs=pl.BlockSpec((bt, bn), lambda j, i: (i, j)),
        out_shape=struct((T, N), BF),
        compiler_params=params(),
        cost_estimate=cost(2 * T * N * deep, 40 * MIB),
        name=name,
    )(*lefts, *rights)


def resid_back_kernel(C, place, *refs):
    terms = refs[:C]
    h_ref, mu_ref, r_ref, dy_ref, w_ref, dh_ref, do_ref = refs[C:]

    @pl.when(pl.program_id(0) == 0)
    def _():
        grad = terms[0][...].astype(F32)
        for k in range(1, C):
            grad += terms[k][...].astype(F32)
        inverse = r_ref[...]
        normed = (h_ref[...] - mu_ref[...]) * inverse
        first = jnp.mean(grad, axis=1, keepdims=True)
        second = jnp.mean(grad * normed, axis=1, keepdims=True)
        dh = dy_ref[...].astype(F32) + inverse * (grad - first - normed * second)
        dh_ref[...] = dh.astype(BF)

    part = w_ref.shape[2]
    total = dot_nt(dh_ref[:, :part], w_ref[0])
    for n in range(1, w_ref.shape[0]):
        total += dot_nt(dh_ref[:, n * part : (n + 1) * part], w_ref[n])
    do_ref[...] = total.astype(BF)


def resid_back(place, terms, h, mu, r, dy, w_out):
    C = len(terms)
    rows, D = terms[0].shape
    bn = 512
    whole = pl.BlockSpec((rows, D), lambda j, p: (0, 0))
    mine = lambda n: pl.BlockSpec((rows, n), lambda j, p: (p[0], 0))
    return pl.pallas_call(
        functools.partial(resid_back_kernel, C),
        grid_spec=pltpu.PrefetchScalarGridSpec(
            num_scalar_prefetch=1,
            grid=(D // bn,),
            in_specs=[whole] * C
            + [
                mine(D),
                mine(1),
                mine(1),
                mine(D),
                pl.BlockSpec((w_out.shape[0], bn, w_out.shape[2]), lambda j, p: (0, j, 0)),
            ],
            out_specs=[whole, pl.BlockSpec((rows, bn), lambda j, p: (0, j))],
        ),
        out_shape=[struct((rows, D), BF), struct((rows, D), BF)],
        compiler_params=params(),
        cost_estimate=cost(2 * rows * D * D, 20 * MIB),
        name="resid_back",
    )(place, *terms, h, mu, r, dy, w_out)


def on_device(R, C, tokens, cotangent, segments, w_query, w_key, w_value, w_out, w_gate, w_up, w_down):
    T, width = tokens.shape
    D = width * C
    rows = T // C
    me = lax.axis_index("col")
    place = me.astype(jnp.int32).reshape(1)

    def shift(values, k):
        return lax.ppermute(values, "col", [(i, (i + k) % C) for i in range(C)])

    def pieces_of(values):
        return [values] + [shift(values, k) for k in range(1, C)]

    def block(values, k, axis):
        size = values.shape[axis] // C
        return lax.dynamic_slice_in_dim(values, lax.rem(me + k, C) * size, size, axis)

    def scattered(values, axis):
        return [block(values, 0, axis)] + [shift(block(values, k, axis), k) for k in range(1, C)]

    def assembled(pieces, axis):
        shape = list(pieces[0].shape)
        size = shape[axis]
        shape[axis] = size * C
        whole = jnp.zeros(shape, pieces[0].dtype)
        for k, piece in enumerate(pieces):
            whole = lax.dynamic_update_slice_in_dim(whole, piece, lax.rem(me - k + C, C) * size, axis)
        return whole

    def total_of(terms):
        total = terms[0].astype(F32)
        for term in terms[1:]:
            total = total + term.astype(F32)
        return total

    gathered = lambda w: lax.all_gather(w, "row", axis=0, tiled=True)

    x_pieces = pieces_of(tokens)
    w_qkv = gathered(jnp.concatenate([w_query, w_key, w_value], axis=1))
    cos_table, sin_table = rope_tables(segments)
    seg_column, seg_row = segments.reshape(T, 1), segments.reshape(-1, 1, SEQ)
    x_full, act_one, q, k, v, mu_one, r_one = norm_and_project(place, x_pieces, w_qkv, cos_table, sin_table)
    out_w = lax.all_gather(assembled(pieces_of(w_out), 0), "row", axis=0, tiled=False)
    gate_w, up_w, down_w = gathered(w_gate), gathered(w_up), gathered(w_down.T)
    attended, log_total = attend(q, k, v, seg_column, seg_row)
    o_full, h_full, act_two, mu_two, r_two = project_and_norm(place, pieces_of(attended), out_w, x_full)
    dy_full = assembled(pieces_of(cotangent), 1)
    hidden, grad_gate_in, grad_up_in = hidden_units(act_two, dy_full, gate_w, up_w, down_w)
    norm_terms = sum_nt([grad_gate_in, grad_up_in], [gate_w, up_w], "norm_terms")
    term_list = scattered(norm_terms, 0)
    grad_down = dot_tn(dy_full, hidden).astype(BF)
    grad_gate = dot_tn(act_two, grad_gate_in).astype(BF)
    grad_up = dot_tn(act_two, grad_up_in).astype(BF)
    out_terms = sum_nt([hidden], [down_w], "out_terms")
    scatter = lambda g: lax.psum_scatter(g, "row", scatter_dimension=0, tiled=True)
    grad_down, grad_gate, grad_up = scatter(grad_down), scatter(grad_gate), scatter(grad_up)

    grad_resid_r, grad_attn = resid_back(place, term_list, h_full, mu_two, r_two, dy_full, out_w)
    both = scattered(jnp.stack([grad_attn, grad_resid_r]), 2)
    whole = assembled(both, 1)
    grad_heads, grad_resid = whole[0], whole[1]
    my_heads = lax.dynamic_slice_in_dim(o_full, me * rows, rows, 0)
    grad_out = scatter(dot_tn(grad_resid_r, my_heads).astype(BF))
    grad_out = total_of(scattered(grad_out, 1)).T

    out_sum = total_of(scattered(out_terms, 1))
    output = (lax.dynamic_slice_in_dim(h_full, me * width, width, 1) + out_sum).astype(BF)

    dq, dk, dv = attend_back(q, k, v, grad_heads, log_total, seg_column, seg_row, cos_table, sin_table)
    w_list = [w_qkv[:, i * width : (i + 1) * width] for i in range(3)]
    input_terms = sum_nt([dq, dk, dv], w_list, "input_terms")
    grad_input = total_of(scattered(input_terms, 1))
    grad_qkv = scatter(dot_tn(act_one, jnp.concatenate([dq, dk, dv], axis=1)).astype(BF)).astype(F32)
    normed = (tokens.astype(F32) - mu_one) * r_one
    sums = lax.psum(jnp.stack([jnp.sum(grad_input, axis=1), jnp.sum(grad_input * normed, axis=1)]), "col")
    grad_tokens = grad_resid.astype(F32) + r_one * (
        grad_input - (sums[0] / D)[:, None] - normed * (sums[1] / D)[:, None]
    )
    return (
        output,
        grad_tokens.astype(BF),
        grad_qkv[:, :width],
        grad_qkv[:, width : 2 * width],
        grad_qkv[:, 2 * width :],
        grad_out,
        grad_gate.astype(F32),
        grad_up.astype(F32),
        grad_down.astype(F32).T,
    )


def solution(mesh):
    here = P("row", "col")
    turned = P("col", "row")
    return jax.shard_map(
        functools.partial(on_device, mesh.shape["row"], mesh.shape["col"]),
        mesh=mesh,
        in_specs=(here, here, P("row"), here, here, here, turned, here, here, turned),
        out_specs=(here, here, here, here, here, turned, here, here, turned),
        check_vma=False,
    )
```

```python
import functools

import jax
import jax.numpy as jnp
from jax import lax
from jax.experimental import pallas as pl
from jax.experimental.pallas import tpu as pltpu
from jax.sharding import PartitionSpec as P

HEAD_DIM = 128
HALF = HEAD_DIM // 2
SEQ = 1024
EPSILON = 1e-05
MASKED = -1e30
SCALE = HEAD_DIM ** (-0.5)
BF = jnp.bfloat16
F32 = jnp.float32
MIB = 1 << 20
ANY = pl.BlockSpec(memory_space=pl.ANY)


def dot_nn(left, right):
    return jnp.dot(left, right, preferred_element_type=F32)


def dot_tn(left, right):
    return lax.dot_general(left, right, (((0,), (0,)), ((), ())), preferred_element_type=F32)


def dot_nt(left, right):
    return lax.dot_general(left, right, (((1,), (1,)), ((), ())), preferred_element_type=F32)


def struct(shape, dtype):
    return jax.ShapeDtypeStruct(shape, dtype)


def params(mib=60):
    return pltpu.CompilerParams(vmem_limit_bytes=mib * MIB)


def cost(flops, moved):
    return pl.CostEstimate(flops=int(flops), bytes_accessed=int(moved), transcendentals=0)


def count_seen(segment_ids):
    places = jnp.arange(segment_ids.shape[0], dtype=jnp.int32)
    causal = places[None, :] <= places[:, None]
    allowed = (segment_ids[:, None] == segment_ids[None, :]) & causal
    return jnp.sum(allowed.astype(jnp.int32), axis=1) - 1


def rope_tables(segments):
    positions = jax.vmap(count_seen)(segments.reshape(-1, SEQ)).reshape(-1)
    inverse = 10000.0 ** (-(jnp.arange(HALF, dtype=F32) * 2.0 / HEAD_DIM))
    angles = positions.astype(F32)[:, None] * inverse[None, :]
    cosine, sine = jnp.cos(angles), jnp.sin(angles)
    return jnp.concatenate([cosine, cosine], 1), jnp.concatenate([-sine, sine], 1)


def turn(values, cos_table, sin_table):
    return values * cos_table + pltpu.roll(values, HALF, 1) * sin_table


MESH = pl.DeviceIdType.MESH
VMEM_SPEC = pl.BlockSpec(memory_space=pltpu.VMEM)
DMA = pltpu.SemaphoreType.DMA


def comm_params(number, mib=60):
    return pltpu.CompilerParams(vmem_limit_bytes=mib * MIB, collective_id=number, has_side_effects=True)


def remote(source, target, send, recv, **device):
    return pltpu.make_async_remote_copy(
        src_ref=source, dst_ref=target, send_sem=send, recv_sem=recv, device_id=device, device_id_type=MESH
    )


def greet(senders, targets):
    semaphore = pltpu.get_barrier_semaphore()
    for device in senders:
        pl.semaphore_signal(semaphore, inc=1, device_id=device, device_id_type=MESH)
    pl.semaphore_wait(semaphore, targets)


def ring_places(C):
    me = lax.axis_index("col")
    return me, lax.rem(me + 1, C), lax.rem(me + C - 1, C)


def row_places(R):
    row = lax.axis_index("row")
    ahead = [lax.rem(row + 2 * k, R) for k in range(R // 2)]
    behind = [lax.rem(row + R - 2 * k, R) for k in range(R // 2)]
    other = row + 1 - 2 * lax.rem(row, 2)
    return row, ahead, behind, other


def gather_kernel(
    R, C, x_ref, wo_ref, wq_ref, wk_ref, wv_ref, xs_ref, wos_ref, w_ref,
    local, x_send, x_recv, o_send, o_recv, w_send, w_recv, f_send, f_recv,
):
    me, right, left = ring_places(C)
    row, ahead, behind, other = row_places(R)
    weights = (wq_ref, wk_ref, wv_ref)
    mine = [
        pltpu.make_async_copy(x_ref, xs_ref.at[me], local.at[0]),
        pltpu.make_async_copy(wo_ref, wos_ref.at[me], local.at[1]),
    ] + [pltpu.make_async_copy(w, w_ref.at[i, row], local.at[2 + i]) for i, w in enumerate(weights)]
    for copy in mine:
        copy.start()
    greet(
        [{"col": left}, {"row": other}] + [{"row": r} for r in behind[1:]],
        1 + R // 2,
    )

    def ring(source, whole, send, recv, step):
        owner = lax.rem(me - step + C, C)
        piece = source if step == 0 else whole.at[owner]
        return remote(piece, whole.at[owner], send.at[step], recv.at[step], col=right)

    x_copies = [ring(x_ref, xs_ref, x_send, x_recv, s) for s in range(C - 1)]
    o_copies = [ring(wo_ref, wos_ref, o_send, o_recv, s) for s in range(C - 1)]
    x_copies[0].start()
    o_copies[0].start()
    spread, forward = [], []
    for i, w in enumerate(weights):
        for k in range(1, R // 2):
            copy = remote(w, w_ref.at[i, row], w_send.at[i, k], w_recv.at[i, k], row=ahead[k])
            copy.start()
            spread.append(copy)
        copy = remote(w, w_ref.at[i, row], f_send.at[i, 0], f_recv.at[i, 0], row=other)
        copy.start()
        forward.append(copy)
    for s in range(1, C - 1):
        x_copies[s - 1].wait_recv()
        x_copies[s].start()
        o_copies[s - 1].wait_recv()
        o_copies[s].start()
    for i in range(3):
        for k in range(1, R // 2):
            spread[i * (R // 2 - 1) + k - 1].wait_recv()
            block = w_ref.at[i, behind[k]]
            copy = remote(block, block, f_send.at[i, k], f_recv.at[i, k], row=other)
            copy.start()
            forward.append(copy)
    x_copies[-1].wait_recv()
    o_copies[-1].wait_recv()
    for copy in forward:
        copy.wait_recv()
    for copy in x_copies + o_copies + spread + forward:
        copy.wait_send()
    for copy in mine:
        copy.wait()


def first_gather(R, C, tokens, w_out, w_query, w_key, w_value):
    depth, width = w_query.shape
    half = R // 2
    return pl.pallas_call(
        functools.partial(gather_kernel, R, C),
        in_specs=[ANY] * 5,
        out_specs=[ANY] * 3,
        out_shape=[
            struct((C,) + tokens.shape, BF),
            struct((C,) + w_out.shape, BF),
            struct((3, R, depth, width), BF),
        ],
        scratch_shapes=[
            DMA((5,)),
            DMA((C - 1,)),
            DMA((C - 1,)),
            DMA((C - 1,)),
            DMA((C - 1,)),
            DMA((3, half)),
            DMA((3, half)),
            DMA((3, half)),
            DMA((3, half)),
        ],
        compiler_params=comm_params(0),
        cost_estimate=cost(6e10, 14 * MIB),
        name="first_gather",
    )(tokens, w_out, w_query, w_key, w_value)


def norm_rows(x):
    centre = jnp.mean(x, axis=-1, keepdims=True)
    spread = jnp.mean(x * x, axis=-1, keepdims=True) - centre * centre
    inverse = lax.rsqrt(spread + EPSILON)
    return centre, inverse


def beside(ref):
    return jnp.concatenate([ref[j] for j in range(ref.shape[0])], axis=1)


def qkv_kernel(xs_ref, w_ref, cos_ref, sin_ref, a_ref, q_ref, k_ref, v_ref, mu_ref, r_ref):
    x = beside(xs_ref).astype(F32)
    centre, inverse = norm_rows(x)
    a = ((x - centre) * inverse).astype(BF)
    a_ref[...] = a
    mu_ref[...] = centre
    r_ref[...] = inverse
    cosine, sine = cos_ref[...], sin_ref[...]
    for index, out in enumerate((q_ref, k_ref, v_ref)):
        product = dot_nn(a, w_ref[index])
        if index == 2:
            out[...] = product.astype(BF)
            continue
        for start in range(0, out.shape[1], HEAD_DIM):
            part = product[:, start : start + HEAD_DIM]
            out[:, start : start + HEAD_DIM] = turn(part, cosine, sine).astype(BF)


def norm_and_project(xs, w_qkv, cos_table, sin_table):
    C, T, width = xs.shape
    D = width * C
    bt = 256
    rows = lambda n: pl.BlockSpec((bt, n), lambda i: (i, 0))
    return pl.pallas_call(
        qkv_kernel,
        grid=(T // bt,),
        in_specs=[
            pl.BlockSpec((C, bt, width), lambda i: (0, i, 0)),
            pl.BlockSpec(w_qkv.shape, lambda i: (0, 0, 0), pipeline_mode=pl.Buffered(1)),
            rows(HEAD_DIM),
            rows(HEAD_DIM),
        ],
        out_specs=[rows(D), rows(width), rows(width), rows(width), rows(1), rows(1)],
        out_shape=[
            struct((T, D), BF),
            struct((T, width), BF),
            struct((T, width), BF),
            struct((T, width), BF),
            struct((T, 1), F32),
            struct((T, 1), F32),
        ],
        compiler_params=params(),
        cost_estimate=cost(2 * T * D * 3 * width, 14 * MIB),
        name="norm_and_project",
    )(xs, w_qkv, cos_table, sin_table)


def allowed_block(seg_key, seg_query, first_query):
    shape = (seg_key.shape[0], seg_query.shape[1])
    keys = lax.broadcasted_iota(jnp.int32, shape, 0)
    queries = lax.broadcasted_iota(jnp.int32, shape, 1) + first_query
    return (seg_key == seg_query) & (keys <= queries)


def attend_kernel(
    R, C, q_ref, k_ref, v_ref, segk_ref, segq_ref, wos_ref, os_ref, log_ref, w_ref,
    o_buf, local, o_send, o_recv, w_send, w_recv, f_send, f_recv,
):
    me, right, left = ring_places(C)
    row, ahead, behind, other = row_places(R)
    T, width = q_ref.shape
    heads, bq = width // HEAD_DIM, 256
    greet([{"col": left}, {"row": other}] + [{"row": r} for r in behind[1:]], 1 + R // 2)
    mine = pltpu.make_async_copy(wos_ref, w_ref.at[row], local.at[0])
    mine.start()
    spread, forward = [], []
    for k in range(1, R // 2):
        copy = remote(wos_ref, w_ref.at[row], w_send.at[k], w_recv.at[k], row=ahead[k])
        copy.start()
        spread.append(copy)
    copy = remote(wos_ref, w_ref.at[row], f_send.at[0], f_recv.at[0], row=other)
    copy.start()
    forward.append(copy)

    def ring(step, head):
        owner = lax.rem(me - step + C, C)
        piece = o_buf.at[head] if step == 0 else os_ref.at[owner, head]
        return remote(piece, os_ref.at[owner, head], o_send.at[step, head], o_recv.at[step, head], col=right)

    def one_head(head, carry):
        columns = pl.ds(pl.multiple_of(head * HEAD_DIM, HEAD_DIM), HEAD_DIM)
        for first in range(0, T, SEQ):
            for start in range(first, first + SEQ, bq):
                stop = start + bq
                scores = dot_nt(k_ref[first:stop, columns], q_ref[start:stop, columns]) * SCALE
                allowed = allowed_block(segk_ref[first:stop], segq_ref[:, start:stop], start - first)
                scores = jnp.where(allowed, scores, MASKED)
                peak = jnp.max(scores, axis=0, keepdims=True)
                exponent = jnp.exp(scores - peak)
                total = jnp.sum(exponent, axis=0, keepdims=True)
                weights = (exponent * (1.0 / total)).astype(BF)
                o_buf[head, start:stop] = dot_tn(v_ref[first:stop, columns], weights).T.astype(BF)
                log_ref[head, :, start:stop] = peak + jnp.log(total)
        ring(0, head).start()
        pltpu.make_async_copy(o_buf.at[head], os_ref.at[me, head], local.at[1 + head]).start()
        return carry

    lax.fori_loop(0, heads, one_head, 0)
    for step in range(1, C - 1):
        for head in range(heads):
            ring(step - 1, head).wait_recv()
            ring(step, head).start()
    for k in range(1, R // 2):
        spread[k - 1].wait_recv()
        block = w_ref.at[behind[k]]
        copy = remote(block, block, f_send.at[k], f_recv.at[k], row=other)
        copy.start()
        forward.append(copy)
    for head in range(heads):
        ring(C - 2, head).wait_recv()
        pltpu.make_async_copy(o_buf.at[head], os_ref.at[me, head], local.at[1 + head]).wait()
        for step in range(C - 1):
            ring(step, head).wait_send()
    for copy in forward:
        copy.wait_recv()
    for copy in spread + forward:
        copy.wait_send()
    mine.wait()


def attend(R, C, q, k, v, seg_column, seg_row, w_part):
    T, width = q.shape
    heads, half = width // HEAD_DIM, R // 2
    return pl.pallas_call(
        functools.partial(attend_kernel, R, C),
        in_specs=[VMEM_SPEC] * 5 + [ANY],
        out_specs=[ANY, VMEM_SPEC, ANY],
        out_shape=[
            struct((C, heads, T, HEAD_DIM), BF),
            struct((heads, 1, T), F32),
            struct((R,) + w_part.shape, BF),
        ],
        scratch_shapes=[
            pltpu.VMEM((heads, T, HEAD_DIM), BF),
            DMA((1 + heads,)),
            DMA((C - 1, heads)),
            DMA((C - 1, heads)),
            DMA((half,)),
            DMA((half,)),
            DMA((half,)),
            DMA((half,)),
        ],
        compiler_params=comm_params(1),
        cost_estimate=cost(7e10, 14 * MIB),
        name="attend",
    )(q, k, v, seg_column, seg_row, w_part)


def feed_kernel(
    C, tiles, os_ref, w_ref, xs_ref, wg_ref, wu_ref, dy_ref,
    h_ref, b_ref, mu_ref, r_ref, hm_ref, slope_ref, silu_ref, dys_ref, normed, local, send, recv,
):
    step = pl.program_id(0)
    me, right, left = ring_places(C)

    def ring(s):
        owner = lax.rem(me - s + C, C)
        piece = dy_ref if s == 0 else dys_ref.at[owner]
        return remote(piece, dys_ref.at[owner], send.at[s], recv.at[s], col=right)

    mine = pltpu.make_async_copy(dy_ref, dys_ref.at[me], local.at[0])
    steps = pl.num_programs(0)

    @pl.when(step == 0)
    def _():
        mine.start()
        greet([{"col": left}], 1)
        ring(0).start()

    for s in range(1, C - 1):

        @pl.when(step == min(tiles + s, tiles + 3))
        def _():
            ring(s - 1).wait_recv()
            ring(s).start()

    @pl.when(step < tiles)
    def _():
        size = h_ref.shape[0]
        blocks, part = w_ref.shape[0], w_ref.shape[2]
        heads = jnp.concatenate(
            [os_ref[j, h] for j in range(os_ref.shape[0]) for h in range(os_ref.shape[1])], axis=1
        )
        x = beside(xs_ref)
        for n in range(blocks):
            columns = slice(n * part, (n + 1) * part)
            h_ref[:, columns] = x[:, columns].astype(F32) + dot_nn(heads, w_ref[n])
        h = h_ref[...]
        centre, inverse = norm_rows(h)
        b = ((h - centre) * inverse).astype(BF)
        b_ref[...] = b
        normed[pl.ds(pl.multiple_of(step * size, size), size), :] = b
        mu_ref[...] = centre
        r_ref[...] = inverse

    @pl.when(step >= tiles)
    def _():
        b = normed[...]
        gate = dot_nn(b, wg_ref[...])
        upward = dot_nn(b, wu_ref[...])
        sigmoid = jax.nn.sigmoid(gate)
        silu = gate * sigmoid
        hm_ref[...] = (silu * upward).astype(BF)
        slope_ref[...] = (upward * sigmoid * (1.0 + gate * (1.0 - sigmoid))).astype(BF)
        silu_ref[...] = silu.astype(BF)

    @pl.when(step == steps - 1)
    def _():
        ring(C - 2).wait_recv()
        for s in range(C - 1):
            ring(s).wait_send()
        mine.wait()


def feed_forward(C, os, w_out, xs, w_gate, w_up, cotangent):
    heads, T = os.shape[1], os.shape[2]
    width = xs.shape[2]
    D, F = w_gate.shape
    bt = 256
    bf = F // 4
    tiles = T // bt
    early = lambda i: jnp.minimum(i, tiles - 1)
    late = lambda i: jnp.maximum(i - tiles, 0)
    rows = lambda n: pl.BlockSpec((bt, n), lambda i: (early(i), 0))
    tile = pl.BlockSpec((T, bf), lambda i: (0, late(i)))
    weight = pl.BlockSpec((D, bf), lambda i: (0, late(i)))
    return pl.pallas_call(
        functools.partial(feed_kernel, C, tiles),
        grid=(tiles + F // bf,),
        in_specs=[
            pl.BlockSpec((C, heads, bt, HEAD_DIM), lambda i: (0, 0, early(i), 0)),
            pl.BlockSpec(w_out.shape, lambda i: (0, 0, 0), pipeline_mode=pl.Buffered(1)),
            pl.BlockSpec((C, bt, width), lambda i: (0, early(i), 0)),
            weight,
            weight,
            ANY,
        ],
        out_specs=[rows(D), rows(D), rows(1), rows(1), tile, tile, tile, ANY],
        out_shape=[
            struct((T, D), F32),
            struct((T, D), BF),
            struct((T, 1), F32),
            struct((T, 1), F32),
            struct((T, F), BF),
            struct((T, F), BF),
            struct((T, F), BF),
            struct((C, T, width), BF),
        ],
        scratch_shapes=[pltpu.VMEM((T, D), BF), DMA((1,)), DMA((C - 1,)), DMA((C - 1,))],
        compiler_params=comm_params(2),
        cost_estimate=cost(7e10, 60 * MIB),
        name="feed_forward",
    )(os, w_out, xs, w_gate, w_up, cotangent)


def hidden_back_kernel(dys_ref, wd_ref, slope_ref, silu_ref, dg_ref, du_ref, dy):
    @pl.when(pl.program_id(0) == 0)
    def _():
        width = dys_ref.shape[2]
        for j in range(dys_ref.shape[0]):
            dy[:, j * width : (j + 1) * width] = dys_ref[j]

    grad_hidden = dot_nn(dy[...], wd_ref[...])
    dg_ref[...] = (grad_hidden * slope_ref[...].astype(F32)).astype(BF)
    du_ref[...] = (grad_hidden * silu_ref[...].astype(F32)).astype(BF)


def hidden_back(dys, w_down, slope, silu):
    C, T, width = dys.shape
    D, F = w_down.shape
    bf = F // 4
    tile = pl.BlockSpec((T, bf), lambda j: (0, j))
    return pl.pallas_call(
        hidden_back_kernel,
        grid=(F // bf,),
        in_specs=[
            pl.BlockSpec(dys.shape, lambda j: (0, 0, 0), pipeline_mode=pl.Buffered(1)),
            pl.BlockSpec((D, bf), lambda j: (0, j)),
            tile,
            tile,
        ],
        out_specs=[tile, tile],
        out_shape=[struct((T, F), BF)] * 2,
        scratch_shapes=[pltpu.VMEM((T, D), BF)],
        compiler_params=params(),
        cost_estimate=cost(2 * T * D * F, 28 * MIB),
        name="hidden_back",
    )(dys, w_down, slope, silu)


def ring_step(step, C, right, first, held, send, recv):
    source = first if step == 0 else held.at[step - 1]
    return remote(source, held.at[step], send.at[step], recv.at[step], col=right)


def add_into(held, terms):
    size = 64

    def body(i, carry):
        rows = pl.ds(pl.multiple_of(i * size, size), size)
        held[rows, :] = (held[rows, :].astype(F32) + terms[rows, :].astype(F32)).astype(BF)
        return carry

    lax.fori_loop(0, held.shape[0] // size, body, 0)


def norm_terms_kernel(
    C, dg_hbm, du_hbm, hm_hbm, wg_hbm, wu_hbm, wd_hbm, b_hbm, dys_hbm,
    sum_ref, gate_hbm, up_hbm, down_hbm, out_hbm,
    dg, du, hm, wg, wu, b, dys, terms, held, stage, load, tile_load, store, send, recv,
):
    me, right, left = ring_places(C)
    D, F = wg.shape
    T = dg.shape[0]
    rows = T // C
    width = D // C
    loads = []

    def fetch(source, target, semaphore):
        copy = pltpu.make_async_copy(source, target, semaphore)
        copy.start()
        return copy

    def chunk(s):
        return pl.ds(pl.multiple_of(lax.rem(me + 2 * C - 1 - s, C) * rows, rows), rows)

    grads_in = []
    for s in range(C):
        part = chunk(s)
        grads_in.append(
            (fetch(dg_hbm.at[part, :], dg.at[part, :], load.at[2 * s]), fetch(du_hbm.at[part, :], du.at[part, :], load.at[2 * s + 1]))
        )
        if s == 0:
            weights_in = []
            for n in range(C):
                cut = pl.ds(n * width, width)
                weights_in.append(
                    (fetch(wg_hbm.at[cut, :], wg.at[cut, :], tile_load.at[2 * n]), fetch(wu_hbm.at[cut, :], wu.at[cut, :], tile_load.at[2 * n + 1]))
                )
    late = [
        fetch(b_hbm, b, load.at[2 * C]),
        fetch(hm_hbm, hm, load.at[2 * C + 1]),
        fetch(dys_hbm, dys, load.at[2 * C + 2]),
    ]
    greet([{"col": left}], 1)

    def term_tile(s, part, n):
        cut = pl.ds(pl.multiple_of(n * width, width), width)
        total = dot_nt(dg[part, :], wg[cut, :]) + dot_nt(du[part, :], wu[cut, :])
        terms[s, :, cut] = total.astype(BF)

    def moves(step):
        return ring_step(step, C, right, terms.at[0], held, send, recv)

    def pass_on(step):
        moves(step - 1).wait_recv()
        add_into(held.at[step - 1], terms.at[step])
        moves(step).start()

    for s in range(C):
        part = chunk(s)
        for copy in grads_in[s]:
            copy.wait()
        if s == 0:
            for n in range(C):
                for copy in weights_in[n]:
                    copy.wait()
                term_tile(s, part, n)
            moves(0).start()
        else:

            def body(n, carry):
                term_tile(s, part, n)
                return carry

            lax.fori_loop(0, C, body, 0)
    down_in = fetch(wd_hbm, wg, tile_load.at[0])
    for copy in late:
        copy.wait()

    def stored(target, t, slot):
        cut = pl.ds(pl.multiple_of(t * width, width), width)
        return pltpu.make_async_copy(stage.at[slot], target.at[cut, :], store.at[slot])

    def product(left_of, right_ref, target):
        def body(t, carry):
            slot = lax.rem(t, 2)

            @pl.when(t >= 2)
            def _():
                stored(target, t, slot).wait()

            stage[slot] = dot_tn(left_of(t), right_ref[...]).astype(BF)
            stored(target, t, slot).start()
            return carry

        lax.fori_loop(0, C, body, 0)
        for slot in range(2):
            stored(target, slot, slot).wait()

    def b_tile(t):
        return b[:, pl.ds(pl.multiple_of(t * width, width), width)]

    middle = max(1, (C - 1) // 2)
    product(b_tile, dg, gate_hbm)
    for step in range(1, middle + 1):
        if step < C - 1:
            pass_on(step)
    product(b_tile, du, up_hbm)
    product(lambda t: dys[t], hm, down_hbm)
    for step in range(middle + 1, C - 1):
        pass_on(step)
    down_in.wait()

    def out_tile(n, carry):
        cut = pl.ds(pl.multiple_of(n * width, width), width)
        terms_out = dot_nt(hm[...], wg[cut, :]).astype(BF)
        dys[0] = terms_out
        copy = pltpu.make_async_copy(dys.at[0], out_hbm.at[n], store.at[0])
        copy.start()
        copy.wait()
        return carry

    lax.fori_loop(0, C, out_tile, 0)
    moves(C - 2).wait_recv()
    sum_ref[...] = held[C - 2].astype(F32) + terms[C - 1].astype(F32)
    for step in range(C - 1):
        moves(step).wait_send()


def norm_terms(C, dg, du, hm, w_gate, w_up, w_down, b, dys):
    T, F = dg.shape
    D = w_gate.shape[0]
    rows, width = T // C, D // C
    return pl.pallas_call(
        functools.partial(norm_terms_kernel, C),
        in_specs=[ANY] * 8,
        out_specs=[VMEM_SPEC, ANY, ANY, ANY, ANY],
        out_shape=[
            struct((rows, D), F32),
            struct((D, F), BF),
            struct((D, F), BF),
            struct((D, F), BF),
            struct((C, T, width), BF),
        ],
        scratch_shapes=[
            pltpu.VMEM((T, F), BF),
            pltpu.VMEM((T, F), BF),
            pltpu.VMEM((T, F), BF),
            pltpu.VMEM((D, F), BF),
            pltpu.VMEM((D, F), BF),
            pltpu.VMEM((T, D), BF),
            pltpu.VMEM((C, T, width), BF),
            pltpu.VMEM((C, rows, D), BF),
            pltpu.VMEM((C - 1, rows, D), BF),
            pltpu.VMEM((2, width, F), BF),
            DMA((2 * C + 3,)),
            DMA((2 * C,)),
            DMA((2,)),
            DMA((C - 1,)),
            DMA((C - 1,)),
        ],
        compiler_params=comm_params(3, 62),
        cost_estimate=cost(9e10, 70 * MIB),
        name="norm_terms",
    )(dg, du, hm, w_gate, w_up, w_down, b, dys)


def resid_back_kernel(
    C, sum_ref, h_ref, mu_ref, r_ref, dys_ref, w_hbm, dh_ref, do_hbm, dhs_hbm,
    w, out, load, local, h_send, h_recv, o_send, o_recv,
):
    me, right, left = ring_places(C)
    blocks, D, part = w.shape
    rows = sum_ref.shape[0]
    width = D // C
    order = [lax.rem(me + k, C) for k in range(1, C)] + [me]
    loads = []
    for k in range(C):
        cut = pl.ds(pl.multiple_of(order[k] * width, width), width)
        copy = pltpu.make_async_copy(w_hbm.at[:, cut, :], w.at[:, cut, :], load.at[k])
        copy.start()
        loads.append(copy)
    greet([{"col": lax.rem(me + k, C)} for k in range(1, C)], C - 1)
    grad = sum_ref[...]
    inverse = r_ref[...]
    normed = (h_ref[...] - mu_ref[...]) * inverse
    first = jnp.mean(grad, axis=1, keepdims=True)
    second = jnp.mean(grad * normed, axis=1, keepdims=True)
    dh = beside(dys_ref).astype(F32) + inverse * (grad - first - normed * second)
    dh_ref[...] = dh.astype(BF)
    mine = pl.ds(pl.multiple_of(me * rows, rows), rows)
    copies = []
    for k in range(C):
        cut = pl.ds(pl.multiple_of(order[k] * width, width), width)
        loads[k].wait()
        total = dot_nt(dh_ref[:, :part], w[0, cut, :])
        for n in range(1, blocks):
            total += dot_nt(dh_ref[:, n * part : (n + 1) * part], w[n, cut, :])
        out[k] = total.astype(BF)
        if k < C - 1:
            copy = remote(out.at[k], do_hbm.at[mine, :], o_send.at[k], o_recv.at[k], col=order[k])
        else:
            copy = pltpu.make_async_copy(out.at[k], do_hbm.at[mine, :], local.at[0])
        copy.start()
        copies.append(copy)
    for k in range(C):
        cut = pl.ds(pl.multiple_of(order[k] * width, width), width)
        if k < C - 1:
            copy = remote(dh_ref.at[:, cut], dhs_hbm.at[mine, :], h_send.at[k], h_recv.at[k], col=order[k])
        else:
            copy = pltpu.make_async_copy(dh_ref.at[:, cut], dhs_hbm.at[mine, :], local.at[1])
        copy.start()
        copies.append(copy)
    for copy in copies:
        copy.wait()


def resid_back(total, h, mu, r, dys, w_out):
    C, rows, width = dys.shape
    T, D = rows * C, width * C
    return pl.pallas_call(
        functools.partial(resid_back_kernel, C),
        in_specs=[VMEM_SPEC] * 5 + [ANY],
        out_specs=[VMEM_SPEC, ANY, ANY],
        out_shape=[struct((rows, D), BF), struct((T, width), BF), struct((T, width), BF)],
        scratch_shapes=[
            pltpu.VMEM(w_out.shape, BF),
            pltpu.VMEM((C, rows, width), BF),
            DMA((C,)),
            DMA((2,)),
            DMA((C - 1,)),
            DMA((C - 1,)),
            DMA((C - 1,)),
            DMA((C - 1,)),
        ],
        compiler_params=comm_params(4),
        cost_estimate=cost(4e10, 20 * MIB),
        name="resid_back",
    )(total, h, mu, r, dys, w_out)


def attend_back_kernel(
    C, q_ref, k_ref, v_ref, do_ref, log_ref, segk_ref, segq_ref, cos_ref, sin_ref, h_ref, terms,
    dq_ref, dk_ref, dv_ref, y_ref, dk_sum, dv_sum, held, send, recv,
):
    me, right, left = ring_places(C)
    T, width = q_ref.shape
    heads, bq = width // HEAD_DIM, 256
    greet([{"col": left}], 1)

    def chunk(s):
        return lax.rem(me + 2 * C - 1 - s, C)

    def moves(step):
        return ring_step(step, C, right, terms.at[chunk(0)], held, send, recv)

    moves(0).start()

    def one_head(head, carry):
        columns = pl.ds(pl.multiple_of(head * HEAD_DIM, HEAD_DIM), HEAD_DIM)
        dk_sum[...] = jnp.zeros_like(dk_sum)
        dv_sum[...] = jnp.zeros_like(dv_sum)
        for first in range(0, T, SEQ):
            for start in range(first, first + SEQ, bq):
                stop = start + bq
                keys = k_ref[first:stop, columns]
                queries = q_ref[start:stop, columns]
                grads = do_ref[start:stop, columns]
                scores = dot_nt(keys, queries) * SCALE
                allowed = allowed_block(segk_ref[first:stop], segq_ref[:, start:stop], start - first)
                scores = jnp.where(allowed, scores, MASKED)
                probs = jnp.exp(scores - log_ref[head, :, start:stop])
                dv_sum[first:stop] += dot_nn(probs.astype(BF), grads)
                grad_probs = dot_nt(v_ref[first:stop, columns], grads)
                inner = jnp.sum(probs * grad_probs, axis=0, keepdims=True)
                grad_scores = (probs * (grad_probs - inner)).astype(BF)
                dk_sum[first:stop] += dot_nn(grad_scores, queries)
                grad_query = dot_tn(keys, grad_scores).T * SCALE
                dq_ref[start:stop, columns] = turn(grad_query, cos_ref[start:stop], -sin_ref[start:stop]).astype(BF)
        dk_ref[:, columns] = turn(dk_sum[...] * SCALE, cos_ref[...], -sin_ref[...]).astype(BF)
        dv_ref[:, columns] = dv_sum[...].astype(BF)
        return carry

    lax.fori_loop(0, heads, one_head, 0)
    for step in range(1, C - 1):
        moves(step - 1).wait_recv()
        add_into(held.at[step - 1], terms.at[chunk(step)])
        moves(step).start()
    moves(C - 2).wait_recv()
    y_ref[...] = (h_ref[...] + held[C - 2].astype(F32) + terms[me].astype(F32)).astype(BF)
    for step in range(C - 1):
        moves(step).wait_send()


def attend_back(q, k, v, do, log_total, seg_column, seg_row, cos_table, sin_table, h_mine, out_terms):
    C = out_terms.shape[0]
    T, width = q.shape
    return pl.pallas_call(
        functools.partial(attend_back_kernel, C),
        in_specs=[VMEM_SPEC] * 11,
        out_specs=[VMEM_SPEC] * 4,
        out_shape=[struct((T, width), BF)] * 4,
        scratch_shapes=[
            pltpu.VMEM((T, HEAD_DIM), F32),
            pltpu.VMEM((T, HEAD_DIM), F32),
            pltpu.VMEM((C - 1, T, width), BF),
            DMA((C - 1,)),
            DMA((C - 1,)),
        ],
        compiler_params=comm_params(5),
        cost_estimate=cost(7e10, 14 * MIB),
        name="attend_back",
    )(q, k, v, do, log_total, seg_column, seg_row, cos_table, sin_table, h_mine, out_terms)


def input_terms_kernel(
    C, dq_ref, dk_ref, dv_ref, w_ref, a_ref, sum_ref, grad_hbm, terms, held, stage, store, send, recv
):
    me, right, left = ring_places(C)
    T, width = dq_ref.shape
    greet([{"col": left}], 1)
    heads = (dq_ref, dk_ref, dv_ref)

    def moves(step):
        return ring_step(step, C, right, terms.at[0], held, send, recv)

    def compute(s):
        cut = pl.ds(pl.multiple_of(lax.rem(me + 2 * C - 1 - s, C) * width, width), width)
        total = dot_nt(dq_ref[...], w_ref[0, cut, :])
        total += dot_nt(dk_ref[...], w_ref[1, cut, :])
        total += dot_nt(dv_ref[...], w_ref[2, cut, :])
        terms[s] = total.astype(BF)

    compute(0)
    moves(0).start()

    def body(s, carry):
        compute(s)
        return carry

    lax.fori_loop(1, C, body, 0)

    def stored(t, slot):
        cut = pl.ds(pl.multiple_of(t * width, width), width)
        return pltpu.make_async_copy(stage.at[slot], grad_hbm.at[cut, :], store.at[slot])

    def grad_tile(t, carry):
        slot = lax.rem(t, 2)

        @pl.when(t >= 2)
        def _():
            stored(t, slot).wait()

        left_tile = a_ref[:, pl.ds(pl.multiple_of(t * width, width), width)]
        for i in range(3):
            stage[slot, :, i * width : (i + 1) * width] = dot_tn(left_tile, heads[i][...]).astype(BF)
        stored(t, slot).start()
        return carry

    lax.fori_loop(0, C, grad_tile, 0)
    for slot in range(2):
        stored(slot, slot).wait()
    for step in range(1, C - 1):
        moves(step - 1).wait_recv()
        add_into(held.at[step - 1], terms.at[step])
        moves(step).start()
    moves(C - 2).wait_recv()
    sum_ref[...] = held[C - 2].astype(F32) + terms[C - 1].astype(F32)
    for step in range(C - 1):
        moves(step).wait_send()


def input_terms(C, dq, dk, dv, w_qkv, a):
    T, width = dq.shape
    D = w_qkv.shape[1]
    return pl.pallas_call(
        functools.partial(input_terms_kernel, C),
        in_specs=[VMEM_SPEC] * 5,
        out_specs=[VMEM_SPEC, ANY],
        out_shape=[struct((T, width), F32), struct((D, 3 * width), BF)],
        scratch_shapes=[
            pltpu.VMEM((C, T, width), BF),
            pltpu.VMEM((C - 1, T, width), BF),
            pltpu.VMEM((2, width, 3 * width), BF),
            DMA((2,)),
            DMA((C - 1,)),
            DMA((C - 1,)),
        ],
        compiler_params=comm_params(6),
        cost_estimate=cost(8e10, 20 * MIB),
        name="input_terms",
    )(dq, dk, dv, w_qkv, a)


def on_device(R, C, tokens, cotangent, segments, w_query, w_key, w_value, w_out, w_gate, w_up, w_down):
    T, width = tokens.shape
    D = width * C
    rows = T // C
    me = lax.axis_index("col")

    def shift(values, k):
        return lax.ppermute(values, "col", [(i, (i + k) % C) for i in range(C)])

    def block(values, k, axis):
        size = values.shape[axis] // C
        return lax.dynamic_slice_in_dim(values, lax.rem(me + k, C) * size, size, axis)

    def scattered(values, axis):
        return [block(values, 0, axis)] + [shift(block(values, k, axis), k) for k in range(1, C)]

    def total_of(terms):
        total = terms[0].astype(F32)
        for term in terms[1:]:
            total = total + term.astype(F32)
        return total

    gathered = lambda w: lax.all_gather(w, "row", axis=0, tiled=True)
    scatter = lambda g: lax.psum_scatter(g, "row", scatter_dimension=0, tiled=True)

    gate_w, up_w, down_w = gathered(w_gate), gathered(w_up), gathered(w_down.T)
    cos_table, sin_table = rope_tables(segments)
    seg_column, seg_row = segments.reshape(T, 1), segments.reshape(1, T)
    xs, out_part, w_qkv = first_gather(R, C, tokens, w_out, w_query, w_key, w_value)
    w_qkv = w_qkv.reshape(3, D, width)
    act_one, q, k, v, mu_one, r_one = norm_and_project(xs, w_qkv, cos_table, sin_table)
    os, log_total, out_w = attend(R, C, q, k, v, seg_column, seg_row, out_part.reshape(D, -1))
    h_full, act_two, mu_two, r_two, hidden, slope, silu, dys = feed_forward(
        C, os, out_w, xs, gate_w, up_w, cotangent
    )
    dg, du = hidden_back(dys, down_w, slope, silu)
    total, grad_gate, grad_up, grad_down, out_terms = norm_terms(
        C, dg, du, hidden, gate_w, up_w, down_w, act_two, dys
    )
    grad_down, grad_gate, grad_up = scatter(grad_down), scatter(grad_gate), scatter(grad_up)
    mine = lambda values, axis: lax.dynamic_slice_in_dim(values, me * rows, rows, axis)
    dh_rows, grad_heads, grad_resid = resid_back(
        total, mine(h_full, 0), mine(mu_two, 0), mine(r_two, 0), mine(dys, 1), out_w
    )
    my_heads = mine(os, 2).transpose(2, 0, 1, 3).reshape(rows, D)
    grad_out = scatter(dot_tn(dh_rows, my_heads).astype(BF))
    h_mine = lax.dynamic_slice_in_dim(h_full, me * width, width, 1)
    dq, dk, dv, output = attend_back(
        q, k, v, grad_heads, log_total, seg_column, seg_row, cos_table, sin_table, h_mine, out_terms
    )
    grad_input, grad_qkv = input_terms(C, dq, dk, dv, w_qkv, act_one)
    grad_qkv = scatter(grad_qkv).astype(F32)
    grad_out = total_of(scattered(grad_out, 1)).T
    normed = (tokens.astype(F32) - mu_one) * r_one
    sums = lax.psum(jnp.stack([jnp.sum(grad_input, axis=1), jnp.sum(grad_input * normed, axis=1)]), "col")
    grad_tokens = grad_resid.astype(F32) + r_one * (
        grad_input - (sums[0] / D)[:, None] - normed * (sums[1] / D)[:, None]
    )
    return (
        output,
        grad_tokens.astype(BF),
        grad_qkv[:, :width],
        grad_qkv[:, width : 2 * width],
        grad_qkv[:, 2 * width :],
        grad_out,
        grad_gate.astype(F32),
        grad_up.astype(F32),
        grad_down.astype(F32).T,
    )


def solution(mesh):
    here = P("row", "col")
    turned = P("col", "row")
    return jax.shard_map(
        functools.partial(on_device, mesh.shape["row"], mesh.shape["col"]),
        mesh=mesh,
        in_specs=(here, here, P("row"), here, here, here, turned, here, here, turned),
        out_specs=(here, here, here, here, here, turned, here, here, turned),
        check_vma=False,
    )
```

```python
import functools

import jax
import jax.numpy as jnp
from jax import lax
from jax.experimental import pallas as pl
from jax.experimental.pallas import tpu as pltpu
from jax.sharding import PartitionSpec as P

HEAD_DIM = 128
HALF = HEAD_DIM // 2
SEQ = 1024
EPSILON = 1e-05
MASKED = -1e30
SCALE = HEAD_DIM ** (-0.5)
BF = jnp.bfloat16
F32 = jnp.float32
MIB = 1 << 20
ANY = pl.BlockSpec(memory_space=pl.ANY)


def dot_nn(left, right):
    return jnp.dot(left, right, preferred_element_type=F32)


def dot_tn(left, right):
    return lax.dot_general(left, right, (((0,), (0,)), ((), ())), preferred_element_type=F32)


def dot_nt(left, right):
    return lax.dot_general(left, right, (((1,), (1,)), ((), ())), preferred_element_type=F32)


def struct(shape, dtype):
    return jax.ShapeDtypeStruct(shape, dtype)


def params(mib=60):
    return pltpu.CompilerParams(vmem_limit_bytes=mib * MIB)


def cost(flops, moved):
    return pl.CostEstimate(flops=int(flops), bytes_accessed=int(moved), transcendentals=0)


def count_seen(segment_ids):
    places = jnp.arange(segment_ids.shape[0], dtype=jnp.int32)
    causal = places[None, :] <= places[:, None]
    allowed = (segment_ids[:, None] == segment_ids[None, :]) & causal
    return jnp.sum(allowed.astype(jnp.int32), axis=1) - 1


def rope_tables(segments):
    positions = jax.vmap(count_seen)(segments.reshape(-1, SEQ)).reshape(-1)
    inverse = 10000.0 ** (-(jnp.arange(HALF, dtype=F32) * 2.0 / HEAD_DIM))
    angles = positions.astype(F32)[:, None] * inverse[None, :]
    cosine, sine = jnp.cos(angles), jnp.sin(angles)
    return jnp.concatenate([cosine, cosine], 1), jnp.concatenate([-sine, sine], 1)


def turn(values, cos_table, sin_table):
    return values * cos_table + pltpu.roll(values, HALF, 1) * sin_table


MESH = pl.DeviceIdType.MESH
VMEM_SPEC = pl.BlockSpec(memory_space=pltpu.VMEM)
DMA = pltpu.SemaphoreType.DMA


def comm_params(number, mib=60):
    return pltpu.CompilerParams(vmem_limit_bytes=mib * MIB, collective_id=number, has_side_effects=True)


def remote(source, target, send, recv, **device):
    return pltpu.make_async_remote_copy(
        src_ref=source, dst_ref=target, send_sem=send, recv_sem=recv, device_id=device, device_id_type=MESH
    )


def greet(senders, targets):
    semaphore = pltpu.get_barrier_semaphore()
    for device in senders:
        pl.semaphore_signal(semaphore, inc=1, device_id=device, device_id_type=MESH)
    pl.semaphore_wait(semaphore, targets)


def ring_places(C):
    me = lax.axis_index("col")
    return me, lax.rem(me + 1, C), lax.rem(me + C - 1, C)


def row_places(R):
    row = lax.axis_index("row")
    ahead = [lax.rem(row + 2 * k, R) for k in range(R // 2)]
    behind = [lax.rem(row + R - 2 * k, R) for k in range(R // 2)]
    other = row + 1 - 2 * lax.rem(row, 2)
    return row, ahead, behind, other


def gather_kernel(
    R, C, x_ref, wo_ref, wq_ref, wk_ref, wv_ref, xs_ref, wos_ref, w_ref,
    local, x_send, x_recv, o_send, o_recv, w_send, w_recv, f_send, f_recv,
):
    me, right, left = ring_places(C)
    row, ahead, behind, other = row_places(R)
    weights = (wq_ref, wk_ref, wv_ref)
    mine = [
        pltpu.make_async_copy(x_ref, xs_ref.at[me], local.at[0]),
        pltpu.make_async_copy(wo_ref, wos_ref.at[me], local.at[1]),
    ] + [pltpu.make_async_copy(w, w_ref.at[i, row], local.at[2 + i]) for i, w in enumerate(weights)]
    for copy in mine:
        copy.start()
    greet(
        [{"col": left}, {"row": other}] + [{"row": r} for r in behind[1:]],
        1 + R // 2,
    )

    def ring(source, whole, send, recv, step):
        owner = lax.rem(me - step + C, C)
        piece = source if step == 0 else whole.at[owner]
        return remote(piece, whole.at[owner], send.at[step], recv.at[step], col=right)

    x_copies = [ring(x_ref, xs_ref, x_send, x_recv, s) for s in range(C - 1)]
    o_copies = [ring(wo_ref, wos_ref, o_send, o_recv, s) for s in range(C - 1)]
    x_copies[0].start()
    o_copies[0].start()
    spread, forward = [], []
    for i, w in enumerate(weights):
        for k in range(1, R // 2):
            copy = remote(w, w_ref.at[i, row], w_send.at[i, k], w_recv.at[i, k], row=ahead[k])
            copy.start()
            spread.append(copy)
        copy = remote(w, w_ref.at[i, row], f_send.at[i, 0], f_recv.at[i, 0], row=other)
        copy.start()
        forward.append(copy)
    for s in range(1, C - 1):
        x_copies[s - 1].wait_recv()
        x_copies[s].start()
        o_copies[s - 1].wait_recv()
        o_copies[s].start()
    for i in range(3):
        for k in range(1, R // 2):
            spread[i * (R // 2 - 1) + k - 1].wait_recv()
            block = w_ref.at[i, behind[k]]
            copy = remote(block, block, f_send.at[i, k], f_recv.at[i, k], row=other)
            copy.start()
            forward.append(copy)
    x_copies[-1].wait_recv()
    o_copies[-1].wait_recv()
    for copy in forward:
        copy.wait_recv()
    for copy in x_copies + o_copies + spread + forward:
        copy.wait_send()
    for copy in mine:
        copy.wait()


def first_gather(R, C, tokens, w_out, w_query, w_key, w_value):
    depth, width = w_query.shape
    half = R // 2
    return pl.pallas_call(
        functools.partial(gather_kernel, R, C),
        in_specs=[ANY] * 5,
        out_specs=[ANY] * 3,
        out_shape=[
            struct((C,) + tokens.shape, BF),
            struct((C,) + w_out.shape, BF),
            struct((3, R, depth, width), BF),
        ],
        scratch_shapes=[
            DMA((5,)),
            DMA((C - 1,)),
            DMA((C - 1,)),
            DMA((C - 1,)),
            DMA((C - 1,)),
            DMA((3, half)),
            DMA((3, half)),
            DMA((3, half)),
            DMA((3, half)),
        ],
        compiler_params=comm_params(0),
        cost_estimate=cost(6e10, 14 * MIB),
        name="first_gather",
    )(tokens, w_out, w_query, w_key, w_value)


def norm_rows(x):
    centre = jnp.mean(x, axis=-1, keepdims=True)
    spread = jnp.mean(x * x, axis=-1, keepdims=True) - centre * centre
    inverse = lax.rsqrt(spread + EPSILON)
    return centre, inverse


def beside(ref):
    return jnp.concatenate([ref[j] for j in range(ref.shape[0])], axis=1)


def qkv_kernel(xs_ref, w_ref, cos_ref, sin_ref, a_ref, q_ref, k_ref, v_ref, mu_ref, r_ref):
    x = beside(xs_ref).astype(F32)
    centre, inverse = norm_rows(x)
    a = ((x - centre) * inverse).astype(BF)
    a_ref[...] = a
    mu_ref[...] = centre
    r_ref[...] = inverse
    cosine, sine = cos_ref[...], sin_ref[...]
    for index, out in enumerate((q_ref, k_ref, v_ref)):
        product = dot_nn(a, w_ref[index])
        if index == 2:
            out[...] = product.astype(BF)
            continue
        for start in range(0, out.shape[1], HEAD_DIM):
            part = product[:, start : start + HEAD_DIM]
            out[:, start : start + HEAD_DIM] = turn(part, cosine, sine).astype(BF)


def norm_and_project(xs, w_qkv, cos_table, sin_table):
    C, T, width = xs.shape
    D = width * C
    bt = 256
    rows = lambda n: pl.BlockSpec((bt, n), lambda i: (i, 0))
    return pl.pallas_call(
        qkv_kernel,
        grid=(T // bt,),
        in_specs=[
            pl.BlockSpec((C, bt, width), lambda i: (0, i, 0)),
            pl.BlockSpec(w_qkv.shape, lambda i: (0, 0, 0), pipeline_mode=pl.Buffered(1)),
            rows(HEAD_DIM),
            rows(HEAD_DIM),
        ],
        out_specs=[rows(D), rows(width), rows(width), rows(width), rows(1), rows(1)],
        out_shape=[
            struct((T, D), BF),
            struct((T, width), BF),
            struct((T, width), BF),
            struct((T, width), BF),
            struct((T, 1), F32),
            struct((T, 1), F32),
        ],
        compiler_params=params(),
        cost_estimate=cost(2 * T * D * 3 * width, 14 * MIB),
        name="norm_and_project",
    )(xs, w_qkv, cos_table, sin_table)


def allowed_block(seg_key, seg_query, first_query):
    shape = (seg_key.shape[0], seg_query.shape[1])
    keys = lax.broadcasted_iota(jnp.int32, shape, 0)
    queries = lax.broadcasted_iota(jnp.int32, shape, 1) + first_query
    return (seg_key == seg_query) & (keys <= queries)


def attend_kernel(
    R, C, q_ref, k_ref, v_ref, segk_ref, segq_ref, wos_ref, os_ref, log_ref, w_ref,
    o_buf, local, o_send, o_recv, w_send, w_recv, f_send, f_recv,
):
    me, right, left = ring_places(C)
    row, ahead, behind, other = row_places(R)
    T, width = q_ref.shape
    heads, bq = width // HEAD_DIM, 256
    greet([{"col": left}, {"row": other}] + [{"row": r} for r in behind[1:]], 1 + R // 2)
    mine = pltpu.make_async_copy(wos_ref, w_ref.at[row], local.at[0])
    mine.start()
    spread, forward = [], []
    for k in range(1, R // 2):
        copy = remote(wos_ref, w_ref.at[row], w_send.at[k], w_recv.at[k], row=ahead[k])
        copy.start()
        spread.append(copy)
    copy = remote(wos_ref, w_ref.at[row], f_send.at[0], f_recv.at[0], row=other)
    copy.start()
    forward.append(copy)

    def ring(step, head):
        owner = lax.rem(me - step + C, C)
        piece = o_buf.at[head] if step == 0 else os_ref.at[owner, head]
        return remote(piece, os_ref.at[owner, head], o_send.at[step, head], o_recv.at[step, head], col=right)

    def one_head(head, carry):
        columns = pl.ds(pl.multiple_of(head * HEAD_DIM, HEAD_DIM), HEAD_DIM)
        for first in range(0, T, SEQ):
            for start in range(first, first + SEQ, bq):
                stop = start + bq
                scores = dot_nt(k_ref[first:stop, columns], q_ref[start:stop, columns]) * SCALE
                allowed = allowed_block(segk_ref[first:stop], segq_ref[:, start:stop], start - first)
                scores = jnp.where(allowed, scores, MASKED)
                peak = jnp.max(scores, axis=0, keepdims=True)
                exponent = jnp.exp(scores - peak)
                total = jnp.sum(exponent, axis=0, keepdims=True)
                weights = (exponent * (1.0 / total)).astype(BF)
                o_buf[head, start:stop] = dot_tn(v_ref[first:stop, columns], weights).T.astype(BF)
                log_ref[head, :, start:stop] = peak + jnp.log(total)
        ring(0, head).start()
        pltpu.make_async_copy(o_buf.at[head], os_ref.at[me, head], local.at[1 + head]).start()
        return carry

    lax.fori_loop(0, heads, one_head, 0)
    for step in range(1, C - 1):
        for head in range(heads):
            ring(step - 1, head).wait_recv()
            ring(step, head).start()
    for k in range(1, R // 2):
        spread[k - 1].wait_recv()
        block = w_ref.at[behind[k]]
        copy = remote(block, block, f_send.at[k], f_recv.at[k], row=other)
        copy.start()
        forward.append(copy)
    for head in range(heads):
        ring(C - 2, head).wait_recv()
        pltpu.make_async_copy(o_buf.at[head], os_ref.at[me, head], local.at[1 + head]).wait()
        for step in range(C - 1):
            ring(step, head).wait_send()
    for copy in forward:
        copy.wait_recv()
    for copy in spread + forward:
        copy.wait_send()
    mine.wait()


def attend(R, C, q, k, v, seg_column, seg_row, w_part):
    T, width = q.shape
    heads, half = width // HEAD_DIM, R // 2
    return pl.pallas_call(
        functools.partial(attend_kernel, R, C),
        in_specs=[VMEM_SPEC] * 5 + [ANY],
        out_specs=[ANY, VMEM_SPEC, ANY],
        out_shape=[
            struct((C, heads, T, HEAD_DIM), BF),
            struct((heads, 1, T), F32),
            struct((R,) + w_part.shape, BF),
        ],
        scratch_shapes=[
            pltpu.VMEM((heads, T, HEAD_DIM), BF),
            DMA((1 + heads,)),
            DMA((C - 1, heads)),
            DMA((C - 1, heads)),
            DMA((half,)),
            DMA((half,)),
            DMA((half,)),
            DMA((half,)),
        ],
        compiler_params=comm_params(1),
        cost_estimate=cost(7e10, 14 * MIB),
        name="attend",
    )(q, k, v, seg_column, seg_row, w_part)


def feed_kernel(
    C, tiles, os_ref, w_ref, xs_ref, wg_ref, wu_ref, dy_ref,
    h_ref, b_ref, hm_ref, slope_ref, silu_ref, dys_ref, normed, local, send, recv,
):
    step = pl.program_id(0)
    me, right, left = ring_places(C)

    def ring(s):
        owner = lax.rem(me - s + C, C)
        piece = dy_ref if s == 0 else dys_ref.at[owner]
        return remote(piece, dys_ref.at[owner], send.at[s], recv.at[s], col=right)

    mine = pltpu.make_async_copy(dy_ref, dys_ref.at[me], local.at[0])
    steps = pl.num_programs(0)

    @pl.when(step == 0)
    def _():
        mine.start()
        greet([{"col": left}], 1)
        ring(0).start()

    for s in range(1, C - 1):

        @pl.when(step == min(tiles + s, tiles + 3))
        def _():
            ring(s - 1).wait_recv()
            ring(s).start()

    @pl.when(step < tiles)
    def _():
        size = h_ref.shape[0]
        blocks, part = w_ref.shape[0], w_ref.shape[2]
        heads = jnp.concatenate(
            [os_ref[j, h] for j in range(os_ref.shape[0]) for h in range(os_ref.shape[1])], axis=1
        )
        x = beside(xs_ref)
        for n in range(blocks):
            columns = slice(n * part, (n + 1) * part)
            h_ref[:, columns] = x[:, columns].astype(F32) + dot_nn(heads, w_ref[n])
        h = h_ref[...]
        centre, inverse = norm_rows(h)
        b = ((h - centre) * inverse).astype(BF)
        b_ref[...] = b
        normed[pl.ds(pl.multiple_of(step * size, size), size), :] = b

    @pl.when(step >= tiles)
    def _():
        b = normed[...]
        gate = dot_nn(b, wg_ref[...])
        upward = dot_nn(b, wu_ref[...])
        sigmoid = jax.nn.sigmoid(gate)
        silu = gate * sigmoid
        hm_ref[...] = (silu * upward).astype(BF)
        slope_ref[...] = (upward * sigmoid * (1.0 + gate * (1.0 - sigmoid))).astype(BF)
        silu_ref[...] = silu.astype(BF)

    @pl.when(step == steps - 1)
    def _():
        ring(C - 2).wait_recv()
        for s in range(C - 1):
            ring(s).wait_send()
        mine.wait()


def feed_forward(C, os, w_out, xs, w_gate, w_up, cotangent):
    heads, T = os.shape[1], os.shape[2]
    width = xs.shape[2]
    D, F = w_gate.shape
    bt = 256
    bf = F // 4
    tiles = T // bt
    early = lambda i: jnp.minimum(i, tiles - 1)
    late = lambda i: jnp.maximum(i - tiles, 0)
    rows = lambda n: pl.BlockSpec((bt, n), lambda i: (early(i), 0))
    tile = pl.BlockSpec((T, bf), lambda i: (0, late(i)))
    weight = pl.BlockSpec((D, bf), lambda i: (0, late(i)))
    return pl.pallas_call(
        functools.partial(feed_kernel, C, tiles),
        grid=(tiles + F // bf,),
        in_specs=[
            pl.BlockSpec((C, heads, bt, HEAD_DIM), lambda i: (0, 0, early(i), 0)),
            pl.BlockSpec(w_out.shape, lambda i: (0, 0, 0), pipeline_mode=pl.Buffered(1)),
            pl.BlockSpec((C, bt, width), lambda i: (0, early(i), 0)),
            weight,
            weight,
            ANY,
        ],
        out_specs=[rows(D), rows(D), tile, tile, tile, ANY],
        out_shape=[
            struct((T, D), F32),
            struct((T, D), BF),
            struct((T, F), BF),
            struct((T, F), BF),
            struct((T, F), BF),
            struct((C, T, width), BF),
        ],
        scratch_shapes=[pltpu.VMEM((T, D), BF), DMA((1,)), DMA((C - 1,)), DMA((C - 1,))],
        compiler_params=comm_params(2),
        cost_estimate=cost(7e10, 60 * MIB),
        name="feed_forward",
    )(os, w_out, xs, w_gate, w_up, cotangent)


def hidden_back_kernel(dys_ref, wd_ref, slope_ref, silu_ref, dg_ref, du_ref, dy):
    @pl.when(pl.program_id(0) == 0)
    def _():
        width = dys_ref.shape[2]
        for j in range(dys_ref.shape[0]):
            dy[:, j * width : (j + 1) * width] = dys_ref[j]

    grad_hidden = dot_nn(dy[...], wd_ref[...])
    dg_ref[...] = (grad_hidden * slope_ref[...].astype(F32)).astype(BF)
    du_ref[...] = (grad_hidden * silu_ref[...].astype(F32)).astype(BF)


def hidden_back(dys, w_down, slope, silu):
    C, T, width = dys.shape
    D, F = w_down.shape
    bf = F // 4
    tile = pl.BlockSpec((T, bf), lambda j: (0, j))
    return pl.pallas_call(
        hidden_back_kernel,
        grid=(F // bf,),
        in_specs=[
            pl.BlockSpec(dys.shape, lambda j: (0, 0, 0), pipeline_mode=pl.Buffered(1)),
            pl.BlockSpec((D, bf), lambda j: (0, j)),
            tile,
            tile,
        ],
        out_specs=[tile, tile],
        out_shape=[struct((T, F), BF)] * 2,
        scratch_shapes=[pltpu.VMEM((T, D), BF)],
        compiler_params=params(),
        cost_estimate=cost(2 * T * D * F, 28 * MIB),
        name="hidden_back",
    )(dys, w_down, slope, silu)


def ring_step(step, C, right, first, held, send, recv):
    source = first if step == 0 else held.at[step - 1]
    return remote(source, held.at[step], send.at[step], recv.at[step], col=right)


def add_into(held, terms):
    size = 64

    def body(i, carry):
        rows = pl.ds(pl.multiple_of(i * size, size), size)
        held[rows, :] = (held[rows, :].astype(F32) + terms[rows, :].astype(F32)).astype(BF)
        return carry

    lax.fori_loop(0, held.shape[0] // size, body, 0)


class RowSum:
    def __init__(self, R, own, twin, exchanged, arrived, semaphores):
        self.R, self.own, self.twin = R, own, twin
        self.exchanged, self.arrived = exchanged, arrived
        self.row, self.ahead, self.behind, self.other = row_places(R)
        self.x_send, self.x_recv, self.y_send, self.y_recv = semaphores

    def exchange(self, k):
        return remote(self.twin(k), self.exchanged.at[k], self.x_send.at[k], self.x_recv.at[k], row=self.other)

    def spread(self, k):
        return remote(self.own(k), self.arrived.at[k - 1], self.y_send.at[k], self.y_recv.at[k], row=self.ahead[k])

    def order(self):
        return list(range(1, self.R // 2)) + [0]

    def relay(self, before=None):
        for k in self.order():
            if before is not None:
                before(k)
            self.exchange(k).wait_recv()
            add_into(self.own(k), self.exchanged.at[k])
            if k:
                self.spread(k).start()

    def finish(self, target):
        for k in range(1, self.R // 2):
            self.spread(k).wait_recv()
        size = min(64, target.shape[0])

        def body(i, carry):
            rows = pl.ds(pl.multiple_of(i * size, size), size)
            total = self.own(0)[rows, :].astype(F32)
            for k in range(1, self.R // 2):
                total += self.arrived[k - 1, rows, :].astype(F32)
            target[rows, :] = total.astype(target.dtype)
            return carry

        lax.fori_loop(0, target.shape[0] // size, body, 0)
        for k in range(self.R // 2):
            self.exchange(k).wait_send()
            if k:
                self.spread(k).wait_send()


def row_sum_semaphores(R):
    return [DMA((R // 2,)) for _ in range(4)]


def held_row_sum(R, grad_hbm, own, exchanged, arrived, load, semaphores):
    row, ahead, behind, other = row_places(R)
    sums = RowSum(R, lambda k: own.at[k], lambda k: grad_hbm.at[lax.rem(other + 2 * k, R)], exchanged, arrived, semaphores)
    loads = [pltpu.make_async_copy(grad_hbm.at[ahead[k]], own.at[k], load.at[k]) for k in range(R // 2)]
    return sums, loads


def norm_terms_kernel(
    C, dg_hbm, du_hbm, hm_hbm, wg_hbm, wu_hbm, wd_hbm, b_hbm, dys_hbm,
    sum_ref, gate_hbm, up_hbm, down_hbm, out_hbm,
    dg, du, hm, wg, wu, b, dys, terms, held, stage, load, tile_load, store, send, recv,
):
    me, right, left = ring_places(C)
    D, F = wg.shape
    T = dg.shape[0]
    rows = T // C
    width = D // C
    loads = []

    def fetch(source, target, semaphore):
        copy = pltpu.make_async_copy(source, target, semaphore)
        copy.start()
        return copy

    def chunk(s):
        return pl.ds(pl.multiple_of(lax.rem(me + 2 * C - 1 - s, C) * rows, rows), rows)

    grads_in = []
    for s in range(C):
        part = chunk(s)
        grads_in.append(
            (fetch(dg_hbm.at[part, :], dg.at[part, :], load.at[2 * s]), fetch(du_hbm.at[part, :], du.at[part, :], load.at[2 * s + 1]))
        )
        if s == 0:
            weights_in = []
            for n in range(C):
                cut = pl.ds(n * width, width)
                weights_in.append(
                    (fetch(wg_hbm.at[cut, :], wg.at[cut, :], tile_load.at[2 * n]), fetch(wu_hbm.at[cut, :], wu.at[cut, :], tile_load.at[2 * n + 1]))
                )
    late = [
        fetch(b_hbm, b, load.at[2 * C]),
        fetch(hm_hbm, hm, load.at[2 * C + 1]),
        fetch(dys_hbm, dys, load.at[2 * C + 2]),
    ]
    greet([{"col": left}], 1)

    def term_tile(s, part, n):
        cut = pl.ds(pl.multiple_of(n * width, width), width)
        total = dot_nt(dg[part, :], wg[cut, :]) + dot_nt(du[part, :], wu[cut, :])
        terms[s, :, cut] = total.astype(BF)

    def moves(step):
        return ring_step(step, C, right, terms.at[0], held, send, recv)

    def pass_on(step):
        moves(step - 1).wait_recv()
        add_into(held.at[step - 1], terms.at[step])
        moves(step).start()

    for s in range(C):
        part = chunk(s)
        for copy in grads_in[s]:
            copy.wait()
        if s == 0:
            for n in range(C):
                for copy in weights_in[n]:
                    copy.wait()
                term_tile(s, part, n)
            moves(0).start()
        else:

            def body(n, carry):
                term_tile(s, part, n)
                return carry

            lax.fori_loop(0, C, body, 0)
    down_in = fetch(wd_hbm, wg, tile_load.at[0])
    for copy in late:
        copy.wait()

    def stored(target, t, slot):
        cut = pl.ds(pl.multiple_of(t * width, width), width)
        return pltpu.make_async_copy(stage.at[slot], target.at[cut, :], store.at[slot])

    def product(left_of, right_ref, target):
        def body(t, carry):
            slot = lax.rem(t, 2)

            @pl.when(t >= 2)
            def _():
                stored(target, t, slot).wait()

            stage[slot] = dot_tn(left_of(t), right_ref[...]).astype(BF)
            stored(target, t, slot).start()
            return carry

        lax.fori_loop(0, C, body, 0)
        for slot in range(2):
            stored(target, slot, slot).wait()

    def b_tile(t):
        return b[:, pl.ds(pl.multiple_of(t * width, width), width)]

    middle = max(1, (C - 1) // 2)
    product(b_tile, dg, gate_hbm)
    for step in range(1, middle + 1):
        if step < C - 1:
            pass_on(step)
    product(b_tile, du, up_hbm)
    product(lambda t: dys[t], hm, down_hbm)
    for step in range(middle + 1, C - 1):
        pass_on(step)
    down_in.wait()

    def out_tile(n, carry):
        cut = pl.ds(pl.multiple_of(n * width, width), width)
        terms_out = dot_nt(hm[...], wg[cut, :]).astype(BF)
        dys[0] = terms_out
        copy = pltpu.make_async_copy(dys.at[0], out_hbm.at[n], store.at[0])
        copy.start()
        copy.wait()
        return carry

    lax.fori_loop(0, C, out_tile, 0)
    moves(C - 2).wait_recv()
    sum_ref[...] = held[C - 2].astype(F32) + terms[C - 1].astype(F32)
    for step in range(C - 1):
        moves(step).wait_send()


def norm_terms(C, dg, du, hm, w_gate, w_up, w_down, b, dys):
    T, F = dg.shape
    D = w_gate.shape[0]
    rows, width = T // C, D // C
    return pl.pallas_call(
        functools.partial(norm_terms_kernel, C),
        in_specs=[ANY] * 8,
        out_specs=[VMEM_SPEC, ANY, ANY, ANY, ANY],
        out_shape=[
            struct((rows, D), F32),
            struct((D, F), BF),
            struct((D, F), BF),
            struct((D, F), BF),
            struct((C, T, width), BF),
        ],
        scratch_shapes=[
            pltpu.VMEM((T, F), BF),
            pltpu.VMEM((T, F), BF),
            pltpu.VMEM((T, F), BF),
            pltpu.VMEM((D, F), BF),
            pltpu.VMEM((D, F), BF),
            pltpu.VMEM((T, D), BF),
            pltpu.VMEM((C, T, width), BF),
            pltpu.VMEM((C, rows, D), BF),
            pltpu.VMEM((C - 1, rows, D), BF),
            pltpu.VMEM((2, width, F), BF),
            DMA((2 * C + 3,)),
            DMA((2 * C,)),
            DMA((2,)),
            DMA((C - 1,)),
            DMA((C - 1,)),
        ],
        compiler_params=comm_params(3, 62),
        cost_estimate=cost(9e10, 70 * MIB),
        name="norm_terms",
    )(dg, du, hm, w_gate, w_up, w_down, b, dys)


def resid_back_kernel(
    R, C, sum_ref, h_hbm, dys_hbm, os_hbm, w_hbm, do_hbm, dhs_hbm, grad_hbm,
    h, dy, heads, w, dh, out, stage, load, w_load, local, store, h_send, h_recv, o_send, o_recv,
):
    me, right, left = ring_places(C)
    blocks, D, part = w.shape
    rows = sum_ref.shape[0]
    width = D // C
    mine = pl.ds(pl.multiple_of(me * rows, rows), rows)
    first_in = [
        pltpu.make_async_copy(h_hbm.at[mine, :], h, load.at[0]),
        pltpu.make_async_copy(dys_hbm.at[:, mine, :], dy, load.at[1]),
    ]
    heads_in = pltpu.make_async_copy(os_hbm.at[:, :, mine, :], heads, load.at[2])
    for copy in first_in:
        copy.start()
    order = [lax.rem(me + k, C) for k in range(1, C)] + [me]
    loads = []
    for k in range(C):
        cut = pl.ds(pl.multiple_of(order[k] * width, width), width)
        copy = pltpu.make_async_copy(w_hbm.at[:, cut, :], w.at[:, cut, :], w_load.at[k])
        copy.start()
        loads.append(copy)
    heads_in.start()
    greet([{"col": lax.rem(me + k, C)} for k in range(1, C)], C - 1)
    for copy in first_in:
        copy.wait()
    grad = sum_ref[...]
    centre, inverse = norm_rows(h[...])
    normed = (h[...] - centre) * inverse
    first = jnp.mean(grad, axis=1, keepdims=True)
    second = jnp.mean(grad * normed, axis=1, keepdims=True)
    dh[...] = (beside(dy).astype(F32) + inverse * (grad - first - normed * second)).astype(BF)
    copies = []
    for k in range(C):
        cut = pl.ds(pl.multiple_of(order[k] * width, width), width)
        loads[k].wait()
        total = dot_nt(dh[:, :part], w[0, cut, :])
        for n in range(1, blocks):
            total += dot_nt(dh[:, n * part : (n + 1) * part], w[n, cut, :])
        out[k] = total.astype(BF)
        if k < C - 1:
            copy = remote(out.at[k], do_hbm.at[mine, :], o_send.at[k], o_recv.at[k], col=order[k])
        else:
            copy = pltpu.make_async_copy(out.at[k], do_hbm.at[mine, :], local.at[0])
        copy.start()
        copies.append(copy)
    for k in range(C):
        cut = pl.ds(pl.multiple_of(order[k] * width, width), width)
        if k < C - 1:
            copy = remote(dh.at[:, cut], dhs_hbm.at[mine, :], h_send.at[k], h_recv.at[k], col=order[k])
        else:
            copy = pltpu.make_async_copy(dh.at[:, cut], dhs_hbm.at[mine, :], local.at[1])
        copy.start()
        copies.append(copy)
    heads_in.wait()
    right_side = jnp.concatenate([heads[j, i] for j in range(C) for i in range(heads.shape[1])], axis=1)
    stores = []
    for t in range(C):
        if t >= 2:
            stores[t - 2].wait()
        stage[t % 2] = dot_tn(dh[:, t * width : (t + 1) * width], right_side).astype(BF)
        copy = pltpu.make_async_copy(stage.at[t % 2], grad_hbm.at[pl.ds(t * width, width), :], store.at[t % 2])
        copy.start()
        stores.append(copy)
    for copy in copies + stores[-2:]:
        copy.wait()


def resid_back(R, total, h, dys, os, w_out):
    C, T, width = dys.shape
    rows, D = total.shape
    return pl.pallas_call(
        functools.partial(resid_back_kernel, R, C),
        in_specs=[VMEM_SPEC] + [ANY] * 4,
        out_specs=[ANY, ANY, ANY],
        out_shape=[struct((T, width), BF), struct((T, width), BF), struct((D, D), BF)],
        scratch_shapes=[
            pltpu.VMEM((rows, D), F32),
            pltpu.VMEM((C, rows, width), BF),
            pltpu.VMEM((C, os.shape[1], rows, HEAD_DIM), BF),
            pltpu.VMEM(w_out.shape, BF),
            pltpu.VMEM((rows, D), BF),
            pltpu.VMEM((C, rows, width), BF),
            pltpu.VMEM((2, width, D), BF),
            DMA((3,)),
            DMA((C,)),
            DMA((2,)),
            DMA((2,)),
            DMA((C - 1,)),
            DMA((C - 1,)),
            DMA((C - 1,)),
            DMA((C - 1,)),
        ],
        compiler_params=comm_params(4),
        cost_estimate=cost(4e10, 20 * MIB),
        name="resid_back",
    )(total, h, dys, os, w_out)


def attend_back_kernel(
    R, C, q_ref, k_ref, v_ref, do_ref, log_ref, segk_ref, segq_ref, cos_ref, sin_ref, terms, h_hbm, grad_hbm,
    dq_ref, dk_ref, dv_ref, y_ref, total_ref, dk_sum, dv_sum, held, h, own, exchanged, arrived,
    send, recv, h_load, load, *semaphores,
):
    me, right, left = ring_places(C)
    row, ahead, behind, other = row_places(R)
    T, width = q_ref.shape
    heads, bq = width // HEAD_DIM, 256
    cut = pl.ds(pl.multiple_of(me * width, width), width)
    h_in = pltpu.make_async_copy(h_hbm.at[:, cut], h, h_load.at[0])
    sums, loads = held_row_sum(R, grad_hbm, own, exchanged, arrived, load, semaphores)
    for copy in loads:
        copy.start()
    h_in.start()
    greet([{"col": left}, {"row": other}] + [{"row": r} for r in behind[1:]], 1 + R // 2)
    for k in sums.order():
        sums.exchange(k).start()

    def chunk(s):
        return lax.rem(me + 2 * C - 1 - s, C)

    def moves(step):
        return ring_step(step, C, right, terms.at[chunk(0)], held, send, recv)

    moves(0).start()

    def one_head(head, carry):
        columns = pl.ds(pl.multiple_of(head * HEAD_DIM, HEAD_DIM), HEAD_DIM)
        dk_sum[...] = jnp.zeros_like(dk_sum)
        dv_sum[...] = jnp.zeros_like(dv_sum)
        for first in range(0, T, SEQ):
            for start in range(first, first + SEQ, bq):
                stop = start + bq
                keys = k_ref[first:stop, columns]
                queries = q_ref[start:stop, columns]
                grads = do_ref[start:stop, columns]
                scores = dot_nt(keys, queries) * SCALE
                allowed = allowed_block(segk_ref[first:stop], segq_ref[:, start:stop], start - first)
                scores = jnp.where(allowed, scores, MASKED)
                probs = jnp.exp(scores - log_ref[head, :, start:stop])
                dv_sum[first:stop] += dot_nn(probs.astype(BF), grads)
                grad_probs = dot_nt(v_ref[first:stop, columns], grads)
                inner = jnp.sum(probs * grad_probs, axis=0, keepdims=True)
                grad_scores = (probs * (grad_probs - inner)).astype(BF)
                dk_sum[first:stop] += dot_nn(grad_scores, queries)
                grad_query = dot_tn(keys, grad_scores).T * SCALE
                dq_ref[start:stop, columns] = turn(grad_query, cos_ref[start:stop], -sin_ref[start:stop]).astype(BF)
        dk_ref[:, columns] = turn(dk_sum[...] * SCALE, cos_ref[...], -sin_ref[...]).astype(BF)
        dv_ref[:, columns] = dv_sum[...].astype(BF)
        return carry

    lax.fori_loop(0, 1, one_head, 0)
    sums.relay(lambda k: loads[k].wait())
    lax.fori_loop(1, heads, one_head, 0)
    for step in range(1, C - 1):
        moves(step - 1).wait_recv()
        add_into(held.at[step - 1], terms.at[chunk(step)])
        moves(step).start()
    sums.finish(total_ref)
    h_in.wait()
    moves(C - 2).wait_recv()
    y_ref[...] = (h[...] + held[C - 2].astype(F32) + terms[me].astype(F32)).astype(BF)
    for step in range(C - 1):
        moves(step).wait_send()


def attend_back(R, q, k, v, do, log_total, seg_column, seg_row, cos_table, sin_table, out_terms, h, grad_out):
    C = out_terms.shape[0]
    T, width = q.shape
    depth, columns = grad_out.shape[1:]
    return pl.pallas_call(
        functools.partial(attend_back_kernel, R, C),
        in_specs=[VMEM_SPEC] * 10 + [ANY] * 2,
        out_specs=[VMEM_SPEC] * 5,
        out_shape=[struct((T, width), BF)] * 4 + [struct((depth, columns), BF)],
        scratch_shapes=[
            pltpu.VMEM((T, HEAD_DIM), F32),
            pltpu.VMEM((T, HEAD_DIM), F32),
            pltpu.VMEM((C - 1, T, width), BF),
            pltpu.VMEM((T, width), F32),
            pltpu.VMEM((R // 2, depth, columns), BF),
            pltpu.VMEM((R // 2, depth, columns), BF),
            pltpu.VMEM((R // 2 - 1, depth, columns), BF),
            DMA((C - 1,)),
            DMA((C - 1,)),
            DMA((1,)),
            DMA((R // 2,)),
        ]
        + row_sum_semaphores(R),
        compiler_params=comm_params(5),
        cost_estimate=cost(7e10, 14 * MIB),
        name="attend_back",
    )(q, k, v, do, log_total, seg_column, seg_row, cos_table, sin_table, out_terms, h, grad_out)


def input_terms_kernel(
    R, C, dq_ref, dk_ref, dv_ref, w_ref, a_ref, x_ref, dh_ref, mu_ref, r_ref, grad_hbm,
    y_ref, qkv_ref, total_ref,
    terms, held, da, stats, stats_in, own, exchanged, arrived, tiles, q_exchanged, q_arrived,
    send, recv, s_send, s_recv, load, *semaphores,
):
    me, right, left = ring_places(C)
    row, ahead, behind, other = row_places(R)
    T, width = dq_ref.shape
    D = width * C
    heads = (dq_ref, dk_ref, dv_ref)
    half, depth = R // 2, tiles.shape[2]
    sums, loads = held_row_sum(R, grad_hbm, own, exchanged, arrived, load, semaphores[:4])
    side = lax.rem(row, 2)
    q_sums = RowSum(
        R, lambda k: tiles.at[k, side], lambda k: tiles.at[k, 1 - side], q_exchanged, q_arrived, semaphores[4:]
    )
    for copy in loads:
        copy.start()
    greet(
        [{"col": lax.rem(me + k, C)} for k in range(1, C)] + [{"row": other}] + [{"row": r} for r in behind[1:]],
        C - 1 + half,
    )
    for k in sums.order():
        sums.exchange(k).start()

    def moves(step):
        return ring_step(step, C, right, terms.at[0], held, send, recv)

    def pass_on(step):
        moves(step - 1).wait_recv()
        add_into(held.at[step - 1], terms.at[step])
        moves(step).start()

    def compute(s):
        cut = pl.ds(pl.multiple_of(lax.rem(me + 2 * C - 1 - s, C) * width, width), width)
        total = dot_nt(dq_ref[...], w_ref[0, cut, :])
        total += dot_nt(dk_ref[...], w_ref[1, cut, :])
        total += dot_nt(dv_ref[...], w_ref[2, cut, :])
        terms[s] = total.astype(BF)

    compute(0)
    moves(0).start()

    def body(s, carry):
        compute(s)
        return carry

    lax.fori_loop(1, C, body, 0)
    sums.relay(lambda k: loads[k].wait())

    def grad_tile(i, carry):
        k = lax.rem(i + 1, half)
        chip = lax.rem(lax.div(row, 2) + k, half)
        left_tile = a_ref[:, pl.ds(pl.multiple_of(chip * 2 * depth, 2 * depth), 2 * depth)]
        for i, right_side in enumerate(heads):
            product = dot_tn(left_tile, right_side[...]).astype(BF)
            tiles[k, 0, :, i * width : (i + 1) * width] = product[:depth]
            tiles[k, 1, :, i * width : (i + 1) * width] = product[depth:]
        q_sums.exchange(k).start()
        return carry

    lax.fori_loop(0, half, grad_tile, 0)
    pass_on(1)
    q_sums.relay()
    for step in range(2, C - 1):
        pass_on(step)
    sums.finish(total_ref)
    moves(C - 2).wait_recv()
    size = 128

    def normed_of(rows):
        return (x_ref[rows, :].astype(F32) - mu_ref[rows, :]) * r_ref[rows, :]

    def sum_rows(i, carry):
        rows = pl.ds(pl.multiple_of(i * size, size), size)
        grad = held[C - 2, rows, :].astype(F32) + terms[C - 1, rows, :].astype(F32)
        da[rows, :] = grad
        lane = lax.broadcasted_iota(jnp.int32, (size, 128), 1)
        first = jnp.sum(grad, axis=1, keepdims=True)
        second = jnp.sum(grad * normed_of(rows), axis=1, keepdims=True)
        packed = jnp.where(lane == 0, first, jnp.where(lane == 1, second, 0.0))
        stats[:, rows] = packed.T[:8]
        return carry

    lax.fori_loop(0, T // size, sum_rows, 0)
    exchanges = [
        remote(stats, stats_in.at[k - 1], s_send.at[k - 1], s_recv.at[k - 1], col=lax.rem(me + k, C)) for k in range(1, C)
    ]
    for copy in exchanges:
        copy.start()
    for copy in exchanges:
        copy.wait_recv()

    def last_rows(i, carry):
        rows = pl.ds(pl.multiple_of(i * size, size), size)
        both = stats[:, rows]
        for k in range(C - 1):
            both += stats_in[k, :, rows]
        columns = jnp.concatenate([both, jnp.zeros((120, size), F32)], axis=0).T * (1.0 / D)
        grad = da[rows, :] - columns[:, 0:1] - normed_of(rows) * columns[:, 1:2]
        y_ref[rows, :] = (dh_ref[rows, :].astype(F32) + r_ref[rows, :] * grad).astype(BF)
        return carry

    lax.fori_loop(0, T // size, last_rows, 0)
    q_sums.finish(qkv_ref)
    for copy in exchanges:
        copy.wait_send()
    for step in range(C - 1):
        moves(step).wait_send()


def input_terms(R, C, dq, dk, dv, w_qkv, a, tokens, dh, mu, r, grad):
    T, width = dq.shape
    D = w_qkv.shape[1]
    half = R // 2
    depth, columns = grad.shape[1:]
    return pl.pallas_call(
        functools.partial(input_terms_kernel, R, C),
        in_specs=[VMEM_SPEC] * 9 + [ANY],
        out_specs=[VMEM_SPEC] * 3,
        out_shape=[struct((T, width), BF), struct((D // R, 3 * width), F32), struct((depth, columns), F32)],
        scratch_shapes=[
            pltpu.VMEM((C, T, width), BF),
            pltpu.VMEM((C - 1, T, width), BF),
            pltpu.VMEM((T, width), F32),
            pltpu.VMEM((8, T), F32),
            pltpu.VMEM((C - 1, 8, T), F32),
            pltpu.VMEM((half, depth, columns), BF),
            pltpu.VMEM((half, depth, columns), BF),
            pltpu.VMEM((half - 1, depth, columns), BF),
            pltpu.VMEM((half, 2, D // R, 3 * width), BF),
            pltpu.VMEM((half, D // R, 3 * width), BF),
            pltpu.VMEM((half - 1, D // R, 3 * width), BF),
            DMA((C - 1,)),
            DMA((C - 1,)),
            DMA((C - 1,)),
            DMA((C - 1,)),
            DMA((half,)),
        ]
        + row_sum_semaphores(R)
        + row_sum_semaphores(R),
        compiler_params=comm_params(6, 63),
        cost_estimate=cost(8e10, 20 * MIB),
        name="input_terms",
    )(dq, dk, dv, w_qkv, a, tokens, dh, mu, r, grad)


def on_device(R, C, tokens, cotangent, segments, w_query, w_key, w_value, w_out, w_gate, w_up, w_down):
    T, width = tokens.shape
    D = width * C
    me = lax.axis_index("col")

    def shift(values, k):
        return lax.ppermute(values, "col", [(i, (i + k) % C) for i in range(C)])

    def block(values, k, axis):
        size = values.shape[axis] // C
        return lax.dynamic_slice_in_dim(values, lax.rem(me + k, C) * size, size, axis)

    def scattered(values, axis):
        return [block(values, 0, axis)] + [shift(block(values, k, axis), k) for k in range(1, C)]

    def total_of(terms):
        total = terms[0].astype(F32)
        for term in terms[1:]:
            total = total + term.astype(F32)
        return total

    gathered = lambda w: lax.all_gather(w, "row", axis=0, tiled=True)
    scatter = lambda g: lax.psum_scatter(g, "row", scatter_dimension=0, tiled=True)

    gate_w, up_w, down_w = gathered(w_gate), gathered(w_up), gathered(w_down.T)
    cos_table, sin_table = rope_tables(segments)
    seg_column, seg_row = segments.reshape(T, 1), segments.reshape(1, T)
    xs, out_part, w_qkv = first_gather(R, C, tokens, w_out, w_query, w_key, w_value)
    w_qkv = w_qkv.reshape(3, D, width)
    act_one, q, k, v, mu_one, r_one = norm_and_project(xs, w_qkv, cos_table, sin_table)
    os, log_total, out_w = attend(R, C, q, k, v, seg_column, seg_row, out_part.reshape(D, -1))
    h_full, act_two, hidden, slope, silu, dys = feed_forward(
        C, os, out_w, xs, gate_w, up_w, cotangent
    )
    dg, du = hidden_back(dys, down_w, slope, silu)
    total, grad_gate, grad_up, grad_down, out_terms = norm_terms(
        C, dg, du, hidden, gate_w, up_w, down_w, act_two, dys
    )
    grad_down, grad_up = scatter(grad_down), scatter(grad_up)
    by_row = lambda values: values.reshape(R, D // R, -1)
    grad_heads, grad_resid, grad_out = resid_back(R, total, h_full, dys, os, out_w)
    dq, dk, dv, output, grad_out = attend_back(
        R, q, k, v, grad_heads, log_total, seg_column, seg_row, cos_table, sin_table, out_terms, h_full, by_row(grad_out)
    )
    grad_out = total_of(scattered(grad_out, 1)).T
    grad_tokens, grad_qkv, grad_gate = input_terms(
        R, C, dq, dk, dv, w_qkv, act_one, tokens, grad_resid, mu_one, r_one, by_row(grad_gate)
    )
    return (
        output,
        grad_tokens,
        grad_qkv[:, :width],
        grad_qkv[:, width : 2 * width],
        grad_qkv[:, 2 * width :],
        grad_out,
        grad_gate,
        grad_up.astype(F32),
        grad_down.astype(F32).T,
    )


def solution(mesh):
    here = P("row", "col")
    turned = P("col", "row")
    return jax.shard_map(
        functools.partial(on_device, mesh.shape["row"], mesh.shape["col"]),
        mesh=mesh,
        in_specs=(here, here, P("row"), here, here, here, turned, here, here, turned),
        out_specs=(here, here, here, here, here, turned, here, here, turned),
        check_vma=False,
    )
```

```python
import functools

import jax
import jax.numpy as jnp
from jax import lax
from jax.experimental import pallas as pl
from jax.experimental.pallas import tpu as pltpu
from jax.sharding import PartitionSpec as P

HEAD_DIM = 128
HALF = HEAD_DIM // 2
SEQ = 1024
EPSILON = 1e-05
MASKED = -1e30
SCALE = HEAD_DIM ** (-0.5)
BF = jnp.bfloat16
F32 = jnp.float32
MIB = 1 << 20
ANY = pl.BlockSpec(memory_space=pl.ANY)


def dot_nn(left, right):
    return jnp.dot(left, right, preferred_element_type=F32)


def dot_tn(left, right):
    return lax.dot_general(left, right, (((0,), (0,)), ((), ())), preferred_element_type=F32)


def dot_nt(left, right):
    return lax.dot_general(left, right, (((1,), (1,)), ((), ())), preferred_element_type=F32)


def struct(shape, dtype):
    return jax.ShapeDtypeStruct(shape, dtype)


def params(mib=60):
    return pltpu.CompilerParams(vmem_limit_bytes=mib * MIB)


def cost(flops, moved):
    return pl.CostEstimate(flops=int(flops), bytes_accessed=int(moved), transcendentals=0)


def count_seen(segment_ids):
    places = jnp.arange(segment_ids.shape[0], dtype=jnp.int32)
    causal = places[None, :] <= places[:, None]
    allowed = (segment_ids[:, None] == segment_ids[None, :]) & causal
    return jnp.sum(allowed.astype(jnp.int32), axis=1) - 1


def rope_tables(segments):
    positions = jax.vmap(count_seen)(segments.reshape(-1, SEQ)).reshape(-1)
    inverse = 10000.0 ** (-(jnp.arange(HALF, dtype=F32) * 2.0 / HEAD_DIM))
    angles = positions.astype(F32)[:, None] * inverse[None, :]
    cosine, sine = jnp.cos(angles), jnp.sin(angles)
    return jnp.concatenate([cosine, cosine], 1), jnp.concatenate([-sine, sine], 1)


def turn(values, cos_table, sin_table):
    return values * cos_table + pltpu.roll(values, HALF, 1) * sin_table


MESH = pl.DeviceIdType.MESH
VMEM_SPEC = pl.BlockSpec(memory_space=pltpu.VMEM)
DMA = pltpu.SemaphoreType.DMA


def comm_params(number, mib=60):
    return pltpu.CompilerParams(vmem_limit_bytes=mib * MIB, collective_id=number, has_side_effects=True)


def remote(source, target, send, recv, **device):
    return pltpu.make_async_remote_copy(
        src_ref=source, dst_ref=target, send_sem=send, recv_sem=recv, device_id=device, device_id_type=MESH
    )


def greet(senders, targets):
    semaphore = pltpu.get_barrier_semaphore()
    for device in senders:
        pl.semaphore_signal(semaphore, inc=1, device_id=device, device_id_type=MESH)
    pl.semaphore_wait(semaphore, targets)


def ring_places(C):
    me = lax.axis_index("col")
    return me, lax.rem(me + 1, C), lax.rem(me + C - 1, C)


def row_places(R):
    row = lax.axis_index("row")
    ahead = [lax.rem(row + 2 * k, R) for k in range(R // 2)]
    behind = [lax.rem(row + R - 2 * k, R) for k in range(R // 2)]
    other = row + 1 - 2 * lax.rem(row, 2)
    return row, ahead, behind, other


def gather_kernel(
    R, C, x_ref, wo_ref, wq_ref, wk_ref, wv_ref, xs_ref, wos_ref, w_ref,
    local, x_send, x_recv, o_send, o_recv, w_send, w_recv, f_send, f_recv,
):
    me, right, left = ring_places(C)
    row, ahead, behind, other = row_places(R)
    weights = (wq_ref, wk_ref, wv_ref)
    mine = [
        pltpu.make_async_copy(x_ref, xs_ref.at[me], local.at[0]),
        pltpu.make_async_copy(wo_ref, wos_ref.at[me], local.at[1]),
    ] + [pltpu.make_async_copy(w, w_ref.at[i, row], local.at[2 + i]) for i, w in enumerate(weights)]
    for copy in mine:
        copy.start()
    greet(
        [{"col": left}, {"row": other}] + [{"row": r} for r in behind[1:]],
        1 + R // 2,
    )

    def ring(source, whole, send, recv, step):
        owner = lax.rem(me - step + C, C)
        piece = source if step == 0 else whole.at[owner]
        return remote(piece, whole.at[owner], send.at[step], recv.at[step], col=right)

    x_copies = [ring(x_ref, xs_ref, x_send, x_recv, s) for s in range(C - 1)]
    o_copies = [ring(wo_ref, wos_ref, o_send, o_recv, s) for s in range(C - 1)]
    x_copies[0].start()
    o_copies[0].start()
    spread, forward = [], []
    for i, w in enumerate(weights):
        for k in range(1, R // 2):
            copy = remote(w, w_ref.at[i, row], w_send.at[i, k], w_recv.at[i, k], row=ahead[k])
            copy.start()
            spread.append(copy)
        copy = remote(w, w_ref.at[i, row], f_send.at[i, 0], f_recv.at[i, 0], row=other)
        copy.start()
        forward.append(copy)
    for s in range(1, C - 1):
        x_copies[s - 1].wait_recv()
        x_copies[s].start()
        o_copies[s - 1].wait_recv()
        o_copies[s].start()
    for i in range(3):
        for k in range(1, R // 2):
            spread[i * (R // 2 - 1) + k - 1].wait_recv()
            block = w_ref.at[i, behind[k]]
            copy = remote(block, block, f_send.at[i, k], f_recv.at[i, k], row=other)
            copy.start()
            forward.append(copy)
    x_copies[-1].wait_recv()
    o_copies[-1].wait_recv()
    for copy in forward:
        copy.wait_recv()
    for copy in x_copies + o_copies + spread + forward:
        copy.wait_send()
    for copy in mine:
        copy.wait()


def first_gather(R, C, tokens, w_out, w_query, w_key, w_value):
    depth, width = w_query.shape
    half = R // 2
    return pl.pallas_call(
        functools.partial(gather_kernel, R, C),
        in_specs=[ANY] * 5,
        out_specs=[ANY] * 3,
        out_shape=[
            struct((C,) + tokens.shape, BF),
            struct((C,) + w_out.shape, BF),
            struct((3, R, depth, width), BF),
        ],
        scratch_shapes=[
            DMA((5,)),
            DMA((C - 1,)),
            DMA((C - 1,)),
            DMA((C - 1,)),
            DMA((C - 1,)),
            DMA((3, half)),
            DMA((3, half)),
            DMA((3, half)),
            DMA((3, half)),
        ],
        compiler_params=comm_params(0),
        cost_estimate=cost(6e10, 14 * MIB),
        name="first_gather",
    )(tokens, w_out, w_query, w_key, w_value)


def norm_rows(x):
    centre = jnp.mean(x, axis=-1, keepdims=True)
    spread = jnp.mean(x * x, axis=-1, keepdims=True) - centre * centre
    inverse = lax.rsqrt(spread + EPSILON)
    return centre, inverse


def beside(ref):
    return jnp.concatenate([ref[j] for j in range(ref.shape[0])], axis=1)


def qkv_kernel(xs_ref, w_ref, cos_ref, sin_ref, a_ref, q_ref, k_ref, v_ref, mu_ref, r_ref):
    x = beside(xs_ref).astype(F32)
    centre, inverse = norm_rows(x)
    a = ((x - centre) * inverse).astype(BF)
    a_ref[...] = a
    mu_ref[...] = centre
    r_ref[...] = inverse
    cosine, sine = cos_ref[...], sin_ref[...]
    for index, out in enumerate((q_ref, k_ref, v_ref)):
        product = dot_nn(a, w_ref[index])
        if index == 2:
            out[...] = product.astype(BF)
            continue
        for start in range(0, out.shape[1], HEAD_DIM):
            part = product[:, start : start + HEAD_DIM]
            out[:, start : start + HEAD_DIM] = turn(part, cosine, sine).astype(BF)


def norm_and_project(xs, w_qkv, cos_table, sin_table):
    C, T, width = xs.shape
    D = width * C
    bt = 256
    rows = lambda n: pl.BlockSpec((bt, n), lambda i: (i, 0))
    return pl.pallas_call(
        qkv_kernel,
        grid=(T // bt,),
        in_specs=[
            pl.BlockSpec((C, bt, width), lambda i: (0, i, 0)),
            pl.BlockSpec(w_qkv.shape, lambda i: (0, 0, 0), pipeline_mode=pl.Buffered(1)),
            rows(HEAD_DIM),
            rows(HEAD_DIM),
        ],
        out_specs=[rows(D), rows(width), rows(width), rows(width), rows(1), rows(1)],
        out_shape=[
            struct((T, D), BF),
            struct((T, width), BF),
            struct((T, width), BF),
            struct((T, width), BF),
            struct((T, 1), F32),
            struct((T, 1), F32),
        ],
        compiler_params=params(),
        cost_estimate=cost(2 * T * D * 3 * width, 14 * MIB),
        name="norm_and_project",
    )(xs, w_qkv, cos_table, sin_table)


def allowed_block(seg_key, seg_query, first_query):
    shape = (seg_key.shape[0], seg_query.shape[1])
    keys = lax.broadcasted_iota(jnp.int32, shape, 0)
    queries = lax.broadcasted_iota(jnp.int32, shape, 1) + first_query
    return (seg_key == seg_query) & (keys <= queries)


def attend_kernel(
    R, C, q_ref, k_ref, v_ref, segk_ref, segq_ref, wos_ref, os_ref, log_ref, w_ref,
    o_buf, local, o_send, o_recv, w_send, w_recv, f_send, f_recv,
):
    me, right, left = ring_places(C)
    row, ahead, behind, other = row_places(R)
    T, width = q_ref.shape
    heads, bq = width // HEAD_DIM, 256
    greet([{"col": left}, {"row": other}] + [{"row": r} for r in behind[1:]], 1 + R // 2)
    mine = pltpu.make_async_copy(wos_ref, w_ref.at[row], local.at[0])
    mine.start()
    spread, forward = [], []
    for k in range(1, R // 2):
        copy = remote(wos_ref, w_ref.at[row], w_send.at[k], w_recv.at[k], row=ahead[k])
        copy.start()
        spread.append(copy)
    copy = remote(wos_ref, w_ref.at[row], f_send.at[0], f_recv.at[0], row=other)
    copy.start()
    forward.append(copy)

    def ring(step, head):
        owner = lax.rem(me - step + C, C)
        piece = o_buf.at[head] if step == 0 else os_ref.at[owner, head]
        return remote(piece, os_ref.at[owner, head], o_send.at[step, head], o_recv.at[step, head], col=right)

    def one_head(head, carry):
        columns = pl.ds(pl.multiple_of(head * HEAD_DIM, HEAD_DIM), HEAD_DIM)
        for first in range(0, T, SEQ):
            for start in range(first, first + SEQ, bq):
                stop = start + bq
                scores = dot_nt(k_ref[first:stop, columns], q_ref[start:stop, columns]) * SCALE
                allowed = allowed_block(segk_ref[first:stop], segq_ref[:, start:stop], start - first)
                scores = jnp.where(allowed, scores, MASKED)
                peak = jnp.max(scores, axis=0, keepdims=True)
                exponent = jnp.exp(scores - peak)
                total = jnp.sum(exponent, axis=0, keepdims=True)
                weights = (exponent * (1.0 / total)).astype(BF)
                o_buf[head, start:stop] = dot_tn(v_ref[first:stop, columns], weights).T.astype(BF)
                log_ref[head, :, start:stop] = peak + jnp.log(total)
        ring(0, head).start()
        pltpu.make_async_copy(o_buf.at[head], os_ref.at[me, head], local.at[1 + head]).start()
        return carry

    lax.fori_loop(0, heads, one_head, 0)
    for step in range(1, C - 1):
        for head in range(heads):
            ring(step - 1, head).wait_recv()
            ring(step, head).start()
    for k in range(1, R // 2):
        spread[k - 1].wait_recv()
        block = w_ref.at[behind[k]]
        copy = remote(block, block, f_send.at[k], f_recv.at[k], row=other)
        copy.start()
        forward.append(copy)
    for head in range(heads):
        ring(C - 2, head).wait_recv()
        pltpu.make_async_copy(o_buf.at[head], os_ref.at[me, head], local.at[1 + head]).wait()
        for step in range(C - 1):
            ring(step, head).wait_send()
    for copy in forward:
        copy.wait_recv()
    for copy in spread + forward:
        copy.wait_send()
    mine.wait()


def attend(R, C, q, k, v, seg_column, seg_row, w_part):
    T, width = q.shape
    heads, half = width // HEAD_DIM, R // 2
    return pl.pallas_call(
        functools.partial(attend_kernel, R, C),
        in_specs=[VMEM_SPEC] * 5 + [ANY],
        out_specs=[ANY, VMEM_SPEC, ANY],
        out_shape=[
            struct((C, heads, T, HEAD_DIM), BF),
            struct((heads, 1, T), F32),
            struct((R,) + w_part.shape, BF),
        ],
        scratch_shapes=[
            pltpu.VMEM((heads, T, HEAD_DIM), BF),
            DMA((1 + heads,)),
            DMA((C - 1, heads)),
            DMA((C - 1, heads)),
            DMA((half,)),
            DMA((half,)),
            DMA((half,)),
            DMA((half,)),
        ],
        compiler_params=comm_params(1),
        cost_estimate=cost(7e10, 14 * MIB),
        name="attend",
    )(q, k, v, seg_column, seg_row, w_part)


def feed_kernel(
    C, tiles, os_ref, w_ref, xs_ref, wg_ref, wu_ref, dy_ref,
    h_ref, b_ref, hm_ref, slope_ref, silu_ref, dys_ref, normed, local, send, recv,
):
    step = pl.program_id(0)
    me, right, left = ring_places(C)

    def ring(s):
        owner = lax.rem(me - s + C, C)
        piece = dy_ref if s == 0 else dys_ref.at[owner]
        return remote(piece, dys_ref.at[owner], send.at[s], recv.at[s], col=right)

    mine = pltpu.make_async_copy(dy_ref, dys_ref.at[me], local.at[0])
    steps = pl.num_programs(0)

    @pl.when(step == 0)
    def _():
        mine.start()
        greet([{"col": left}], 1)
        ring(0).start()

    for s in range(1, C - 1):

        @pl.when(step == min(tiles + s, tiles + 3))
        def _():
            ring(s - 1).wait_recv()
            ring(s).start()

    @pl.when(step < tiles)
    def _():
        size = h_ref.shape[0]
        blocks, part = w_ref.shape[0], w_ref.shape[2]
        heads = jnp.concatenate(
            [os_ref[j, h] for j in range(os_ref.shape[0]) for h in range(os_ref.shape[1])], axis=1
        )
        x = beside(xs_ref)
        for n in range(blocks):
            columns = slice(n * part, (n + 1) * part)
            h_ref[:, columns] = x[:, columns].astype(F32) + dot_nn(heads, w_ref[n])
        h = h_ref[...]
        centre, inverse = norm_rows(h)
        b = ((h - centre) * inverse).astype(BF)
        b_ref[...] = b
        normed[pl.ds(pl.multiple_of(step * size, size), size), :] = b

    @pl.when(step >= tiles)
    def _():
        b = normed[...]
        gate = dot_nn(b, wg_ref[...])
        upward = dot_nn(b, wu_ref[...])
        sigmoid = jax.nn.sigmoid(gate)
        silu = gate * sigmoid
        hm_ref[...] = (silu * upward).astype(BF)
        slope_ref[...] = (upward * sigmoid * (1.0 + gate * (1.0 - sigmoid))).astype(BF)
        silu_ref[...] = silu.astype(BF)

    @pl.when(step == steps - 1)
    def _():
        ring(C - 2).wait_recv()
        for s in range(C - 1):
            ring(s).wait_send()
        mine.wait()


def feed_forward(C, os, w_out, xs, w_gate, w_up, cotangent):
    heads, T = os.shape[1], os.shape[2]
    width = xs.shape[2]
    D, F = w_gate.shape
    bt = 256
    bf = F // 4
    tiles = T // bt
    early = lambda i: jnp.minimum(i, tiles - 1)
    late = lambda i: jnp.maximum(i - tiles, 0)
    rows = lambda n: pl.BlockSpec((bt, n), lambda i: (early(i), 0))
    tile = pl.BlockSpec((T, bf), lambda i: (0, late(i)))
    weight = pl.BlockSpec((D, bf), lambda i: (0, late(i)))
    return pl.pallas_call(
        functools.partial(feed_kernel, C, tiles),
        grid=(tiles + F // bf,),
        in_specs=[
            pl.BlockSpec((C, heads, bt, HEAD_DIM), lambda i: (0, 0, early(i), 0)),
            pl.BlockSpec(w_out.shape, lambda i: (0, 0, 0), pipeline_mode=pl.Buffered(1)),
            pl.BlockSpec((C, bt, width), lambda i: (0, early(i), 0)),
            weight,
            weight,
            ANY,
        ],
        out_specs=[rows(D), rows(D), tile, tile, tile, ANY],
        out_shape=[
            struct((T, D), F32),
            struct((T, D), BF),
            struct((T, F), BF),
            struct((T, F), BF),
            struct((T, F), BF),
            struct((C, T, width), BF),
        ],
        scratch_shapes=[pltpu.VMEM((T, D), BF), DMA((1,)), DMA((C - 1,)), DMA((C - 1,))],
        compiler_params=comm_params(2),
        cost_estimate=cost(7e10, 60 * MIB),
        name="feed_forward",
    )(os, w_out, xs, w_gate, w_up, cotangent)


def hidden_back_kernel(dys_ref, wd_ref, slope_ref, silu_ref, dg_ref, du_ref, dy):
    @pl.when(pl.program_id(0) == 0)
    def _():
        width = dys_ref.shape[2]
        for j in range(dys_ref.shape[0]):
            dy[:, j * width : (j + 1) * width] = dys_ref[j]

    grad_hidden = dot_nn(dy[...], wd_ref[...])
    dg_ref[...] = (grad_hidden * slope_ref[...].astype(F32)).astype(BF)
    du_ref[...] = (grad_hidden * silu_ref[...].astype(F32)).astype(BF)


def hidden_back(dys, w_down, slope, silu):
    C, T, width = dys.shape
    D, F = w_down.shape
    bf = F // 4
    tile = pl.BlockSpec((T, bf), lambda j: (0, j))
    return pl.pallas_call(
        hidden_back_kernel,
        grid=(F // bf,),
        in_specs=[
            pl.BlockSpec(dys.shape, lambda j: (0, 0, 0), pipeline_mode=pl.Buffered(1)),
            pl.BlockSpec((D, bf), lambda j: (0, j)),
            tile,
            tile,
        ],
        out_specs=[tile, tile],
        out_shape=[struct((T, F), BF)] * 2,
        scratch_shapes=[pltpu.VMEM((T, D), BF)],
        compiler_params=params(),
        cost_estimate=cost(2 * T * D * F, 28 * MIB),
        name="hidden_back",
    )(dys, w_down, slope, silu)


def ring_step(step, C, right, first, held, send, recv):
    source = first if step == 0 else held.at[step - 1]
    return remote(source, held.at[step], send.at[step], recv.at[step], col=right)


def add_into(held, terms):
    size = 64

    def body(i, carry):
        rows = pl.ds(pl.multiple_of(i * size, size), size)
        held[rows, :] = (held[rows, :].astype(F32) + terms[rows, :].astype(F32)).astype(BF)
        return carry

    lax.fori_loop(0, held.shape[0] // size, body, 0)


class RowSum:
    def __init__(self, R, own, twin, exchanged, arrived, semaphores):
        self.P = R // 4
        self.own, self.twin, self.exchanged, self.arrived = own, twin, exchanged, arrived
        self.x_send, self.x_recv, self.y_send, self.y_recv = semaphores
        self.width = arrived.shape[2]
        self.places = row_of(R)
        self.peers = row_peers(R)

    def part(self, ref, side):
        return ref.at[:, pl.ds(side * self.width, self.width)]

    def exchange(self, slot):
        return remote(
            self.twin(slot), self.exchanged.at[slot], self.x_send.at[slot], self.x_recv.at[slot], row=self.places(0, True)
        )

    def send(self, slot, side, index, target):
        return remote(
            self.part(self.own(slot), side), self.arrived.at[index], self.y_send.at[index], self.y_recv.at[index],
            row=self.places(target),
        )

    def left_one(self, dp):
        return self.send(2 * dp + 1, 0, dp, 1)

    def left_two(self, dp):
        return self.send(2 * dp, 0, self.P + dp - 1, 2 * dp)

    def right_one(self, dp, dq):
        return self.send(2 * dp + dq, 1, 2 * self.P - 1 + 2 * (dp - 1) + dq, 2 * dp)

    def right_two(self):
        return self.send(1, 1, 4 * self.P - 3, 1)

    def order(self):
        return (
            [2 * dp + 1 for dp in range(1, self.P)] + [1] + [2 * dp for dp in range(1, self.P)] + [0]
        )

    def relay(self, before=None):
        for slot in self.order():
            if before is not None:
                before(slot)
            self.exchange(slot).wait_recv()
            add_into(self.own(slot), self.exchanged.at[slot])
            dp, dq = divmod(slot, 2)
            if dq:
                self.left_one(dp).start()
            if dp:
                self.right_one(dp, dq).start()

    def relay_again(self):
        for dp in range(1, self.P):
            self.left_one(dp).wait_recv()
            add_into(self.part(self.own(2 * dp), 0), self.arrived.at[dp])
            self.left_two(dp).start()
        for dp in range(1, self.P):
            copy = self.right_one(dp, 1)
            copy.wait_recv()
            add_into(self.part(self.own(1), 1), self.arrived.at[2 * self.P - 1 + 2 * (dp - 1) + 1])
        self.right_two().start()

    def finish(self, write, size=64):
        P, width = self.P, self.width
        self.left_one(0).wait_recv()
        self.right_two().wait_recv()
        for dp in range(1, P):
            self.left_two(dp).wait_recv()
            self.right_one(dp, 0).wait_recv()
        lefts = [0] + [P + dp - 1 for dp in range(1, P)]
        rights = [4 * P - 3] + [2 * P - 1 + 2 * (dp - 1) for dp in range(1, P)]

        def body(i, carry):
            rows = pl.ds(pl.multiple_of(i * size, size), size)
            total = self.own(0)[rows, :].astype(F32)
            halves = []
            for side, places in enumerate((lefts, rights)):
                half = total[:, side * width : (side + 1) * width]
                for index in places:
                    half += self.arrived[index, rows, :].astype(F32)
                halves.append(half)
            write(rows, jnp.concatenate(halves, axis=1))
            return carry

        lax.fori_loop(0, self.exchanged.shape[1] // size, body, 0)
        for slot in range(2 * P):
            self.exchange(slot).wait_send()
        self.left_one(0).wait_send()
        self.right_two().wait_send()
        for dp in range(1, P):
            self.left_one(dp).wait_send()
            self.left_two(dp).wait_send()
            self.right_one(dp, 0).wait_send()
            self.right_one(dp, 1).wait_send()


def row_of(R):
    row = lax.axis_index("row")
    side, chip = lax.rem(row, 2), lax.div(row, 2)
    p, q = lax.div(chip, 2), lax.rem(chip, 2)

    def place(slot, twin=False):
        dp, dq = divmod(slot, 2)
        chip_there = 2 * lax.rem(p + dp, R // 4) + lax.rem(q + dq, 2)
        return 2 * chip_there + (1 - side if twin else side)

    return place


def row_peers(R):
    place = row_of(R)
    return [{"row": place(0, True)}, {"row": place(1)}] + [{"row": place(2 * dp)} for dp in range(1, R // 4)]


def row_sum_semaphores(R):
    return [DMA((R // 2,)), DMA((R // 2,)), DMA((R - 2,)), DMA((R - 2,))]


def row_sum_buffers(R, depth, columns):
    return [
        pltpu.VMEM((R // 2, depth, columns), BF),
        pltpu.VMEM((R - 2, depth, columns // 2), BF),
    ]


def held_row_sum(R, grad_hbm, own, exchanged, arrived, load, semaphores):
    place = row_of(R)
    sums = RowSum(R, lambda i: own.at[i], lambda i: grad_hbm.at[place(i, True)], exchanged, arrived, semaphores)
    loads = [pltpu.make_async_copy(grad_hbm.at[place(i)], own.at[i], load.at[i]) for i in range(R // 2)]
    return sums, loads


def norm_terms_kernel(
    C, dg_hbm, du_hbm, hm_hbm, wg_hbm, wu_hbm, wd_hbm, b_hbm, dys_hbm,
    sum_ref, gate_hbm, up_hbm, down_hbm, out_hbm,
    dg, du, hm, wg, wu, b, dys, terms, held, stage, load, tile_load, store, send, recv,
):
    me, right, left = ring_places(C)
    D, F = wg.shape
    T = dg.shape[0]
    rows = T // C
    width = D // C
    loads = []

    def fetch(source, target, semaphore):
        copy = pltpu.make_async_copy(source, target, semaphore)
        copy.start()
        return copy

    def chunk(s):
        return pl.ds(pl.multiple_of(lax.rem(me + 2 * C - 1 - s, C) * rows, rows), rows)

    grads_in = []
    for s in range(C):
        part = chunk(s)
        grads_in.append(
            (fetch(dg_hbm.at[part, :], dg.at[part, :], load.at[2 * s]), fetch(du_hbm.at[part, :], du.at[part, :], load.at[2 * s + 1]))
        )
        if s == 0:
            weights_in = []
            for n in range(C):
                cut = pl.ds(n * width, width)
                weights_in.append(
                    (fetch(wg_hbm.at[cut, :], wg.at[cut, :], tile_load.at[2 * n]), fetch(wu_hbm.at[cut, :], wu.at[cut, :], tile_load.at[2 * n + 1]))
                )
    late = [
        fetch(b_hbm, b, load.at[2 * C]),
        fetch(hm_hbm, hm, load.at[2 * C + 1]),
        fetch(dys_hbm, dys, load.at[2 * C + 2]),
    ]
    greet([{"col": left}], 1)

    def term_tile(s, part, n):
        cut = pl.ds(pl.multiple_of(n * width, width), width)
        total = dot_nt(dg[part, :], wg[cut, :]) + dot_nt(du[part, :], wu[cut, :])
        terms[s, :, cut] = total.astype(BF)

    def moves(step):
        return ring_step(step, C, right, terms.at[0], held, send, recv)

    def pass_on(step):
        moves(step - 1).wait_recv()
        add_into(held.at[step - 1], terms.at[step])
        moves(step).start()

    for s in range(C):
        part = chunk(s)
        for copy in grads_in[s]:
            copy.wait()
        if s == 0:
            for n in range(C):
                for copy in weights_in[n]:
                    copy.wait()
                term_tile(s, part, n)
            moves(0).start()
        else:

            def body(n, carry):
                term_tile(s, part, n)
                return carry

            lax.fori_loop(0, C, body, 0)
    down_in = fetch(wd_hbm, wg, tile_load.at[0])
    for copy in late:
        copy.wait()

    def stored(target, t, slot):
        cut = pl.ds(pl.multiple_of(t * width, width), width)
        return pltpu.make_async_copy(stage.at[slot], target.at[cut, :], store.at[slot])

    def product(left_of, right_ref, target):
        def body(t, carry):
            slot = lax.rem(t, 2)

            @pl.when(t >= 2)
            def _():
                stored(target, t, slot).wait()

            stage[slot] = dot_tn(left_of(t), right_ref[...]).astype(BF)
            stored(target, t, slot).start()
            return carry

        lax.fori_loop(0, C, body, 0)
        for slot in range(2):
            stored(target, slot, slot).wait()

    def b_tile(t):
        return b[:, pl.ds(pl.multiple_of(t * width, width), width)]

    middle = max(1, (C - 1) // 2)
    product(b_tile, dg, gate_hbm)
    for step in range(1, middle + 1):
        if step < C - 1:
            pass_on(step)
    product(b_tile, du, up_hbm)
    product(lambda t: dys[t], hm, down_hbm)
    for step in range(middle + 1, C - 1):
        pass_on(step)
    down_in.wait()

    def out_tile(n, carry):
        cut = pl.ds(pl.multiple_of(n * width, width), width)
        terms_out = dot_nt(hm[...], wg[cut, :]).astype(BF)
        dys[0] = terms_out
        copy = pltpu.make_async_copy(dys.at[0], out_hbm.at[n], store.at[0])
        copy.start()
        copy.wait()
        return carry

    lax.fori_loop(0, C, out_tile, 0)
    moves(C - 2).wait_recv()
    sum_ref[...] = held[C - 2].astype(F32) + terms[C - 1].astype(F32)
    for step in range(C - 1):
        moves(step).wait_send()


def norm_terms(C, dg, du, hm, w_gate, w_up, w_down, b, dys):
    T, F = dg.shape
    D = w_gate.shape[0]
    rows, width = T // C, D // C
    return pl.pallas_call(
        functools.partial(norm_terms_kernel, C),
        in_specs=[ANY] * 8,
        out_specs=[VMEM_SPEC, ANY, ANY, ANY, ANY],
        out_shape=[
            struct((rows, D), F32),
            struct((D, F), BF),
            struct((D, F), BF),
            struct((D, F), BF),
            struct((C, T, width), BF),
        ],
        scratch_shapes=[
            pltpu.VMEM((T, F), BF),
            pltpu.VMEM((T, F), BF),
            pltpu.VMEM((T, F), BF),
            pltpu.VMEM((D, F), BF),
            pltpu.VMEM((D, F), BF),
            pltpu.VMEM((T, D), BF),
            pltpu.VMEM((C, T, width), BF),
            pltpu.VMEM((C, rows, D), BF),
            pltpu.VMEM((C - 1, rows, D), BF),
            pltpu.VMEM((2, width, F), BF),
            DMA((2 * C + 3,)),
            DMA((2 * C,)),
            DMA((2,)),
            DMA((C - 1,)),
            DMA((C - 1,)),
        ],
        compiler_params=comm_params(3, 62),
        cost_estimate=cost(9e10, 70 * MIB),
        name="norm_terms",
    )(dg, du, hm, w_gate, w_up, w_down, b, dys)


def resid_back_kernel(
    R, C, sum_ref, h_hbm, dys_hbm, os_hbm, w_hbm, down_hbm, do_hbm, dhs_hbm, grad_hbm, down_ref,
    h, dy, heads, w, dh, out, stage, own, exchanged, arrived,
    load, w_load, local, store, h_send, h_recv, o_send, o_recv, own_load, *semaphores,
):
    me, right, left = ring_places(C)
    blocks, D, part = w.shape
    rows = sum_ref.shape[0]
    width = D // C
    mine = pl.ds(pl.multiple_of(me * rows, rows), rows)
    first_in = [
        pltpu.make_async_copy(h_hbm.at[mine, :], h, load.at[0]),
        pltpu.make_async_copy(dys_hbm.at[:, mine, :], dy, load.at[1]),
    ]
    heads_in = pltpu.make_async_copy(os_hbm.at[:, :, mine, :], heads, load.at[2])
    for copy in first_in:
        copy.start()
    order = [lax.rem(me + k, C) for k in range(1, C)] + [me]
    loads = []
    for k in range(C):
        cut = pl.ds(pl.multiple_of(order[k] * width, width), width)
        copy = pltpu.make_async_copy(w_hbm.at[:, cut, :], w.at[:, cut, :], w_load.at[k])
        copy.start()
        loads.append(copy)
    sums, own_loads = held_row_sum(R, down_hbm, own, exchanged, arrived, own_load, semaphores)
    for copy in own_loads:
        copy.start()
    heads_in.start()
    greet([{"col": lax.rem(me + k, C)} for k in range(1, C)] + sums.peers, C - 1 + len(sums.peers))
    for slot in sums.order():
        sums.exchange(slot).start()
    for copy in first_in:
        copy.wait()
    grad = sum_ref[...]
    centre, inverse = norm_rows(h[...])
    normed = (h[...] - centre) * inverse
    first = jnp.mean(grad, axis=1, keepdims=True)
    second = jnp.mean(grad * normed, axis=1, keepdims=True)
    dh[...] = (beside(dy).astype(F32) + inverse * (grad - first - normed * second)).astype(BF)
    copies = []
    for k in range(C):
        cut = pl.ds(pl.multiple_of(order[k] * width, width), width)
        loads[k].wait()
        total = dot_nt(dh[:, :part], w[0, cut, :])
        for n in range(1, blocks):
            total += dot_nt(dh[:, n * part : (n + 1) * part], w[n, cut, :])
        out[k] = total.astype(BF)
        if k < C - 1:
            copy = remote(out.at[k], do_hbm.at[mine, :], o_send.at[k], o_recv.at[k], col=order[k])
        else:
            copy = pltpu.make_async_copy(out.at[k], do_hbm.at[mine, :], local.at[0])
        copy.start()
        copies.append(copy)
    for k in range(C):
        cut = pl.ds(pl.multiple_of(order[k] * width, width), width)
        if k < C - 1:
            copy = remote(dh.at[:, cut], dhs_hbm.at[mine, :], h_send.at[k], h_recv.at[k], col=order[k])
        else:
            copy = pltpu.make_async_copy(dh.at[:, cut], dhs_hbm.at[mine, :], local.at[1])
        copy.start()
        copies.append(copy)
    sums.relay(lambda slot: own_loads[slot].wait())
    heads_in.wait()
    right_side = jnp.concatenate([heads[j, i] for j in range(C) for i in range(heads.shape[1])], axis=1)
    stores = []
    for t in range(C):
        if t >= 2:
            stores[t - 2].wait()
        stage[t % 2] = dot_tn(dh[:, t * width : (t + 1) * width], right_side).astype(BF)
        copy = pltpu.make_async_copy(stage.at[t % 2], grad_hbm.at[pl.ds(t * width, width), :], store.at[t % 2])
        copy.start()
        stores.append(copy)
    sums.relay_again()

    def write(part, values):
        down_ref[:, part] = values.T

    sums.finish(write, 128)
    for copy in copies + stores[-2:]:
        copy.wait()


def resid_back(R, total, h, dys, os, w_out, grad_down):
    C, T, width = dys.shape
    rows, D = total.shape
    depth, columns = grad_down.shape[1:]
    return pl.pallas_call(
        functools.partial(resid_back_kernel, R, C),
        in_specs=[VMEM_SPEC] + [ANY] * 5,
        out_specs=[ANY, ANY, ANY, VMEM_SPEC],
        out_shape=[
            struct((T, width), BF),
            struct((T, width), BF),
            struct((D, D), BF),
            struct((columns, depth), F32),
        ],
        scratch_shapes=[
            pltpu.VMEM((rows, D), F32),
            pltpu.VMEM((C, rows, width), BF),
            pltpu.VMEM((C, os.shape[1], rows, HEAD_DIM), BF),
            pltpu.VMEM(w_out.shape, BF),
            pltpu.VMEM((rows, D), BF),
            pltpu.VMEM((C, rows, width), BF),
            pltpu.VMEM((2, width, D), BF),
            pltpu.VMEM((R // 2, depth, columns), BF),
        ]
        + row_sum_buffers(R, depth, columns)
        + [
            DMA((3,)),
            DMA((C,)),
            DMA((2,)),
            DMA((2,)),
            DMA((C - 1,)),
            DMA((C - 1,)),
            DMA((C - 1,)),
            DMA((C - 1,)),
            DMA((R // 2,)),
        ]
        + row_sum_semaphores(R),
        compiler_params=comm_params(4),
        cost_estimate=cost(4e10, 20 * MIB),
        name="resid_back",
    )(total, h, dys, os, w_out, grad_down)


def attend_back_kernel(
    R, C, q_ref, k_ref, v_ref, do_ref, log_ref, segk_ref, segq_ref, cos_ref, sin_ref, terms, h_hbm, out_hbm, up_hbm,
    dq_ref, dk_ref, dv_ref, y_ref, out_ref, up_ref, dk_sum, dv_sum, held, h,
    out_own, out_exchanged, out_arrived, up_own, up_exchanged, up_arrived,
    send, recv, h_load, out_load, up_load, *semaphores,
):
    me, right, left = ring_places(C)
    T, width = q_ref.shape
    heads, bq = width // HEAD_DIM, 256
    cut = pl.ds(pl.multiple_of(me * width, width), width)
    h_in = pltpu.make_async_copy(h_hbm.at[:, cut], h, h_load.at[0])
    up_sums, up_loads = held_row_sum(R, up_hbm, up_own, up_exchanged, up_arrived, up_load, semaphores[:4])
    out_sums, out_loads = held_row_sum(R, out_hbm, out_own, out_exchanged, out_arrived, out_load, semaphores[4:])
    for copy in up_loads + out_loads:
        copy.start()
    h_in.start()
    greet([{"col": left}] + up_sums.peers, 1 + len(up_sums.peers))
    for sums in (up_sums, out_sums):
        for slot in sums.order():
            sums.exchange(slot).start()

    def chunk(s):
        return lax.rem(me + 2 * C - 1 - s, C)

    def moves(step):
        return ring_step(step, C, right, terms.at[chunk(0)], held, send, recv)

    moves(0).start()

    def one_head(head, carry):
        columns = pl.ds(pl.multiple_of(head * HEAD_DIM, HEAD_DIM), HEAD_DIM)
        dk_sum[...] = jnp.zeros_like(dk_sum)
        dv_sum[...] = jnp.zeros_like(dv_sum)
        for first in range(0, T, SEQ):
            for start in range(first, first + SEQ, bq):
                stop = start + bq
                keys = k_ref[first:stop, columns]
                queries = q_ref[start:stop, columns]
                grads = do_ref[start:stop, columns]
                scores = dot_nt(keys, queries) * SCALE
                allowed = allowed_block(segk_ref[first:stop], segq_ref[:, start:stop], start - first)
                scores = jnp.where(allowed, scores, MASKED)
                probs = jnp.exp(scores - log_ref[head, :, start:stop])
                dv_sum[first:stop] += dot_nn(probs.astype(BF), grads)
                grad_probs = dot_nt(v_ref[first:stop, columns], grads)
                inner = jnp.sum(probs * grad_probs, axis=0, keepdims=True)
                grad_scores = (probs * (grad_probs - inner)).astype(BF)
                dk_sum[first:stop] += dot_nn(grad_scores, queries)
                grad_query = dot_tn(keys, grad_scores).T * SCALE
                dq_ref[start:stop, columns] = turn(grad_query, cos_ref[start:stop], -sin_ref[start:stop]).astype(BF)
        dk_ref[:, columns] = turn(dk_sum[...] * SCALE, cos_ref[...], -sin_ref[...]).astype(BF)
        dv_ref[:, columns] = dv_sum[...].astype(BF)
        return carry

    lax.fori_loop(0, heads // 2, one_head, 0)
    up_sums.relay(lambda slot: up_loads[slot].wait())
    lax.fori_loop(heads // 2, heads, one_head, 0)
    out_sums.relay(lambda slot: out_loads[slot].wait())
    for step in range(1, C - 1):
        moves(step - 1).wait_recv()
        add_into(held.at[step - 1], terms.at[chunk(step)])
        moves(step).start()
        if step == 1:
            up_sums.relay_again()
    out_sums.relay_again()

    def write_up(part, values):
        up_ref[part, :] = values

    def write_out(part, values):
        out_ref[part, :] = values.astype(BF)

    up_sums.finish(write_up)
    out_sums.finish(write_out)
    h_in.wait()
    moves(C - 2).wait_recv()
    y_ref[...] = (h[...] + held[C - 2].astype(F32) + terms[me].astype(F32)).astype(BF)
    for step in range(C - 1):
        moves(step).wait_send()


def attend_back(R, q, k, v, do, log_total, seg_column, seg_row, cos_table, sin_table, out_terms, h, grad_out, grad_up):
    C = out_terms.shape[0]
    T, width = q.shape
    shapes = (grad_out.shape[1:], grad_up.shape[1:])
    return pl.pallas_call(
        functools.partial(attend_back_kernel, R, C),
        in_specs=[VMEM_SPEC] * 10 + [ANY] * 3,
        out_specs=[VMEM_SPEC] * 6,
        out_shape=[struct((T, width), BF)] * 4 + [struct(shapes[0], BF), struct(shapes[1], F32)],
        scratch_shapes=[
            pltpu.VMEM((T, HEAD_DIM), F32),
            pltpu.VMEM((T, HEAD_DIM), F32),
            pltpu.VMEM((C - 1, T, width), BF),
            pltpu.VMEM((T, width), F32),
        ]
        + [
            buffer
            for shape in shapes
            for buffer in [pltpu.VMEM((R // 2,) + shape, BF)] + row_sum_buffers(R, *shape)
        ]
        + [
            DMA((C - 1,)),
            DMA((C - 1,)),
            DMA((1,)),
            DMA((R // 2,)),
            DMA((R // 2,)),
        ]
        + row_sum_semaphores(R)
        + row_sum_semaphores(R),
        compiler_params=comm_params(5),
        cost_estimate=cost(7e10, 14 * MIB),
        name="attend_back",
    )(q, k, v, do, log_total, seg_column, seg_row, cos_table, sin_table, out_terms, h, grad_out, grad_up)


def input_terms_kernel(
    R, C, dq_ref, dk_ref, dv_ref, w_ref, a_ref, x_ref, dh_ref, mu_ref, r_ref, out_ref, grad_hbm,
    y_ref, gq_ref, gk_ref, gv_ref, total_ref, gout_ref,
    terms, held, da, stats, stats_in, out_in, own, exchanged, arrived, tiles, q_exchanged, q_arrived,
    send, recv, s_send, s_recv, o_send, o_recv, load, *semaphores,
):
    me, right, left = ring_places(C)
    T, width = dq_ref.shape
    D = width * C
    heads = (dq_ref, dk_ref, dv_ref)
    depth = tiles.shape[2]
    sums, loads = held_row_sum(R, grad_hbm, own, exchanged, arrived, load, semaphores[:4])
    side = lax.rem(lax.axis_index("row"), 2)
    q_sums = RowSum(
        R, lambda i: tiles.at[i, side], lambda i: tiles.at[i, 1 - side], q_exchanged, q_arrived, semaphores[4:]
    )
    for copy in loads:
        copy.start()
    greet([{"col": lax.rem(me + k, C)} for k in range(1, C)] + sums.peers, C - 1 + len(sums.peers))
    for slot in sums.order():
        sums.exchange(slot).start()

    def block_of(k):
        return out_ref.at[:, pl.ds(pl.multiple_of(lax.rem(me + k, C) * width, width), width)]

    out_copies = [
        remote(block_of(k), out_in.at[k - 1], o_send.at[k - 1], o_recv.at[k - 1], col=lax.rem(me + k, C))
        for k in range(1, C)
    ]

    def moves(step):
        return ring_step(step, C, right, terms.at[0], held, send, recv)

    def pass_on(step):
        moves(step - 1).wait_recv()
        add_into(held.at[step - 1], terms.at[step])
        moves(step).start()

    def compute(s):
        cut = pl.ds(pl.multiple_of(lax.rem(me + 2 * C - 1 - s, C) * width, width), width)
        total = dot_nt(dq_ref[...], w_ref[0, cut, :])
        total += dot_nt(dk_ref[...], w_ref[1, cut, :])
        total += dot_nt(dv_ref[...], w_ref[2, cut, :])
        terms[s] = total.astype(BF)

    compute(0)
    moves(0).start()

    def body(s, carry):
        compute(s)
        return carry

    lax.fori_loop(1, C, body, 0)
    for copy in out_copies:
        copy.start()
    sums.relay(lambda slot: loads[slot].wait())
    for slot in q_sums.order():
        start = pl.multiple_of(lax.div(q_sums.places(slot), 2) * 2 * depth, 2 * depth)
        left_tile = a_ref[:, pl.ds(start, 2 * depth)]
        for i, right_side in enumerate(heads):
            product = dot_tn(left_tile, right_side[...]).astype(BF)
            tiles[slot, 0, :, i * width : (i + 1) * width] = product[:depth]
            tiles[slot, 1, :, i * width : (i + 1) * width] = product[depth:]
        q_sums.exchange(slot).start()
    q_sums.relay()
    pass_on(1)
    sums.relay_again()
    q_sums.relay_again()
    for copy in out_copies:
        copy.wait_recv()
    out_total = block_of(0)[...].astype(F32)
    for k in range(C - 1):
        out_total += out_in[k].astype(F32)
    gout_ref[...] = out_total.T
    for step in range(2, C - 1):
        pass_on(step)

    def write(part, values):
        total_ref[part, :] = values

    def write_qkv(part, values):
        for i, target in enumerate((gq_ref, gk_ref, gv_ref)):
            target[part, :] = values[:, i * width : (i + 1) * width]

    sums.finish(write)
    q_sums.finish(write_qkv)
    moves(C - 2).wait_recv()
    size = 128

    def normed_of(rows):
        return (x_ref[rows, :].astype(F32) - mu_ref[rows, :]) * r_ref[rows, :]

    def sum_rows(i, carry):
        rows = pl.ds(pl.multiple_of(i * size, size), size)
        grad = held[C - 2, rows, :].astype(F32) + terms[C - 1, rows, :].astype(F32)
        da[rows, :] = grad
        lane = lax.broadcasted_iota(jnp.int32, (size, 128), 1)
        first = jnp.sum(grad, axis=1, keepdims=True)
        second = jnp.sum(grad * normed_of(rows), axis=1, keepdims=True)
        packed = jnp.where(lane == 0, first, jnp.where(lane == 1, second, 0.0))
        stats[:, rows] = packed.T[:8]
        return carry

    lax.fori_loop(0, T // size, sum_rows, 0)
    exchanges = [
        remote(stats, stats_in.at[k - 1], s_send.at[k - 1], s_recv.at[k - 1], col=lax.rem(me + k, C)) for k in range(1, C)
    ]
    for copy in exchanges:
        copy.start()
    for copy in exchanges:
        copy.wait_recv()

    def last_rows(i, carry):
        rows = pl.ds(pl.multiple_of(i * size, size), size)
        both = stats[:, rows]
        for k in range(C - 1):
            both += stats_in[k, :, rows]
        columns = jnp.concatenate([both, jnp.zeros((120, size), F32)], axis=0).T * (1.0 / D)
        grad = da[rows, :] - columns[:, 0:1] - normed_of(rows) * columns[:, 1:2]
        y_ref[rows, :] = (dh_ref[rows, :].astype(F32) + r_ref[rows, :] * grad).astype(BF)
        return carry

    lax.fori_loop(0, T // size, last_rows, 0)
    for copy in exchanges + out_copies:
        copy.wait_send()
    for step in range(C - 1):
        moves(step).wait_send()


def input_terms(R, C, dq, dk, dv, w_qkv, a, tokens, dh, mu, r, grad_out, grad):
    T, width = dq.shape
    D = w_qkv.shape[1]
    half, low = R // 2, D // R
    depth, columns = grad.shape[1:]
    return pl.pallas_call(
        functools.partial(input_terms_kernel, R, C),
        in_specs=[VMEM_SPEC] * 10 + [ANY],
        out_specs=[VMEM_SPEC] * 6,
        out_shape=[struct((T, width), BF)]
        + [struct((low, width), F32)] * 3
        + [struct((depth, columns), F32), struct((width, low), F32)],
        scratch_shapes=[
            pltpu.VMEM((C, T, width), BF),
            pltpu.VMEM((C - 1, T, width), BF),
            pltpu.VMEM((T, width), F32),
            pltpu.VMEM((8, T), F32),
            pltpu.VMEM((C - 1, 8, T), F32),
            pltpu.VMEM((C - 1, low, width), BF),
            pltpu.VMEM((half, depth, columns), BF),
        ]
        + row_sum_buffers(R, depth, columns)
        + [pltpu.VMEM((half, 2, low, 3 * width), BF)]
        + row_sum_buffers(R, low, 3 * width)
        + [
            DMA((C - 1,)),
            DMA((C - 1,)),
            DMA((C - 1,)),
            DMA((C - 1,)),
            DMA((C - 1,)),
            DMA((C - 1,)),
            DMA((half,)),
        ]
        + row_sum_semaphores(R)
        + row_sum_semaphores(R),
        compiler_params=comm_params(6, 63),
        cost_estimate=cost(8e10, 20 * MIB),
        name="input_terms",
    )(dq, dk, dv, w_qkv, a, tokens, dh, mu, r, grad_out, grad)


def on_device(R, C, tokens, cotangent, segments, w_query, w_key, w_value, w_out, w_gate, w_up, w_down):
    T, width = tokens.shape
    D = width * C
    gathered = lambda w: lax.all_gather(w, "row", axis=0, tiled=True)

    gate_w, up_w, down_w = gathered(w_gate), gathered(w_up), gathered(w_down.T)
    cos_table, sin_table = rope_tables(segments)
    seg_column, seg_row = segments.reshape(T, 1), segments.reshape(1, T)
    xs, out_part, w_qkv = first_gather(R, C, tokens, w_out, w_query, w_key, w_value)
    w_qkv = w_qkv.reshape(3, D, width)
    act_one, q, k, v, mu_one, r_one = norm_and_project(xs, w_qkv, cos_table, sin_table)
    os, log_total, out_w = attend(R, C, q, k, v, seg_column, seg_row, out_part.reshape(D, -1))
    h_full, act_two, hidden, slope, silu, dys = feed_forward(
        C, os, out_w, xs, gate_w, up_w, cotangent
    )
    dg, du = hidden_back(dys, down_w, slope, silu)
    total, grad_gate, grad_up, grad_down, out_terms = norm_terms(
        C, dg, du, hidden, gate_w, up_w, down_w, act_two, dys
    )
    by_row = lambda values: values.reshape(R, D // R, -1)
    grad_heads, grad_resid, grad_out, grad_down = resid_back(R, total, h_full, dys, os, out_w, by_row(grad_down))
    dq, dk, dv, output, grad_out, grad_up = attend_back(
        R, q, k, v, grad_heads, log_total, seg_column, seg_row, cos_table, sin_table, out_terms, h_full,
        by_row(grad_out), by_row(grad_up),
    )
    grad_tokens, grad_query, grad_key, grad_value, grad_gate, grad_out = input_terms(
        R, C, dq, dk, dv, w_qkv, act_one, tokens, grad_resid, mu_one, r_one, grad_out, by_row(grad_gate)
    )
    return (output, grad_tokens, grad_query, grad_key, grad_value, grad_out, grad_gate, grad_up, grad_down)


def solution(mesh):
    here = P("row", "col")
    turned = P("col", "row")
    return jax.shard_map(
        functools.partial(on_device, mesh.shape["row"], mesh.shape["col"]),
        mesh=mesh,
        in_specs=(here, here, P("row"), here, here, here, turned, here, here, turned),
        out_specs=(here, here, here, here, here, turned, here, here, turned),
        check_vma=False,
    )
```

```python
import functools

import jax
import jax.numpy as jnp
from jax import lax
from jax.experimental import pallas as pl
from jax.experimental.pallas import tpu as pltpu
from jax.sharding import PartitionSpec as P

HEAD_DIM = 128
HALF = HEAD_DIM // 2
SEQ = 1024
EPSILON = 1e-05
MASKED = -1e30
SCALE = HEAD_DIM ** (-0.5)
BF = jnp.bfloat16
F32 = jnp.float32
MIB = 1 << 20
ANY = pl.BlockSpec(memory_space=pl.ANY)


def dot_nn(left, right):
    return jnp.dot(left, right, preferred_element_type=F32)


def dot_tn(left, right):
    return lax.dot_general(left, right, (((0,), (0,)), ((), ())), preferred_element_type=F32)


def dot_nt(left, right):
    return lax.dot_general(left, right, (((1,), (1,)), ((), ())), preferred_element_type=F32)


def struct(shape, dtype):
    return jax.ShapeDtypeStruct(shape, dtype)


def params(mib=60):
    return pltpu.CompilerParams(vmem_limit_bytes=mib * MIB)


def cost(flops, moved):
    return pl.CostEstimate(flops=int(flops), bytes_accessed=int(moved), transcendentals=0)


def turn(values, cos_table, sin_table):
    return values * cos_table + pltpu.roll(values, HALF, 1) * sin_table


MESH = pl.DeviceIdType.MESH
VMEM_SPEC = pl.BlockSpec(memory_space=pltpu.VMEM)
DMA = pltpu.SemaphoreType.DMA


def comm_params(number, mib=60):
    return pltpu.CompilerParams(vmem_limit_bytes=mib * MIB, collective_id=number, has_side_effects=True)


def remote(source, target, send, recv, **device):
    return pltpu.make_async_remote_copy(
        src_ref=source, dst_ref=target, send_sem=send, recv_sem=recv, device_id=device, device_id_type=MESH
    )


def greet(senders, targets):
    semaphore = pltpu.get_barrier_semaphore()
    for device in senders:
        pl.semaphore_signal(semaphore, inc=1, device_id=device, device_id_type=MESH)
    pl.semaphore_wait(semaphore, targets)


def ring_places(C):
    me = lax.axis_index("col")
    return me, lax.rem(me + 1, C), lax.rem(me + C - 1, C)


def row_places(R):
    row = lax.axis_index("row")
    ahead = [lax.rem(row + 2 * k, R) for k in range(R // 2)]
    behind = [lax.rem(row + R - 2 * k, R) for k in range(R // 2)]
    other = row + 1 - 2 * lax.rem(row, 2)
    return row, ahead, behind, other


def gather_ring(C, source, whole, send, recv):
    me, right, left = ring_places(C)
    copies = []
    for step in range(C - 1):
        owner = lax.rem(me - step + C, C)
        piece = source if step == 0 else whole.at[owner]
        copies.append(remote(piece, whole.at[owner], send.at[step], recv.at[step], col=right))
    return copies


def gather_kernel(
    R, C, segk_ref, segq_ref, rate_ref, x_ref, wq_ref, wk_ref, wv_ref, xs_ref, w_ref, cos_ref, sin_ref,
    local, x_send, x_recv, w_send, w_recv, f_send, f_recv,
):
    me, right, left = ring_places(C)
    row, ahead, behind, other = row_places(R)
    weights = (wq_ref, wk_ref, wv_ref)
    mine = [
        pltpu.make_async_copy(x_ref, xs_ref.at[me], local.at[0]),
    ] + [pltpu.make_async_copy(w, w_ref.at[i, row], local.at[1 + i]) for i, w in enumerate(weights)]
    for copy in mine:
        copy.start()
    greet(
        [{"col": left}, {"row": other}] + [{"row": r} for r in behind[1:]],
        1 + R // 2,
    )

    x_copies = gather_ring(C, x_ref, xs_ref, x_send, x_recv)
    x_copies[0].start()
    spread, forward = [], []
    for i, w in enumerate(weights):
        for k in range(1, R // 2):
            copy = remote(w, w_ref.at[i, row], w_send.at[i, k], w_recv.at[i, k], row=ahead[k])
            copy.start()
            spread.append(copy)
        copy = remote(w, w_ref.at[i, row], f_send.at[i, 0], f_recv.at[i, 0], row=other)
        copy.start()
        forward.append(copy)
    T = cos_ref.shape[0]
    size = 128

    def table_rows(i, carry):
        rows = pl.ds(pl.multiple_of(i * size, size), size)
        first = SEQ * lax.div(i * size, SEQ)
        shape = (size, T)
        queries = lax.broadcasted_iota(jnp.int32, shape, 0) + i * size
        keys = lax.broadcasted_iota(jnp.int32, shape, 1)
        seen = (segk_ref[rows, :] == segq_ref[...]) & (keys <= queries) & (keys >= first)
        place = jnp.sum(jnp.where(seen, 1.0, 0.0), axis=1, keepdims=True) - 1.0
        angles = place * rate_ref[...]
        lane = lax.broadcasted_iota(jnp.int32, angles.shape, 1)
        sine = jnp.sin(angles)
        cos_ref[rows, :] = jnp.cos(angles)
        sin_ref[rows, :] = jnp.where(lane < HALF, -sine, sine)
        return carry

    lax.fori_loop(0, T // size, table_rows, 0)
    for s in range(1, C - 1):
        x_copies[s - 1].wait_recv()
        x_copies[s].start()
    for i in range(3):
        for k in range(1, R // 2):
            spread[i * (R // 2 - 1) + k - 1].wait_recv()
            block = w_ref.at[i, behind[k]]
            copy = remote(block, block, f_send.at[i, k], f_recv.at[i, k], row=other)
            copy.start()
            forward.append(copy)
    x_copies[-1].wait_recv()
    for copy in forward:
        copy.wait_recv()
    for copy in x_copies + spread + forward:
        copy.wait_send()
    for copy in mine:
        copy.wait()


def first_gather(R, C, seg_column, seg_row, tokens, w_query, w_key, w_value):
    depth, width = w_query.shape
    T = tokens.shape[0]
    half = R // 2
    rate = 10000.0 ** (-(jnp.arange(HALF, dtype=F32) * 2.0 / HEAD_DIM))
    rate = jnp.concatenate([rate, rate]).reshape(1, HEAD_DIM)
    return pl.pallas_call(
        functools.partial(gather_kernel, R, C),
        in_specs=[VMEM_SPEC] * 3 + [ANY] * 4,
        out_specs=[ANY] * 2 + [VMEM_SPEC] * 2,
        out_shape=[
            struct((C,) + tokens.shape, BF),
            struct((3, R, depth, width), BF),
            struct((T, HEAD_DIM), F32),
            struct((T, HEAD_DIM), F32),
        ],
        scratch_shapes=[
            DMA((4,)),
            DMA((C - 1,)),
            DMA((C - 1,)),
            DMA((3, half)),
            DMA((3, half)),
            DMA((3, half)),
            DMA((3, half)),
        ],
        compiler_params=comm_params(0),
        cost_estimate=cost(6e10, 14 * MIB),
        name="first_gather",
    )(seg_column, seg_row, rate, tokens, w_query, w_key, w_value)


def norm_rows(x):
    centre = jnp.mean(x, axis=-1, keepdims=True)
    spread = jnp.mean(x * x, axis=-1, keepdims=True) - centre * centre
    inverse = lax.rsqrt(spread + EPSILON)
    return centre, inverse


def beside(ref):
    return jnp.concatenate([ref[j] for j in range(ref.shape[0])], axis=1)


def qkv_kernel(
    C, xs_ref, w_ref, cos_ref, sin_ref, wo_ref, a_ref, q_ref, k_ref, v_ref, mu_ref, r_ref, wos_ref, local, send, recv
):
    step, steps = pl.program_id(0), pl.num_programs(0)
    me, right, left = ring_places(C)
    copies = gather_ring(C, wo_ref, wos_ref, send, recv)
    mine = pltpu.make_async_copy(wo_ref, wos_ref.at[me], local.at[0])

    @pl.when(step == 0)
    def _():
        mine.start()
        greet([{"col": left}], 1)
        copies[0].start()

    for s in range(1, C - 1):

        @pl.when(step == jnp.minimum(2 * s, steps - 1))
        def _():
            copies[s - 1].wait_recv()
            copies[s].start()

    x = beside(xs_ref).astype(F32)
    centre, inverse = norm_rows(x)
    a = ((x - centre) * inverse).astype(BF)
    a_ref[...] = a
    mu_ref[...] = centre
    r_ref[...] = inverse
    cosine, sine = cos_ref[...], sin_ref[...]
    for index, out in enumerate((q_ref, k_ref, v_ref)):
        product = dot_nn(a, w_ref[index])
        if index == 2:
            out[...] = product.astype(BF)
            continue
        for start in range(0, out.shape[1], HEAD_DIM):
            part = product[:, start : start + HEAD_DIM]
            out[:, start : start + HEAD_DIM] = turn(part, cosine, sine).astype(BF)

    @pl.when(step == steps - 1)
    def _():
        copies[-1].wait_recv()
        for copy in copies:
            copy.wait_send()
        mine.wait()


def norm_and_project(xs, w_qkv, cos_table, sin_table, w_out):
    C, T, width = xs.shape
    D = width * C
    bt = 256
    rows = lambda n: pl.BlockSpec((bt, n), lambda i: (i, 0))
    return pl.pallas_call(
        functools.partial(qkv_kernel, C),
        grid=(T // bt,),
        in_specs=[
            pl.BlockSpec((C, bt, width), lambda i: (0, i, 0)),
            pl.BlockSpec(w_qkv.shape, lambda i: (0, 0, 0), pipeline_mode=pl.Buffered(1)),
            rows(HEAD_DIM),
            rows(HEAD_DIM),
            ANY,
        ],
        out_specs=[rows(D), rows(width), rows(width), rows(width), rows(1), rows(1), ANY],
        out_shape=[
            struct((T, D), BF),
            struct((T, width), BF),
            struct((T, width), BF),
            struct((T, width), BF),
            struct((T, 1), F32),
            struct((T, 1), F32),
            struct((C,) + w_out.shape, BF),
        ],
        scratch_shapes=[DMA((1,)), DMA((C - 1,)), DMA((C - 1,))],
        compiler_params=comm_params(7),
        cost_estimate=cost(2e10, 14 * MIB),
        name="norm_and_project",
    )(xs, w_qkv, cos_table, sin_table, w_out)


def allowed_block(seg_key, seg_query, first_query):
    shape = (seg_key.shape[0], seg_query.shape[1])
    keys = lax.broadcasted_iota(jnp.int32, shape, 0)
    queries = lax.broadcasted_iota(jnp.int32, shape, 1) + first_query
    return (seg_key == seg_query) & (keys <= queries)


def attend_kernel(
    R, C, q_ref, k_ref, v_ref, segk_ref, segq_ref, wos_ref, os_ref, log_ref, w_ref,
    o_buf, local, o_send, o_recv, w_send, w_recv, f_send, f_recv,
):
    me, right, left = ring_places(C)
    row, ahead, behind, other = row_places(R)
    T, width = q_ref.shape
    heads, bq = width // HEAD_DIM, 256
    greet([{"col": left}, {"row": other}] + [{"row": r} for r in behind[1:]], 1 + R // 2)
    mine = pltpu.make_async_copy(wos_ref, w_ref.at[row], local.at[0])
    mine.start()
    spread, forward = [], []
    for k in range(1, R // 2):
        copy = remote(wos_ref, w_ref.at[row], w_send.at[k], w_recv.at[k], row=ahead[k])
        copy.start()
        spread.append(copy)
    copy = remote(wos_ref, w_ref.at[row], f_send.at[0], f_recv.at[0], row=other)
    copy.start()
    forward.append(copy)

    def ring(step, head):
        owner = lax.rem(me - step + C, C)
        piece = o_buf.at[head] if step == 0 else os_ref.at[owner, head]
        return remote(piece, os_ref.at[owner, head], o_send.at[step, head], o_recv.at[step, head], col=right)

    def one_head(head, carry):
        columns = pl.ds(pl.multiple_of(head * HEAD_DIM, HEAD_DIM), HEAD_DIM)
        for first in range(0, T, SEQ):
            for start in range(first, first + SEQ, bq):
                stop = start + bq
                scores = dot_nt(k_ref[first:stop, columns], q_ref[start:stop, columns]) * SCALE
                allowed = allowed_block(segk_ref[first:stop], segq_ref[:, start:stop], start - first)
                scores = jnp.where(allowed, scores, MASKED)
                peak = jnp.max(scores, axis=0, keepdims=True)
                exponent = jnp.exp(scores - peak)
                total = jnp.sum(exponent, axis=0, keepdims=True)
                weights = (exponent * (1.0 / total)).astype(BF)
                o_buf[head, start:stop] = dot_tn(v_ref[first:stop, columns], weights).T.astype(BF)
                log_ref[head, :, start:stop] = peak + jnp.log(total)
        ring(0, head).start()
        pltpu.make_async_copy(o_buf.at[head], os_ref.at[me, head], local.at[1 + head]).start()
        return carry

    lax.fori_loop(0, heads, one_head, 0)
    for step in range(1, C - 1):
        for head in range(heads):
            ring(step - 1, head).wait_recv()
            ring(step, head).start()
    for k in range(1, R // 2):
        spread[k - 1].wait_recv()
        block = w_ref.at[behind[k]]
        copy = remote(block, block, f_send.at[k], f_recv.at[k], row=other)
        copy.start()
        forward.append(copy)
    for head in range(heads):
        ring(C - 2, head).wait_recv()
        pltpu.make_async_copy(o_buf.at[head], os_ref.at[me, head], local.at[1 + head]).wait()
        for step in range(C - 1):
            ring(step, head).wait_send()
    for copy in forward:
        copy.wait_recv()
    for copy in spread + forward:
        copy.wait_send()
    mine.wait()


def attend(R, C, q, k, v, seg_column, seg_row, w_part):
    T, width = q.shape
    heads, half = width // HEAD_DIM, R // 2
    return pl.pallas_call(
        functools.partial(attend_kernel, R, C),
        in_specs=[VMEM_SPEC] * 5 + [ANY],
        out_specs=[ANY, VMEM_SPEC, ANY],
        out_shape=[
            struct((C, heads, T, HEAD_DIM), BF),
            struct((heads, 1, T), F32),
            struct((R,) + w_part.shape, BF),
        ],
        scratch_shapes=[
            pltpu.VMEM((heads, T, HEAD_DIM), BF),
            DMA((1 + heads,)),
            DMA((C - 1, heads)),
            DMA((C - 1, heads)),
            DMA((half,)),
            DMA((half,)),
            DMA((half,)),
            DMA((half,)),
        ],
        compiler_params=comm_params(1),
        cost_estimate=cost(7e10, 14 * MIB),
        name="attend",
    )(q, k, v, seg_column, seg_row, w_part)


def feed_kernel(
    C, tiles, os_ref, w_ref, xs_ref, wg_ref, wu_ref, dy_ref,
    h_ref, b_ref, hm_ref, slope_ref, silu_ref, dys_ref, normed, local, send, recv,
):
    step = pl.program_id(0)
    me, right, left = ring_places(C)

    def ring(s):
        owner = lax.rem(me - s + C, C)
        piece = dy_ref if s == 0 else dys_ref.at[owner]
        return remote(piece, dys_ref.at[owner], send.at[s], recv.at[s], col=right)

    mine = pltpu.make_async_copy(dy_ref, dys_ref.at[me], local.at[0])
    steps = pl.num_programs(0)

    @pl.when(step == 0)
    def _():
        mine.start()
        greet([{"col": left}], 1)
        ring(0).start()

    for s in range(1, C - 1):

        @pl.when(step == min(tiles + s, tiles + 3))
        def _():
            ring(s - 1).wait_recv()
            ring(s).start()

    @pl.when(step < tiles)
    def _():
        size = h_ref.shape[0]
        blocks, part = w_ref.shape[0], w_ref.shape[2]
        heads = jnp.concatenate(
            [os_ref[j, h] for j in range(os_ref.shape[0]) for h in range(os_ref.shape[1])], axis=1
        )
        x = beside(xs_ref)
        for n in range(blocks):
            columns = slice(n * part, (n + 1) * part)
            h_ref[:, columns] = x[:, columns].astype(F32) + dot_nn(heads, w_ref[n])
        h = h_ref[...]
        centre, inverse = norm_rows(h)
        b = ((h - centre) * inverse).astype(BF)
        b_ref[...] = b
        normed[pl.ds(pl.multiple_of(step * size, size), size), :] = b

    @pl.when(step >= tiles)
    def _():
        b = normed[...]
        gate = dot_nn(b, wg_ref[...])
        upward = dot_nn(b, wu_ref[...])
        sigmoid = jax.nn.sigmoid(gate)
        silu = gate * sigmoid
        hm_ref[...] = (silu * upward).astype(BF)
        slope_ref[...] = (upward * sigmoid * (1.0 + gate * (1.0 - sigmoid))).astype(BF)
        silu_ref[...] = silu.astype(BF)

    @pl.when(step == steps - 1)
    def _():
        ring(C - 2).wait_recv()
        for s in range(C - 1):
            ring(s).wait_send()
        mine.wait()


def feed_forward(C, os, w_out, xs, w_gate, w_up, cotangent):
    heads, T = os.shape[1], os.shape[2]
    width = xs.shape[2]
    D, F = w_gate.shape
    bt = 256
    bf = F // 4
    tiles = T // bt
    early = lambda i: jnp.minimum(i, tiles - 1)
    late = lambda i: jnp.maximum(i - tiles, 0)
    rows = lambda n: pl.BlockSpec((bt, n), lambda i: (early(i), 0))
    tile = pl.BlockSpec((T, bf), lambda i: (0, late(i)))
    weight = pl.BlockSpec((D, bf), lambda i: (0, late(i)))
    return pl.pallas_call(
        functools.partial(feed_kernel, C, tiles),
        grid=(tiles + F // bf,),
        in_specs=[
            pl.BlockSpec((C, heads, bt, HEAD_DIM), lambda i: (0, 0, early(i), 0)),
            pl.BlockSpec(w_out.shape, lambda i: (0, 0, 0), pipeline_mode=pl.Buffered(1)),
            pl.BlockSpec((C, bt, width), lambda i: (0, early(i), 0)),
            weight,
            weight,
            ANY,
        ],
        out_specs=[rows(D), rows(D), tile, tile, tile, ANY],
        out_shape=[
            struct((T, D), F32),
            struct((T, D), BF),
            struct((T, F), BF),
            struct((T, F), BF),
            struct((T, F), BF),
            struct((C, T, width), BF),
        ],
        scratch_shapes=[pltpu.VMEM((T, D), BF), DMA((1,)), DMA((C - 1,)), DMA((C - 1,))],
        compiler_params=comm_params(2),
        cost_estimate=cost(7e10, 60 * MIB),
        name="feed_forward",
    )(os, w_out, xs, w_gate, w_up, cotangent)


def hidden_back_kernel(dys_ref, wd_ref, slope_ref, silu_ref, dg_ref, du_ref, dy):
    @pl.when(pl.program_id(0) == 0)
    def _():
        width = dys_ref.shape[2]
        for j in range(dys_ref.shape[0]):
            dy[:, j * width : (j + 1) * width] = dys_ref[j]

    grad_hidden = dot_nn(dy[...], wd_ref[...])
    dg_ref[...] = (grad_hidden * slope_ref[...].astype(F32)).astype(BF)
    du_ref[...] = (grad_hidden * silu_ref[...].astype(F32)).astype(BF)


def hidden_back(dys, w_down, slope, silu):
    C, T, width = dys.shape
    D, F = w_down.shape
    bf = F // 4
    tile = pl.BlockSpec((T, bf), lambda j: (0, j))
    return pl.pallas_call(
        hidden_back_kernel,
        grid=(F // bf,),
        in_specs=[
            pl.BlockSpec(dys.shape, lambda j: (0, 0, 0), pipeline_mode=pl.Buffered(1)),
            pl.BlockSpec((D, bf), lambda j: (0, j)),
            tile,
            tile,
        ],
        out_specs=[tile, tile],
        out_shape=[struct((T, F), BF)] * 2,
        scratch_shapes=[pltpu.VMEM((T, D), BF)],
        compiler_params=params(),
        cost_estimate=cost(2 * T * D * F, 28 * MIB),
        name="hidden_back",
    )(dys, w_down, slope, silu)


def ring_step(step, C, right, first, held, send, recv):
    source = first if step == 0 else held.at[step - 1]
    return remote(source, held.at[step], send.at[step], recv.at[step], col=right)


def add_into(held, terms):
    size = 64

    def body(i, carry):
        rows = pl.ds(pl.multiple_of(i * size, size), size)
        held[rows, :] = (held[rows, :].astype(F32) + terms[rows, :].astype(F32)).astype(BF)
        return carry

    lax.fori_loop(0, held.shape[0] // size, body, 0)


class RowSum:
    def __init__(self, R, own, twin, exchanged, arrived, semaphores):
        self.P = R // 4
        self.own, self.twin, self.exchanged, self.arrived = own, twin, exchanged, arrived
        self.x_send, self.x_recv, self.y_send, self.y_recv = semaphores
        self.width = arrived.shape[2]
        self.places = row_of(R)
        self.peers = row_peers(R)

    def part(self, ref, side):
        return ref.at[:, pl.ds(side * self.width, self.width)]

    def exchange(self, slot):
        return remote(
            self.twin(slot), self.exchanged.at[slot], self.x_send.at[slot], self.x_recv.at[slot], row=self.places(0, True)
        )

    def send(self, slot, side, index, target):
        return remote(
            self.part(self.own(slot), side), self.arrived.at[index], self.y_send.at[index], self.y_recv.at[index],
            row=self.places(target),
        )

    def left_one(self, dp):
        return self.send(2 * dp + 1, 0, dp, 1)

    def left_two(self, dp):
        return self.send(2 * dp, 0, self.P + dp - 1, 2 * dp)

    def right_one(self, dp, dq):
        return self.send(2 * dp + dq, 1, 2 * self.P - 1 + 2 * (dp - 1) + dq, 2 * dp)

    def right_two(self):
        return self.send(1, 1, 4 * self.P - 3, 1)

    def order(self):
        return (
            [2 * dp + 1 for dp in range(1, self.P)] + [1] + [2 * dp for dp in range(1, self.P)] + [0]
        )

    def relay(self, before=None):
        for slot in self.order():
            if before is not None:
                before(slot)
            self.exchange(slot).wait_recv()
            add_into(self.own(slot), self.exchanged.at[slot])
            dp, dq = divmod(slot, 2)
            if dq:
                self.left_one(dp).start()
            if dp:
                self.right_one(dp, dq).start()

    def relay_again(self):
        for dp in range(1, self.P):
            self.left_one(dp).wait_recv()
            add_into(self.part(self.own(2 * dp), 0), self.arrived.at[dp])
            self.left_two(dp).start()
        for dp in range(1, self.P):
            copy = self.right_one(dp, 1)
            copy.wait_recv()
            add_into(self.part(self.own(1), 1), self.arrived.at[2 * self.P - 1 + 2 * (dp - 1) + 1])
        self.right_two().start()

    def finish(self, write, size=64):
        P, width = self.P, self.width
        self.left_one(0).wait_recv()
        self.right_two().wait_recv()
        for dp in range(1, P):
            self.left_two(dp).wait_recv()
            self.right_one(dp, 0).wait_recv()
        lefts = [0] + [P + dp - 1 for dp in range(1, P)]
        rights = [4 * P - 3] + [2 * P - 1 + 2 * (dp - 1) for dp in range(1, P)]

        def body(i, carry):
            rows = pl.ds(pl.multiple_of(i * size, size), size)
            total = self.own(0)[rows, :].astype(F32)
            halves = []
            for side, places in enumerate((lefts, rights)):
                half = total[:, side * width : (side + 1) * width]
                for index in places:
                    half += self.arrived[index, rows, :].astype(F32)
                halves.append(half)
            write(rows, jnp.concatenate(halves, axis=1))
            return carry

        lax.fori_loop(0, self.exchanged.shape[1] // size, body, 0)
        for slot in range(2 * P):
            self.exchange(slot).wait_send()
        self.left_one(0).wait_send()
        self.right_two().wait_send()
        for dp in range(1, P):
            self.left_one(dp).wait_send()
            self.left_two(dp).wait_send()
            self.right_one(dp, 0).wait_send()
            self.right_one(dp, 1).wait_send()


def row_of(R):
    row = lax.axis_index("row")
    side, chip = lax.rem(row, 2), lax.div(row, 2)
    p, q = lax.div(chip, 2), lax.rem(chip, 2)

    def place(slot, twin=False):
        dp, dq = divmod(slot, 2)
        chip_there = 2 * lax.rem(p + dp, R // 4) + lax.rem(q + dq, 2)
        return 2 * chip_there + (1 - side if twin else side)

    return place


def row_peers(R):
    place = row_of(R)
    return [{"row": place(0, True)}, {"row": place(1)}] + [{"row": place(2 * dp)} for dp in range(1, R // 4)]


def row_sum_semaphores(R):
    return [DMA((R // 2,)), DMA((R // 2,)), DMA((R - 2,)), DMA((R - 2,))]


def row_sum_buffers(R, depth, columns):
    return [
        pltpu.VMEM((R // 2, depth, columns), BF),
        pltpu.VMEM((R - 2, depth, columns // 2), BF),
    ]


def held_row_sum(R, grad_hbm, own, exchanged, arrived, load, semaphores):
    place = row_of(R)
    sums = RowSum(R, lambda i: own.at[i], lambda i: grad_hbm.at[place(i, True)], exchanged, arrived, semaphores)
    loads = [pltpu.make_async_copy(grad_hbm.at[place(i)], own.at[i], load.at[i]) for i in range(R // 2)]
    return sums, loads


def norm_terms_kernel(
    C, dg_hbm, du_hbm, hm_hbm, wg_hbm, wu_hbm, wd_hbm, b_hbm, dys_hbm,
    sum_ref, gate_hbm, up_hbm, down_hbm, out_hbm,
    dg, du, hm, wg, wu, b, dys, terms, held, stage, load, tile_load, store, send, recv,
):
    me, right, left = ring_places(C)
    D, F = wg.shape
    T = dg.shape[0]
    rows = T // C
    width = D // C
    loads = []

    def fetch(source, target, semaphore):
        copy = pltpu.make_async_copy(source, target, semaphore)
        copy.start()
        return copy

    def chunk(s):
        return pl.ds(pl.multiple_of(lax.rem(me + 2 * C - 1 - s, C) * rows, rows), rows)

    grads_in = []
    for s in range(C):
        part = chunk(s)
        grads_in.append(
            (fetch(dg_hbm.at[part, :], dg.at[part, :], load.at[2 * s]), fetch(du_hbm.at[part, :], du.at[part, :], load.at[2 * s + 1]))
        )
        if s == 0:
            weights_in = []
            for n in range(C):
                cut = pl.ds(n * width, width)
                weights_in.append(
                    (fetch(wg_hbm.at[cut, :], wg.at[cut, :], tile_load.at[2 * n]), fetch(wu_hbm.at[cut, :], wu.at[cut, :], tile_load.at[2 * n + 1]))
                )
    late = [
        fetch(b_hbm, b, load.at[2 * C]),
        fetch(hm_hbm, hm, load.at[2 * C + 1]),
        fetch(dys_hbm, dys, load.at[2 * C + 2]),
    ]
    greet([{"col": left}], 1)

    def term_tile(s, part, n):
        cut = pl.ds(pl.multiple_of(n * width, width), width)
        total = dot_nt(dg[part, :], wg[cut, :]) + dot_nt(du[part, :], wu[cut, :])
        terms[s, :, cut] = total.astype(BF)

    def moves(step):
        return ring_step(step, C, right, terms.at[0], held, send, recv)

    def pass_on(step):
        moves(step - 1).wait_recv()
        add_into(held.at[step - 1], terms.at[step])
        moves(step).start()

    for s in range(C):
        part = chunk(s)
        for copy in grads_in[s]:
            copy.wait()
        if s == 0:
            for n in range(C):
                for copy in weights_in[n]:
                    copy.wait()
                term_tile(s, part, n)
            moves(0).start()
        else:

            def body(n, carry):
                term_tile(s, part, n)
                return carry

            lax.fori_loop(0, C, body, 0)
    down_in = fetch(wd_hbm, wg, tile_load.at[0])
    for copy in late:
        copy.wait()

    def stored(target, t, slot):
        cut = pl.ds(pl.multiple_of(t * width, width), width)
        return pltpu.make_async_copy(stage.at[slot], target.at[cut, :], store.at[slot])

    def product(left_of, right_ref, target):
        def body(t, carry):
            slot = lax.rem(t, 2)

            @pl.when(t >= 2)
            def _():
                stored(target, t, slot).wait()

            stage[slot] = dot_tn(left_of(t), right_ref[...]).astype(BF)
            stored(target, t, slot).start()
            return carry

        lax.fori_loop(0, C, body, 0)
        for slot in range(2):
            stored(target, slot, slot).wait()

    def b_tile(t):
        return b[:, pl.ds(pl.multiple_of(t * width, width), width)]

    middle = max(1, (C - 1) // 2)
    product(b_tile, dg, gate_hbm)
    for step in range(1, middle + 1):
        if step < C - 1:
            pass_on(step)
    product(b_tile, du, up_hbm)
    product(lambda t: dys[t], hm, down_hbm)
    for step in range(middle + 1, C - 1):
        pass_on(step)
    down_in.wait()

    def out_tile(n, carry):
        cut = pl.ds(pl.multiple_of(n * width, width), width)
        terms_out = dot_nt(hm[...], wg[cut, :]).astype(BF)
        dys[0] = terms_out
        copy = pltpu.make_async_copy(dys.at[0], out_hbm.at[n], store.at[0])
        copy.start()
        copy.wait()
        return carry

    lax.fori_loop(0, C, out_tile, 0)
    moves(C - 2).wait_recv()
    sum_ref[...] = held[C - 2].astype(F32) + terms[C - 1].astype(F32)
    for step in range(C - 1):
        moves(step).wait_send()


def norm_terms(C, dg, du, hm, w_gate, w_up, w_down, b, dys):
    T, F = dg.shape
    D = w_gate.shape[0]
    rows, width = T // C, D // C
    return pl.pallas_call(
        functools.partial(norm_terms_kernel, C),
        in_specs=[ANY] * 8,
        out_specs=[VMEM_SPEC, ANY, ANY, ANY, ANY],
        out_shape=[
            struct((rows, D), F32),
            struct((D, F), BF),
            struct((D, F), BF),
            struct((D, F), BF),
            struct((C, T, width), BF),
        ],
        scratch_shapes=[
            pltpu.VMEM((T, F), BF),
            pltpu.VMEM((T, F), BF),
            pltpu.VMEM((T, F), BF),
            pltpu.VMEM((D, F), BF),
            pltpu.VMEM((D, F), BF),
            pltpu.VMEM((T, D), BF),
            pltpu.VMEM((C, T, width), BF),
            pltpu.VMEM((C, rows, D), BF),
            pltpu.VMEM((C - 1, rows, D), BF),
            pltpu.VMEM((2, width, F), BF),
            DMA((2 * C + 3,)),
            DMA((2 * C,)),
            DMA((2,)),
            DMA((C - 1,)),
            DMA((C - 1,)),
        ],
        compiler_params=comm_params(3, 62),
        cost_estimate=cost(9e10, 70 * MIB),
        name="norm_terms",
    )(dg, du, hm, w_gate, w_up, w_down, b, dys)


def resid_back_kernel(
    R, C, sum_ref, h_hbm, dys_hbm, w_hbm, down_hbm, do_hbm, dhs_hbm, down_ref,
    h, dy, w, dh, out, own, exchanged, arrived,
    load, w_load, local, h_send, h_recv, o_send, o_recv, own_load, *semaphores,
):
    me, right, left = ring_places(C)
    blocks, D, part = w.shape
    rows = sum_ref.shape[0]
    width = D // C
    mine = pl.ds(pl.multiple_of(me * rows, rows), rows)
    first_in = [
        pltpu.make_async_copy(h_hbm.at[mine, :], h, load.at[0]),
        pltpu.make_async_copy(dys_hbm.at[:, mine, :], dy, load.at[1]),
    ]
    for copy in first_in:
        copy.start()
    order = [lax.rem(me + k, C) for k in range(1, C)] + [me]
    loads = []
    for k in range(C):
        cut = pl.ds(pl.multiple_of(order[k] * width, width), width)
        copy = pltpu.make_async_copy(w_hbm.at[:, cut, :], w.at[:, cut, :], w_load.at[k])
        copy.start()
        loads.append(copy)
    sums, own_loads = held_row_sum(R, down_hbm, own, exchanged, arrived, own_load, semaphores)
    for copy in own_loads:
        copy.start()
    greet([{"col": lax.rem(me + k, C)} for k in range(1, C)] + sums.peers, C - 1 + len(sums.peers))
    for slot in sums.order():
        sums.exchange(slot).start()
    for copy in first_in:
        copy.wait()
    grad = sum_ref[...]
    centre, inverse = norm_rows(h[...])
    normed = (h[...] - centre) * inverse
    first = jnp.mean(grad, axis=1, keepdims=True)
    second = jnp.mean(grad * normed, axis=1, keepdims=True)
    dh[...] = (beside(dy).astype(F32) + inverse * (grad - first - normed * second)).astype(BF)
    copies = []
    for k in range(C):
        cut = pl.ds(pl.multiple_of(order[k] * width, width), width)
        loads[k].wait()
        total = dot_nt(dh[:, :part], w[0, cut, :])
        for n in range(1, blocks):
            total += dot_nt(dh[:, n * part : (n + 1) * part], w[n, cut, :])
        out[k] = total.astype(BF)
        if k < C - 1:
            copy = remote(out.at[k], do_hbm.at[mine, :], o_send.at[k], o_recv.at[k], col=order[k])
        else:
            copy = pltpu.make_async_copy(out.at[k], do_hbm.at[mine, :], local.at[0])
        copy.start()
        copies.append(copy)
    for k in range(C):
        cut = pl.ds(pl.multiple_of(order[k] * width, width), width)
        if k < C - 1:
            copy = remote(dh.at[:, cut], dhs_hbm.at[mine, :], h_send.at[k], h_recv.at[k], col=order[k])
        else:
            copy = pltpu.make_async_copy(dh.at[:, cut], dhs_hbm.at[mine, :], local.at[1])
        copy.start()
        copies.append(copy)
    sums.relay(lambda slot: own_loads[slot].wait())
    sums.relay_again()

    def write(part, values):
        down_ref[:, part] = values.T

    sums.finish(write, 128)
    for copy in copies:
        copy.wait()


def resid_back(R, total, h, dys, w_out, grad_down):
    C, T, width = dys.shape
    rows, D = total.shape
    depth, columns = grad_down.shape[1:]
    return pl.pallas_call(
        functools.partial(resid_back_kernel, R, C),
        in_specs=[VMEM_SPEC] + [ANY] * 4,
        out_specs=[ANY, ANY, VMEM_SPEC],
        out_shape=[
            struct((T, width), BF),
            struct((T, width), BF),
            struct((columns, depth), F32),
        ],
        scratch_shapes=[
            pltpu.VMEM((rows, D), F32),
            pltpu.VMEM((C, rows, width), BF),
            pltpu.VMEM(w_out.shape, BF),
            pltpu.VMEM((rows, D), BF),
            pltpu.VMEM((C, rows, width), BF),
            pltpu.VMEM((R // 2, depth, columns), BF),
        ]
        + row_sum_buffers(R, depth, columns)
        + [
            DMA((2,)),
            DMA((C,)),
            DMA((2,)),
            DMA((C - 1,)),
            DMA((C - 1,)),
            DMA((C - 1,)),
            DMA((C - 1,)),
            DMA((R // 2,)),
        ]
        + row_sum_semaphores(R),
        compiler_params=comm_params(4),
        cost_estimate=cost(4e10, 20 * MIB),
        name="resid_back",
    )(total, h, dys, w_out, grad_down)


def attend_back_kernel(
    R, C, log_ref, segk_ref, segq_ref, cos_ref, sin_ref,
    q_hbm, k_hbm, v_hbm, do_hbm, terms_hbm, h_hbm, up_hbm, dh_hbm, os_hbm,
    dq_ref, dk_ref, dv_ref, y_ref, up_ref, out_ref,
    q_ref, k_ref, v_ref, do_ref, terms, dk_sum, dv_sum, held, h, dh, os, mine, theirs,
    up_own, up_exchanged, up_arrived, tiles, o_exchanged, o_arrived,
    send, recv, term_load, head_load, out_load, h_load, up_load, own_send, own_recv, *semaphores,
):
    me, right, left = ring_places(C)
    T, width = q_ref.shape
    heads, bq = width // HEAD_DIM, 256
    row = lax.axis_index("row")
    side, partner_row, partner_col = lax.rem(row, 2), 2 * me + lax.rem(row, 2), lax.div(row, 2)
    apart = partner_col != me

    def term_in(s):
        return pltpu.make_async_copy(terms_hbm.at[chunk(s)], terms.at[s], term_load.at[s])

    def chunk(s):
        return lax.rem(me + 2 * C - 1 - s, C)

    cut = pl.ds(pl.multiple_of(me * width, width), width)
    head_loads = [
        pltpu.make_async_copy(source, target, head_load.at[i])
        for i, (source, target) in enumerate(((q_hbm, q_ref), (k_hbm, k_ref), (v_hbm, v_ref), (do_hbm, do_ref)))
    ]
    out_loads = [
        pltpu.make_async_copy(dh_hbm, dh, out_load.at[0]),
        pltpu.make_async_copy(os_hbm, os, out_load.at[1]),
    ]
    h_in = pltpu.make_async_copy(h_hbm.at[:, cut], h, h_load.at[0])
    up_sums, up_loads = held_row_sum(R, up_hbm, up_own, up_exchanged, up_arrived, up_load, semaphores[:4])
    out_sums = RowSum(
        R, lambda i: tiles.at[i, side], lambda i: tiles.at[i, 1 - side], o_exchanged, o_arrived, semaphores[4:]
    )
    term_in(0).start()
    for copy in head_loads + up_loads + out_loads:
        copy.start()
    for s in range(1, C):
        term_in(s).start()
    h_in.start()
    @pl.when(apart)
    def _():
        greet([{"col": left}, {"row": partner_row, "col": partner_col}] + up_sums.peers, 2 + len(up_sums.peers))

    @pl.when(jnp.logical_not(apart))
    def _():
        greet([{"col": left}] + up_sums.peers, 1 + len(up_sums.peers))

    for slot in up_sums.order():
        up_sums.exchange(slot).start()
    term_in(0).wait()

    def moves(step):
        return ring_step(step, C, right, terms.at[0], held, send, recv)

    moves(0).start()
    for copy in head_loads:
        copy.wait()

    def one_head(head, carry):
        columns = pl.ds(pl.multiple_of(head * HEAD_DIM, HEAD_DIM), HEAD_DIM)
        dk_sum[...] = jnp.zeros_like(dk_sum)
        dv_sum[...] = jnp.zeros_like(dv_sum)
        for first in range(0, T, SEQ):
            for start in range(first, first + SEQ, bq):
                stop = start + bq
                keys = k_ref[first:stop, columns]
                queries = q_ref[start:stop, columns]
                grads = do_ref[start:stop, columns]
                scores = dot_nt(keys, queries) * SCALE
                allowed = allowed_block(segk_ref[first:stop], segq_ref[:, start:stop], start - first)
                scores = jnp.where(allowed, scores, MASKED)
                probs = jnp.exp(scores - log_ref[head, :, start:stop])
                dv_sum[first:stop] += dot_nn(probs.astype(BF), grads)
                grad_probs = dot_nt(v_ref[first:stop, columns], grads)
                inner = jnp.sum(probs * grad_probs, axis=0, keepdims=True)
                grad_scores = (probs * (grad_probs - inner)).astype(BF)
                dk_sum[first:stop] += dot_nn(grad_scores, queries)
                grad_query = dot_tn(keys, grad_scores).T * SCALE
                dq_ref[start:stop, columns] = turn(grad_query, cos_ref[start:stop], -sin_ref[start:stop]).astype(BF)
        dk_ref[:, columns] = turn(dk_sum[...] * SCALE, cos_ref[...], -sin_ref[...]).astype(BF)
        dv_ref[:, columns] = dv_sum[...].astype(BF)
        return carry

    lax.fori_loop(0, 1, one_head, 0)
    up_sums.relay(lambda slot: up_loads[slot].wait())
    for copy in out_loads:
        copy.wait()
    depth = tiles.shape[2]
    for slot in out_sums.order():
        chip = lax.div(out_sums.places(slot), 2)
        right_side = jnp.concatenate([os[chip, i] for i in range(heads)], axis=1)
        product = dot_tn(dh[...], right_side).astype(BF)
        tiles[slot, 0] = product[:depth]
        tiles[slot, 1] = product[depth:]
        out_sums.exchange(slot).start()
    lax.fori_loop(1, heads, one_head, 0)
    out_sums.relay()
    for s in range(1, C):
        term_in(s).wait()
    for step in range(1, C - 1):
        moves(step - 1).wait_recv()
        add_into(held.at[step - 1], terms.at[step])
        moves(step).start()
        if step == 1:
            out_sums.relay_again()
            up_sums.relay_again()

    def write_up(part, values):
        up_ref[part, :] = values

    def write_out(part, values):
        mine[part, :] = values.astype(BF)

    out_sums.finish(write_out)
    handed = remote(mine, theirs, own_send.at[0], own_recv.at[0], row=partner_row, col=partner_col)

    @pl.when(apart)
    def _():
        handed.start()

    up_sums.finish(write_up)
    h_in.wait()
    moves(C - 2).wait_recv()
    y_ref[...] = (h[...] + held[C - 2].astype(F32) + terms[C - 1].astype(F32)).astype(BF)

    @pl.when(apart)
    def _():
        handed.wait()
        out_ref[...] = theirs[...].astype(F32).T

    @pl.when(jnp.logical_not(apart))
    def _():
        out_ref[...] = mine[...].astype(F32).T

    for step in range(C - 1):
        moves(step).wait_send()


def attend_back(R, q, k, v, do, log_total, seg_column, seg_row, cos_table, sin_table, out_terms, h, grad_up, dh, os):
    C = out_terms.shape[0]
    T, width = q.shape
    assert R == 2 * C
    depth, columns = grad_up.shape[1:]
    one = pltpu.VMEM((T, width), BF)
    return pl.pallas_call(
        functools.partial(attend_back_kernel, R, C),
        in_specs=[VMEM_SPEC] * 5 + [ANY] * 9,
        out_specs=[VMEM_SPEC] * 6,
        out_shape=[struct((T, width), BF)] * 4 + [struct((depth, columns), F32), struct((width, depth), F32)],
        scratch_shapes=[
            one,
            one,
            one,
            one,
            pltpu.VMEM((C, T, width), BF),
            pltpu.VMEM((T, HEAD_DIM), F32),
            pltpu.VMEM((T, HEAD_DIM), F32),
            pltpu.VMEM((C - 1, T, width), BF),
            pltpu.VMEM((T, width), F32),
            one,
            pltpu.VMEM(os.shape, BF),
            pltpu.VMEM((depth, width), BF),
            pltpu.VMEM((depth, width), BF),
            pltpu.VMEM((R // 2, depth, columns), BF),
        ]
        + row_sum_buffers(R, depth, columns)
        + [pltpu.VMEM((R // 2, 2, depth, width), BF)]
        + row_sum_buffers(R, depth, width)
        + [
            DMA((C - 1,)),
            DMA((C - 1,)),
            DMA((C,)),
            DMA((4,)),
            DMA((2,)),
            DMA((1,)),
            DMA((R // 2,)),
            DMA((1,)),
            DMA((1,)),
        ]
        + row_sum_semaphores(R)
        + row_sum_semaphores(R),
        compiler_params=comm_params(5),
        cost_estimate=cost(7e10, 14 * MIB),
        name="attend_back",
    )(log_total, seg_column, seg_row, cos_table, sin_table, q, k, v, do, out_terms, h, grad_up, dh, os)


def input_terms_kernel(
    R, C, dq_ref, dk_ref, dv_ref, mu_hbm, r_hbm, w_hbm, a_hbm, x_hbm, dh_hbm, grad_hbm,
    y_ref, gq_ref, gk_ref, gv_ref, total_ref,
    mu_ref, r_ref, w_ref, a_ref, x_ref, dh_ref,
    terms, held, da, stats, stats_in, own, exchanged, arrived, tiles, q_exchanged, q_arrived,
    send, recv, s_send, s_recv, w_load, late_load, load, *semaphores,
):
    me, right, left = ring_places(C)
    T, width = dq_ref.shape
    D = width * C
    heads = (dq_ref, dk_ref, dv_ref)

    def cut_of(s):
        return pl.ds(pl.multiple_of(lax.rem(me + 2 * C - 1 - s, C) * width, width), width)

    def weight_in(s):
        return pltpu.make_async_copy(w_hbm.at[:, cut_of(s), :], w_ref.at[:, cut_of(s), :], w_load.at[s])

    for s in range(C):
        weight_in(s).start()
    late = [
        pltpu.make_async_copy(source, target, late_load.at[i])
        for i, (source, target) in enumerate(
            ((a_hbm, a_ref), (x_hbm, x_ref), (dh_hbm, dh_ref), (mu_hbm, mu_ref), (r_hbm, r_ref))
        )
    ]
    for copy in late:
        copy.start()
    depth = tiles.shape[2]
    sums, loads = held_row_sum(R, grad_hbm, own, exchanged, arrived, load, semaphores[:4])
    side = lax.rem(lax.axis_index("row"), 2)
    q_sums = RowSum(
        R, lambda i: tiles.at[i, side], lambda i: tiles.at[i, 1 - side], q_exchanged, q_arrived, semaphores[4:]
    )
    for copy in loads:
        copy.start()
    greet([{"col": lax.rem(me + k, C)} for k in range(1, C)] + sums.peers, C - 1 + len(sums.peers))
    for slot in sums.order():
        sums.exchange(slot).start()

    def moves(step):
        return ring_step(step, C, right, terms.at[0], held, send, recv)

    def pass_on(step):
        moves(step - 1).wait_recv()
        add_into(held.at[step - 1], terms.at[step])
        moves(step).start()

    def compute(s):
        cut = cut_of(s)
        weight_in(s).wait()
        total = dot_nt(dq_ref[...], w_ref[0, cut, :])
        total += dot_nt(dk_ref[...], w_ref[1, cut, :])
        total += dot_nt(dv_ref[...], w_ref[2, cut, :])
        terms[s] = total.astype(BF)

    compute(0)
    moves(0).start()

    def body(s, carry):
        compute(s)
        return carry

    lax.fori_loop(1, C, body, 0)
    for copy in late:
        copy.wait()
    sums.relay(lambda slot: loads[slot].wait())
    for slot in q_sums.order():
        start = pl.multiple_of(lax.div(q_sums.places(slot), 2) * 2 * depth, 2 * depth)
        left_tile = a_ref[:, pl.ds(start, 2 * depth)]
        for i, right_side in enumerate(heads):
            product = dot_tn(left_tile, right_side[...]).astype(BF)
            tiles[slot, 0, :, i * width : (i + 1) * width] = product[:depth]
            tiles[slot, 1, :, i * width : (i + 1) * width] = product[depth:]
        q_sums.exchange(slot).start()
    q_sums.relay()
    pass_on(1)
    sums.relay_again()
    q_sums.relay_again()
    for step in range(2, C - 1):
        pass_on(step)

    def write(part, values):
        total_ref[part, :] = values

    def write_qkv(part, values):
        for i, target in enumerate((gq_ref, gk_ref, gv_ref)):
            target[part, :] = values[:, i * width : (i + 1) * width]

    sums.finish(write)
    q_sums.finish(write_qkv)
    moves(C - 2).wait_recv()
    size = 128

    def normed_of(rows):
        return (x_ref[rows, :].astype(F32) - mu_ref[rows, :]) * r_ref[rows, :]

    def sum_rows(i, carry):
        rows = pl.ds(pl.multiple_of(i * size, size), size)
        grad = held[C - 2, rows, :].astype(F32) + terms[C - 1, rows, :].astype(F32)
        da[rows, :] = grad
        lane = lax.broadcasted_iota(jnp.int32, (size, 128), 1)
        first = jnp.sum(grad, axis=1, keepdims=True)
        second = jnp.sum(grad * normed_of(rows), axis=1, keepdims=True)
        packed = jnp.where(lane == 0, first, jnp.where(lane == 1, second, 0.0))
        stats[:, rows] = packed.T[:8]
        return carry

    lax.fori_loop(0, T // size, sum_rows, 0)
    exchanges = [
        remote(stats, stats_in.at[k - 1], s_send.at[k - 1], s_recv.at[k - 1], col=lax.rem(me + k, C)) for k in range(1, C)
    ]
    for copy in exchanges:
        copy.start()
    for copy in exchanges:
        copy.wait_recv()

    def last_rows(i, carry):
        rows = pl.ds(pl.multiple_of(i * size, size), size)
        both = stats[:, rows]
        for k in range(C - 1):
            both += stats_in[k, :, rows]
        columns = jnp.concatenate([both, jnp.zeros((120, size), F32)], axis=0).T * (1.0 / D)
        grad = da[rows, :] - columns[:, 0:1] - normed_of(rows) * columns[:, 1:2]
        y_ref[rows, :] = (dh_ref[rows, :].astype(F32) + r_ref[rows, :] * grad).astype(BF)
        return carry

    lax.fori_loop(0, T // size, last_rows, 0)
    for copy in exchanges:
        copy.wait_send()
    for step in range(C - 1):
        moves(step).wait_send()


def input_terms(R, C, dq, dk, dv, w_qkv, a, tokens, dh, mu, r, grad):
    T, width = dq.shape
    D = w_qkv.shape[1]
    half, low = R // 2, D // R
    depth, columns = grad.shape[1:]
    return pl.pallas_call(
        functools.partial(input_terms_kernel, R, C),
        in_specs=[VMEM_SPEC] * 3 + [ANY] * 7,
        out_specs=[VMEM_SPEC] * 5,
        out_shape=[struct((T, width), BF)]
        + [struct((low, width), F32)] * 3
        + [struct((depth, columns), F32)],
        scratch_shapes=[
            pltpu.VMEM((T, 1), F32),
            pltpu.VMEM((T, 1), F32),
            pltpu.VMEM((3, D, width), BF),
            pltpu.VMEM((T, D), BF),
            pltpu.VMEM((T, width), BF),
            pltpu.VMEM((T, width), BF),
            pltpu.VMEM((C, T, width), BF),
            pltpu.VMEM((C - 1, T, width), BF),
            pltpu.VMEM((T, width), F32),
            pltpu.VMEM((8, T), F32),
            pltpu.VMEM((C - 1, 8, T), F32),
            pltpu.VMEM((half, depth, columns), BF),
        ]
        + row_sum_buffers(R, depth, columns)
        + [pltpu.VMEM((half, 2, low, 3 * width), BF)]
        + row_sum_buffers(R, low, 3 * width)
        + [
            DMA((C - 1,)),
            DMA((C - 1,)),
            DMA((C - 1,)),
            DMA((C - 1,)),
            DMA((C,)),
            DMA((5,)),
            DMA((half,)),
        ]
        + row_sum_semaphores(R)
        + row_sum_semaphores(R),
        compiler_params=comm_params(6, 63),
        cost_estimate=cost(8e10, 20 * MIB),
        name="input_terms",
    )(dq, dk, dv, mu, r, w_qkv, a, tokens, dh, grad)


def on_device(R, C, tokens, cotangent, segments, w_query, w_key, w_value, w_out, w_gate, w_up, w_down):
    T, width = tokens.shape
    D = width * C
    gathered = lambda w: lax.all_gather(w, "row", axis=0, tiled=True)

    gate_w, up_w, down_w = gathered(w_gate), gathered(w_up), gathered(w_down.T)
    seg_column, seg_row = segments.reshape(T, 1), segments.reshape(1, T)
    xs, w_qkv, cos_table, sin_table = first_gather(R, C, seg_column, seg_row, tokens, w_query, w_key, w_value)
    w_qkv = w_qkv.reshape(3, D, width)
    act_one, q, k, v, mu_one, r_one, out_part = norm_and_project(xs, w_qkv, cos_table, sin_table, w_out)
    os, log_total, out_w = attend(R, C, q, k, v, seg_column, seg_row, out_part.reshape(D, -1))
    h_full, act_two, hidden, slope, silu, dys = feed_forward(
        C, os, out_w, xs, gate_w, up_w, cotangent
    )
    dg, du = hidden_back(dys, down_w, slope, silu)
    total, grad_gate, grad_up, grad_down, out_terms = norm_terms(
        C, dg, du, hidden, gate_w, up_w, down_w, act_two, dys
    )
    by_row = lambda values: values.reshape(R, D // R, -1)
    grad_heads, grad_resid, grad_down = resid_back(R, total, h_full, dys, out_w, by_row(grad_down))
    dq, dk, dv, output, grad_up, grad_out = attend_back(
        R, q, k, v, grad_heads, log_total, seg_column, seg_row, cos_table, sin_table, out_terms, h_full,
        by_row(grad_up), grad_resid, os,
    )
    grad_tokens, grad_query, grad_key, grad_value, grad_gate = input_terms(
        R, C, dq, dk, dv, w_qkv, act_one, tokens, grad_resid, mu_one, r_one, by_row(grad_gate)
    )
    return (output, grad_tokens, grad_query, grad_key, grad_value, grad_out, grad_gate, grad_up, grad_down)


def solution(mesh):
    here = P("row", "col")
    turned = P("col", "row")
    return jax.shard_map(
        functools.partial(on_device, mesh.shape["row"], mesh.shape["col"]),
        mesh=mesh,
        in_specs=(here, here, P("row"), here, here, here, turned, here, here, turned),
        out_specs=(here, here, here, here, here, turned, here, here, turned),
        check_vma=False,
    )
```

```python
import functools

import jax
import jax.numpy as jnp
from jax import lax
from jax.experimental import pallas as pl
from jax.experimental.pallas import tpu as pltpu
from jax.sharding import PartitionSpec as P

HEAD_DIM = 128
HALF = HEAD_DIM // 2
SEQ = 1024
EPSILON = 1e-05
MASKED = -1e30
SCALE = HEAD_DIM ** (-0.5)
BF = jnp.bfloat16
F32 = jnp.float32
MIB = 1 << 20
ANY = pl.BlockSpec(memory_space=pl.ANY)


def dot_nn(left, right):
    return jnp.dot(left, right, preferred_element_type=F32)


def dot_tn(left, right):
    return lax.dot_general(left, right, (((0,), (0,)), ((), ())), preferred_element_type=F32)


def dot_nt(left, right):
    return lax.dot_general(left, right, (((1,), (1,)), ((), ())), preferred_element_type=F32)


def struct(shape, dtype):
    return jax.ShapeDtypeStruct(shape, dtype)


def params(mib=60):
    return pltpu.CompilerParams(vmem_limit_bytes=mib * MIB)


def cost(flops, moved):
    return pl.CostEstimate(flops=int(flops), bytes_accessed=int(moved), transcendentals=0)


def turn(values, cos_table, sin_table):
    return values * cos_table + pltpu.roll(values, HALF, 1) * sin_table


MESH = pl.DeviceIdType.MESH
VMEM_SPEC = pl.BlockSpec(memory_space=pltpu.VMEM)
DMA = pltpu.SemaphoreType.DMA


def comm_params(number, mib=60):
    return pltpu.CompilerParams(vmem_limit_bytes=mib * MIB, collective_id=number, has_side_effects=True)


def remote(source, target, send, recv, **device):
    return pltpu.make_async_remote_copy(
        src_ref=source, dst_ref=target, send_sem=send, recv_sem=recv, device_id=device, device_id_type=MESH
    )


def greet(senders, targets):
    semaphore = pltpu.get_barrier_semaphore()
    for device in senders:
        pl.semaphore_signal(semaphore, inc=1, device_id=device, device_id_type=MESH)
    pl.semaphore_wait(semaphore, targets)


def ring_places(C):
    me = lax.axis_index("col")
    return me, lax.rem(me + 1, C), lax.rem(me + C - 1, C)


def row_places(R):
    row = lax.axis_index("row")
    ahead = [lax.rem(row + 2 * k, R) for k in range(R // 2)]
    behind = [lax.rem(row + R - 2 * k, R) for k in range(R // 2)]
    other = row + 1 - 2 * lax.rem(row, 2)
    return row, ahead, behind, other


def gather_ring(C, source, whole, send, recv):
    me, right, left = ring_places(C)
    copies = []
    for step in range(C - 1):
        owner = lax.rem(me - step + C, C)
        piece = source if step == 0 else whole.at[owner]
        copies.append(remote(piece, whole.at[owner], send.at[step], recv.at[step], col=right))
    return copies


def gather_kernel(
    R, C, segk_ref, segq_ref, rate_ref, x_ref, wq_ref, wk_ref, wv_ref, xs_ref, w_ref, cos_ref, sin_ref,
    local, x_send, x_recv, w_send, w_recv, f_send, f_recv,
):
    me, right, left = ring_places(C)
    row, ahead, behind, other = row_places(R)
    weights = (wq_ref, wk_ref, wv_ref)
    mine = [
        pltpu.make_async_copy(x_ref, xs_ref.at[me], local.at[0]),
    ] + [pltpu.make_async_copy(w, w_ref.at[i, row], local.at[1 + i]) for i, w in enumerate(weights)]
    for copy in mine:
        copy.start()
    greet(
        [{"col": left}, {"row": other}] + [{"row": r} for r in behind[1:]],
        1 + R // 2,
    )

    x_copies = gather_ring(C, x_ref, xs_ref, x_send, x_recv)
    x_copies[0].start()
    spread, forward = [], []
    for i, w in enumerate(weights):
        for k in range(1, R // 2):
            copy = remote(w, w_ref.at[i, row], w_send.at[i, k], w_recv.at[i, k], row=ahead[k])
            copy.start()
            spread.append(copy)
        copy = remote(w, w_ref.at[i, row], f_send.at[i, 0], f_recv.at[i, 0], row=other)
        copy.start()
        forward.append(copy)
    T = cos_ref.shape[0]
    size = 128

    def table_rows(i, carry):
        rows = pl.ds(pl.multiple_of(i * size, size), size)
        first = SEQ * lax.div(i * size, SEQ)
        shape = (size, T)
        queries = lax.broadcasted_iota(jnp.int32, shape, 0) + i * size
        keys = lax.broadcasted_iota(jnp.int32, shape, 1)
        seen = (segk_ref[rows, :] == segq_ref[...]) & (keys <= queries) & (keys >= first)
        place = jnp.sum(jnp.where(seen, 1.0, 0.0), axis=1, keepdims=True) - 1.0
        angles = place * rate_ref[...]
        lane = lax.broadcasted_iota(jnp.int32, angles.shape, 1)
        sine = jnp.sin(angles)
        cos_ref[rows, :] = jnp.cos(angles)
        sin_ref[rows, :] = jnp.where(lane < HALF, -sine, sine)
        return carry

    lax.fori_loop(0, T // size, table_rows, 0)
    for s in range(1, C - 1):
        x_copies[s - 1].wait_recv()
        x_copies[s].start()
    for i in range(3):
        for k in range(1, R // 2):
            spread[i * (R // 2 - 1) + k - 1].wait_recv()
            block = w_ref.at[i, behind[k]]
            copy = remote(block, block, f_send.at[i, k], f_recv.at[i, k], row=other)
            copy.start()
            forward.append(copy)
    x_copies[-1].wait_recv()
    for copy in forward:
        copy.wait_recv()
    for copy in x_copies + spread + forward:
        copy.wait_send()
    for copy in mine:
        copy.wait()


def first_gather(R, C, seg_column, seg_row, tokens, w_query, w_key, w_value):
    depth, width = w_query.shape
    T = tokens.shape[0]
    half = R // 2
    rate = 10000.0 ** (-(jnp.arange(HALF, dtype=F32) * 2.0 / HEAD_DIM))
    rate = jnp.concatenate([rate, rate]).reshape(1, HEAD_DIM)
    return pl.pallas_call(
        functools.partial(gather_kernel, R, C),
        in_specs=[VMEM_SPEC] * 3 + [ANY] * 4,
        out_specs=[ANY] * 2 + [VMEM_SPEC] * 2,
        out_shape=[
            struct((C,) + tokens.shape, BF),
            struct((3, R, depth, width), BF),
            struct((T, HEAD_DIM), F32),
            struct((T, HEAD_DIM), F32),
        ],
        scratch_shapes=[
            DMA((4,)),
            DMA((C - 1,)),
            DMA((C - 1,)),
            DMA((3, half)),
            DMA((3, half)),
            DMA((3, half)),
            DMA((3, half)),
        ],
        compiler_params=comm_params(0),
        cost_estimate=cost(6e10, 14 * MIB),
        name="first_gather",
    )(seg_column, seg_row, rate, tokens, w_query, w_key, w_value)


def norm_rows(x):
    centre = jnp.mean(x, axis=-1, keepdims=True)
    spread = jnp.mean(x * x, axis=-1, keepdims=True) - centre * centre
    inverse = lax.rsqrt(spread + EPSILON)
    return centre, inverse


def beside(ref):
    return jnp.concatenate([ref[j] for j in range(ref.shape[0])], axis=1)


def qkv_kernel(
    C, xs_ref, w_ref, cos_ref, sin_ref, wo_ref, a_ref, q_ref, k_ref, v_ref, mu_ref, r_ref, wos_ref, local, send, recv
):
    step, steps = pl.program_id(0), pl.num_programs(0)
    me, right, left = ring_places(C)
    copies = gather_ring(C, wo_ref, wos_ref, send, recv)
    mine = pltpu.make_async_copy(wo_ref, wos_ref.at[me], local.at[0])

    @pl.when(step == 0)
    def _():
        mine.start()
        greet([{"col": left}], 1)
        copies[0].start()

    for s in range(1, C - 1):

        @pl.when(step == jnp.minimum(2 * s, steps - 1))
        def _():
            copies[s - 1].wait_recv()
            copies[s].start()

    x = beside(xs_ref).astype(F32)
    centre, inverse = norm_rows(x)
    a = ((x - centre) * inverse).astype(BF)
    a_ref[...] = a
    mu_ref[...] = centre
    r_ref[...] = inverse
    cosine, sine = cos_ref[...], sin_ref[...]
    for index, out in enumerate((q_ref, k_ref, v_ref)):
        product = dot_nn(a, w_ref[index])
        if index == 2:
            out[...] = product.astype(BF)
            continue
        for start in range(0, out.shape[1], HEAD_DIM):
            part = product[:, start : start + HEAD_DIM]
            out[:, start : start + HEAD_DIM] = turn(part, cosine, sine).astype(BF)

    @pl.when(step == steps - 1)
    def _():
        copies[-1].wait_recv()
        for copy in copies:
            copy.wait_send()
        mine.wait()


def norm_and_project(xs, w_qkv, cos_table, sin_table, w_out):
    C, T, width = xs.shape
    D = width * C
    bt = 256
    rows = lambda n: pl.BlockSpec((bt, n), lambda i: (i, 0))
    return pl.pallas_call(
        functools.partial(qkv_kernel, C),
        grid=(T // bt,),
        in_specs=[
            pl.BlockSpec((C, bt, width), lambda i: (0, i, 0)),
            pl.BlockSpec(w_qkv.shape, lambda i: (0, 0, 0), pipeline_mode=pl.Buffered(1)),
            rows(HEAD_DIM),
            rows(HEAD_DIM),
            ANY,
        ],
        out_specs=[rows(D), rows(width), rows(width), rows(width), rows(1), rows(1), ANY],
        out_shape=[
            struct((T, D), BF),
            struct((T, width), BF),
            struct((T, width), BF),
            struct((T, width), BF),
            struct((T, 1), F32),
            struct((T, 1), F32),
            struct((C,) + w_out.shape, BF),
        ],
        scratch_shapes=[DMA((1,)), DMA((C - 1,)), DMA((C - 1,))],
        compiler_params=comm_params(7),
        cost_estimate=cost(2e10, 14 * MIB),
        name="norm_and_project",
    )(xs, w_qkv, cos_table, sin_table, w_out)


def allowed_block(seg_key, seg_query, first_query):
    shape = (seg_key.shape[0], seg_query.shape[1])
    keys = lax.broadcasted_iota(jnp.int32, shape, 0)
    queries = lax.broadcasted_iota(jnp.int32, shape, 1) + first_query
    return (seg_key == seg_query) & (keys <= queries)


def attend_kernel(
    R, C, q_ref, k_ref, v_ref, segk_ref, segq_ref, wos_ref, os_ref, log_ref, w_ref,
    o_buf, local, o_send, o_recv, w_send, w_recv, f_send, f_recv,
):
    me, right, left = ring_places(C)
    row, ahead, behind, other = row_places(R)
    T, width = q_ref.shape
    heads, bq = width // HEAD_DIM, 256
    greet([{"col": left}, {"row": other}] + [{"row": r} for r in behind[1:]], 1 + R // 2)
    mine = pltpu.make_async_copy(wos_ref, w_ref.at[row], local.at[0])
    mine.start()
    spread, forward = [], []
    for k in range(1, R // 2):
        copy = remote(wos_ref, w_ref.at[row], w_send.at[k], w_recv.at[k], row=ahead[k])
        copy.start()
        spread.append(copy)
    copy = remote(wos_ref, w_ref.at[row], f_send.at[0], f_recv.at[0], row=other)
    copy.start()
    forward.append(copy)

    def ring(step, head):
        owner = lax.rem(me - step + C, C)
        piece = o_buf.at[head] if step == 0 else os_ref.at[owner, head]
        return remote(piece, os_ref.at[owner, head], o_send.at[step, head], o_recv.at[step, head], col=right)

    def one_head(head, carry):
        columns = pl.ds(pl.multiple_of(head * HEAD_DIM, HEAD_DIM), HEAD_DIM)
        for first in range(0, T, SEQ):
            for start in range(first, first + SEQ, bq):
                stop = start + bq
                scores = dot_nt(k_ref[first:stop, columns], q_ref[start:stop, columns]) * SCALE
                allowed = allowed_block(segk_ref[first:stop], segq_ref[:, start:stop], start - first)
                scores = jnp.where(allowed, scores, MASKED)
                peak = jnp.max(scores, axis=0, keepdims=True)
                exponent = jnp.exp(scores - peak)
                total = jnp.sum(exponent, axis=0, keepdims=True)
                weights = (exponent * (1.0 / total)).astype(BF)
                o_buf[head, start:stop] = dot_tn(v_ref[first:stop, columns], weights).T.astype(BF)
                log_ref[head, :, start:stop] = peak + jnp.log(total)
        ring(0, head).start()
        pltpu.make_async_copy(o_buf.at[head], os_ref.at[me, head], local.at[1 + head]).start()
        return carry

    lax.fori_loop(0, heads, one_head, 0)
    for step in range(1, C - 1):
        for head in range(heads):
            ring(step - 1, head).wait_recv()
            ring(step, head).start()
    for k in range(1, R // 2):
        spread[k - 1].wait_recv()
        block = w_ref.at[behind[k]]
        copy = remote(block, block, f_send.at[k], f_recv.at[k], row=other)
        copy.start()
        forward.append(copy)
    for head in range(heads):
        ring(C - 2, head).wait_recv()
        pltpu.make_async_copy(o_buf.at[head], os_ref.at[me, head], local.at[1 + head]).wait()
        for step in range(C - 1):
            ring(step, head).wait_send()
    for copy in forward:
        copy.wait_recv()
    for copy in spread + forward:
        copy.wait_send()
    mine.wait()


def attend(R, C, q, k, v, seg_column, seg_row, w_part):
    T, width = q.shape
    heads, half = width // HEAD_DIM, R // 2
    return pl.pallas_call(
        functools.partial(attend_kernel, R, C),
        in_specs=[VMEM_SPEC] * 5 + [ANY],
        out_specs=[ANY, VMEM_SPEC, ANY],
        out_shape=[
            struct((C, heads, T, HEAD_DIM), BF),
            struct((heads, 1, T), F32),
            struct((R,) + w_part.shape, BF),
        ],
        scratch_shapes=[
            pltpu.VMEM((heads, T, HEAD_DIM), BF),
            DMA((1 + heads,)),
            DMA((C - 1, heads)),
            DMA((C - 1, heads)),
            DMA((half,)),
            DMA((half,)),
            DMA((half,)),
            DMA((half,)),
        ],
        compiler_params=comm_params(1),
        cost_estimate=cost(7e10, 14 * MIB),
        name="attend",
    )(q, k, v, seg_column, seg_row, w_part)


def ring_step(step, C, right, first, held, send, recv):
    source = first if step == 0 else held.at[step - 1]
    return remote(source, held.at[step], send.at[step], recv.at[step], col=right)


def add_into(held, terms):
    size = 64

    def body(i, carry):
        rows = pl.ds(pl.multiple_of(i * size, size), size)
        held[rows, :] = (held[rows, :].astype(F32) + terms[rows, :].astype(F32)).astype(BF)
        return carry

    lax.fori_loop(0, held.shape[0] // size, body, 0)


class RowSum:
    def __init__(self, R, own, twin, exchanged, arrived, semaphores):
        self.P = R // 4
        self.own, self.twin, self.exchanged, self.arrived = own, twin, exchanged, arrived
        self.x_send, self.x_recv, self.y_send, self.y_recv = semaphores
        self.width = arrived.shape[2]
        self.places = row_of(R)
        self.peers = row_peers(R)

    def part(self, ref, side):
        return ref.at[:, pl.ds(side * self.width, self.width)]

    def exchange(self, slot):
        return remote(
            self.twin(slot), self.exchanged.at[slot], self.x_send.at[slot], self.x_recv.at[slot], row=self.places(0, True)
        )

    def send(self, slot, side, index, target):
        return remote(
            self.part(self.own(slot), side), self.arrived.at[index], self.y_send.at[index], self.y_recv.at[index],
            row=self.places(target),
        )

    def left_one(self, dp):
        return self.send(2 * dp + 1, 0, dp, 1)

    def left_two(self, dp):
        return self.send(2 * dp, 0, self.P + dp - 1, 2 * dp)

    def right_one(self, dp, dq):
        return self.send(2 * dp + dq, 1, 2 * self.P - 1 + 2 * (dp - 1) + dq, 2 * dp)

    def right_two(self):
        return self.send(1, 1, 4 * self.P - 3, 1)

    def order(self):
        return (
            [2 * dp + 1 for dp in range(1, self.P)] + [1] + [2 * dp for dp in range(1, self.P)] + [0]
        )

    def relay(self, before=None):
        for slot in self.order():
            if before is not None:
                before(slot)
            self.exchange(slot).wait_recv()
            add_into(self.own(slot), self.exchanged.at[slot])
            dp, dq = divmod(slot, 2)
            if dq:
                self.left_one(dp).start()
            if dp:
                self.right_one(dp, dq).start()

    def relay_again(self):
        for dp in range(1, self.P):
            self.left_one(dp).wait_recv()
            add_into(self.part(self.own(2 * dp), 0), self.arrived.at[dp])
            self.left_two(dp).start()
        for dp in range(1, self.P):
            copy = self.right_one(dp, 1)
            copy.wait_recv()
            add_into(self.part(self.own(1), 1), self.arrived.at[2 * self.P - 1 + 2 * (dp - 1) + 1])
        self.right_two().start()

    def finish(self, write, size=64):
        P, width = self.P, self.width
        self.left_one(0).wait_recv()
        self.right_two().wait_recv()
        for dp in range(1, P):
            self.left_two(dp).wait_recv()
            self.right_one(dp, 0).wait_recv()
        lefts = [0] + [P + dp - 1 for dp in range(1, P)]
        rights = [4 * P - 3] + [2 * P - 1 + 2 * (dp - 1) for dp in range(1, P)]

        def body(i, carry):
            rows = pl.ds(pl.multiple_of(i * size, size), size)
            total = self.own(0)[rows, :].astype(F32)
            halves = []
            for side, places in enumerate((lefts, rights)):
                half = total[:, side * width : (side + 1) * width]
                for index in places:
                    half += self.arrived[index, rows, :].astype(F32)
                halves.append(half)
            write(rows, jnp.concatenate(halves, axis=1))
            return carry

        lax.fori_loop(0, self.exchanged.shape[1] // size, body, 0)
        for slot in range(2 * P):
            self.exchange(slot).wait_send()
        self.left_one(0).wait_send()
        self.right_two().wait_send()
        for dp in range(1, P):
            self.left_one(dp).wait_send()
            self.left_two(dp).wait_send()
            self.right_one(dp, 0).wait_send()
            self.right_one(dp, 1).wait_send()


def row_of(R):
    row = lax.axis_index("row")
    side, chip = lax.rem(row, 2), lax.div(row, 2)
    p, q = lax.div(chip, 2), lax.rem(chip, 2)

    def place(slot, twin=False):
        dp, dq = divmod(slot, 2)
        chip_there = 2 * lax.rem(p + dp, R // 4) + lax.rem(q + dq, 2)
        return 2 * chip_there + (1 - side if twin else side)

    return place


def row_peers(R):
    place = row_of(R)
    return [{"row": place(0, True)}, {"row": place(1)}] + [{"row": place(2 * dp)} for dp in range(1, R // 4)]


def row_sum_semaphores(R):
    return [DMA((R // 2,)), DMA((R // 2,)), DMA((R - 2,)), DMA((R - 2,))]


def row_sum_buffers(R, depth, columns):
    return [
        pltpu.VMEM((R // 2, depth, columns), BF),
        pltpu.VMEM((R - 2, depth, columns // 2), BF),
    ]


def held_row_sum(R, grad_hbm, own, exchanged, arrived, load, semaphores):
    place = row_of(R)
    sums = RowSum(R, lambda i: own.at[i], lambda i: grad_hbm.at[place(i, True)], exchanged, arrived, semaphores)
    loads = [pltpu.make_async_copy(grad_hbm.at[place(i)], own.at[i], load.at[i]) for i in range(R // 2)]
    return sums, loads


class LineGather:
    def __init__(self, C, source, whole, up, down):
        self.C, self.source, self.whole, self.up, self.down = C, source, whole, up, down
        self.me = lax.axis_index("col")

    def upward(self, step):
        owner = self.me - step
        piece = self.source if step == 0 else self.whole.at[owner]
        return remote(piece, self.whole.at[owner], self.up[0].at[step], self.up[1].at[step], col=self.me + 1)

    def downward(self, step):
        owner = self.me + step
        piece = self.source if step == 0 else self.whole.at[owner]
        return remote(piece, self.whole.at[owner], self.down[0].at[step], self.down[1].at[step], col=self.me - 1)

    def arrival(self, step, rises):
        sender = self.me - 1 if rises else self.me + 1
        send, recv = self.up if rises else self.down
        target = self.whole.at[sender - step if rises else sender + step]
        return remote(target, target, send.at[step], recv.at[step], col=sender)

    def event(self, step):
        me, last = self.me, self.C - 1
        if step:

            @pl.when(me >= step)
            def _():
                self.arrival(step - 1, True).wait_recv()

            @pl.when(me + step <= last)
            def _():
                self.arrival(step - 1, False).wait_recv()

        if step < last:

            @pl.when((me >= step) & (me < last))
            def _():
                self.upward(step).start()

            @pl.when((me + step <= last) & (me > 0))
            def _():
                self.downward(step).start()

    def finish(self):
        me, last = self.me, self.C - 1
        for step in range(last):

            @pl.when((me >= step) & (me < last))
            def _():
                self.upward(step).wait_send()

            @pl.when((me + step <= last) & (me > 0))
            def _():
                self.downward(step).wait_send()


class LineSum:
    def __init__(self, C, terms, rising, falling, up, down):
        self.C, self.terms, self.rising, self.falling, self.up, self.down = C, terms, rising, falling, up, down
        self.me = lax.axis_index("col")

    def upward(self, m, alone):
        source = self.terms.at[self.C - 1 - m] if alone else self.rising.at[m]
        return remote(source, self.rising.at[m], self.up[0].at[m], self.up[1].at[m], col=lax.rem(self.me + 1, self.C))

    def downward(self, m, alone):
        source = self.terms.at[m] if alone else self.falling.at[m]
        return remote(
            source, self.falling.at[m], self.down[0].at[m], self.down[1].at[m], col=lax.rem(self.me + self.C - 1, self.C)
        )

    def level(self, t):
        me, last = self.me, self.C - 1
        rise, fall = t - me, t - (last - me)
        if t < last:

            @pl.when(me == 0)
            def _():
                if t:
                    self.upward(t - 1, True).wait_send()
                self.upward(t, True).start()

            @pl.when(me == last)
            def _():
                if t:
                    self.downward(t - 1, True).wait_send()
                self.downward(t, True).start()

        if t:

            @pl.when((me > 0) & (rise >= 0))
            def _():
                self.upward(rise, False).wait_recv()
                if t < last:
                    add_into(self.rising.at[rise], self.terms.at[last - rise])
                    self.upward(rise, False).start()

            @pl.when((me < last) & (fall >= 0))
            def _():
                self.downward(fall, False).wait_recv()
                if t < last:
                    add_into(self.falling.at[fall], self.terms.at[fall])
                    self.downward(fall, False).start()

    def finish(self):
        me, last = self.me, self.C - 1

        @pl.when(me == 0)
        def _():
            self.upward(last - 1, True).wait_send()

        @pl.when(me == last)
        def _():
            self.downward(last - 1, True).wait_send()

        for m in range(last):

            @pl.when((me > 0) & (m < last - me))
            def _():
                self.upward(m, False).wait_send()

            @pl.when((me < last) & (m < me))
            def _():
                self.downward(m, False).wait_send()


def line_semaphores(C):
    return [DMA((C,)) for _ in range(4)]


def greet_line(C, others):
    me, last = lax.axis_index("col"), C - 1
    above, below = {"col": me + 1}, {"col": me - 1}

    @pl.when(me == 0)
    def _():
        greet([above] + others, 1 + len(others))

    @pl.when(me == last)
    def _():
        greet([below] + others, 1 + len(others))

    @pl.when((me > 0) & (me < last))
    def _():
        greet([above, below] + others, 2 + len(others))


def feed_kernel(
    R, C, os_hbm, w_hbm, xs_hbm, wg_hbm, wu_hbm, wd_hbm, dy_hbm,
    h_hbm, b_hbm, dg_hbm, du_hbm, dys_hbm, grad_hbm, down_hbm, y_ref,
    big, hidden, slope, silu, b, gates, ups, terms, rising, falling, dys, stage, h, h_mine,
    load, block_load, tile_load, store, w_send, w_recv, f_send, f_recv, *semaphores,
):
    me = lax.axis_index("col")
    row, ahead, behind, other = row_places(R)
    parts, heads, T = os_hbm.shape[0], os_hbm.shape[1], os_hbm.shape[2]
    D, F = wg_hbm.shape
    width, depth = D // C, D // R
    size, tiles, group = 256, 8, R // C
    bf = F // tiles
    up, down = semaphores[:2], semaphores[2:4]
    gather = LineGather(C, dy_hbm, dys, up, down)
    sums = LineSum(C, terms, rising, falling, semaphores[4:6], semaphores[6:8])

    def began(source, target, semaphore):
        copy = pltpu.make_async_copy(source, target, semaphore)
        copy.start()
        return copy

    def block_in(i):
        rows = pl.ds(i * size, size)
        copies = [
            pltpu.make_async_copy(
                os_hbm.at[j, n, rows, :], hidden.at[rows, pl.ds((j * heads + n) * HEAD_DIM, HEAD_DIM)], block_load.at[i, j * heads + n]
            )
            for j in range(parts)
            for n in range(heads)
        ]
        return copies + [
            pltpu.make_async_copy(
                xs_hbm.at[j, rows, :], slope.at[rows, pl.ds(j * width, width)], block_load.at[i, parts * heads + j]
            )
            for j in range(C)
        ]

    def tile_in(i):
        cut = pl.ds(i * bf, bf)
        return [
            pltpu.make_async_copy(wg_hbm.at[:, cut], gates.at[i % 2], tile_load.at[0, i % 2]),
            pltpu.make_async_copy(wu_hbm.at[:, cut], ups.at[i % 2], tile_load.at[1, i % 2]),
        ]

    blocks = [block_in(i) for i in range(T // size)]
    for copy in blocks[0]:
        copy.start()
    out_w = [
        began(w_hbm.at[:, j], big.at[:, :, pl.ds(j * width, width)], load.at[j]) for j in range(C)
    ]
    dy_mine = began(dy_hbm, dys.at[me], load.at[R])
    down_mine = began(wd_hbm, down_hbm.at[row], load.at[R + 1])
    for copies in blocks[1:] + [tile_in(0), tile_in(1)]:
        for copy in copies:
            copy.start()
    greet_line(C, [{"row": other}] + [{"row": ahead[k]} for k in range(1, R // 2)])
    gather.event(0)
    spread = [
        remote(wd_hbm, down_hbm.at[row], w_send.at[k], w_recv.at[k], row=ahead[k]) for k in range(1, R // 2)
    ]
    forward = [remote(wd_hbm, down_hbm.at[row], f_send.at[0], f_recv.at[0], row=other)]
    for copy in spread + forward:
        copy.start()

    stores = []
    mine = pl.ds(pl.multiple_of(me * width, width), width)
    for copy in out_w:
        copy.wait()
    for i in range(T // size):
        rows = pl.ds(i * size, size)
        for copy in blocks[i]:
            copy.wait()
        if i:
            stores[-1].wait()
        left = hidden[rows, :D]
        for j in range(C):
            columns = slice(j * width, (j + 1) * width)
            right = big[j * group : (j + 1) * group, :, :D].reshape(width, D)
            h[:, columns] = slope[rows, columns].astype(F32) + dot_nt(left, right)
        h_mine[rows, :] = h[:, mine]
        values = h[...]
        centre, inverse = norm_rows(values)
        b[rows, :] = ((values - centre) * inverse).astype(BF)
        stores.append(began(h, h_hbm.at[rows, :], store.at[0]))
    stores[-1].wait()
    b_out = began(b, b_hbm, store.at[1])
    for i in range(tiles):
        cut = slice(i * bf, (i + 1) * bf)
        for copy in tile_in(i):
            copy.wait()
        values = b[...]
        gate = dot_nn(values, gates[i % 2])
        upward = dot_nn(values, ups[i % 2])
        sigmoid = jax.nn.sigmoid(gate)
        silued = gate * sigmoid
        hidden[:, cut] = (silued * upward).astype(BF)
        slope[:, cut] = (upward * sigmoid * (1.0 + gate * (1.0 - sigmoid))).astype(BF)
        silu[:, cut] = silued.astype(BF)
        if i + 2 < tiles:
            for copy in tile_in(i + 2):
                copy.start()
        if i == 3:
            gather.event(1)
    for k in range(1, R // 2):
        spread[k - 1].wait_recv()
        block = down_hbm.at[behind[k]]
        copy = remote(block, block, f_send.at[k], f_recv.at[k], row=other)
        copy.start()
        forward.append(copy)
    for step in range(2, max(3, C - 1)):
        if step < C:
            gather.event(step)
    for copy in forward:
        copy.wait_recv()
    down_mine.wait()
    began(down_hbm, big.at[:, :, pl.ds(0, F)], load.at[0]).wait()
    half = lax.div(me, C // 2)

    def out_tile(k):
        j = (C - 1 - k) * (1 - half) + k * half
        right = big[pl.ds(j * group, group), :, :F].reshape(width, F)
        terms[j] = dot_nt(hidden[:, :F], right).astype(BF)

    out_tile(0)
    sums.level(0)
    for k in range(1, C):
        out_tile(k)
    for step in range(max(3, C - 1), C):
        gather.event(step)
    dy_mine.wait()
    b_out.wait()
    joined = [began(dys.at[j], b.at[:, pl.ds(j * width, width)], load.at[j]) for j in range(C)]
    saved = [began(dys, dys_hbm, store.at[1])]
    for copy in joined:
        copy.wait()
    sums.level(1)
    for i in range(tiles):
        cut = slice(i * bf, (i + 1) * bf)
        grad_hidden = dot_nn(b[...], big[:, :, cut].reshape(D, bf))
        slope[:, cut] = (grad_hidden * slope[:, cut].astype(F32)).astype(BF)
        silu[:, cut] = (grad_hidden * silu[:, cut].astype(F32)).astype(BF)
    saved.append(began(slope.at[:, pl.ds(0, F)], dg_hbm, store.at[2]))
    saved.append(began(silu.at[:, pl.ds(0, F)], du_hbm, store.at[3]))

    def grads(first, stop):
        copies = []
        for j in range(first, stop):
            if len(copies) >= 2:
                copies[-2].wait()
            stage[j % 2] = dot_tn(dys[j], hidden[:, :F]).astype(BF)
            copies.append(began(stage.at[j % 2], grad_hbm.at[pl.ds(j * width, width), :], load.at[j % 2]))
        for copy in copies[-2:]:
            copy.wait()

    grads(0, C // 2)
    for t in range(2, C - 1):
        sums.level(t)
    grads(C // 2, C)
    sums.level(C - 1)
    last = C - 1
    y_ref[...] = terms[me]

    @pl.when(me == 0)
    def _():
        y_ref[...] = (h_mine[...] + terms[me].astype(F32) + falling[0].astype(F32)).astype(BF)

    @pl.when(me == last)
    def _():
        y_ref[...] = (h_mine[...] + terms[me].astype(F32) + rising[0].astype(F32)).astype(BF)

    @pl.when((me > 0) & (me < last))
    def _():
        y_ref[...] = (
            h_mine[...] + terms[me].astype(F32) + rising[last - me].astype(F32) + falling[me].astype(F32)
        ).astype(BF)

    sums.finish()
    gather.finish()
    for copy in spread + forward:
        copy.wait_send()
    for copy in saved:
        copy.wait()


def feed_forward(R, C, os, w_out, xs, w_gate, w_up, w_down, cotangent):
    heads, T = os.shape[1], os.shape[2]
    width = xs.shape[2]
    D, F = w_gate.shape
    most = max(D, F)
    flat = pltpu.VMEM((T, most), BF)
    return pl.pallas_call(
        functools.partial(feed_kernel, R, C),
        in_specs=[ANY] * 7,
        out_specs=[ANY] * 7 + [VMEM_SPEC],
        out_shape=[
            struct((T, D), F32),
            struct((T, D), BF),
            struct((T, F), BF),
            struct((T, F), BF),
            struct((C, T, width), BF),
            struct((D, F), BF),
            struct((R, D // R, F), BF),
            struct((T, width), BF),
        ],
        scratch_shapes=[
            pltpu.VMEM((R, D // R, most), BF),
            flat,
            flat,
            pltpu.VMEM((T, F), BF),
            pltpu.VMEM((T, D), BF),
            pltpu.VMEM((2, D, F // 8), BF),
            pltpu.VMEM((2, D, F // 8), BF),
            pltpu.VMEM((C, T, width), BF),
            pltpu.VMEM((C - 1, T, width), BF),
            pltpu.VMEM((C - 1, T, width), BF),
            pltpu.VMEM((C, T, width), BF),
            pltpu.VMEM((2, width, F), BF),
            pltpu.VMEM((256, D), F32),
            pltpu.VMEM((T, width), F32),
            DMA((R + 2,)),
            DMA((T // 256, C * heads + C)),
            DMA((2, 2)),
            DMA((4,)),
            DMA((R // 2,)),
            DMA((R // 2,)),
            DMA((R // 2,)),
            DMA((R // 2,)),
        ]
        + line_semaphores(C)
        + line_semaphores(C),
        compiler_params=comm_params(2, 63),
        cost_estimate=cost(1.2e11, 90 * MIB),
        name="feed_forward",
    )(os, w_out, xs, w_gate, w_up, w_down, cotangent)


def norm_terms_kernel(
    R, C, dg_hbm, du_hbm, wg_hbm, wu_hbm, b_hbm, down_hbm,
    sum_ref, gate_hbm, up_hbm, down_ref,
    dg, du, wg, wu, b, terms, held, stage, own, exchanged, arrived,
    load, tile_load, store, own_load, send, recv, *semaphores,
):
    me, right, left = ring_places(C)
    D, F = wg.shape
    T = dg.shape[0]
    rows = T // C
    width = D // C

    def fetch(source, target, semaphore):
        copy = pltpu.make_async_copy(source, target, semaphore)
        copy.start()
        return copy

    def chunk(s):
        return pl.ds(pl.multiple_of(lax.rem(me + 2 * C - 1 - s, C) * rows, rows), rows)

    grads_in = []
    for s in range(C):
        part = chunk(s)
        grads_in.append(
            (fetch(dg_hbm.at[part, :], dg.at[part, :], load.at[2 * s]), fetch(du_hbm.at[part, :], du.at[part, :], load.at[2 * s + 1]))
        )
        if s == 0:
            weights_in = []
            for n in range(C):
                cut = pl.ds(n * width, width)
                weights_in.append(
                    (fetch(wg_hbm.at[cut, :], wg.at[cut, :], tile_load.at[2 * n]), fetch(wu_hbm.at[cut, :], wu.at[cut, :], tile_load.at[2 * n + 1]))
                )
    b_in = fetch(b_hbm, b, load.at[2 * C])
    sums, own_loads = held_row_sum(R, down_hbm, own, exchanged, arrived, own_load, semaphores)
    for copy in own_loads:
        copy.start()
    greet([{"col": left}] + sums.peers, 1 + len(sums.peers))
    for slot in sums.order():
        sums.exchange(slot).start()

    def term_tile(s, part, n):
        cut = pl.ds(pl.multiple_of(n * width, width), width)
        total = dot_nt(dg[part, :], wg[cut, :]) + dot_nt(du[part, :], wu[cut, :])
        terms[s, :, cut] = total.astype(BF)

    def moves(step):
        return ring_step(step, C, right, terms.at[0], held, send, recv)

    def pass_on(step):
        moves(step - 1).wait_recv()
        add_into(held.at[step - 1], terms.at[step])
        moves(step).start()

    for s in range(C):
        part = chunk(s)
        for copy in grads_in[s]:
            copy.wait()
        if s == 0:
            for n in range(C):
                for copy in weights_in[n]:
                    copy.wait()
                term_tile(s, part, n)
            moves(0).start()
            sums.relay(lambda slot: own_loads[slot].wait())
        else:

            def body(n, carry):
                term_tile(s, part, n)
                return carry

            lax.fori_loop(0, C, body, 0)
    b_in.wait()

    def stored(target, t, slot):
        cut = pl.ds(pl.multiple_of(t * width, width), width)
        return pltpu.make_async_copy(stage.at[slot], target.at[cut, :], store.at[slot])

    def product(right_ref, target):
        def body(t, carry):
            slot = lax.rem(t, 2)

            @pl.when(t >= 2)
            def _():
                stored(target, t, slot).wait()

            left_tile = b[:, pl.ds(pl.multiple_of(t * width, width), width)]
            stage[slot] = dot_tn(left_tile, right_ref[...]).astype(BF)
            stored(target, t, slot).start()
            return carry

        lax.fori_loop(0, C, body, 0)
        for slot in range(2):
            stored(target, slot, slot).wait()

    middle = max(1, (C - 1) // 2)
    for step in range(1, middle + 1):
        if step < C - 1:
            pass_on(step)
    product(dg, gate_hbm)
    sums.relay_again()
    product(du, up_hbm)
    for step in range(middle + 1, C - 1):
        pass_on(step)

    def write(part, values):
        down_ref[:, part] = values.T

    sums.finish(write, 128)
    moves(C - 2).wait_recv()
    sum_ref[...] = held[C - 2].astype(F32) + terms[C - 1].astype(F32)
    for step in range(C - 1):
        moves(step).wait_send()


def norm_terms(R, C, dg, du, w_gate, w_up, b, grad_down):
    T, F = dg.shape
    D = w_gate.shape[0]
    rows, width = T // C, D // C
    depth, columns = grad_down.shape[1:]
    return pl.pallas_call(
        functools.partial(norm_terms_kernel, R, C),
        in_specs=[ANY] * 6,
        out_specs=[VMEM_SPEC, ANY, ANY, VMEM_SPEC],
        out_shape=[struct((rows, D), F32), struct((D, F), BF), struct((D, F), BF), struct((columns, depth), F32)],
        scratch_shapes=[
            pltpu.VMEM((T, F), BF),
            pltpu.VMEM((T, F), BF),
            pltpu.VMEM((D, F), BF),
            pltpu.VMEM((D, F), BF),
            pltpu.VMEM((T, D), BF),
            pltpu.VMEM((C, rows, D), BF),
            pltpu.VMEM((C - 1, rows, D), BF),
            pltpu.VMEM((2, width, F), BF),
            pltpu.VMEM((R // 2, depth, columns), BF),
        ]
        + row_sum_buffers(R, depth, columns)
        + [
            DMA((2 * C + 1,)),
            DMA((2 * C,)),
            DMA((2,)),
            DMA((R // 2,)),
            DMA((C - 1,)),
            DMA((C - 1,)),
        ]
        + row_sum_semaphores(R),
        compiler_params=comm_params(3, 63),
        cost_estimate=cost(9e10, 70 * MIB),
        name="norm_terms",
    )(dg, du, w_gate, w_up, b, grad_down)


def attend_back_kernel(
    R, C, sum_ref, log_ref, segk_ref, segq_ref, cos_ref, sin_ref,
    q_hbm, k_hbm, v_hbm, h_hbm, dys_hbm, w_hbm, gate_hbm,
    dq_ref, dk_ref, dv_ref, gate_ref, dhs_hbm,
    h, dy, w, dh, out, q_ref, k_ref, v_ref, do_ref, dk_sum, dv_sum, own, exchanged, arrived,
    load, w_load, local, h_send, h_recv, o_send, o_recv, own_load, *semaphores,
):
    me, right, left = ring_places(C)
    rows, D = sum_ref.shape
    T, width = q_ref.shape
    heads, bq = width // HEAD_DIM, 256
    mine = pl.ds(pl.multiple_of(me * rows, rows), rows)
    first_in = [
        pltpu.make_async_copy(h_hbm.at[mine, :], h, load.at[0]),
        pltpu.make_async_copy(dys_hbm.at[:, mine, :], dy, load.at[1]),
    ]
    head_loads = [
        pltpu.make_async_copy(source, target, load.at[2 + i])
        for i, (source, target) in enumerate(((q_hbm, q_ref), (k_hbm, k_ref), (v_hbm, v_ref)))
    ]
    for copy in first_in:
        copy.start()
    order = [lax.rem(me + k, C) for k in range(1, C)] + [me]
    cuts = [pl.ds(pl.multiple_of(place * width, width), width) for place in order]
    loads = [pltpu.make_async_copy(w_hbm.at[:, order[k]], w.at[k], w_load.at[k]) for k in range(C)]
    sums, own_loads = held_row_sum(R, gate_hbm, own, exchanged, arrived, own_load, semaphores)
    for copy in loads + own_loads + head_loads:
        copy.start()
    greet([{"col": lax.rem(me + k, C)} for k in range(1, C)] + sums.peers, C - 1 + len(sums.peers))
    for slot in sums.order():
        sums.exchange(slot).start()
    for copy in first_in:
        copy.wait()
    grad = sum_ref[...]
    centre, inverse = norm_rows(h[...])
    normed = (h[...] - centre) * inverse
    first = jnp.mean(grad, axis=1, keepdims=True)
    second = jnp.mean(grad * normed, axis=1, keepdims=True)
    dh[...] = (beside(dy).astype(F32) + inverse * (grad - first - normed * second)).astype(BF)
    do_copies, dh_copies = [], []
    for k in range(C):
        loads[k].wait()
        out[k] = dot_nn(dh[...], w[k].reshape(D, width)).astype(BF)
        if k < C - 1:
            copy = remote(out.at[k], do_ref.at[mine, :], o_send.at[k], o_recv.at[k], col=order[k])
        else:
            copy = pltpu.make_async_copy(out.at[k], do_ref.at[mine, :], local.at[0])
        copy.start()
        do_copies.append(copy)
    sums.relay(lambda slot: own_loads[slot].wait())
    for copy in do_copies[:-1]:
        copy.wait_recv()
    do_copies[-1].wait()
    for k in range(C):
        if k < C - 1:
            copy = remote(dh.at[:, cuts[k]], dhs_hbm.at[mine, :], h_send.at[k], h_recv.at[k], col=order[k])
        else:
            copy = pltpu.make_async_copy(dh.at[:, cuts[k]], dhs_hbm.at[mine, :], local.at[1])
        copy.start()
        dh_copies.append(copy)
    for copy in head_loads:
        copy.wait()

    def one_head(head, carry):
        columns = pl.ds(pl.multiple_of(head * HEAD_DIM, HEAD_DIM), HEAD_DIM)
        dk_sum[...] = jnp.zeros_like(dk_sum)
        dv_sum[...] = jnp.zeros_like(dv_sum)
        for first in range(0, T, SEQ):
            for start in range(first, first + SEQ, bq):
                stop = start + bq
                keys = k_ref[first:stop, columns]
                queries = q_ref[start:stop, columns]
                grads = do_ref[start:stop, columns]
                scores = dot_nt(keys, queries) * SCALE
                allowed = allowed_block(segk_ref[first:stop], segq_ref[:, start:stop], start - first)
                scores = jnp.where(allowed, scores, MASKED)
                probs = jnp.exp(scores - log_ref[head, :, start:stop])
                dv_sum[first:stop] += dot_nn(probs.astype(BF), grads)
                grad_probs = dot_nt(v_ref[first:stop, columns], grads)
                inner = jnp.sum(probs * grad_probs, axis=0, keepdims=True)
                grad_scores = (probs * (grad_probs - inner)).astype(BF)
                dk_sum[first:stop] += dot_nn(grad_scores, queries)
                grad_query = dot_tn(keys, grad_scores).T * SCALE
                dq_ref[start:stop, columns] = turn(grad_query, cos_ref[start:stop], -sin_ref[start:stop]).astype(BF)
        dk_ref[:, columns] = turn(dk_sum[...] * SCALE, cos_ref[...], -sin_ref[...]).astype(BF)
        dv_ref[:, columns] = dv_sum[...].astype(BF)
        return carry

    lax.fori_loop(0, heads // 2, one_head, 0)
    sums.relay_again()
    lax.fori_loop(heads // 2, heads, one_head, 0)

    def write(part, values):
        gate_ref[part, :] = values

    sums.finish(write)
    for copy in do_copies[:-1]:
        copy.wait_send()
    for copy in dh_copies:
        copy.wait()


def attend_back(R, total, log_total, seg_column, seg_row, cos_table, sin_table, q, k, v, h, dys, w_out, grad_gate):
    C, T, width = dys.shape
    rows, D = total.shape
    depth, columns = grad_gate.shape[1:]
    one = pltpu.VMEM((T, width), BF)
    return pl.pallas_call(
        functools.partial(attend_back_kernel, R, C),
        in_specs=[VMEM_SPEC] * 6 + [ANY] * 7,
        out_specs=[VMEM_SPEC] * 4 + [ANY],
        out_shape=[struct((T, width), BF)] * 3 + [struct((depth, columns), F32), struct((T, width), BF)],
        scratch_shapes=[
            pltpu.VMEM((rows, D), F32),
            pltpu.VMEM((C, rows, width), BF),
            pltpu.VMEM((C, R, D // R, width), BF),
            pltpu.VMEM((rows, D), BF),
            pltpu.VMEM((C, rows, width), BF),
            one,
            one,
            one,
            one,
            pltpu.VMEM((T, HEAD_DIM), F32),
            pltpu.VMEM((T, HEAD_DIM), F32),
            pltpu.VMEM((R // 2, depth, columns), BF),
        ]
        + row_sum_buffers(R, depth, columns)
        + [
            DMA((5,)),
            DMA((C,)),
            DMA((2,)),
            DMA((C - 1,)),
            DMA((C - 1,)),
            DMA((C - 1,)),
            DMA((C - 1,)),
            DMA((R // 2,)),
        ]
        + row_sum_semaphores(R),
        compiler_params=comm_params(5),
        cost_estimate=cost(5e10, 30 * MIB),
        name="attend_back",
    )(total, log_total, seg_column, seg_row, cos_table, sin_table, q, k, v, h, dys, w_out, grad_gate)


def input_terms_kernel(
    R, C, dq_ref, dk_ref, dv_ref, mu_hbm, r_hbm, w_hbm, a_hbm, x_hbm, dh_hbm, grad_hbm, os_hbm,
    y_ref, gq_ref, gk_ref, gv_ref, total_ref, out_ref,
    mu_ref, r_ref, w_ref, a_ref, x_ref, dh_ref, block, mine, theirs,
    terms, held, stats, stats_in, own, exchanged, arrived, tiles, q_exchanged, q_arrived, o_tiles, o_exchanged, o_arrived,
    send, recv, s_send, s_recv, w_load, late_load, load, block_load, own_send, own_recv, *semaphores,
):
    me, right, left = ring_places(C)
    T, width = dq_ref.shape
    D = width * C
    heads = (dq_ref, dk_ref, dv_ref)
    side_row = lax.rem(lax.axis_index("row"), 2)
    partner = {"row": 2 * me + side_row, "col": lax.div(lax.axis_index("row"), 2)}
    direct = [{"col": lax.rem(me + k, C)} for k in range(1, C)]
    apart = partner["col"] != me

    def cut_of(s):
        return pl.ds(pl.multiple_of(lax.rem(me + 2 * C - 1 - s, C) * width, width), width)

    def weight_in(s):
        return pltpu.make_async_copy(w_hbm.at[:, cut_of(s), :], w_ref.at[:, cut_of(s), :], w_load.at[s])

    for s in range(C):
        weight_in(s).start()
    late = [
        pltpu.make_async_copy(source, target, late_load.at[i])
        for i, (source, target) in enumerate(
            ((a_hbm, a_ref), (x_hbm, x_ref), (dh_hbm, dh_ref), (mu_hbm, mu_ref), (r_hbm, r_ref))
        )
    ]
    for copy in late:
        copy.start()
    depth = tiles.shape[2]
    sums, loads = held_row_sum(R, grad_hbm, own, exchanged, arrived, load, semaphores[:4])
    side = lax.rem(lax.axis_index("row"), 2)
    q_sums = RowSum(
        R, lambda i: tiles.at[i, side], lambda i: tiles.at[i, 1 - side], q_exchanged, q_arrived, semaphores[4:8]
    )
    o_sums = RowSum(
        R, lambda i: o_tiles.at[i, side], lambda i: o_tiles.at[i, 1 - side], o_exchanged, o_arrived, semaphores[8:]
    )

    def block_in(i):
        chip = lax.div(o_sums.places(o_sums.order()[i]), 2)
        return [
            pltpu.make_async_copy(
                os_hbm.at[chip, n], block.at[i % 2, :, pl.ds(n * HEAD_DIM, HEAD_DIM)], block_load.at[i % 2, n]
            )
            for n in range(os_hbm.shape[1])
        ]

    for copy in loads + block_in(0) + block_in(1):
        copy.start()

    @pl.when(apart)
    def _():
        greet(direct + sums.peers + [partner], C + len(sums.peers))

    @pl.when(jnp.logical_not(apart))
    def _():
        greet(direct + sums.peers, C - 1 + len(sums.peers))

    for slot in sums.order():
        sums.exchange(slot).start()

    def moves(step):
        return ring_step(step, C, right, terms.at[0], held, send, recv)

    def pass_on(step):
        moves(step - 1).wait_recv()
        add_into(held.at[step - 1], terms.at[step])
        moves(step).start()

    def compute(s):
        cut = cut_of(s)
        weight_in(s).wait()
        total = dot_nt(dq_ref[...], w_ref[0, cut, :])
        total += dot_nt(dk_ref[...], w_ref[1, cut, :])
        total += dot_nt(dv_ref[...], w_ref[2, cut, :])
        terms[s] = total.astype(BF)

    compute(0)
    moves(0).start()

    def body(s, carry):
        compute(s)
        return carry

    lax.fori_loop(1, C, body, 0)
    for copy in late:
        copy.wait()
    sums.relay(lambda slot: loads[slot].wait())
    for slot in q_sums.order():
        start = pl.multiple_of(lax.div(q_sums.places(slot), 2) * 2 * depth, 2 * depth)
        left_tile = a_ref[:, pl.ds(start, 2 * depth)]
        for i, right_side in enumerate(heads):
            product = dot_tn(left_tile, right_side[...]).astype(BF)
            tiles[slot, 0, :, i * width : (i + 1) * width] = product[:depth]
            tiles[slot, 1, :, i * width : (i + 1) * width] = product[depth:]
        q_sums.exchange(slot).start()
    pass_on(1)
    q_sums.relay()
    for i, slot in enumerate(o_sums.order()):
        for copy in block_in(i):
            copy.wait()
        product = dot_tn(dh_ref[...], block[i % 2]).astype(BF)
        o_tiles[slot, 0] = product[:depth]
        o_tiles[slot, 1] = product[depth:]
        o_sums.exchange(slot).start()
        if i + 2 < R // 2:
            for copy in block_in(i + 2):
                copy.start()
    sums.relay_again()
    o_sums.relay()
    q_sums.relay_again()
    for step in range(2, C - 1):
        pass_on(step)

    def write(part, values):
        total_ref[part, :] = values

    def write_qkv(part, values):
        for i, target in enumerate((gq_ref, gk_ref, gv_ref)):
            target[part, :] = values[:, i * width : (i + 1) * width]

    def write_out(part, values):
        mine[part, :] = values.astype(BF)

    o_sums.relay_again()
    o_sums.finish(write_out)
    handed = remote(mine, theirs, own_send.at[0], own_recv.at[0], **partner)

    @pl.when(apart)
    def _():
        handed.start()

    sums.finish(write)
    q_sums.finish(write_qkv)

    @pl.when(apart)
    def _():
        handed.wait()
        out_ref[...] = theirs[...].astype(F32).T

    @pl.when(jnp.logical_not(apart))
    def _():
        out_ref[...] = mine[...].astype(F32).T

    moves(C - 2).wait_recv()
    size = 128

    def grad_of(rows):
        return held[C - 2, rows, :].astype(F32) + terms[C - 1, rows, :].astype(F32)

    def normed_of(rows):
        return (x_ref[rows, :].astype(F32) - mu_ref[rows, :]) * r_ref[rows, :]

    def sum_rows(i, carry):
        rows = pl.ds(pl.multiple_of(i * size, size), size)
        grad = grad_of(rows)
        lane = lax.broadcasted_iota(jnp.int32, (size, 128), 1)
        first = jnp.sum(grad, axis=1, keepdims=True)
        second = jnp.sum(grad * normed_of(rows), axis=1, keepdims=True)
        packed = jnp.where(lane == 0, first, jnp.where(lane == 1, second, 0.0))
        stats[:, rows] = packed.T[:8]
        return carry

    lax.fori_loop(0, T // size, sum_rows, 0)
    exchanges = [
        remote(stats, stats_in.at[k - 1], s_send.at[k - 1], s_recv.at[k - 1], col=lax.rem(me + k, C)) for k in range(1, C)
    ]
    for copy in exchanges:
        copy.start()
    for copy in exchanges:
        copy.wait_recv()

    def last_rows(i, carry):
        rows = pl.ds(pl.multiple_of(i * size, size), size)
        both = stats[:, rows]
        for k in range(C - 1):
            both += stats_in[k, :, rows]
        columns = jnp.concatenate([both, jnp.zeros((120, size), F32)], axis=0).T * (1.0 / D)
        grad = grad_of(rows) - columns[:, 0:1] - normed_of(rows) * columns[:, 1:2]
        y_ref[rows, :] = (dh_ref[rows, :].astype(F32) + r_ref[rows, :] * grad).astype(BF)
        return carry

    lax.fori_loop(0, T // size, last_rows, 0)
    for copy in exchanges:
        copy.wait_send()
    for step in range(C - 1):
        moves(step).wait_send()


def input_terms(R, C, dq, dk, dv, w_qkv, a, tokens, dh, mu, r, grad, os):
    T, width = dq.shape
    D = w_qkv.shape[1]
    half, low = R // 2, D // R
    depth, columns = grad.shape[1:]
    assert R == 2 * C
    return pl.pallas_call(
        functools.partial(input_terms_kernel, R, C),
        in_specs=[VMEM_SPEC] * 3 + [ANY] * 8,
        out_specs=[VMEM_SPEC] * 6,
        out_shape=[struct((T, width), BF)]
        + [struct((low, width), F32)] * 3
        + [struct((depth, columns), F32), struct((width, low), F32)],
        scratch_shapes=[
            pltpu.VMEM((T, 1), F32),
            pltpu.VMEM((T, 1), F32),
            pltpu.VMEM((3, D, width), BF),
            pltpu.VMEM((T, D), BF),
            pltpu.VMEM((T, width), BF),
            pltpu.VMEM((T, width), BF),
            pltpu.VMEM((2, T, width), BF),
            pltpu.VMEM((low, width), BF),
            pltpu.VMEM((low, width), BF),
            pltpu.VMEM((C, T, width), BF),
            pltpu.VMEM((C - 1, T, width), BF),
            pltpu.VMEM((8, T), F32),
            pltpu.VMEM((C - 1, 8, T), F32),
            pltpu.VMEM((half, depth, columns), BF),
        ]
        + row_sum_buffers(R, depth, columns)
        + [pltpu.VMEM((half, 2, low, 3 * width), BF)]
        + row_sum_buffers(R, low, 3 * width)
        + [pltpu.VMEM((half, 2, low, width), BF)]
        + row_sum_buffers(R, low, width)
        + [
            DMA((C - 1,)),
            DMA((C - 1,)),
            DMA((C - 1,)),
            DMA((C - 1,)),
            DMA((C,)),
            DMA((5,)),
            DMA((half,)),
            DMA((2, os.shape[1])),
            DMA((1,)),
            DMA((1,)),
        ]
        + row_sum_semaphores(R)
        + row_sum_semaphores(R)
        + row_sum_semaphores(R),
        compiler_params=comm_params(6, 63),
        cost_estimate=cost(8e10, 20 * MIB),
        name="input_terms",
    )(dq, dk, dv, mu, r, w_qkv, a, tokens, dh, grad, os)


def on_device(R, C, tokens, cotangent, segments, w_query, w_key, w_value, w_out, w_gate, w_up, w_down):
    T, width = tokens.shape
    D = width * C
    gathered = lambda w: lax.all_gather(w, "row", axis=0, tiled=True)

    gate_w, up_w = gathered(w_gate), gathered(w_up)
    seg_column, seg_row = segments.reshape(T, 1), segments.reshape(1, T)
    xs, w_qkv, cos_table, sin_table = first_gather(R, C, seg_column, seg_row, tokens, w_query, w_key, w_value)
    w_qkv = w_qkv.reshape(3, D, width)
    act_one, q, k, v, mu_one, r_one, out_part = norm_and_project(xs, w_qkv, cos_table, sin_table, w_out.T)
    os, log_total, out_w = attend(R, C, q, k, v, seg_column, seg_row, out_part)
    h_full, act_two, dg, du, dys, grad_down, _, output = feed_forward(
        R, C, os, out_w, xs, gate_w, up_w, w_down.T, cotangent
    )
    by_row = lambda values: values.reshape(R, D // R, -1)
    total, grad_gate, grad_up, grad_down = norm_terms(R, C, dg, du, gate_w, up_w, act_two, by_row(grad_down))
    dq, dk, dv, grad_gate, dh = attend_back(
        R, total, log_total, seg_column, seg_row, cos_table, sin_table, q, k, v, h_full, dys, out_w, by_row(grad_gate)
    )
    grad_tokens, grad_query, grad_key, grad_value, grad_up, grad_out = input_terms(
        R, C, dq, dk, dv, w_qkv, act_one, tokens, dh, mu_one, r_one, by_row(grad_up), os
    )
    return (output, grad_tokens, grad_query, grad_key, grad_value, grad_out, grad_gate, grad_up, grad_down)


def solution(mesh):
    here = P("row", "col")
    turned = P("col", "row")
    return jax.shard_map(
        functools.partial(on_device, mesh.shape["row"], mesh.shape["col"]),
        mesh=mesh,
        in_specs=(here, here, P("row"), here, here, here, turned, here, here, turned),
        out_specs=(here, here, here, here, here, turned, here, here, turned),
        check_vma=False,
    )
```

```python
import functools

import jax
import jax.numpy as jnp
from jax import lax
from jax.experimental import pallas as pl
from jax.experimental.pallas import tpu as pltpu
from jax.sharding import PartitionSpec as P

HEAD_DIM = 128
HALF = HEAD_DIM // 2
SEQ = 1024
EPSILON = 1e-05
MASKED = -1e30
SCALE = HEAD_DIM ** (-0.5)
BF = jnp.bfloat16
F32 = jnp.float32
MIB = 1 << 20
ANY = pl.BlockSpec(memory_space=pl.ANY)


def dot_nn(left, right):
    return jnp.dot(left, right, preferred_element_type=F32)


def dot_tn(left, right):
    return lax.dot_general(left, right, (((0,), (0,)), ((), ())), preferred_element_type=F32)


def dot_nt(left, right):
    return lax.dot_general(left, right, (((1,), (1,)), ((), ())), preferred_element_type=F32)


def struct(shape, dtype):
    return jax.ShapeDtypeStruct(shape, dtype)


def params(mib=60):
    return pltpu.CompilerParams(vmem_limit_bytes=mib * MIB)


def cost(flops, moved):
    return pl.CostEstimate(flops=int(flops), bytes_accessed=int(moved), transcendentals=0)


def turn(values, cos_table, sin_table):
    return values * cos_table + pltpu.roll(values, HALF, 1) * sin_table


MESH = pl.DeviceIdType.MESH
VMEM_SPEC = pl.BlockSpec(memory_space=pltpu.VMEM)
DMA = pltpu.SemaphoreType.DMA


def comm_params(number, mib=60):
    return pltpu.CompilerParams(vmem_limit_bytes=mib * MIB, collective_id=number, has_side_effects=True)


def remote(source, target, send, recv, **device):
    return pltpu.make_async_remote_copy(
        src_ref=source, dst_ref=target, send_sem=send, recv_sem=recv, device_id=device, device_id_type=MESH
    )


def greet(senders, targets):
    semaphore = pltpu.get_barrier_semaphore()
    for device in senders:
        pl.semaphore_signal(semaphore, inc=1, device_id=device, device_id_type=MESH)
    pl.semaphore_wait(semaphore, targets)


def ring_places(C):
    me = lax.axis_index("col")
    return me, lax.rem(me + 1, C), lax.rem(me + C - 1, C)


def row_places(R):
    row = lax.axis_index("row")
    ahead = [lax.rem(row + 2 * k, R) for k in range(R // 2)]
    behind = [lax.rem(row + R - 2 * k, R) for k in range(R // 2)]
    other = row + 1 - 2 * lax.rem(row, 2)
    return row, ahead, behind, other


def gather_ring(C, source, whole, send, recv):
    me, right, left = ring_places(C)
    copies = []
    for step in range(C - 1):
        owner = lax.rem(me - step + C, C)
        piece = source if step == 0 else whole.at[owner]
        copies.append(remote(piece, whole.at[owner], send.at[step], recv.at[step], col=right))
    return copies


def gather_kernel(
    R, C, segk_ref, segq_ref, rate_ref, x_ref, wq_ref, wk_ref, wv_ref, xs_ref, w_ref, cos_ref, sin_ref,
    local, x_send, x_recv, w_send, w_recv, f_send, f_recv,
):
    me, right, left = ring_places(C)
    row, ahead, behind, other = row_places(R)
    weights = (wq_ref, wk_ref, wv_ref)
    mine = [
        pltpu.make_async_copy(x_ref, xs_ref.at[me], local.at[0]),
    ] + [pltpu.make_async_copy(w, w_ref.at[i, row], local.at[1 + i]) for i, w in enumerate(weights)]
    for copy in mine:
        copy.start()
    greet(
        [{"col": left}, {"row": other}] + [{"row": r} for r in behind[1:]],
        1 + R // 2,
    )

    x_copies = gather_ring(C, x_ref, xs_ref, x_send, x_recv)
    x_copies[0].start()
    spread, forward = [], []
    for i, w in enumerate(weights):
        for k in range(1, R // 2):
            copy = remote(w, w_ref.at[i, row], w_send.at[i, k], w_recv.at[i, k], row=ahead[k])
            copy.start()
            spread.append(copy)
        copy = remote(w, w_ref.at[i, row], f_send.at[i, 0], f_recv.at[i, 0], row=other)
        copy.start()
        forward.append(copy)
    T = cos_ref.shape[0]
    size = 128

    def table_rows(i, carry):
        rows = pl.ds(pl.multiple_of(i * size, size), size)
        first = SEQ * lax.div(i * size, SEQ)
        shape = (size, T)
        queries = lax.broadcasted_iota(jnp.int32, shape, 0) + i * size
        keys = lax.broadcasted_iota(jnp.int32, shape, 1)
        seen = (segk_ref[rows, :] == segq_ref[...]) & (keys <= queries) & (keys >= first)
        place = jnp.sum(jnp.where(seen, 1.0, 0.0), axis=1, keepdims=True) - 1.0
        angles = place * rate_ref[...]
        lane = lax.broadcasted_iota(jnp.int32, angles.shape, 1)
        sine = jnp.sin(angles)
        cos_ref[rows, :] = jnp.cos(angles)
        sin_ref[rows, :] = jnp.where(lane < HALF, -sine, sine)
        return carry

    lax.fori_loop(0, T // size, table_rows, 0)
    for s in range(1, C - 1):
        x_copies[s - 1].wait_recv()
        x_copies[s].start()
    for i in range(3):
        for k in range(1, R // 2):
            spread[i * (R // 2 - 1) + k - 1].wait_recv()
            block = w_ref.at[i, behind[k]]
            copy = remote(block, block, f_send.at[i, k], f_recv.at[i, k], row=other)
            copy.start()
            forward.append(copy)
    x_copies[-1].wait_recv()
    for copy in forward:
        copy.wait_recv()
    for copy in x_copies + spread + forward:
        copy.wait_send()
    for copy in mine:
        copy.wait()


def first_gather(R, C, seg_column, seg_row, tokens, w_query, w_key, w_value):
    depth, width = w_query.shape
    T = tokens.shape[0]
    half = R // 2
    rate = 10000.0 ** (-(jnp.arange(HALF, dtype=F32) * 2.0 / HEAD_DIM))
    rate = jnp.concatenate([rate, rate]).reshape(1, HEAD_DIM)
    return pl.pallas_call(
        functools.partial(gather_kernel, R, C),
        in_specs=[VMEM_SPEC] * 3 + [ANY] * 4,
        out_specs=[ANY] * 2 + [VMEM_SPEC] * 2,
        out_shape=[
            struct((C,) + tokens.shape, BF),
            struct((3, R, depth, width), BF),
            struct((T, HEAD_DIM), F32),
            struct((T, HEAD_DIM), F32),
        ],
        scratch_shapes=[
            DMA((4,)),
            DMA((C - 1,)),
            DMA((C - 1,)),
            DMA((3, half)),
            DMA((3, half)),
            DMA((3, half)),
            DMA((3, half)),
        ],
        compiler_params=comm_params(0),
        cost_estimate=cost(6e10, 14 * MIB),
        name="first_gather",
    )(seg_column, seg_row, rate, tokens, w_query, w_key, w_value)


def norm_rows(x):
    centre = jnp.mean(x, axis=-1, keepdims=True)
    spread = jnp.mean(x * x, axis=-1, keepdims=True) - centre * centre
    inverse = lax.rsqrt(spread + EPSILON)
    return centre, inverse


def beside(ref):
    return jnp.concatenate([ref[j] for j in range(ref.shape[0])], axis=1)


def qkv_kernel(
    C, xs_ref, w_ref, cos_ref, sin_ref, wo_ref, a_ref, q_ref, k_ref, v_ref, mu_ref, r_ref, wos_ref, local, send, recv
):
    step, steps = pl.program_id(0), pl.num_programs(0)
    me, right, left = ring_places(C)
    copies = gather_ring(C, wo_ref, wos_ref, send, recv)
    mine = pltpu.make_async_copy(wo_ref, wos_ref.at[me], local.at[0])

    @pl.when(step == 0)
    def _():
        mine.start()
        greet([{"col": left}], 1)
        copies[0].start()

    for s in range(1, C - 1):

        @pl.when(step == jnp.minimum(2 * s, steps - 1))
        def _():
            copies[s - 1].wait_recv()
            copies[s].start()

    x = beside(xs_ref).astype(F32)
    centre, inverse = norm_rows(x)
    a = ((x - centre) * inverse).astype(BF)
    a_ref[...] = a
    mu_ref[...] = centre
    r_ref[...] = inverse
    cosine, sine = cos_ref[...], sin_ref[...]
    for index, out in enumerate((q_ref, k_ref, v_ref)):
        product = dot_nn(a, w_ref[index])
        if index == 2:
            out[...] = product.astype(BF)
            continue
        for start in range(0, out.shape[1], HEAD_DIM):
            part = product[:, start : start + HEAD_DIM]
            out[:, start : start + HEAD_DIM] = turn(part, cosine, sine).astype(BF)

    @pl.when(step == steps - 1)
    def _():
        copies[-1].wait_recv()
        for copy in copies:
            copy.wait_send()
        mine.wait()


def norm_and_project(xs, w_qkv, cos_table, sin_table, w_out):
    C, T, width = xs.shape
    D = width * C
    bt = 256
    rows = lambda n: pl.BlockSpec((bt, n), lambda i: (i, 0))
    return pl.pallas_call(
        functools.partial(qkv_kernel, C),
        grid=(T // bt,),
        in_specs=[
            pl.BlockSpec((C, bt, width), lambda i: (0, i, 0)),
            pl.BlockSpec(w_qkv.shape, lambda i: (0, 0, 0), pipeline_mode=pl.Buffered(1)),
            rows(HEAD_DIM),
            rows(HEAD_DIM),
            ANY,
        ],
        out_specs=[rows(D), rows(width), rows(width), rows(width), rows(1), rows(1), ANY],
        out_shape=[
            struct((T, D), BF),
            struct((T, width), BF),
            struct((T, width), BF),
            struct((T, width), BF),
            struct((T, 1), F32),
            struct((T, 1), F32),
            struct((C,) + w_out.shape, BF),
        ],
        scratch_shapes=[DMA((1,)), DMA((C - 1,)), DMA((C - 1,))],
        compiler_params=comm_params(7),
        cost_estimate=cost(2e10, 14 * MIB),
        name="norm_and_project",
    )(xs, w_qkv, cos_table, sin_table, w_out)


def allowed_block(seg_key, seg_query, first_query):
    shape = (seg_key.shape[0], seg_query.shape[1])
    keys = lax.broadcasted_iota(jnp.int32, shape, 0)
    queries = lax.broadcasted_iota(jnp.int32, shape, 1) + first_query
    return (seg_key == seg_query) & (keys <= queries)


def attend_kernel(
    R, C, q_ref, k_ref, v_ref, segk_ref, segq_ref, wos_ref, os_ref, log_ref, w_ref,
    o_buf, local, o_send, o_recv, w_send, w_recv, f_send, f_recv,
):
    me, right, left = ring_places(C)
    row, ahead, behind, other = row_places(R)
    T, width = q_ref.shape
    heads, bq = width // HEAD_DIM, 256
    greet([{"col": left}, {"row": other}] + [{"row": r} for r in behind[1:]], 1 + R // 2)
    mine = pltpu.make_async_copy(wos_ref, w_ref.at[row], local.at[0])
    mine.start()
    spread, forward = [], []
    for k in range(1, R // 2):
        copy = remote(wos_ref, w_ref.at[row], w_send.at[k], w_recv.at[k], row=ahead[k])
        copy.start()
        spread.append(copy)
    copy = remote(wos_ref, w_ref.at[row], f_send.at[0], f_recv.at[0], row=other)
    copy.start()
    forward.append(copy)

    def ring(step, head):
        owner = lax.rem(me - step + C, C)
        piece = o_buf.at[head] if step == 0 else os_ref.at[owner, head]
        return remote(piece, os_ref.at[owner, head], o_send.at[step, head], o_recv.at[step, head], col=right)

    def one_head(head, carry):
        columns = pl.ds(pl.multiple_of(head * HEAD_DIM, HEAD_DIM), HEAD_DIM)
        for first in range(0, T, SEQ):
            for start in range(first, first + SEQ, bq):
                stop = start + bq
                scores = dot_nt(k_ref[first:stop, columns], q_ref[start:stop, columns]) * SCALE
                allowed = allowed_block(segk_ref[first:stop], segq_ref[:, start:stop], start - first)
                scores = jnp.where(allowed, scores, MASKED)
                peak = jnp.max(scores, axis=0, keepdims=True)
                exponent = jnp.exp(scores - peak)
                total = jnp.sum(exponent, axis=0, keepdims=True)
                weights = (exponent * (1.0 / total)).astype(BF)
                o_buf[head, start:stop] = dot_tn(v_ref[first:stop, columns], weights).T.astype(BF)
                log_ref[head, :, start:stop] = peak + jnp.log(total)
        ring(0, head).start()
        pltpu.make_async_copy(o_buf.at[head], os_ref.at[me, head], local.at[1 + head]).start()
        return carry

    lax.fori_loop(0, heads, one_head, 0)
    for step in range(1, C - 1):
        for head in range(heads):
            ring(step - 1, head).wait_recv()
            ring(step, head).start()
    for k in range(1, R // 2):
        spread[k - 1].wait_recv()
        block = w_ref.at[behind[k]]
        copy = remote(block, block, f_send.at[k], f_recv.at[k], row=other)
        copy.start()
        forward.append(copy)
    for head in range(heads):
        ring(C - 2, head).wait_recv()
        pltpu.make_async_copy(o_buf.at[head], os_ref.at[me, head], local.at[1 + head]).wait()
        for step in range(C - 1):
            ring(step, head).wait_send()
    for copy in forward:
        copy.wait_recv()
    for copy in spread + forward:
        copy.wait_send()
    mine.wait()


def attend(R, C, q, k, v, seg_column, seg_row, w_part):
    T, width = q.shape
    heads, half = width // HEAD_DIM, R // 2
    return pl.pallas_call(
        functools.partial(attend_kernel, R, C),
        in_specs=[VMEM_SPEC] * 5 + [ANY],
        out_specs=[ANY, VMEM_SPEC, ANY],
        out_shape=[
            struct((C, heads, T, HEAD_DIM), BF),
            struct((heads, 1, T), F32),
            struct((R,) + w_part.shape, BF),
        ],
        scratch_shapes=[
            pltpu.VMEM((heads, T, HEAD_DIM), BF),
            DMA((1 + heads,)),
            DMA((C - 1, heads)),
            DMA((C - 1, heads)),
            DMA((half,)),
            DMA((half,)),
            DMA((half,)),
            DMA((half,)),
        ],
        compiler_params=comm_params(1),
        cost_estimate=cost(7e10, 14 * MIB),
        name="attend",
    )(q, k, v, seg_column, seg_row, w_part)


def ring_step(step, C, right, first, held, send, recv):
    source = first if step == 0 else held.at[step - 1]
    return remote(source, held.at[step], send.at[step], recv.at[step], col=right)


def add_into(held, terms):
    size = 64

    def body(i, carry):
        rows = pl.ds(pl.multiple_of(i * size, size), size)
        held[rows, :] = (held[rows, :].astype(F32) + terms[rows, :].astype(F32)).astype(BF)
        return carry

    lax.fori_loop(0, held.shape[0] // size, body, 0)


class RowSum:
    def __init__(self, R, own, twin, exchanged, arrived, semaphores):
        self.P = R // 4
        self.own, self.twin, self.exchanged, self.arrived = own, twin, exchanged, arrived
        self.x_send, self.x_recv, self.y_send, self.y_recv = semaphores
        self.width = arrived.shape[2]
        self.places = row_of(R)
        self.peers = row_peers(R)

    def part(self, ref, side):
        return ref.at[:, pl.ds(side * self.width, self.width)]

    def exchange(self, slot):
        return remote(
            self.twin(slot), self.exchanged.at[slot], self.x_send.at[slot], self.x_recv.at[slot], row=self.places(0, True)
        )

    def send(self, slot, side, index, target):
        return remote(
            self.part(self.own(slot), side), self.arrived.at[index], self.y_send.at[index], self.y_recv.at[index],
            row=self.places(target),
        )

    def left_one(self, dp):
        return self.send(2 * dp + 1, 0, dp, 1)

    def left_two(self, dp):
        return self.send(2 * dp, 0, self.P + dp - 1, 2 * dp)

    def right_one(self, dp, dq):
        return self.send(2 * dp + dq, 1, 2 * self.P - 1 + 2 * (dp - 1) + dq, 2 * dp)

    def right_two(self):
        return self.send(1, 1, 4 * self.P - 3, 1)

    def order(self):
        return (
            [2 * dp + 1 for dp in range(1, self.P)] + [1] + [2 * dp for dp in range(1, self.P)] + [0]
        )

    def relay(self, before=None):
        for slot in self.order():
            if before is not None:
                before(slot)
            self.exchange(slot).wait_recv()
            add_into(self.own(slot), self.exchanged.at[slot])
            dp, dq = divmod(slot, 2)
            if dq:
                self.left_one(dp).start()
            if dp:
                self.right_one(dp, dq).start()

    def relay_again(self):
        for dp in range(1, self.P):
            self.left_one(dp).wait_recv()
            add_into(self.part(self.own(2 * dp), 0), self.arrived.at[dp])
            self.left_two(dp).start()
        for dp in range(1, self.P):
            copy = self.right_one(dp, 1)
            copy.wait_recv()
            add_into(self.part(self.own(1), 1), self.arrived.at[2 * self.P - 1 + 2 * (dp - 1) + 1])
        self.right_two().start()

    def finish(self, write, size=64):
        P, width = self.P, self.width
        self.left_one(0).wait_recv()
        self.right_two().wait_recv()
        for dp in range(1, P):
            self.left_two(dp).wait_recv()
            self.right_one(dp, 0).wait_recv()
        lefts = [0] + [P + dp - 1 for dp in range(1, P)]
        rights = [4 * P - 3] + [2 * P - 1 + 2 * (dp - 1) for dp in range(1, P)]

        def body(i, carry):
            rows = pl.ds(pl.multiple_of(i * size, size), size)
            total = self.own(0)[rows, :].astype(F32)
            halves = []
            for side, places in enumerate((lefts, rights)):
                half = total[:, side * width : (side + 1) * width]
                for index in places:
                    half += self.arrived[index, rows, :].astype(F32)
                halves.append(half)
            write(rows, jnp.concatenate(halves, axis=1))
            return carry

        lax.fori_loop(0, self.exchanged.shape[1] // size, body, 0)
        for slot in range(2 * P):
            self.exchange(slot).wait_send()
        self.left_one(0).wait_send()
        self.right_two().wait_send()
        for dp in range(1, P):
            self.left_one(dp).wait_send()
            self.left_two(dp).wait_send()
            self.right_one(dp, 0).wait_send()
            self.right_one(dp, 1).wait_send()


def row_of(R):
    row = lax.axis_index("row")
    side, chip = lax.rem(row, 2), lax.div(row, 2)
    p, q = lax.div(chip, 2), lax.rem(chip, 2)

    def place(slot, twin=False):
        dp, dq = divmod(slot, 2)
        chip_there = 2 * lax.rem(p + dp, R // 4) + lax.rem(q + dq, 2)
        return 2 * chip_there + (1 - side if twin else side)

    return place


def row_peers(R):
    place = row_of(R)
    return [{"row": place(0, True)}, {"row": place(1)}] + [{"row": place(2 * dp)} for dp in range(1, R // 4)]


def row_sum_semaphores(R):
    return [DMA((R // 2,)), DMA((R // 2,)), DMA((R - 2,)), DMA((R - 2,))]


def row_sum_buffers(R, depth, columns):
    return [
        pltpu.VMEM((R // 2, depth, columns), BF),
        pltpu.VMEM((R - 2, depth, columns // 2), BF),
    ]


def held_row_sum(R, grad_hbm, own, exchanged, arrived, load, semaphores):
    place = row_of(R)
    sums = RowSum(R, lambda i: own.at[i], lambda i: grad_hbm.at[place(i, True)], exchanged, arrived, semaphores)
    loads = [pltpu.make_async_copy(grad_hbm.at[place(i)], own.at[i], load.at[i]) for i in range(R // 2)]
    return sums, loads


class LineGather:
    def __init__(self, C, source, whole, up, down):
        self.C, self.source, self.whole, self.up, self.down = C, source, whole, up, down
        self.me = lax.axis_index("col")

    def upward(self, step):
        owner = self.me - step
        piece = self.source if step == 0 else self.whole.at[owner]
        return remote(piece, self.whole.at[owner], self.up[0].at[step], self.up[1].at[step], col=self.me + 1)

    def downward(self, step):
        owner = self.me + step
        piece = self.source if step == 0 else self.whole.at[owner]
        return remote(piece, self.whole.at[owner], self.down[0].at[step], self.down[1].at[step], col=self.me - 1)

    def arrival(self, step, rises):
        sender = self.me - 1 if rises else self.me + 1
        send, recv = self.up if rises else self.down
        target = self.whole.at[sender - step if rises else sender + step]
        return remote(target, target, send.at[step], recv.at[step], col=sender)

    def event(self, step):
        me, last = self.me, self.C - 1
        if step:

            @pl.when(me >= step)
            def _():
                self.arrival(step - 1, True).wait_recv()

            @pl.when(me + step <= last)
            def _():
                self.arrival(step - 1, False).wait_recv()

        if step < last:

            @pl.when((me >= step) & (me < last))
            def _():
                self.upward(step).start()

            @pl.when((me + step <= last) & (me > 0))
            def _():
                self.downward(step).start()

    def finish(self):
        me, last = self.me, self.C - 1
        for step in range(last):

            @pl.when((me >= step) & (me < last))
            def _():
                self.upward(step).wait_send()

            @pl.when((me + step <= last) & (me > 0))
            def _():
                self.downward(step).wait_send()


class LineSum:
    def __init__(self, C, terms, rising, falling, up, down):
        self.C, self.terms, self.rising, self.falling, self.up, self.down = C, terms, rising, falling, up, down
        self.me = lax.axis_index("col")

    def upward(self, m, alone):
        source = self.terms.at[self.C - 1 - m] if alone else self.rising.at[m]
        return remote(source, self.rising.at[m], self.up[0].at[m], self.up[1].at[m], col=lax.rem(self.me + 1, self.C))

    def downward(self, m, alone):
        source = self.terms.at[m] if alone else self.falling.at[m]
        return remote(
            source, self.falling.at[m], self.down[0].at[m], self.down[1].at[m], col=lax.rem(self.me + self.C - 1, self.C)
        )

    def level(self, t):
        me, last = self.me, self.C - 1
        rise, fall = t - me, t - (last - me)
        if t < last:

            @pl.when(me == 0)
            def _():
                if t:
                    self.upward(t - 1, True).wait_send()
                self.upward(t, True).start()

            @pl.when(me == last)
            def _():
                if t:
                    self.downward(t - 1, True).wait_send()
                self.downward(t, True).start()

        if t:

            @pl.when((me > 0) & (rise >= 0))
            def _():
                self.upward(rise, False).wait_recv()
                if t < last:
                    add_into(self.rising.at[rise], self.terms.at[last - rise])
                    self.upward(rise, False).start()

            @pl.when((me < last) & (fall >= 0))
            def _():
                self.downward(fall, False).wait_recv()
                if t < last:
                    add_into(self.falling.at[fall], self.terms.at[fall])
                    self.downward(fall, False).start()

    def finish(self):
        me, last = self.me, self.C - 1

        @pl.when(me == 0)
        def _():
            self.upward(last - 1, True).wait_send()

        @pl.when(me == last)
        def _():
            self.downward(last - 1, True).wait_send()

        for m in range(last):

            @pl.when((me > 0) & (m < last - me))
            def _():
                self.upward(m, False).wait_send()

            @pl.when((me < last) & (m < me))
            def _():
                self.downward(m, False).wait_send()


def line_semaphores(C):
    return [DMA((C,)) for _ in range(4)]


def greet_line(C, others):
    me, last = lax.axis_index("col"), C - 1
    above, below = {"col": me + 1}, {"col": me - 1}

    @pl.when(me == 0)
    def _():
        greet([above] + others, 1 + len(others))

    @pl.when(me == last)
    def _():
        greet([below] + others, 1 + len(others))

    @pl.when((me > 0) & (me < last))
    def _():
        greet([above, below] + others, 2 + len(others))


def feed_kernel(
    R, C, os_hbm, w_hbm, xs_hbm, wg_hbm, wu_hbm, wd_hbm, dy_hbm,
    h_hbm, b_hbm, dg_hbm, du_hbm, dys_hbm, grad_hbm, down_hbm, y_ref,
    big, hidden, slope, silu, b, gates, ups, terms, rising, falling, dys, stage, h, h_mine,
    load, block_load, tile_load, store, w_send, w_recv, f_send, f_recv, *semaphores,
):
    me = lax.axis_index("col")
    row, ahead, behind, other = row_places(R)
    parts, heads, T = os_hbm.shape[0], os_hbm.shape[1], os_hbm.shape[2]
    D, F = wg_hbm.shape
    width, depth = D // C, D // R
    size, tiles, group = 256, 8, R // C
    bf = F // tiles
    up, down = semaphores[:2], semaphores[2:4]
    gather = LineGather(C, dy_hbm, dys, up, down)
    sums = LineSum(C, terms, rising, falling, semaphores[4:6], semaphores[6:8])

    def began(source, target, semaphore):
        copy = pltpu.make_async_copy(source, target, semaphore)
        copy.start()
        return copy

    def block_in(i):
        rows = pl.ds(i * size, size)
        copies = [
            pltpu.make_async_copy(
                os_hbm.at[j, n, rows, :], hidden.at[rows, pl.ds((j * heads + n) * HEAD_DIM, HEAD_DIM)], block_load.at[i, j * heads + n]
            )
            for j in range(parts)
            for n in range(heads)
        ]
        return copies + [
            pltpu.make_async_copy(
                xs_hbm.at[j, rows, :], slope.at[rows, pl.ds(j * width, width)], block_load.at[i, parts * heads + j]
            )
            for j in range(C)
        ]

    def tile_in(i):
        cut = pl.ds(i * bf, bf)
        return [
            pltpu.make_async_copy(wg_hbm.at[:, cut], gates.at[i % 2], tile_load.at[0, i % 2]),
            pltpu.make_async_copy(wu_hbm.at[:, cut], ups.at[i % 2], tile_load.at[1, i % 2]),
        ]

    blocks = [block_in(i) for i in range(T // size)]
    for copy in blocks[0]:
        copy.start()
    out_w = [
        began(w_hbm.at[:, j], big.at[:, :, pl.ds(j * width, width)], load.at[j]) for j in range(C)
    ]
    dy_mine = began(dy_hbm, dys.at[me], load.at[R])
    down_mine = began(wd_hbm, down_hbm.at[row], load.at[R + 1])
    for copies in blocks[1:] + [tile_in(0), tile_in(1)]:
        for copy in copies:
            copy.start()
    greet_line(C, [{"row": other}] + [{"row": ahead[k]} for k in range(1, R // 2)])
    gather.event(0)
    spread = [
        remote(wd_hbm, down_hbm.at[row], w_send.at[k], w_recv.at[k], row=ahead[k]) for k in range(1, R // 2)
    ]
    forward = [remote(wd_hbm, down_hbm.at[row], f_send.at[0], f_recv.at[0], row=other)]
    for copy in spread + forward:
        copy.start()

    stores = []
    mine = pl.ds(pl.multiple_of(me * width, width), width)
    for copy in out_w:
        copy.wait()
    for i in range(T // size):
        rows = pl.ds(i * size, size)
        for copy in blocks[i]:
            copy.wait()
        if i:
            stores[-1].wait()
        left = hidden[rows, :D]
        for j in range(C):
            columns = slice(j * width, (j + 1) * width)
            right = big[j * group : (j + 1) * group, :, :D].reshape(width, D)
            h[:, columns] = slope[rows, columns].astype(F32) + dot_nt(left, right)
        h_mine[rows, :] = h[:, mine]
        values = h[...]
        centre, inverse = norm_rows(values)
        b[rows, :] = ((values - centre) * inverse).astype(BF)
        stores.append(began(h, h_hbm.at[rows, :], store.at[0]))
    stores[-1].wait()
    b_out = began(b, b_hbm, store.at[1])
    for i in range(tiles):
        cut = slice(i * bf, (i + 1) * bf)
        for copy in tile_in(i):
            copy.wait()
        values = b[...]
        gate = dot_nn(values, gates[i % 2])
        upward = dot_nn(values, ups[i % 2])
        sigmoid = jax.nn.sigmoid(gate)
        silued = gate * sigmoid
        hidden[:, cut] = (silued * upward).astype(BF)
        slope[:, cut] = (upward * sigmoid * (1.0 + gate * (1.0 - sigmoid))).astype(BF)
        silu[:, cut] = silued.astype(BF)
        if i + 2 < tiles:
            for copy in tile_in(i + 2):
                copy.start()
        if i == 3:
            gather.event(1)
    for k in range(1, R // 2):
        spread[k - 1].wait_recv()
        block = down_hbm.at[behind[k]]
        copy = remote(block, block, f_send.at[k], f_recv.at[k], row=other)
        copy.start()
        forward.append(copy)
    for step in range(2, max(3, C - 1)):
        if step < C:
            gather.event(step)
    for copy in forward:
        copy.wait_recv()
    down_mine.wait()
    began(down_hbm, big.at[:, :, pl.ds(0, F)], load.at[0]).wait()
    half = lax.div(me, C // 2)

    def out_tile(k):
        j = (C - 1 - k) * (1 - half) + k * half
        right = big[pl.ds(j * group, group), :, :F].reshape(width, F)
        terms[j] = dot_nt(hidden[:, :F], right).astype(BF)

    out_tile(0)
    sums.level(0)
    for k in range(1, C):
        out_tile(k)
    for step in range(max(3, C - 1), C):
        gather.event(step)
    dy_mine.wait()
    b_out.wait()
    joined = [began(dys.at[j], b.at[:, pl.ds(j * width, width)], load.at[j]) for j in range(C)]
    saved = [began(dys, dys_hbm, store.at[1])]
    for copy in joined:
        copy.wait()
    sums.level(1)
    for i in range(tiles):
        cut = slice(i * bf, (i + 1) * bf)
        grad_hidden = dot_nn(b[...], big[:, :, cut].reshape(D, bf))
        slope[:, cut] = (grad_hidden * slope[:, cut].astype(F32)).astype(BF)
        silu[:, cut] = (grad_hidden * silu[:, cut].astype(F32)).astype(BF)
    saved.append(began(slope.at[:, pl.ds(0, F)], dg_hbm, store.at[2]))
    saved.append(began(silu.at[:, pl.ds(0, F)], du_hbm, store.at[3]))

    def grads(first, stop):
        copies = []
        for j in range(first, stop):
            if len(copies) >= 2:
                copies[-2].wait()
            stage[j % 2] = dot_tn(dys[j], hidden[:, :F]).astype(BF)
            copies.append(began(stage.at[j % 2], grad_hbm.at[pl.ds(j * width, width), :], load.at[j % 2]))
        for copy in copies[-2:]:
            copy.wait()

    grads(0, C // 2)
    for t in range(2, C - 1):
        sums.level(t)
    grads(C // 2, C)
    sums.level(C - 1)
    last = C - 1
    y_ref[...] = terms[me]

    @pl.when(me == 0)
    def _():
        y_ref[...] = (h_mine[...] + terms[me].astype(F32) + falling[0].astype(F32)).astype(BF)

    @pl.when(me == last)
    def _():
        y_ref[...] = (h_mine[...] + terms[me].astype(F32) + rising[0].astype(F32)).astype(BF)

    @pl.when((me > 0) & (me < last))
    def _():
        y_ref[...] = (
            h_mine[...] + terms[me].astype(F32) + rising[last - me].astype(F32) + falling[me].astype(F32)
        ).astype(BF)

    sums.finish()
    gather.finish()
    for copy in spread + forward:
        copy.wait_send()
    for copy in saved:
        copy.wait()


def feed_forward(R, C, os, w_out, xs, w_gate, w_up, w_down, cotangent):
    heads, T = os.shape[1], os.shape[2]
    width = xs.shape[2]
    D, F = w_gate.shape
    most = max(D, F)
    flat = pltpu.VMEM((T, most), BF)
    return pl.pallas_call(
        functools.partial(feed_kernel, R, C),
        in_specs=[ANY] * 7,
        out_specs=[ANY] * 7 + [VMEM_SPEC],
        out_shape=[
            struct((T, D), F32),
            struct((T, D), BF),
            struct((T, F), BF),
            struct((T, F), BF),
            struct((C, T, width), BF),
            struct((D, F), BF),
            struct((R, D // R, F), BF),
            struct((T, width), BF),
        ],
        scratch_shapes=[
            pltpu.VMEM((R, D // R, most), BF),
            flat,
            flat,
            pltpu.VMEM((T, F), BF),
            pltpu.VMEM((T, D), BF),
            pltpu.VMEM((2, D, F // 8), BF),
            pltpu.VMEM((2, D, F // 8), BF),
            pltpu.VMEM((C, T, width), BF),
            pltpu.VMEM((C - 1, T, width), BF),
            pltpu.VMEM((C - 1, T, width), BF),
            pltpu.VMEM((C, T, width), BF),
            pltpu.VMEM((2, width, F), BF),
            pltpu.VMEM((256, D), F32),
            pltpu.VMEM((T, width), F32),
            DMA((R + 2,)),
            DMA((T // 256, C * heads + C)),
            DMA((2, 2)),
            DMA((4,)),
            DMA((R // 2,)),
            DMA((R // 2,)),
            DMA((R // 2,)),
            DMA((R // 2,)),
        ]
        + line_semaphores(C)
        + line_semaphores(C),
        compiler_params=comm_params(2, 63),
        cost_estimate=cost(1.2e11, 90 * MIB),
        name="feed_forward",
    )(os, w_out, xs, w_gate, w_up, w_down, cotangent)


def norm_terms_kernel(
    R, C, dg_hbm, du_hbm, wg_hbm, wu_hbm, b_hbm, down_hbm,
    sum_ref, gate_hbm, up_hbm, down_ref,
    dg, du, wg, wu, b, terms, held, stage, own, exchanged, arrived,
    load, tile_load, store, own_load, send, recv, *semaphores,
):
    me, right, left = ring_places(C)
    D, F = wg.shape
    T = dg.shape[0]
    rows = T // C
    width = D // C

    def fetch(source, target, semaphore):
        copy = pltpu.make_async_copy(source, target, semaphore)
        copy.start()
        return copy

    def chunk(s):
        return pl.ds(pl.multiple_of(lax.rem(me + 2 * C - 1 - s, C) * rows, rows), rows)

    grads_in = []
    for s in range(C):
        part = chunk(s)
        grads_in.append(
            (fetch(dg_hbm.at[part, :], dg.at[part, :], load.at[2 * s]), fetch(du_hbm.at[part, :], du.at[part, :], load.at[2 * s + 1]))
        )
        if s == 0:
            weights_in = []
            for n in range(C):
                cut = pl.ds(n * width, width)
                weights_in.append(
                    (fetch(wg_hbm.at[cut, :], wg.at[cut, :], tile_load.at[2 * n]), fetch(wu_hbm.at[cut, :], wu.at[cut, :], tile_load.at[2 * n + 1]))
                )
    b_in = fetch(b_hbm, b, load.at[2 * C])
    sums, own_loads = held_row_sum(R, down_hbm, own, exchanged, arrived, own_load, semaphores)
    for copy in own_loads:
        copy.start()
    greet([{"col": left}] + sums.peers, 1 + len(sums.peers))
    for slot in sums.order():
        sums.exchange(slot).start()

    def term_tile(s, part, n):
        cut = pl.ds(pl.multiple_of(n * width, width), width)
        total = dot_nt(dg[part, :], wg[cut, :]) + dot_nt(du[part, :], wu[cut, :])
        terms[s, :, cut] = total.astype(BF)

    def moves(step):
        return ring_step(step, C, right, terms.at[0], held, send, recv)

    def pass_on(step):
        moves(step - 1).wait_recv()
        add_into(held.at[step - 1], terms.at[step])
        moves(step).start()

    for s in range(C):
        part = chunk(s)
        for copy in grads_in[s]:
            copy.wait()
        if s == 0:
            for n in range(C):
                for copy in weights_in[n]:
                    copy.wait()
                term_tile(s, part, n)
            moves(0).start()
            sums.relay(lambda slot: own_loads[slot].wait())
        else:

            def body(n, carry):
                term_tile(s, part, n)
                return carry

            lax.fori_loop(0, C, body, 0)
    b_in.wait()

    def stored(target, t, slot):
        cut = pl.ds(pl.multiple_of(t * width, width), width)
        return pltpu.make_async_copy(stage.at[slot], target.at[cut, :], store.at[slot])

    def product(right_ref, target):
        def body(t, carry):
            slot = lax.rem(t, 2)

            @pl.when(t >= 2)
            def _():
                stored(target, t, slot).wait()

            left_tile = b[:, pl.ds(pl.multiple_of(t * width, width), width)]
            stage[slot] = dot_tn(left_tile, right_ref[...]).astype(BF)
            stored(target, t, slot).start()
            return carry

        lax.fori_loop(0, C, body, 0)
        for slot in range(2):
            stored(target, slot, slot).wait()

    middle = max(1, (C - 1) // 2)
    for step in range(1, middle + 1):
        if step < C - 1:
            pass_on(step)
    product(dg, gate_hbm)
    sums.relay_again()
    product(du, up_hbm)
    for step in range(middle + 1, C - 1):
        pass_on(step)

    def write(part, values):
        down_ref[:, part] = values.T

    sums.finish(write, 128)
    moves(C - 2).wait_recv()
    sum_ref[...] = held[C - 2].astype(F32) + terms[C - 1].astype(F32)
    for step in range(C - 1):
        moves(step).wait_send()


def norm_terms(R, C, dg, du, w_gate, w_up, b, grad_down):
    T, F = dg.shape
    D = w_gate.shape[0]
    rows, width = T // C, D // C
    depth, columns = grad_down.shape[1:]
    return pl.pallas_call(
        functools.partial(norm_terms_kernel, R, C),
        in_specs=[ANY] * 6,
        out_specs=[VMEM_SPEC, ANY, ANY, VMEM_SPEC],
        out_shape=[struct((rows, D), F32), struct((D, F), BF), struct((D, F), BF), struct((columns, depth), F32)],
        scratch_shapes=[
            pltpu.VMEM((T, F), BF),
            pltpu.VMEM((T, F), BF),
            pltpu.VMEM((D, F), BF),
            pltpu.VMEM((D, F), BF),
            pltpu.VMEM((T, D), BF),
            pltpu.VMEM((C, rows, D), BF),
            pltpu.VMEM((C - 1, rows, D), BF),
            pltpu.VMEM((2, width, F), BF),
            pltpu.VMEM((R // 2, depth, columns), BF),
        ]
        + row_sum_buffers(R, depth, columns)
        + [
            DMA((2 * C + 1,)),
            DMA((2 * C,)),
            DMA((2,)),
            DMA((R // 2,)),
            DMA((C - 1,)),
            DMA((C - 1,)),
        ]
        + row_sum_semaphores(R),
        compiler_params=comm_params(3, 63),
        cost_estimate=cost(9e10, 70 * MIB),
        name="norm_terms",
    )(dg, du, w_gate, w_up, b, grad_down)


def attend_back_kernel(
    R, C, sum_ref, log_ref, segk_ref, segq_ref, cos_ref, sin_ref,
    q_hbm, k_hbm, v_hbm, h_hbm, dys_hbm, w_hbm, gate_hbm,
    dq_ref, dk_ref, dv_ref, gate_ref, dhs_hbm,
    h, dy, w, dh, out, q_ref, k_ref, v_ref, do_ref, dk_sum, dv_sum, own, exchanged, arrived,
    load, w_load, local, h_send, h_recv, o_send, o_recv, own_load, *semaphores,
):
    me, right, left = ring_places(C)
    rows, D = sum_ref.shape
    T, width = q_ref.shape
    heads, bq = width // HEAD_DIM, 256
    mine = pl.ds(pl.multiple_of(me * rows, rows), rows)
    first_in = [
        pltpu.make_async_copy(h_hbm.at[mine, :], h, load.at[0]),
        pltpu.make_async_copy(dys_hbm.at[:, mine, :], dy, load.at[1]),
    ]
    head_loads = [
        pltpu.make_async_copy(source, target, load.at[2 + i])
        for i, (source, target) in enumerate(((q_hbm, q_ref), (k_hbm, k_ref), (v_hbm, v_ref)))
    ]
    for copy in first_in:
        copy.start()
    order = [lax.rem(me + k, C) for k in range(1, C)] + [me]
    cuts = [pl.ds(pl.multiple_of(place * width, width), width) for place in order]
    loads = [pltpu.make_async_copy(w_hbm.at[:, order[k]], w.at[k], w_load.at[k]) for k in range(C)]
    sums, own_loads = held_row_sum(R, gate_hbm, own, exchanged, arrived, own_load, semaphores)
    for copy in loads + own_loads + head_loads:
        copy.start()
    greet([{"col": lax.rem(me + k, C)} for k in range(1, C)] + sums.peers, C - 1 + len(sums.peers))
    for slot in sums.order():
        sums.exchange(slot).start()
    for copy in first_in:
        copy.wait()
    grad = sum_ref[...]
    centre, inverse = norm_rows(h[...])
    normed = (h[...] - centre) * inverse
    first = jnp.mean(grad, axis=1, keepdims=True)
    second = jnp.mean(grad * normed, axis=1, keepdims=True)
    dh[...] = (beside(dy).astype(F32) + inverse * (grad - first - normed * second)).astype(BF)
    do_copies, dh_copies = [], []
    for k in range(C):
        loads[k].wait()
        out[k] = dot_nn(dh[...], w[k].reshape(D, width)).astype(BF)
        if k < C - 1:
            copy = remote(out.at[k], do_ref.at[mine, :], o_send.at[k], o_recv.at[k], col=order[k])
        else:
            copy = pltpu.make_async_copy(out.at[k], do_ref.at[mine, :], local.at[0])
        copy.start()
        do_copies.append(copy)
    sums.relay(lambda slot: own_loads[slot].wait())
    for copy in do_copies[:-1]:
        copy.wait_recv()
    do_copies[-1].wait()
    for k in range(C):
        if k < C - 1:
            copy = remote(dh.at[:, cuts[k]], dhs_hbm.at[mine, :], h_send.at[k], h_recv.at[k], col=order[k])
        else:
            copy = pltpu.make_async_copy(dh.at[:, cuts[k]], dhs_hbm.at[mine, :], local.at[1])
        copy.start()
        dh_copies.append(copy)
    for copy in head_loads:
        copy.wait()

    def one_head(head, carry):
        columns = pl.ds(pl.multiple_of(head * HEAD_DIM, HEAD_DIM), HEAD_DIM)
        dk_sum[...] = jnp.zeros_like(dk_sum)
        dv_sum[...] = jnp.zeros_like(dv_sum)
        for first in range(0, T, SEQ):
            for start in range(first, first + SEQ, bq):
                stop = start + bq
                keys = k_ref[first:stop, columns]
                queries = q_ref[start:stop, columns]
                grads = do_ref[start:stop, columns]
                scores = dot_nt(keys, queries) * SCALE
                allowed = allowed_block(segk_ref[first:stop], segq_ref[:, start:stop], start - first)
                scores = jnp.where(allowed, scores, MASKED)
                probs = jnp.exp(scores - log_ref[head, :, start:stop])
                dv_sum[first:stop] += dot_nn(probs.astype(BF), grads)
                grad_probs = dot_nt(v_ref[first:stop, columns], grads)
                inner = jnp.sum(probs * grad_probs, axis=0, keepdims=True)
                grad_scores = (probs * (grad_probs - inner)).astype(BF)
                dk_sum[first:stop] += dot_nn(grad_scores, queries)
                grad_query = dot_tn(keys, grad_scores).T * SCALE
                dq_ref[start:stop, columns] = turn(grad_query, cos_ref[start:stop], -sin_ref[start:stop]).astype(BF)
        dk_ref[:, columns] = turn(dk_sum[...] * SCALE, cos_ref[...], -sin_ref[...]).astype(BF)
        dv_ref[:, columns] = dv_sum[...].astype(BF)
        return carry

    lax.fori_loop(0, heads // 2, one_head, 0)
    sums.relay_again()
    lax.fori_loop(heads // 2, heads, one_head, 0)

    def write(part, values):
        gate_ref[part, :] = values

    sums.finish(write)
    for copy in do_copies[:-1]:
        copy.wait_send()
    for copy in dh_copies:
        copy.wait()


def attend_back(R, total, log_total, seg_column, seg_row, cos_table, sin_table, q, k, v, h, dys, w_out, grad_gate):
    C, T, width = dys.shape
    rows, D = total.shape
    depth, columns = grad_gate.shape[1:]
    one = pltpu.VMEM((T, width), BF)
    return pl.pallas_call(
        functools.partial(attend_back_kernel, R, C),
        in_specs=[VMEM_SPEC] * 6 + [ANY] * 7,
        out_specs=[VMEM_SPEC] * 4 + [ANY],
        out_shape=[struct((T, width), BF)] * 3 + [struct((depth, columns), F32), struct((T, width), BF)],
        scratch_shapes=[
            pltpu.VMEM((rows, D), F32),
            pltpu.VMEM((C, rows, width), BF),
            pltpu.VMEM((C, R, D // R, width), BF),
            pltpu.VMEM((rows, D), BF),
            pltpu.VMEM((C, rows, width), BF),
            one,
            one,
            one,
            one,
            pltpu.VMEM((T, HEAD_DIM), F32),
            pltpu.VMEM((T, HEAD_DIM), F32),
            pltpu.VMEM((R // 2, depth, columns), BF),
        ]
        + row_sum_buffers(R, depth, columns)
        + [
            DMA((5,)),
            DMA((C,)),
            DMA((2,)),
            DMA((C - 1,)),
            DMA((C - 1,)),
            DMA((C - 1,)),
            DMA((C - 1,)),
            DMA((R // 2,)),
        ]
        + row_sum_semaphores(R),
        compiler_params=comm_params(5),
        cost_estimate=cost(5e10, 30 * MIB),
        name="attend_back",
    )(total, log_total, seg_column, seg_row, cos_table, sin_table, q, k, v, h, dys, w_out, grad_gate)


def input_terms_kernel(
    R, C, dq_ref, dk_ref, dv_ref, mu_hbm, r_hbm, w_hbm, a_hbm, x_hbm, dh_hbm, os_hbm,
    y_ref, gq_ref, gk_ref, gv_ref, out_ref,
    mu_ref, r_ref, w_ref, a_ref, x_ref, dh_ref, block, product, mine, by_column, by_row,
    terms, held, stats, stats_in, tiles, q_exchanged, q_arrived, o_tiles, o_exchanged, o_arrived,
    send, recv, s_send, s_recv, w_load, late_load, block_load, c_send, c_recv, r_send, r_recv, local, *semaphores,
):
    me, right, left = ring_places(C)
    T, width = dq_ref.shape
    D = width * C
    heads = (dq_ref, dk_ref, dv_ref)
    row = lax.axis_index("row")
    thin = width // R

    def cut_of(s):
        return pl.ds(pl.multiple_of(lax.rem(me + 2 * C - 1 - s, C) * width, width), width)

    def weight_in(s):
        return pltpu.make_async_copy(w_hbm.at[:, cut_of(s), :], w_ref.at[:, cut_of(s), :], w_load.at[s])

    for s in range(C):
        weight_in(s).start()
    late = [
        pltpu.make_async_copy(source, target, late_load.at[i])
        for i, (source, target) in enumerate(
            ((a_hbm, a_ref), (x_hbm, x_ref), (dh_hbm, dh_ref), (mu_hbm, mu_ref), (r_hbm, r_ref))
        )
    ]
    for copy in late:
        copy.start()
    depth = tiles.shape[2]
    side = lax.rem(lax.axis_index("row"), 2)
    q_sums = RowSum(
        R, lambda i: tiles.at[i, side], lambda i: tiles.at[i, 1 - side], q_exchanged, q_arrived, semaphores[:4]
    )
    o_sums = RowSum(
        R, lambda i: o_tiles.at[i, side], lambda i: o_tiles.at[i, 1 - side], o_exchanged, o_arrived, semaphores[4:]
    )

    def block_in(i):
        return [
            pltpu.make_async_copy(
                os_hbm.at[i, n], block.at[i % 2, :, pl.ds(n * HEAD_DIM, HEAD_DIM)], block_load.at[i % 2, n]
            )
            for n in range(os_hbm.shape[1])
        ]

    for copy in block_in(0) + block_in(1):
        copy.start()
    greet(
        [{"col": lax.rem(me + k, C)} for k in range(1, C)] + [{"row": lax.rem(row + k, R)} for k in range(1, R)],
        C + R - 2,
    )

    def moves(step):
        return ring_step(step, C, right, terms.at[0], held, send, recv)

    def pass_on(step):
        moves(step - 1).wait_recv()
        add_into(held.at[step - 1], terms.at[step])
        moves(step).start()

    def compute(s):
        cut = cut_of(s)
        weight_in(s).wait()
        total = dot_nt(dq_ref[...], w_ref[0, cut, :])
        total += dot_nt(dk_ref[...], w_ref[1, cut, :])
        total += dot_nt(dv_ref[...], w_ref[2, cut, :])
        terms[s] = total.astype(BF)

    compute(0)
    moves(0).start()

    def body(s, carry):
        compute(s)
        return carry

    late[2].wait()
    for j in range(C):
        for copy in block_in(j):
            copy.wait()
        product[...] = dot_tn(block[j % 2], dh_ref[...]).astype(BF)
        for slot in range(R // 2):
            for place in range(2):
                rows = 2 * lax.div(o_sums.places(slot), 2) + place
                o_tiles[slot, place, j * thin : (j + 1) * thin] = product[pl.ds(pl.multiple_of(rows * thin, thin), thin), :]
        if j + 2 < C:
            for copy in block_in(j + 2):
                copy.start()
    for slot in o_sums.order():
        o_sums.exchange(slot).start()
    o_sums.relay()
    lax.fori_loop(1, C, body, 0)
    for i, copy in enumerate(late):
        if i != 2:
            copy.wait()
    for slot in q_sums.order():
        start = pl.multiple_of(lax.div(q_sums.places(slot), 2) * 2 * depth, 2 * depth)
        left_tile = a_ref[:, pl.ds(start, 2 * depth)]
        for i, right_side in enumerate(heads):
            product = dot_tn(left_tile, right_side[...]).astype(BF)
            tiles[slot, 0, :, i * width : (i + 1) * width] = product[:depth]
            tiles[slot, 1, :, i * width : (i + 1) * width] = product[depth:]
        q_sums.exchange(slot).start()
    o_sums.relay_again()
    pass_on(1)
    q_sums.relay()

    def write_out(part, values):
        mine[part, :] = values.astype(BF)

    o_sums.finish(write_out)
    columns_out = []
    for k in range(1, C):
        place = lax.rem(me + k, C)
        rows = pl.ds(pl.multiple_of(place * thin, thin), thin)
        columns_out.append(remote(mine.at[rows, :], by_column.at[me], c_send.at[k - 1], c_recv.at[k - 1], col=place))
    stay = pltpu.make_async_copy(
        mine.at[pl.ds(pl.multiple_of(me * thin, thin), thin), :], by_column.at[me], local.at[0]
    )
    for copy in columns_out + [stay]:
        copy.start()
    size = 128

    def sum_rows(i, carry):
        rows = pl.ds(pl.multiple_of(i * size, size), size)
        lane = lax.broadcasted_iota(jnp.int32, (size, 128), 1)
        total = jnp.zeros((size, 1), F32)
        second = jnp.zeros((size, 1), F32)
        for s in range(C):
            grad = terms[s, rows, :].astype(F32)
            total += jnp.sum(grad, axis=1, keepdims=True)
            second += jnp.sum(grad * a_ref[rows, cut_of(s)].astype(F32), axis=1, keepdims=True)
        packed = jnp.where(lane == 0, total, jnp.where(lane == 1, second, 0.0))
        stats[:, rows] = packed.T[:8]
        return carry

    lax.fori_loop(0, T // size, sum_rows, 0)
    exchanges = [
        remote(stats, stats_in.at[k - 1], s_send.at[k - 1], s_recv.at[k - 1], col=lax.rem(me + k, C)) for k in range(1, C)
    ]
    for copy in exchanges:
        copy.start()
    for copy in columns_out:
        copy.wait_recv()
    stay.wait()

    def piece_of(place):
        return by_column.at[lax.div(place * C, R), :, pl.ds(pl.multiple_of(lax.rem(place, R // C) * depth, depth), depth)]

    rows_out = []
    for k in range(1, R):
        place = lax.rem(row + k, R)
        rows_out.append(remote(piece_of(place), by_row.at[row], r_send.at[k - 1], r_recv.at[k - 1], row=place))
    keep = pltpu.make_async_copy(piece_of(row), by_row.at[row], local.at[1])
    for copy in rows_out + [keep]:
        copy.start()
    for step in range(2, C - 1):
        pass_on(step)
    q_sums.relay_again()
    for copy in rows_out:
        copy.wait_recv()
    keep.wait()
    for n in range(R):
        out_ref[n * thin : (n + 1) * thin, :] = by_row[n].astype(F32)

    def write_qkv(part, values):
        for i, target in enumerate((gq_ref, gk_ref, gv_ref)):
            target[part, :] = values[:, i * width : (i + 1) * width]

    q_sums.finish(write_qkv)
    for copy in exchanges:
        copy.wait_recv()
    moves(C - 2).wait_recv()

    def last_rows(i, carry):
        rows = pl.ds(pl.multiple_of(i * size, size), size)
        both = stats[:, rows]
        for k in range(C - 1):
            both += stats_in[k, :, rows]
        columns = jnp.concatenate([both, jnp.zeros((120, size), F32)], axis=0).T * (1.0 / D)
        normed = (x_ref[rows, :].astype(F32) - mu_ref[rows, :]) * r_ref[rows, :]
        grad = held[C - 2, rows, :].astype(F32) + terms[C - 1, rows, :].astype(F32)
        grad = grad - columns[:, 0:1] - normed * columns[:, 1:2]
        y_ref[rows, :] = (dh_ref[rows, :].astype(F32) + r_ref[rows, :] * grad).astype(BF)
        return carry

    lax.fori_loop(0, T // size, last_rows, 0)
    for copy in exchanges + columns_out + rows_out:
        copy.wait_send()
    for step in range(C - 1):
        moves(step).wait_send()


def input_terms(R, C, dq, dk, dv, w_qkv, a, tokens, dh, mu, r, os):
    T, width = dq.shape
    D = w_qkv.shape[1]
    half, low = R // 2, D // R
    thin = width // R
    return pl.pallas_call(
        functools.partial(input_terms_kernel, R, C),
        in_specs=[VMEM_SPEC] * 3 + [ANY] * 7,
        out_specs=[VMEM_SPEC] * 5,
        out_shape=[struct((T, width), BF)]
        + [struct((low, width), F32)] * 3
        + [struct((width, low), F32)],
        scratch_shapes=[
            pltpu.VMEM((T, 1), F32),
            pltpu.VMEM((T, 1), F32),
            pltpu.VMEM((3, D, width), BF),
            pltpu.VMEM((T, D), BF),
            pltpu.VMEM((T, width), BF),
            pltpu.VMEM((T, width), BF),
            pltpu.VMEM((2, T, width), BF),
            pltpu.VMEM((width, width), BF),
            pltpu.VMEM((C * thin, width), BF),
            pltpu.VMEM((C, thin, width), BF),
            pltpu.VMEM((R, thin, low), BF),
            pltpu.VMEM((C, T, width), BF),
            pltpu.VMEM((C - 1, T, width), BF),
            pltpu.VMEM((8, T), F32),
            pltpu.VMEM((C - 1, 8, T), F32),
            pltpu.VMEM((half, 2, low, 3 * width), BF),
        ]
        + row_sum_buffers(R, low, 3 * width)
        + [pltpu.VMEM((half, 2, C * thin, width), BF)]
        + row_sum_buffers(R, C * thin, width)
        + [
            DMA((C - 1,)),
            DMA((C - 1,)),
            DMA((C - 1,)),
            DMA((C - 1,)),
            DMA((C,)),
            DMA((5,)),
            DMA((2, os.shape[1])),
            DMA((C - 1,)),
            DMA((C - 1,)),
            DMA((R - 1,)),
            DMA((R - 1,)),
            DMA((2,)),
        ]
        + row_sum_semaphores(R)
        + row_sum_semaphores(R),
        compiler_params=comm_params(6, 63),
        cost_estimate=cost(8e10, 20 * MIB),
        name="input_terms",
    )(dq, dk, dv, mu, r, w_qkv, a, tokens, dh, os)


def on_device(R, C, tokens, cotangent, segments, w_query, w_key, w_value, w_out, w_gate, w_up, w_down):
    T, width = tokens.shape
    D = width * C
    gathered = lambda w: lax.all_gather(w, "row", axis=0, tiled=True)

    gate_w, up_w = gathered(w_gate), gathered(w_up)
    seg_column, seg_row = segments.reshape(T, 1), segments.reshape(1, T)
    xs, w_qkv, cos_table, sin_table = first_gather(R, C, seg_column, seg_row, tokens, w_query, w_key, w_value)
    w_qkv = w_qkv.reshape(3, D, width)
    act_one, q, k, v, mu_one, r_one, out_part = norm_and_project(xs, w_qkv, cos_table, sin_table, w_out.T)
    os, log_total, out_w = attend(R, C, q, k, v, seg_column, seg_row, out_part)
    h_full, act_two, dg, du, dys, grad_down, _, output = feed_forward(
        R, C, os, out_w, xs, gate_w, up_w, w_down.T, cotangent
    )
    by_row = lambda values: values.reshape(R, D // R, -1)
    total, grad_gate, grad_up, grad_down = norm_terms(R, C, dg, du, gate_w, up_w, act_two, by_row(grad_down))
    grad_up = lax.psum_scatter(grad_up, "row", scatter_dimension=0, tiled=True).astype(F32)
    dq, dk, dv, grad_gate, dh = attend_back(
        R, total, log_total, seg_column, seg_row, cos_table, sin_table, q, k, v, h_full, dys, out_w, by_row(grad_gate)
    )
    grad_tokens, grad_query, grad_key, grad_value, grad_out = input_terms(
        R, C, dq, dk, dv, w_qkv, act_one, tokens, dh, mu_one, r_one, os
    )
    return (output, grad_tokens, grad_query, grad_key, grad_value, grad_out, grad_gate, grad_up, grad_down)


def solution(mesh):
    here = P("row", "col")
    turned = P("col", "row")
    return jax.shard_map(
        functools.partial(on_device, mesh.shape["row"], mesh.shape["col"]),
        mesh=mesh,
        in_specs=(here, here, P("row"), here, here, here, turned, here, here, turned),
        out_specs=(here, here, here, here, here, turned, here, here, turned),
        check_vma=False,
    )
```

```python
import functools

import jax
import jax.numpy as jnp
from jax import lax
from jax.experimental import pallas as pl
from jax.experimental.pallas import tpu as pltpu
from jax.sharding import PartitionSpec as P

HEAD_DIM = 128
HALF = HEAD_DIM // 2
SEQ = 1024
EPSILON = 1e-05
MASKED = -1e30
SCALE = HEAD_DIM ** (-0.5)
BF = jnp.bfloat16
F32 = jnp.float32
MIB = 1 << 20
ANY = pl.BlockSpec(memory_space=pl.ANY)


def dot_nn(left, right):
    return jnp.dot(left, right, preferred_element_type=F32)


def dot_tn(left, right):
    return lax.dot_general(left, right, (((0,), (0,)), ((), ())), preferred_element_type=F32)


def dot_nt(left, right):
    return lax.dot_general(left, right, (((1,), (1,)), ((), ())), preferred_element_type=F32)


def struct(shape, dtype):
    return jax.ShapeDtypeStruct(shape, dtype)


def params(mib=60):
    return pltpu.CompilerParams(vmem_limit_bytes=mib * MIB)


def cost(flops, moved):
    return pl.CostEstimate(flops=int(flops), bytes_accessed=int(moved), transcendentals=0)


def turn(values, cos_table, sin_table):
    return values * cos_table + pltpu.roll(values, HALF, 1) * sin_table


MESH = pl.DeviceIdType.MESH
VMEM_SPEC = pl.BlockSpec(memory_space=pltpu.VMEM)
DMA = pltpu.SemaphoreType.DMA


def comm_params(number, mib=60):
    return pltpu.CompilerParams(vmem_limit_bytes=mib * MIB, collective_id=number, has_side_effects=True)


def remote(source, target, send, recv, **device):
    return pltpu.make_async_remote_copy(
        src_ref=source, dst_ref=target, send_sem=send, recv_sem=recv, device_id=device, device_id_type=MESH
    )


def greet(senders, targets):
    semaphore = pltpu.get_barrier_semaphore()
    for device in senders:
        pl.semaphore_signal(semaphore, inc=1, device_id=device, device_id_type=MESH)
    pl.semaphore_wait(semaphore, targets)


def ring_places(C):
    me = lax.axis_index("col")
    return me, lax.rem(me + 1, C), lax.rem(me + C - 1, C)


def row_places(R):
    row = lax.axis_index("row")
    ahead = [lax.rem(row + 2 * k, R) for k in range(R // 2)]
    behind = [lax.rem(row + R - 2 * k, R) for k in range(R // 2)]
    other = row + 1 - 2 * lax.rem(row, 2)
    return row, ahead, behind, other


def gather_ring(C, source, whole, send, recv):
    me, right, left = ring_places(C)
    copies = []
    for step in range(C - 1):
        owner = lax.rem(me - step + C, C)
        piece = source if step == 0 else whole.at[owner]
        copies.append(remote(piece, whole.at[owner], send.at[step], recv.at[step], col=right))
    return copies


def gather_kernel(
    R, C, segq_ref, rate_ref, wo_ref, wd_ref, x_ref, wq_ref, wk_ref, wv_ref,
    xs_ref, w_ref, cos_ref, sin_ref, segk_ref, wo_turned, wd_turned,
    local, x_send, x_recv, w_send, w_recv, f_send, f_recv,
):
    me, right, left = ring_places(C)
    row, ahead, behind, other = row_places(R)
    weights = (wq_ref, wk_ref, wv_ref)
    mine = [
        pltpu.make_async_copy(x_ref, xs_ref.at[me], local.at[0]),
    ] + [pltpu.make_async_copy(w, w_ref.at[i, row], local.at[1 + i]) for i, w in enumerate(weights)]
    for copy in mine:
        copy.start()
    greet(
        [{"col": left}, {"row": other}] + [{"row": r} for r in behind[1:]],
        1 + R // 2,
    )

    x_copies = gather_ring(C, x_ref, xs_ref, x_send, x_recv)
    x_copies[0].start()
    spread, forward = [], []
    for i, w in enumerate(weights):
        for k in range(1, R // 2):
            copy = remote(w, w_ref.at[i, row], w_send.at[i, k], w_recv.at[i, k], row=ahead[k])
            copy.start()
            spread.append(copy)
        copy = remote(w, w_ref.at[i, row], f_send.at[i, 0], f_recv.at[i, 0], row=other)
        copy.start()
        forward.append(copy)
    T = cos_ref.shape[0]
    size = 128

    def table_rows(i, carry):
        rows = pl.ds(pl.multiple_of(i * size, size), size)
        first = SEQ * lax.div(i * size, SEQ)
        here = jnp.broadcast_to(segq_ref[:, rows].astype(F32), (size, size)).T[:, :1]
        segk_ref[rows, :] = here.astype(jnp.int32)
        shape = (size, T)
        queries = lax.broadcasted_iota(jnp.int32, shape, 0) + i * size
        keys = lax.broadcasted_iota(jnp.int32, shape, 1)
        seen = (here == segq_ref[...].astype(F32)) & (keys <= queries) & (keys >= first)
        place = jnp.sum(jnp.where(seen, 1.0, 0.0), axis=1, keepdims=True) - 1.0
        angles = place * rate_ref[...]
        lane = lax.broadcasted_iota(jnp.int32, angles.shape, 1)
        sine = jnp.sin(angles)
        cos_ref[rows, :] = jnp.cos(angles)
        sin_ref[rows, :] = jnp.where(lane < HALF, -sine, sine)
        return carry

    lax.fori_loop(0, T // size, table_rows, 0)

    def turn_rows(source, target):
        def body(i, carry):
            cut = pl.ds(pl.multiple_of(i * size, size), size)
            target[:, cut] = source[cut, :].astype(F32).T.astype(BF)
            return carry

        lax.fori_loop(0, source.shape[0] // size, body, 0)

    turn_rows(wo_ref, wo_turned)
    turn_rows(wd_ref, wd_turned)
    for s in range(1, C - 1):
        x_copies[s - 1].wait_recv()
        x_copies[s].start()
    for i in range(3):
        for k in range(1, R // 2):
            spread[i * (R // 2 - 1) + k - 1].wait_recv()
            block = w_ref.at[i, behind[k]]
            copy = remote(block, block, f_send.at[i, k], f_recv.at[i, k], row=other)
            copy.start()
            forward.append(copy)
    x_copies[-1].wait_recv()
    for copy in forward:
        copy.wait_recv()
    for copy in x_copies + spread + forward:
        copy.wait_send()
    for copy in mine:
        copy.wait()


def first_gather(R, C, seg_row, tokens, w_query, w_key, w_value, w_out, w_down):
    depth, width = w_query.shape
    T = tokens.shape[0]
    half = R // 2
    rate = 10000.0 ** (-(jnp.arange(HALF, dtype=F32) * 2.0 / HEAD_DIM))
    rate = jnp.concatenate([rate, rate]).reshape(1, HEAD_DIM)
    return pl.pallas_call(
        functools.partial(gather_kernel, R, C),
        in_specs=[VMEM_SPEC] * 4 + [ANY] * 4,
        out_specs=[ANY] * 2 + [VMEM_SPEC] * 5,
        out_shape=[
            struct((C,) + tokens.shape, BF),
            struct((3, R, depth, width), BF),
            struct((T, HEAD_DIM), F32),
            struct((T, HEAD_DIM), F32),
            struct((T, 1), jnp.int32),
            struct(w_out.shape[::-1], BF),
            struct(w_down.shape[::-1], BF),
        ],
        scratch_shapes=[
            DMA((4,)),
            DMA((C - 1,)),
            DMA((C - 1,)),
            DMA((3, half)),
            DMA((3, half)),
            DMA((3, half)),
            DMA((3, half)),
        ],
        compiler_params=comm_params(0),
        cost_estimate=cost(6e10, 14 * MIB),
        name="first_gather",
    )(seg_row, rate, w_out, w_down, tokens, w_query, w_key, w_value)


def norm_rows(x):
    centre = jnp.mean(x, axis=-1, keepdims=True)
    spread = jnp.mean(x * x, axis=-1, keepdims=True) - centre * centre
    inverse = lax.rsqrt(spread + EPSILON)
    return centre, inverse


def beside(ref):
    return jnp.concatenate([ref[j] for j in range(ref.shape[0])], axis=1)


def qkv_kernel(
    C, xs_ref, w_ref, cos_ref, sin_ref, wo_ref, a_ref, q_ref, k_ref, v_ref, mu_ref, r_ref, wos_ref, local, send, recv
):
    step, steps = pl.program_id(0), pl.num_programs(0)
    me, right, left = ring_places(C)
    copies = gather_ring(C, wo_ref, wos_ref, send, recv)
    mine = pltpu.make_async_copy(wo_ref, wos_ref.at[me], local.at[0])

    @pl.when(step == 0)
    def _():
        mine.start()
        greet([{"col": left}], 1)
        copies[0].start()

    for s in range(1, C - 1):

        @pl.when(step == jnp.minimum(2 * s, steps - 1))
        def _():
            copies[s - 1].wait_recv()
            copies[s].start()

    x = beside(xs_ref).astype(F32)
    centre, inverse = norm_rows(x)
    a = ((x - centre) * inverse).astype(BF)
    a_ref[...] = a
    mu_ref[...] = centre
    r_ref[...] = inverse
    cosine, sine = cos_ref[...], sin_ref[...]
    for index, out in enumerate((q_ref, k_ref, v_ref)):
        product = dot_nn(a, w_ref[index])
        if index == 2:
            out[...] = product.astype(BF)
            continue
        for start in range(0, out.shape[1], HEAD_DIM):
            part = product[:, start : start + HEAD_DIM]
            out[:, start : start + HEAD_DIM] = turn(part, cosine, sine).astype(BF)

    @pl.when(step == steps - 1)
    def _():
        copies[-1].wait_recv()
        for copy in copies:
            copy.wait_send()
        mine.wait()


def norm_and_project(xs, w_qkv, cos_table, sin_table, w_out):
    C, T, width = xs.shape
    D = width * C
    bt = 256
    rows = lambda n: pl.BlockSpec((bt, n), lambda i: (i, 0))
    return pl.pallas_call(
        functools.partial(qkv_kernel, C),
        grid=(T // bt,),
        in_specs=[
            pl.BlockSpec((C, bt, width), lambda i: (0, i, 0)),
            pl.BlockSpec(w_qkv.shape, lambda i: (0, 0, 0), pipeline_mode=pl.Buffered(1)),
            rows(HEAD_DIM),
            rows(HEAD_DIM),
            ANY,
        ],
        out_specs=[rows(D), rows(width), rows(width), rows(width), rows(1), rows(1), ANY],
        out_shape=[
            struct((T, D), BF),
            struct((T, width), BF),
            struct((T, width), BF),
            struct((T, width), BF),
            struct((T, 1), F32),
            struct((T, 1), F32),
            struct((C,) + w_out.shape, BF),
        ],
        scratch_shapes=[DMA((1,)), DMA((C - 1,)), DMA((C - 1,))],
        compiler_params=comm_params(7),
        cost_estimate=cost(2e10, 14 * MIB),
        name="norm_and_project",
    )(xs, w_qkv, cos_table, sin_table, w_out)


def allowed_block(seg_key, seg_query, first_query):
    shape = (seg_key.shape[0], seg_query.shape[1])
    keys = lax.broadcasted_iota(jnp.int32, shape, 0)
    queries = lax.broadcasted_iota(jnp.int32, shape, 1) + first_query
    return (seg_key == seg_query) & (keys <= queries)


def attend_kernel(
    R, C, q_ref, k_ref, v_ref, segk_ref, segq_ref, wos_ref, os_ref, log_ref, w_ref,
    o_buf, local, o_send, o_recv, w_send, w_recv, f_send, f_recv,
):
    me, right, left = ring_places(C)
    row, ahead, behind, other = row_places(R)
    T, width = q_ref.shape
    heads, bq = width // HEAD_DIM, 256
    greet([{"col": left}, {"row": other}] + [{"row": r} for r in behind[1:]], 1 + R // 2)
    mine = pltpu.make_async_copy(wos_ref, w_ref.at[row], local.at[0])
    mine.start()
    spread, forward = [], []
    for k in range(1, R // 2):
        copy = remote(wos_ref, w_ref.at[row], w_send.at[k], w_recv.at[k], row=ahead[k])
        copy.start()
        spread.append(copy)
    copy = remote(wos_ref, w_ref.at[row], f_send.at[0], f_recv.at[0], row=other)
    copy.start()
    forward.append(copy)

    def ring(step, head):
        owner = lax.rem(me - step + C, C)
        piece = o_buf.at[head] if step == 0 else os_ref.at[owner, head]
        return remote(piece, os_ref.at[owner, head], o_send.at[step, head], o_recv.at[step, head], col=right)

    def one_head(head, carry):
        columns = pl.ds(pl.multiple_of(head * HEAD_DIM, HEAD_DIM), HEAD_DIM)
        for first in range(0, T, SEQ):
            for start in range(first, first + SEQ, bq):
                stop = start + bq
                scores = dot_nt(k_ref[first:stop, columns], q_ref[start:stop, columns]) * SCALE
                allowed = allowed_block(segk_ref[first:stop], segq_ref[:, start:stop], start - first)
                scores = jnp.where(allowed, scores, MASKED)
                peak = jnp.max(scores, axis=0, keepdims=True)
                exponent = jnp.exp(scores - peak)
                total = jnp.sum(exponent, axis=0, keepdims=True)
                weights = (exponent * (1.0 / total)).astype(BF)
                o_buf[head, start:stop] = dot_tn(v_ref[first:stop, columns], weights).T.astype(BF)
                log_ref[head, :, start:stop] = peak + jnp.log(total)
        ring(0, head).start()
        pltpu.make_async_copy(o_buf.at[head], os_ref.at[me, head], local.at[1 + head]).start()
        return carry

    lax.fori_loop(0, heads, one_head, 0)
    for step in range(1, C - 1):
        for head in range(heads):
            ring(step - 1, head).wait_recv()
            ring(step, head).start()
    for k in range(1, R // 2):
        spread[k - 1].wait_recv()
        block = w_ref.at[behind[k]]
        copy = remote(block, block, f_send.at[k], f_recv.at[k], row=other)
        copy.start()
        forward.append(copy)
    for head in range(heads):
        ring(C - 2, head).wait_recv()
        pltpu.make_async_copy(o_buf.at[head], os_ref.at[me, head], local.at[1 + head]).wait()
        for step in range(C - 1):
            ring(step, head).wait_send()
    for copy in forward:
        copy.wait_recv()
    for copy in spread + forward:
        copy.wait_send()
    mine.wait()


def attend(R, C, q, k, v, seg_column, seg_row, w_part):
    T, width = q.shape
    heads, half = width // HEAD_DIM, R // 2
    return pl.pallas_call(
        functools.partial(attend_kernel, R, C),
        in_specs=[VMEM_SPEC] * 5 + [ANY],
        out_specs=[ANY, VMEM_SPEC, ANY],
        out_shape=[
            struct((C, heads, T, HEAD_DIM), BF),
            struct((heads, 1, T), F32),
            struct((R,) + w_part.shape, BF),
        ],
        scratch_shapes=[
            pltpu.VMEM((heads, T, HEAD_DIM), BF),
            DMA((1 + heads,)),
            DMA((C - 1, heads)),
            DMA((C - 1, heads)),
            DMA((half,)),
            DMA((half,)),
            DMA((half,)),
            DMA((half,)),
        ],
        compiler_params=comm_params(1),
        cost_estimate=cost(7e10, 14 * MIB),
        name="attend",
    )(q, k, v, seg_column, seg_row, w_part)


def ring_step(step, C, right, first, held, send, recv):
    source = first if step == 0 else held.at[step - 1]
    return remote(source, held.at[step], send.at[step], recv.at[step], col=right)


def add_into(held, terms):
    size = 64

    def body(i, carry):
        rows = pl.ds(pl.multiple_of(i * size, size), size)
        held[rows, :] = (held[rows, :].astype(F32) + terms[rows, :].astype(F32)).astype(BF)
        return carry

    lax.fori_loop(0, held.shape[0] // size, body, 0)


class RowSum:
    def __init__(self, R, own, twin, exchanged, arrived, semaphores):
        self.P = R // 4
        self.own, self.twin, self.exchanged, self.arrived = own, twin, exchanged, arrived
        self.x_send, self.x_recv, self.y_send, self.y_recv = semaphores
        self.width = arrived.shape[2]
        self.places = row_of(R)
        self.peers = row_peers(R)

    def part(self, ref, side):
        return ref.at[:, pl.ds(side * self.width, self.width)]

    def exchange(self, slot):
        return remote(
            self.twin(slot), self.exchanged.at[slot], self.x_send.at[slot], self.x_recv.at[slot], row=self.places(0, True)
        )

    def send(self, slot, side, index, target):
        return remote(
            self.part(self.own(slot), side), self.arrived.at[index], self.y_send.at[index], self.y_recv.at[index],
            row=self.places(target),
        )

    def left_one(self, dp):
        return self.send(2 * dp + 1, 0, dp, 1)

    def left_two(self, dp):
        return self.send(2 * dp, 0, self.P + dp - 1, 2 * dp)

    def right_one(self, dp, dq):
        return self.send(2 * dp + dq, 1, 2 * self.P - 1 + 2 * (dp - 1) + dq, 2 * dp)

    def right_two(self):
        return self.send(1, 1, 4 * self.P - 3, 1)

    def order(self):
        return (
            [2 * dp + 1 for dp in range(1, self.P)] + [1] + [2 * dp for dp in range(1, self.P)] + [0]
        )

    def relay(self, before=None):
        for slot in self.order():
            if before is not None:
                before(slot)
            self.exchange(slot).wait_recv()
            add_into(self.own(slot), self.exchanged.at[slot])
            dp, dq = divmod(slot, 2)
            if dq:
                self.left_one(dp).start()
            if dp:
                self.right_one(dp, dq).start()

    def relay_again(self):
        for dp in range(1, self.P):
            self.left_one(dp).wait_recv()
            add_into(self.part(self.own(2 * dp), 0), self.arrived.at[dp])
            self.left_two(dp).start()
        for dp in range(1, self.P):
            copy = self.right_one(dp, 1)
            copy.wait_recv()
            add_into(self.part(self.own(1), 1), self.arrived.at[2 * self.P - 1 + 2 * (dp - 1) + 1])
        self.right_two().start()

    def finish(self, write, size=64):
        P, width = self.P, self.width
        self.left_one(0).wait_recv()
        self.right_two().wait_recv()
        for dp in range(1, P):
            self.left_two(dp).wait_recv()
            self.right_one(dp, 0).wait_recv()
        lefts = [0] + [P + dp - 1 for dp in range(1, P)]
        rights = [4 * P - 3] + [2 * P - 1 + 2 * (dp - 1) for dp in range(1, P)]

        def body(i, carry):
            rows = pl.ds(pl.multiple_of(i * size, size), size)
            total = self.own(0)[rows, :].astype(F32)
            halves = []
            for side, places in enumerate((lefts, rights)):
                half = total[:, side * width : (side + 1) * width]
                for index in places:
                    half += self.arrived[index, rows, :].astype(F32)
                halves.append(half)
            write(rows, jnp.concatenate(halves, axis=1))
            return carry

        lax.fori_loop(0, self.exchanged.shape[1] // size, body, 0)
        for slot in range(2 * P):
            self.exchange(slot).wait_send()
        self.left_one(0).wait_send()
        self.right_two().wait_send()
        for dp in range(1, P):
            self.left_one(dp).wait_send()
            self.left_two(dp).wait_send()
            self.right_one(dp, 0).wait_send()
            self.right_one(dp, 1).wait_send()


def row_of(R):
    row = lax.axis_index("row")
    side, chip = lax.rem(row, 2), lax.div(row, 2)
    p, q = lax.div(chip, 2), lax.rem(chip, 2)

    def place(slot, twin=False):
        dp, dq = divmod(slot, 2)
        chip_there = 2 * lax.rem(p + dp, R // 4) + lax.rem(q + dq, 2)
        return 2 * chip_there + (1 - side if twin else side)

    return place


def row_peers(R):
    place = row_of(R)
    return [{"row": place(0, True)}, {"row": place(1)}] + [{"row": place(2 * dp)} for dp in range(1, R // 4)]


def row_sum_semaphores(R):
    return [DMA((R // 2,)), DMA((R // 2,)), DMA((R - 2,)), DMA((R - 2,))]


def row_sum_buffers(R, depth, columns):
    return [
        pltpu.VMEM((R // 2, depth, columns), BF),
        pltpu.VMEM((R - 2, depth, columns // 2), BF),
    ]


def held_row_sum(R, grad_hbm, own, exchanged, arrived, load, semaphores):
    place = row_of(R)
    sums = RowSum(R, lambda i: own.at[i], lambda i: grad_hbm.at[place(i, True)], exchanged, arrived, semaphores)
    loads = [pltpu.make_async_copy(grad_hbm.at[place(i)], own.at[i], load.at[i]) for i in range(R // 2)]
    return sums, loads


class LineGather:
    def __init__(self, C, source, whole, up, down):
        self.C, self.source, self.whole, self.up, self.down = C, source, whole, up, down
        self.me = lax.axis_index("col")

    def upward(self, step):
        owner = self.me - step
        piece = self.source if step == 0 else self.whole.at[owner]
        return remote(piece, self.whole.at[owner], self.up[0].at[step], self.up[1].at[step], col=self.me + 1)

    def downward(self, step):
        owner = self.me + step
        piece = self.source if step == 0 else self.whole.at[owner]
        return remote(piece, self.whole.at[owner], self.down[0].at[step], self.down[1].at[step], col=self.me - 1)

    def arrival(self, step, rises):
        sender = self.me - 1 if rises else self.me + 1
        send, recv = self.up if rises else self.down
        target = self.whole.at[sender - step if rises else sender + step]
        return remote(target, target, send.at[step], recv.at[step], col=sender)

    def event(self, step):
        me, last = self.me, self.C - 1
        if step:

            @pl.when(me >= step)
            def _():
                self.arrival(step - 1, True).wait_recv()

            @pl.when(me + step <= last)
            def _():
                self.arrival(step - 1, False).wait_recv()

        if step < last:

            @pl.when((me >= step) & (me < last))
            def _():
                self.upward(step).start()

            @pl.when((me + step <= last) & (me > 0))
            def _():
                self.downward(step).start()

    def finish(self):
        me, last = self.me, self.C - 1
        for step in range(last):

            @pl.when((me >= step) & (me < last))
            def _():
                self.upward(step).wait_send()

            @pl.when((me + step <= last) & (me > 0))
            def _():
                self.downward(step).wait_send()


class LineSum:
    def __init__(self, C, terms, rising, falling, up, down):
        self.C, self.terms, self.rising, self.falling, self.up, self.down = C, terms, rising, falling, up, down
        self.me = lax.axis_index("col")

    def upward(self, m, alone):
        source = self.terms.at[self.C - 1 - m] if alone else self.rising.at[m]
        return remote(source, self.rising.at[m], self.up[0].at[m], self.up[1].at[m], col=lax.rem(self.me + 1, self.C))

    def downward(self, m, alone):
        source = self.terms.at[m] if alone else self.falling.at[m]
        return remote(
            source, self.falling.at[m], self.down[0].at[m], self.down[1].at[m], col=lax.rem(self.me + self.C - 1, self.C)
        )

    def level(self, t):
        me, last = self.me, self.C - 1
        rise, fall = t - me, t - (last - me)
        if t < last:

            @pl.when(me == 0)
            def _():
                if t:
                    self.upward(t - 1, True).wait_send()
                self.upward(t, True).start()

            @pl.when(me == last)
            def _():
                if t:
                    self.downward(t - 1, True).wait_send()
                self.downward(t, True).start()

        if t:

            @pl.when((me > 0) & (rise >= 0))
            def _():
                self.upward(rise, False).wait_recv()
                if t < last:
                    add_into(self.rising.at[rise], self.terms.at[last - rise])
                    self.upward(rise, False).start()

            @pl.when((me < last) & (fall >= 0))
            def _():
                self.downward(fall, False).wait_recv()
                if t < last:
                    add_into(self.falling.at[fall], self.terms.at[fall])
                    self.downward(fall, False).start()

    def finish(self):
        me, last = self.me, self.C - 1

        @pl.when(me == 0)
        def _():
            self.upward(last - 1, True).wait_send()

        @pl.when(me == last)
        def _():
            self.downward(last - 1, True).wait_send()

        for m in range(last):

            @pl.when((me > 0) & (m < last - me))
            def _():
                self.upward(m, False).wait_send()

            @pl.when((me < last) & (m < me))
            def _():
                self.downward(m, False).wait_send()


def line_semaphores(C):
    return [DMA((C,)) for _ in range(4)]


def greet_line(C, others):
    me, last = lax.axis_index("col"), C - 1
    above, below = {"col": me + 1}, {"col": me - 1}

    @pl.when(me == 0)
    def _():
        greet([above] + others, 1 + len(others))

    @pl.when(me == last)
    def _():
        greet([below] + others, 1 + len(others))

    @pl.when((me > 0) & (me < last))
    def _():
        greet([above, below] + others, 2 + len(others))


def feed_kernel(
    R, C, os_hbm, w_hbm, xs_hbm, wg_hbm, wu_hbm, wd_hbm, dy_hbm,
    h_hbm, b_hbm, dg_hbm, du_hbm, dys_hbm, down_hbm, y_ref, grad_ref,
    big, hidden, slope, silu, b, gates, ups, terms, rising, falling, dys, h, exchanged, arrived,
    load, block_load, tile_load, store, h_load, w_send, w_recv, f_send, f_recv, *semaphores,
):
    me = lax.axis_index("col")
    row, ahead, behind, other = row_places(R)
    parts, heads, T = os_hbm.shape[0], os_hbm.shape[1], os_hbm.shape[2]
    D, F = wg_hbm.shape
    width, depth = D // C, D // R
    size, tiles, group = 256, 8, R // C
    bf = F // tiles
    up, down = semaphores[:2], semaphores[2:4]
    gather = LineGather(C, dy_hbm, dys, up, down)
    sums = LineSum(C, terms, rising, falling, semaphores[4:6], semaphores[6:8])
    place = row_of(R)
    row_sums = RowSum(
        R, lambda i: big.at[place(i), :, pl.ds(0, F)], lambda i: big.at[place(i, True), :, pl.ds(0, F)],
        exchanged, arrived, semaphores[8:],
    )

    def began(source, target, semaphore):
        copy = pltpu.make_async_copy(source, target, semaphore)
        copy.start()
        return copy

    def block_in(i):
        rows = pl.ds(i * size, size)
        copies = [
            pltpu.make_async_copy(
                os_hbm.at[j, n, rows, :], hidden.at[rows, pl.ds((j * heads + n) * HEAD_DIM, HEAD_DIM)], block_load.at[i, j * heads + n]
            )
            for j in range(parts)
            for n in range(heads)
        ]
        return copies + [
            pltpu.make_async_copy(
                xs_hbm.at[j, rows, :], slope.at[rows, pl.ds(j * width, width)], block_load.at[i, parts * heads + j]
            )
            for j in range(C)
        ]

    def tile_in(i):
        cut = pl.ds(i * bf, bf)
        return [
            pltpu.make_async_copy(wg_hbm.at[:, cut], gates.at[i % 2], tile_load.at[0, i % 2]),
            pltpu.make_async_copy(wu_hbm.at[:, cut], ups.at[i % 2], tile_load.at[1, i % 2]),
        ]

    blocks = [block_in(i) for i in range(T // size)]
    for copy in blocks[0]:
        copy.start()
    out_w = [
        began(w_hbm.at[:, j], big.at[:, :, pl.ds(j * width, width)], load.at[j]) for j in range(C)
    ]
    dy_mine = began(dy_hbm, dys.at[me], load.at[R])
    down_mine = began(wd_hbm, down_hbm.at[row], load.at[R + 1])
    for copies in blocks[1:] + [tile_in(0), tile_in(1)]:
        for copy in copies:
            copy.start()
    greet_line(C, [{"row": other}] + [{"row": ahead[k]} for k in range(1, R // 2)])
    gather.event(0)
    spread = [
        remote(wd_hbm, down_hbm.at[row], w_send.at[k], w_recv.at[k], row=ahead[k]) for k in range(1, R // 2)
    ]
    forward = [remote(wd_hbm, down_hbm.at[row], f_send.at[0], f_recv.at[0], row=other)]
    for copy in spread + forward:
        copy.start()

    stores = []
    mine = pl.ds(pl.multiple_of(me * width, width), width)
    for copy in out_w:
        copy.wait()
    for i in range(T // size):
        rows = pl.ds(i * size, size)
        for copy in blocks[i]:
            copy.wait()
        if i:
            stores[-1].wait()
        left = hidden[rows, :D]
        for j in range(C):
            columns = slice(j * width, (j + 1) * width)
            right = big[j * group : (j + 1) * group, :, :D].reshape(width, D)
            h[:, columns] = slope[rows, columns].astype(F32) + dot_nt(left, right)
        values = h[...]
        centre, inverse = norm_rows(values)
        b[rows, :] = ((values - centre) * inverse).astype(BF)
        stores.append(began(h, h_hbm.at[rows, :], store.at[0]))
    stores[-1].wait()
    b_out = began(b, b_hbm, store.at[1])
    h_back = [
        began(h_hbm.at[pl.ds(i * size, size), mine], h.at[:, pl.ds(i * width, width)], h_load.at[i])
        for i in range(T // size)
    ]
    for i in range(tiles):
        cut = slice(i * bf, (i + 1) * bf)
        for copy in tile_in(i):
            copy.wait()
        values = b[...]
        gate = dot_nn(values, gates[i % 2])
        upward = dot_nn(values, ups[i % 2])
        sigmoid = jax.nn.sigmoid(gate)
        silued = gate * sigmoid
        hidden[:, cut] = (silued * upward).astype(BF)
        slope[:, cut] = (upward * sigmoid * (1.0 + gate * (1.0 - sigmoid))).astype(BF)
        silu[:, cut] = silued.astype(BF)
        if i + 2 < tiles:
            for copy in tile_in(i + 2):
                copy.start()
        if i == 3:
            gather.event(1)
    for k in range(1, R // 2):
        spread[k - 1].wait_recv()
        block = down_hbm.at[behind[k]]
        copy = remote(block, block, f_send.at[k], f_recv.at[k], row=other)
        copy.start()
        forward.append(copy)
    for step in range(2, max(3, C - 1)):
        if step < C:
            gather.event(step)
    for copy in forward:
        copy.wait_recv()
    down_mine.wait()
    began(down_hbm, big.at[:, :, pl.ds(0, F)], load.at[0]).wait()
    half = lax.div(me, C // 2)

    def out_tile(k):
        j = (C - 1 - k) * (1 - half) + k * half
        right = big[pl.ds(j * group, group), :, :F].reshape(width, F)
        terms[j] = dot_nt(hidden[:, :F], right).astype(BF)

    out_tile(0)
    sums.level(0)
    for k in range(1, C):
        out_tile(k)
    for step in range(max(3, C - 1), C):
        gather.event(step)
    dy_mine.wait()
    b_out.wait()
    joined = [began(dys.at[j], b.at[:, pl.ds(j * width, width)], load.at[j]) for j in range(C)]
    saved = [began(dys, dys_hbm, store.at[1])]
    for copy in joined:
        copy.wait()
    sums.level(1)
    for i in range(tiles):
        cut = slice(i * bf, (i + 1) * bf)
        grad_hidden = dot_nn(b[...], big[:, :, cut].reshape(D, bf))
        slope[:, cut] = (grad_hidden * slope[:, cut].astype(F32)).astype(BF)
        silu[:, cut] = (grad_hidden * silu[:, cut].astype(F32)).astype(BF)
    saved.append(began(slope.at[:, pl.ds(0, F)], dg_hbm, store.at[2]))
    saved.append(began(silu.at[:, pl.ds(0, F)], du_hbm, store.at[3]))

    for slot in row_sums.order():
        chip = lax.div(place(slot), 2)
        product = dot_tn(dys[chip], hidden[:, :F]).astype(BF)
        for n in range(2):
            big[2 * chip + n, :, :F] = product[n * depth : (n + 1) * depth]
        row_sums.exchange(slot).start()
    row_sums.relay()
    for t in range(2, C - 1):
        sums.level(t)
    row_sums.relay_again()
    sums.level(C - 1)
    last = C - 1
    for copy in h_back:
        copy.wait()

    def result(more):
        for i in range(T // size):
            rows = pl.ds(i * size, size)
            total = h[:, i * width : (i + 1) * width] + terms[me, rows, :].astype(F32)
            for buffer, slot in more:
                total += buffer[slot, rows, :].astype(F32)
            y_ref[rows, :] = total.astype(BF)

    @pl.when(me == 0)
    def _():
        result([(falling, 0)])

    @pl.when(me == last)
    def _():
        result([(rising, 0)])

    @pl.when((me > 0) & (me < last))
    def _():
        result([(rising, last - me), (falling, me)])

    def write(part, values):
        grad_ref[:, part] = values.T

    row_sums.finish(write, 128)
    sums.finish()
    gather.finish()
    for copy in spread + forward:
        copy.wait_send()
    for copy in saved:
        copy.wait()


def feed_forward(R, C, os, w_out, xs, w_gate, w_up, w_down, cotangent):
    heads, T = os.shape[1], os.shape[2]
    width = xs.shape[2]
    D, F = w_gate.shape
    most = max(D, F)
    flat = pltpu.VMEM((T, most), BF)
    return pl.pallas_call(
        functools.partial(feed_kernel, R, C),
        in_specs=[ANY] * 7,
        out_specs=[ANY] * 6 + [VMEM_SPEC] * 2,
        out_shape=[
            struct((T, D), F32),
            struct((T, D), BF),
            struct((T, F), BF),
            struct((T, F), BF),
            struct((C, T, width), BF),
            struct((R, D // R, F), BF),
            struct((T, width), BF),
            struct((F, D // R), F32),
        ],
        scratch_shapes=[
            pltpu.VMEM((R, D // R, most), BF),
            flat,
            flat,
            pltpu.VMEM((T, F), BF),
            pltpu.VMEM((T, D), BF),
            pltpu.VMEM((2, D, F // 8), BF),
            pltpu.VMEM((2, D, F // 8), BF),
            pltpu.VMEM((C, T, width), BF),
            pltpu.VMEM((C - 1, T, width), BF),
            pltpu.VMEM((C - 1, T, width), BF),
            pltpu.VMEM((C, T, width), BF),
            pltpu.VMEM((256, D), F32),
        ]
        + row_sum_buffers(R, D // R, F)
        + [
            DMA((R + 2,)),
            DMA((T // 256, C * heads + C)),
            DMA((2, 2)),
            DMA((4,)),
            DMA((T // 256,)),
            DMA((R // 2,)),
            DMA((R // 2,)),
            DMA((R // 2,)),
            DMA((R // 2,)),
        ]
        + line_semaphores(C)
        + line_semaphores(C)
        + row_sum_semaphores(R),
        compiler_params=comm_params(2, 63),
        cost_estimate=cost(1.2e11, 90 * MIB),
        name="feed_forward",
    )(os, w_out, xs, w_gate, w_up, w_down, cotangent)


def norm_terms_kernel(
    R, C, dg_hbm, du_hbm, wg_hbm, wu_hbm, b_hbm,
    sum_ref, up_hbm, gate_ref,
    dg, du, wg, wu, b, terms, held, stage, exchanged, arrived,
    load, tile_load, store, send, recv, *semaphores,
):
    me, right, left = ring_places(C)
    D, F = wg.shape
    T = dg.shape[0]
    rows = T // C
    width = D // C

    def fetch(source, target, semaphore):
        copy = pltpu.make_async_copy(source, target, semaphore)
        copy.start()
        return copy

    def chunk(s):
        return pl.ds(pl.multiple_of(lax.rem(me + 2 * C - 1 - s, C) * rows, rows), rows)

    grads_in = []
    for s in range(C):
        part = chunk(s)
        grads_in.append(
            (fetch(dg_hbm.at[part, :], dg.at[part, :], load.at[2 * s]), fetch(du_hbm.at[part, :], du.at[part, :], load.at[2 * s + 1]))
        )
        if s == 0:
            weights_in = []
            for n in range(C):
                cut = pl.ds(n * width, width)
                weights_in.append(
                    (fetch(wg_hbm.at[cut, :], wg.at[cut, :], tile_load.at[2 * n]), fetch(wu_hbm.at[cut, :], wu.at[cut, :], tile_load.at[2 * n + 1]))
                )
    b_in = fetch(b_hbm, b, load.at[2 * C])
    place, depth = row_of(R), D // R

    def block(places):
        return wu.at[pl.ds(pl.multiple_of(places * depth, depth), depth), :]

    sums = RowSum(R, lambda i: block(place(i)), lambda i: block(place(i, True)), exchanged, arrived, semaphores)
    greet([{"col": left}] + sums.peers, 1 + len(sums.peers))

    def term_tile(s, part, n):
        cut = pl.ds(pl.multiple_of(n * width, width), width)
        total = dot_nt(dg[part, :], wg[cut, :]) + dot_nt(du[part, :], wu[cut, :])
        terms[s, :, cut] = total.astype(BF)

    def moves(step):
        return ring_step(step, C, right, terms.at[0], held, send, recv)

    def pass_on(step):
        moves(step - 1).wait_recv()
        add_into(held.at[step - 1], terms.at[step])
        moves(step).start()

    for s in range(C):
        part = chunk(s)
        for copy in grads_in[s]:
            copy.wait()
        if s == 0:
            for n in range(C):
                for copy in weights_in[n]:
                    copy.wait()
                term_tile(s, part, n)
            moves(0).start()
        else:

            def body(n, carry):
                term_tile(s, part, n)
                return carry

            lax.fori_loop(0, C, body, 0)
    b_in.wait()

    def stored(target, t, slot):
        cut = pl.ds(pl.multiple_of(t * width, width), width)
        return pltpu.make_async_copy(stage.at[slot], target.at[cut, :], store.at[slot])

    def product(right_ref, target):
        def body(t, carry):
            slot = lax.rem(t, 2)

            @pl.when(t >= 2)
            def _():
                stored(target, t, slot).wait()

            left_tile = b[:, pl.ds(pl.multiple_of(t * width, width), width)]
            stage[slot] = dot_tn(left_tile, right_ref[...]).astype(BF)
            stored(target, t, slot).start()
            return carry

        lax.fori_loop(0, C, body, 0)
        for slot in range(2):
            stored(target, slot, slot).wait()

    middle = max(1, (C - 1) // 2)
    for step in range(1, middle + 1):
        if step < C - 1:
            pass_on(step)
    for slot in sums.order():
        cut = pl.ds(pl.multiple_of(lax.div(place(slot), 2) * 2 * depth, 2 * depth), 2 * depth)
        wu[cut, :] = dot_tn(b[:, cut], dg[...]).astype(BF)
        sums.exchange(slot).start()
    sums.relay()
    product(du, up_hbm)
    for step in range(middle + 1, C - 1):
        pass_on(step)
    sums.relay_again()

    def write(part, values):
        gate_ref[part, :] = values

    sums.finish(write)
    moves(C - 2).wait_recv()
    sum_ref[...] = held[C - 2].astype(F32) + terms[C - 1].astype(F32)
    for step in range(C - 1):
        moves(step).wait_send()


def norm_terms(R, C, dg, du, w_gate, w_up, b):
    T, F = dg.shape
    D = w_gate.shape[0]
    rows, width = T // C, D // C
    return pl.pallas_call(
        functools.partial(norm_terms_kernel, R, C),
        in_specs=[ANY] * 5,
        out_specs=[VMEM_SPEC, ANY, VMEM_SPEC],
        out_shape=[struct((rows, D), F32), struct((D, F), BF), struct((D // R, F), F32)],
        scratch_shapes=[
            pltpu.VMEM((T, F), BF),
            pltpu.VMEM((T, F), BF),
            pltpu.VMEM((D, F), BF),
            pltpu.VMEM((D, F), BF),
            pltpu.VMEM((T, D), BF),
            pltpu.VMEM((C, rows, D), BF),
            pltpu.VMEM((C - 1, rows, D), BF),
            pltpu.VMEM((2, width, F), BF),
        ]
        + row_sum_buffers(R, D // R, F)
        + [
            DMA((2 * C + 1,)),
            DMA((2 * C,)),
            DMA((2,)),
            DMA((C - 1,)),
            DMA((C - 1,)),
        ]
        + row_sum_semaphores(R),
        compiler_params=comm_params(3, 63),
        cost_estimate=cost(9e10, 70 * MIB),
        name="norm_terms",
    )(dg, du, w_gate, w_up, b)


def attend_back_kernel(
    R, C, sum_ref, log_ref, segk_ref, segq_ref, cos_ref, sin_ref,
    q_hbm, k_hbm, v_hbm, h_hbm, dys_hbm, w_hbm, gate_hbm,
    dq_ref, dk_ref, dv_ref, gate_ref, dhs_hbm,
    h, dy, w, dh, out, q_ref, k_ref, v_ref, do_ref, dk_sum, dv_sum, own, exchanged, arrived,
    load, w_load, local, h_send, h_recv, o_send, o_recv, own_load, *semaphores,
):
    me, right, left = ring_places(C)
    rows, D = sum_ref.shape
    T, width = q_ref.shape
    heads, bq = width // HEAD_DIM, 256
    mine = pl.ds(pl.multiple_of(me * rows, rows), rows)
    first_in = [
        pltpu.make_async_copy(h_hbm.at[mine, :], h, load.at[0]),
        pltpu.make_async_copy(dys_hbm.at[:, mine, :], dy, load.at[1]),
    ]
    head_loads = [
        pltpu.make_async_copy(source, target, load.at[2 + i])
        for i, (source, target) in enumerate(((q_hbm, q_ref), (k_hbm, k_ref), (v_hbm, v_ref)))
    ]
    for copy in first_in:
        copy.start()
    order = [lax.rem(me + k, C) for k in range(1, C)] + [me]
    cuts = [pl.ds(pl.multiple_of(place * width, width), width) for place in order]
    loads = [pltpu.make_async_copy(w_hbm.at[:, order[k]], w.at[k], w_load.at[k]) for k in range(C)]
    sums, own_loads = held_row_sum(R, gate_hbm, own, exchanged, arrived, own_load, semaphores)
    for copy in loads + own_loads + head_loads:
        copy.start()
    greet([{"col": lax.rem(me + k, C)} for k in range(1, C)] + sums.peers, C - 1 + len(sums.peers))
    for slot in sums.order():
        sums.exchange(slot).start()
    for copy in first_in:
        copy.wait()
    grad = sum_ref[...]
    centre, inverse = norm_rows(h[...])
    normed = (h[...] - centre) * inverse
    first = jnp.mean(grad, axis=1, keepdims=True)
    second = jnp.mean(grad * normed, axis=1, keepdims=True)
    dh[...] = (beside(dy).astype(F32) + inverse * (grad - first - normed * second)).astype(BF)
    do_copies, dh_copies = [], []
    for k in range(C):
        loads[k].wait()
        out[k] = dot_nn(dh[...], w[k].reshape(D, width)).astype(BF)
        if k < C - 1:
            copy = remote(out.at[k], do_ref.at[mine, :], o_send.at[k], o_recv.at[k], col=order[k])
        else:
            copy = pltpu.make_async_copy(out.at[k], do_ref.at[mine, :], local.at[0])
        copy.start()
        do_copies.append(copy)
    sums.relay(lambda slot: own_loads[slot].wait())
    for copy in do_copies[:-1]:
        copy.wait_recv()
    do_copies[-1].wait()
    for k in range(C):
        if k < C - 1:
            copy = remote(dh.at[:, cuts[k]], dhs_hbm.at[mine, :], h_send.at[k], h_recv.at[k], col=order[k])
        else:
            copy = pltpu.make_async_copy(dh.at[:, cuts[k]], dhs_hbm.at[mine, :], local.at[1])
        copy.start()
        dh_copies.append(copy)
    for copy in head_loads:
        copy.wait()

    def one_head(head, carry):
        columns = pl.ds(pl.multiple_of(head * HEAD_DIM, HEAD_DIM), HEAD_DIM)
        dk_sum[...] = jnp.zeros_like(dk_sum)
        dv_sum[...] = jnp.zeros_like(dv_sum)
        for first in range(0, T, SEQ):
            for start in range(first, first + SEQ, bq):
                stop = start + bq
                keys = k_ref[first:stop, columns]
                queries = q_ref[start:stop, columns]
                grads = do_ref[start:stop, columns]
                scores = dot_nt(keys, queries) * SCALE
                allowed = allowed_block(segk_ref[first:stop], segq_ref[:, start:stop], start - first)
                scores = jnp.where(allowed, scores, MASKED)
                probs = jnp.exp(scores - log_ref[head, :, start:stop])
                dv_sum[first:stop] += dot_nn(probs.astype(BF), grads)
                grad_probs = dot_nt(v_ref[first:stop, columns], grads)
                inner = jnp.sum(probs * grad_probs, axis=0, keepdims=True)
                grad_scores = (probs * (grad_probs - inner)).astype(BF)
                dk_sum[first:stop] += dot_nn(grad_scores, queries)
                grad_query = dot_tn(keys, grad_scores).T * SCALE
                dq_ref[start:stop, columns] = turn(grad_query, cos_ref[start:stop], -sin_ref[start:stop]).astype(BF)
        dk_ref[:, columns] = turn(dk_sum[...] * SCALE, cos_ref[...], -sin_ref[...]).astype(BF)
        dv_ref[:, columns] = dv_sum[...].astype(BF)
        return carry

    lax.fori_loop(0, heads // 2, one_head, 0)
    sums.relay_again()
    lax.fori_loop(heads // 2, heads, one_head, 0)

    def write(part, values):
        gate_ref[part, :] = values

    sums.finish(write)
    for copy in do_copies[:-1]:
        copy.wait_send()
    for copy in dh_copies:
        copy.wait()


def attend_back(R, total, log_total, seg_column, seg_row, cos_table, sin_table, q, k, v, h, dys, w_out, grad_gate):
    C, T, width = dys.shape
    rows, D = total.shape
    depth, columns = grad_gate.shape[1:]
    one = pltpu.VMEM((T, width), BF)
    return pl.pallas_call(
        functools.partial(attend_back_kernel, R, C),
        in_specs=[VMEM_SPEC] * 6 + [ANY] * 7,
        out_specs=[VMEM_SPEC] * 4 + [ANY],
        out_shape=[struct((T, width), BF)] * 3 + [struct((depth, columns), F32), struct((T, width), BF)],
        scratch_shapes=[
            pltpu.VMEM((rows, D), F32),
            pltpu.VMEM((C, rows, width), BF),
            pltpu.VMEM((C, R, D // R, width), BF),
            pltpu.VMEM((rows, D), BF),
            pltpu.VMEM((C, rows, width), BF),
            one,
            one,
            one,
            one,
            pltpu.VMEM((T, HEAD_DIM), F32),
            pltpu.VMEM((T, HEAD_DIM), F32),
            pltpu.VMEM((R // 2, depth, columns), BF),
        ]
        + row_sum_buffers(R, depth, columns)
        + [
            DMA((5,)),
            DMA((C,)),
            DMA((2,)),
            DMA((C - 1,)),
            DMA((C - 1,)),
            DMA((C - 1,)),
            DMA((C - 1,)),
            DMA((R // 2,)),
        ]
        + row_sum_semaphores(R),
        compiler_params=comm_params(5),
        cost_estimate=cost(5e10, 30 * MIB),
        name="attend_back",
    )(total, log_total, seg_column, seg_row, cos_table, sin_table, q, k, v, h, dys, w_out, grad_gate)


def input_terms_kernel(
    R, C, dq_ref, dk_ref, dv_ref, mu_hbm, r_hbm, w_hbm, a_hbm, x_hbm, dh_hbm, os_hbm,
    y_ref, gq_ref, gk_ref, gv_ref, out_ref,
    mu_ref, r_ref, w_ref, a_ref, x_ref, dh_ref, block, product, mine, by_column, by_row,
    terms, held, stats, stats_in, tiles, q_exchanged, q_arrived, o_tiles, o_exchanged, o_arrived,
    send, recv, s_send, s_recv, w_load, late_load, block_load, c_send, c_recv, r_send, r_recv, local, *semaphores,
):
    me, right, left = ring_places(C)
    T, width = dq_ref.shape
    D = width * C
    heads = (dq_ref, dk_ref, dv_ref)
    row = lax.axis_index("row")
    thin = width // R

    def cut_of(s):
        return pl.ds(pl.multiple_of(lax.rem(me + 2 * C - 1 - s, C) * width, width), width)

    def weight_in(s):
        return pltpu.make_async_copy(w_hbm.at[:, cut_of(s), :], w_ref.at[:, cut_of(s), :], w_load.at[s])

    for s in range(C):
        weight_in(s).start()
    late = [
        pltpu.make_async_copy(source, target, late_load.at[i])
        for i, (source, target) in enumerate(
            ((a_hbm, a_ref), (x_hbm, x_ref), (dh_hbm, dh_ref), (mu_hbm, mu_ref), (r_hbm, r_ref))
        )
    ]
    for copy in late:
        copy.start()
    depth = tiles.shape[2]
    side = lax.rem(lax.axis_index("row"), 2)
    q_sums = RowSum(
        R, lambda i: tiles.at[i, side], lambda i: tiles.at[i, 1 - side], q_exchanged, q_arrived, semaphores[:4]
    )
    o_sums = RowSum(
        R, lambda i: o_tiles.at[i, side], lambda i: o_tiles.at[i, 1 - side], o_exchanged, o_arrived, semaphores[4:]
    )

    def block_in(i):
        return [
            pltpu.make_async_copy(
                os_hbm.at[i, n], block.at[i % 2, :, pl.ds(n * HEAD_DIM, HEAD_DIM)], block_load.at[i % 2, n]
            )
            for n in range(os_hbm.shape[1])
        ]

    for copy in block_in(0) + block_in(1):
        copy.start()
    greet(
        [{"col": lax.rem(me + k, C)} for k in range(1, C)] + [{"row": lax.rem(row + k, R)} for k in range(1, R)],
        C + R - 2,
    )

    def moves(step):
        return ring_step(step, C, right, terms.at[0], held, send, recv)

    def pass_on(step):
        moves(step - 1).wait_recv()
        add_into(held.at[step - 1], terms.at[step])
        moves(step).start()

    def compute(s):
        cut = cut_of(s)
        weight_in(s).wait()
        total = dot_nt(dq_ref[...], w_ref[0, cut, :])
        total += dot_nt(dk_ref[...], w_ref[1, cut, :])
        total += dot_nt(dv_ref[...], w_ref[2, cut, :])
        terms[s] = total.astype(BF)

    compute(0)
    moves(0).start()

    def body(s, carry):
        compute(s)
        return carry

    late[2].wait()
    for j in range(C):
        for copy in block_in(j):
            copy.wait()
        product[...] = dot_tn(block[j % 2], dh_ref[...]).astype(BF)
        for slot in range(R // 2):
            for place in range(2):
                rows = 2 * lax.div(o_sums.places(slot), 2) + place
                o_tiles[slot, place, j * thin : (j + 1) * thin] = product[pl.ds(pl.multiple_of(rows * thin, thin), thin), :]
        if j + 2 < C:
            for copy in block_in(j + 2):
                copy.start()
    for slot in o_sums.order():
        o_sums.exchange(slot).start()
    o_sums.relay()
    lax.fori_loop(1, C, body, 0)
    for i, copy in enumerate(late):
        if i != 2:
            copy.wait()
    for slot in q_sums.order():
        start = pl.multiple_of(lax.div(q_sums.places(slot), 2) * 2 * depth, 2 * depth)
        left_tile = a_ref[:, pl.ds(start, 2 * depth)]
        for i, right_side in enumerate(heads):
            product = dot_tn(left_tile, right_side[...]).astype(BF)
            tiles[slot, 0, :, i * width : (i + 1) * width] = product[:depth]
            tiles[slot, 1, :, i * width : (i + 1) * width] = product[depth:]
        q_sums.exchange(slot).start()
    o_sums.relay_again()
    pass_on(1)
    q_sums.relay()

    def write_out(part, values):
        mine[part, :] = values.astype(BF)

    o_sums.finish(write_out)
    columns_out = []
    for k in range(1, C):
        place = lax.rem(me + k, C)
        rows = pl.ds(pl.multiple_of(place * thin, thin), thin)
        columns_out.append(remote(mine.at[rows, :], by_column.at[me], c_send.at[k - 1], c_recv.at[k - 1], col=place))
    stay = pltpu.make_async_copy(
        mine.at[pl.ds(pl.multiple_of(me * thin, thin), thin), :], by_column.at[me], local.at[0]
    )
    for copy in columns_out + [stay]:
        copy.start()
    size = 128

    def sum_rows(i, carry):
        rows = pl.ds(pl.multiple_of(i * size, size), size)
        lane = lax.broadcasted_iota(jnp.int32, (size, 128), 1)
        total = jnp.zeros((size, 1), F32)
        second = jnp.zeros((size, 1), F32)
        for s in range(C):
            grad = terms[s, rows, :].astype(F32)
            total += jnp.sum(grad, axis=1, keepdims=True)
            second += jnp.sum(grad * a_ref[rows, cut_of(s)].astype(F32), axis=1, keepdims=True)
        packed = jnp.where(lane == 0, total, jnp.where(lane == 1, second, 0.0))
        stats[:, rows] = packed.T[:8]
        return carry

    lax.fori_loop(0, T // size, sum_rows, 0)
    exchanges = [
        remote(stats, stats_in.at[k - 1], s_send.at[k - 1], s_recv.at[k - 1], col=lax.rem(me + k, C)) for k in range(1, C)
    ]
    for copy in exchanges:
        copy.start()
    for copy in columns_out:
        copy.wait_recv()
    stay.wait()

    def piece_of(place):
        return by_column.at[lax.div(place * C, R), :, pl.ds(pl.multiple_of(lax.rem(place, R // C) * depth, depth), depth)]

    rows_out = []
    for k in range(1, R):
        place = lax.rem(row + k, R)
        rows_out.append(remote(piece_of(place), by_row.at[row], r_send.at[k - 1], r_recv.at[k - 1], row=place))
    keep = pltpu.make_async_copy(piece_of(row), by_row.at[row], local.at[1])
    for copy in rows_out + [keep]:
        copy.start()
    for step in range(2, C - 1):
        pass_on(step)
    q_sums.relay_again()
    for copy in rows_out:
        copy.wait_recv()
    keep.wait()
    for n in range(R):
        out_ref[n * thin : (n + 1) * thin, :] = by_row[n].astype(F32)

    def write_qkv(part, values):
        for i, target in enumerate((gq_ref, gk_ref, gv_ref)):
            target[part, :] = values[:, i * width : (i + 1) * width]

    q_sums.finish(write_qkv)
    for copy in exchanges:
        copy.wait_recv()
    moves(C - 2).wait_recv()

    def last_rows(i, carry):
        rows = pl.ds(pl.multiple_of(i * size, size), size)
        both = stats[:, rows]
        for k in range(C - 1):
            both += stats_in[k, :, rows]
        columns = jnp.concatenate([both, jnp.zeros((120, size), F32)], axis=0).T * (1.0 / D)
        normed = (x_ref[rows, :].astype(F32) - mu_ref[rows, :]) * r_ref[rows, :]
        grad = held[C - 2, rows, :].astype(F32) + terms[C - 1, rows, :].astype(F32)
        grad = grad - columns[:, 0:1] - normed * columns[:, 1:2]
        y_ref[rows, :] = (dh_ref[rows, :].astype(F32) + r_ref[rows, :] * grad).astype(BF)
        return carry

    lax.fori_loop(0, T // size, last_rows, 0)
    for copy in exchanges + columns_out + rows_out:
        copy.wait_send()
    for step in range(C - 1):
        moves(step).wait_send()


def input_terms(R, C, dq, dk, dv, w_qkv, a, tokens, dh, mu, r, os):
    T, width = dq.shape
    D = w_qkv.shape[1]
    half, low = R // 2, D // R
    thin = width // R
    return pl.pallas_call(
        functools.partial(input_terms_kernel, R, C),
        in_specs=[VMEM_SPEC] * 3 + [ANY] * 7,
        out_specs=[VMEM_SPEC] * 5,
        out_shape=[struct((T, width), BF)]
        + [struct((low, width), F32)] * 3
        + [struct((width, low), F32)],
        scratch_shapes=[
            pltpu.VMEM((T, 1), F32),
            pltpu.VMEM((T, 1), F32),
            pltpu.VMEM((3, D, width), BF),
            pltpu.VMEM((T, D), BF),
            pltpu.VMEM((T, width), BF),
            pltpu.VMEM((T, width), BF),
            pltpu.VMEM((2, T, width), BF),
            pltpu.VMEM((width, width), BF),
            pltpu.VMEM((C * thin, width), BF),
            pltpu.VMEM((C, thin, width), BF),
            pltpu.VMEM((R, thin, low), BF),
            pltpu.VMEM((C, T, width), BF),
            pltpu.VMEM((C - 1, T, width), BF),
            pltpu.VMEM((8, T), F32),
            pltpu.VMEM((C - 1, 8, T), F32),
            pltpu.VMEM((half, 2, low, 3 * width), BF),
        ]
        + row_sum_buffers(R, low, 3 * width)
        + [pltpu.VMEM((half, 2, C * thin, width), BF)]
        + row_sum_buffers(R, C * thin, width)
        + [
            DMA((C - 1,)),
            DMA((C - 1,)),
            DMA((C - 1,)),
            DMA((C - 1,)),
            DMA((C,)),
            DMA((5,)),
            DMA((2, os.shape[1])),
            DMA((C - 1,)),
            DMA((C - 1,)),
            DMA((R - 1,)),
            DMA((R - 1,)),
            DMA((2,)),
        ]
        + row_sum_semaphores(R)
        + row_sum_semaphores(R),
        compiler_params=comm_params(6, 63),
        cost_estimate=cost(8e10, 20 * MIB),
        name="input_terms",
    )(dq, dk, dv, mu, r, w_qkv, a, tokens, dh, os)


def on_device(R, C, tokens, cotangent, segments, w_query, w_key, w_value, w_out, w_gate, w_up, w_down):
    T, width = tokens.shape
    D = width * C
    gathered = lambda w: lax.all_gather(w, "row", axis=0, tiled=True)

    gate_w, up_w = gathered(w_gate), gathered(w_up)
    seg_row = segments.reshape(1, T)
    xs, w_qkv, cos_table, sin_table, seg_column, out_part, down_part = first_gather(
        R, C, seg_row, tokens, w_query, w_key, w_value, w_out, w_down
    )
    w_qkv = w_qkv.reshape(3, D, width)
    act_one, q, k, v, mu_one, r_one, out_part = norm_and_project(xs, w_qkv, cos_table, sin_table, out_part)
    os, log_total, out_w = attend(R, C, q, k, v, seg_column, seg_row, out_part)
    h_full, act_two, dg, du, dys, _, output, grad_down = feed_forward(
        R, C, os, out_w, xs, gate_w, up_w, down_part, cotangent
    )
    total, grad_up, grad_gate = norm_terms(R, C, dg, du, gate_w, up_w, act_two)
    grad_up = grad_up.reshape(R, D // R, -1)
    dq, dk, dv, grad_up, dh = attend_back(
        R, total, log_total, seg_column, seg_row, cos_table, sin_table, q, k, v, h_full, dys, out_w, grad_up
    )
    grad_tokens, grad_query, grad_key, grad_value, grad_out = input_terms(
        R, C, dq, dk, dv, w_qkv, act_one, tokens, dh, mu_one, r_one, os
    )
    return (output, grad_tokens, grad_query, grad_key, grad_value, grad_out, grad_gate, grad_up, grad_down)


def solution(mesh):
    here = P("row", "col")
    turned = P("col", "row")
    return jax.shard_map(
        functools.partial(on_device, mesh.shape["row"], mesh.shape["col"]),
        mesh=mesh,
        in_specs=(here, here, P("row"), here, here, here, turned, here, here, turned),
        out_specs=(here, here, here, here, here, turned, here, here, turned),
        check_vma=False,
    )
```

```python
import functools

import jax
import jax.numpy as jnp
from jax import lax
from jax.experimental import pallas as pl
from jax.experimental.pallas import tpu as pltpu
from jax.sharding import PartitionSpec as P

HEAD_DIM = 128
HALF = HEAD_DIM // 2
SEQ = 1024
EPSILON = 1e-05
MASKED = -1e30
SCALE = HEAD_DIM ** (-0.5)
BF = jnp.bfloat16
F32 = jnp.float32
MIB = 1 << 20
ANY = pl.BlockSpec(memory_space=pl.ANY)


def dot_nn(left, right):
    return jnp.dot(left, right, preferred_element_type=F32)


def dot_tn(left, right):
    return lax.dot_general(left, right, (((0,), (0,)), ((), ())), preferred_element_type=F32)


def dot_nt(left, right):
    return lax.dot_general(left, right, (((1,), (1,)), ((), ())), preferred_element_type=F32)


def struct(shape, dtype):
    return jax.ShapeDtypeStruct(shape, dtype)


def params(mib=60):
    return pltpu.CompilerParams(vmem_limit_bytes=mib * MIB)


def cost(flops, moved):
    return pl.CostEstimate(flops=int(flops), bytes_accessed=int(moved), transcendentals=0)


def turn(values, cos_table, sin_table):
    return values * cos_table + pltpu.roll(values, HALF, 1) * sin_table


MESH = pl.DeviceIdType.MESH
VMEM_SPEC = pl.BlockSpec(memory_space=pltpu.VMEM)
DMA = pltpu.SemaphoreType.DMA


def comm_params(number, mib=60):
    return pltpu.CompilerParams(vmem_limit_bytes=mib * MIB, collective_id=number, has_side_effects=True)


def remote(source, target, send, recv, **device):
    return pltpu.make_async_remote_copy(
        src_ref=source, dst_ref=target, send_sem=send, recv_sem=recv, device_id=device, device_id_type=MESH
    )


def greet(senders, targets):
    semaphore = pltpu.get_barrier_semaphore()
    for device in senders:
        pl.semaphore_signal(semaphore, inc=1, device_id=device, device_id_type=MESH)
    pl.semaphore_wait(semaphore, targets)


def ring_places(C):
    me = lax.axis_index("col")
    return me, lax.rem(me + 1, C), lax.rem(me + C - 1, C)


def row_places(R):
    row = lax.axis_index("row")
    ahead = [lax.rem(row + 2 * k, R) for k in range(R // 2)]
    behind = [lax.rem(row + R - 2 * k, R) for k in range(R // 2)]
    other = row + 1 - 2 * lax.rem(row, 2)
    return row, ahead, behind, other


class GatherRing:
    def __init__(self, C, source, whole, send, recv):
        me, right, left = ring_places(C)
        self.C = C
        size = source.shape[0] // 2
        self.copies = []
        for step in range(C - 1):
            owner = lax.rem(me - step + C, C)
            pair = []
            for half in range(2):
                rows = pl.ds(half * size, size)
                piece = source.at[rows, :] if step == 0 else whole.at[owner, rows, :]
                pair.append(
                    remote(piece, whole.at[owner, rows, :], send.at[step, half], recv.at[step, half], col=right)
                )
            self.copies.append(pair)

    def start(self):
        for copy in self.copies[0]:
            copy.start()

    def pass_on(self, step):
        for half in range(2):
            self.copies[step - 1][half].wait_recv()
            self.copies[step][half].start()

    def arrived(self):
        for copy in self.copies[-1]:
            copy.wait_recv()

    def sent(self):
        for pair in self.copies:
            for copy in pair:
                copy.wait_send()


def gather_kernel(
    R, C, segq_ref, rate_ref, wo_ref, wd_ref, x_ref, wq_ref, wk_ref, wv_ref,
    xs_ref, w_ref, cos_ref, sin_ref, segk_ref, wo_turned, wd_turned,
    local, x_send, x_recv, w_send, w_recv, f_send, f_recv,
):
    me, right, left = ring_places(C)
    row, ahead, behind, other = row_places(R)
    weights = (wq_ref, wk_ref, wv_ref)
    mine = [
        pltpu.make_async_copy(x_ref, xs_ref.at[me], local.at[0]),
    ] + [pltpu.make_async_copy(w, w_ref.at[i, row], local.at[1 + i]) for i, w in enumerate(weights)]
    for copy in mine:
        copy.start()
    greet(
        [{"col": left}, {"row": other}] + [{"row": r} for r in behind[1:]],
        1 + R // 2,
    )

    ring = GatherRing(C, x_ref, xs_ref, x_send, x_recv)
    ring.start()
    spread, forward = [], []
    for i, w in enumerate(weights):
        for k in range(1, R // 2):
            copy = remote(w, w_ref.at[i, row], w_send.at[i, k], w_recv.at[i, k], row=ahead[k])
            copy.start()
            spread.append(copy)
        copy = remote(w, w_ref.at[i, row], f_send.at[i, 0], f_recv.at[i, 0], row=other)
        copy.start()
        forward.append(copy)
    T = cos_ref.shape[0]
    size = 128

    def table_rows(i, carry):
        rows = pl.ds(pl.multiple_of(i * size, size), size)
        first = SEQ * lax.div(i * size, SEQ)
        here = jnp.broadcast_to(segq_ref[:, rows].astype(F32), (size, size)).T[:, :1]
        segk_ref[rows, :] = here.astype(jnp.int32)
        shape = (size, T)
        queries = lax.broadcasted_iota(jnp.int32, shape, 0) + i * size
        keys = lax.broadcasted_iota(jnp.int32, shape, 1)
        seen = (here == segq_ref[...].astype(F32)) & (keys <= queries) & (keys >= first)
        place = jnp.sum(jnp.where(seen, 1.0, 0.0), axis=1, keepdims=True) - 1.0
        angles = place * rate_ref[...]
        lane = lax.broadcasted_iota(jnp.int32, angles.shape, 1)
        sine = jnp.sin(angles)
        cos_ref[rows, :] = jnp.cos(angles)
        sin_ref[rows, :] = jnp.where(lane < HALF, -sine, sine)
        return carry

    lax.fori_loop(0, T // size, table_rows, 0)

    def turn_rows(source, target):
        def body(i, carry):
            cut = pl.ds(pl.multiple_of(i * size, size), size)
            target[:, cut] = source[cut, :].astype(F32).T.astype(BF)
            return carry

        lax.fori_loop(0, source.shape[0] // size, body, 0)

    turn_rows(wo_ref, wo_turned)
    turn_rows(wd_ref, wd_turned)
    for s in range(1, C - 1):
        ring.pass_on(s)
    for i in range(3):
        for k in range(1, R // 2):
            spread[i * (R // 2 - 1) + k - 1].wait_recv()
            block = w_ref.at[i, behind[k]]
            copy = remote(block, block, f_send.at[i, k], f_recv.at[i, k], row=other)
            copy.start()
            forward.append(copy)
    ring.arrived()
    for copy in forward:
        copy.wait_recv()
    ring.sent()
    for copy in spread + forward:
        copy.wait_send()
    for copy in mine:
        copy.wait()


def first_gather(R, C, seg_row, tokens, w_query, w_key, w_value, w_out, w_down):
    depth, width = w_query.shape
    T = tokens.shape[0]
    half = R // 2
    rate = 10000.0 ** (-(jnp.arange(HALF, dtype=F32) * 2.0 / HEAD_DIM))
    rate = jnp.concatenate([rate, rate]).reshape(1, HEAD_DIM)
    return pl.pallas_call(
        functools.partial(gather_kernel, R, C),
        in_specs=[VMEM_SPEC] * 4 + [ANY] * 4,
        out_specs=[ANY] * 2 + [VMEM_SPEC] * 5,
        out_shape=[
            struct((C,) + tokens.shape, BF),
            struct((3, R, depth, width), BF),
            struct((T, HEAD_DIM), F32),
            struct((T, HEAD_DIM), F32),
            struct((T, 1), jnp.int32),
            struct(w_out.shape[::-1], BF),
            struct(w_down.shape[::-1], BF),
        ],
        scratch_shapes=[
            DMA((4,)),
            DMA((C - 1, 2)),
            DMA((C - 1, 2)),
            DMA((3, half)),
            DMA((3, half)),
            DMA((3, half)),
            DMA((3, half)),
        ],
        compiler_params=comm_params(0),
        cost_estimate=cost(6e10, 14 * MIB),
        name="first_gather",
    )(seg_row, rate, w_out, w_down, tokens, w_query, w_key, w_value)


def norm_rows(x):
    centre = jnp.mean(x, axis=-1, keepdims=True)
    spread = jnp.mean(x * x, axis=-1, keepdims=True) - centre * centre
    inverse = lax.rsqrt(spread + EPSILON)
    return centre, inverse


def beside(ref):
    return jnp.concatenate([ref[j] for j in range(ref.shape[0])], axis=1)


def qkv_kernel(
    C, xs_ref, w_ref, cos_ref, sin_ref, wo_ref, a_ref, q_ref, k_ref, v_ref, mu_ref, r_ref, wos_ref, local, send, recv
):
    step, steps = pl.program_id(0), pl.num_programs(0)
    me, right, left = ring_places(C)
    ring = GatherRing(C, wo_ref, wos_ref, send, recv)
    mine = pltpu.make_async_copy(wo_ref, wos_ref.at[me], local.at[0])

    @pl.when(step == 0)
    def _():
        mine.start()
        greet([{"col": left}], 1)
        ring.start()

    @pl.when(step == steps // 2)
    def _():
        ring.pass_on(1)

    x = beside(xs_ref).astype(F32)
    centre, inverse = norm_rows(x)
    a = ((x - centre) * inverse).astype(BF)
    a_ref[...] = a
    mu_ref[...] = centre
    r_ref[...] = inverse
    cosine, sine = cos_ref[...], sin_ref[...]
    for index, out in enumerate((q_ref, k_ref, v_ref)):
        product = dot_nn(a, w_ref[index])
        if index == 2:
            out[...] = product.astype(BF)
            continue
        for start in range(0, out.shape[1], HEAD_DIM):
            part = product[:, start : start + HEAD_DIM]
            out[:, start : start + HEAD_DIM] = turn(part, cosine, sine).astype(BF)

    @pl.when(step == steps - 1)
    def _():
        for s in range(2, C - 1):
            ring.pass_on(s)
        ring.arrived()
        ring.sent()
        mine.wait()


def norm_and_project(xs, w_qkv, cos_table, sin_table, w_out):
    C, T, width = xs.shape
    D = width * C
    bt = 256
    rows = lambda n: pl.BlockSpec((bt, n), lambda i: (i, 0))
    return pl.pallas_call(
        functools.partial(qkv_kernel, C),
        grid=(T // bt,),
        in_specs=[
            pl.BlockSpec((C, bt, width), lambda i: (0, i, 0)),
            pl.BlockSpec(w_qkv.shape, lambda i: (0, 0, 0), pipeline_mode=pl.Buffered(1)),
            rows(HEAD_DIM),
            rows(HEAD_DIM),
            ANY,
        ],
        out_specs=[rows(D), rows(width), rows(width), rows(width), rows(1), rows(1), ANY],
        out_shape=[
            struct((T, D), BF),
            struct((T, width), BF),
            struct((T, width), BF),
            struct((T, width), BF),
            struct((T, 1), F32),
            struct((T, 1), F32),
            struct((C,) + w_out.shape, BF),
        ],
        scratch_shapes=[DMA((1,)), DMA((C - 1, 2)), DMA((C - 1, 2))],
        compiler_params=comm_params(7),
        cost_estimate=cost(2e10, 14 * MIB),
        name="norm_and_project",
    )(xs, w_qkv, cos_table, sin_table, w_out)


def allowed_block(seg_key, seg_query, first_query):
    shape = (seg_key.shape[0], seg_query.shape[1])
    keys = lax.broadcasted_iota(jnp.int32, shape, 0)
    queries = lax.broadcasted_iota(jnp.int32, shape, 1) + first_query
    return (seg_key == seg_query) & (keys <= queries)


def attend_kernel(
    R, C, q_ref, k_ref, v_ref, segk_ref, segq_ref, wos_ref, os_ref, log_ref, w_ref,
    o_buf, local, o_send, o_recv, w_send, w_recv, f_send, f_recv,
):
    me, right, left = ring_places(C)
    row, ahead, behind, other = row_places(R)
    T, width = q_ref.shape
    heads, bq = width // HEAD_DIM, 256
    greet([{"col": left}, {"row": other}] + [{"row": r} for r in behind[1:]], 1 + R // 2)
    mine = pltpu.make_async_copy(wos_ref, w_ref.at[row], local.at[0])
    mine.start()
    spread, forward = [], []
    for k in range(1, R // 2):
        copy = remote(wos_ref, w_ref.at[row], w_send.at[k], w_recv.at[k], row=ahead[k])
        copy.start()
        spread.append(copy)
    copy = remote(wos_ref, w_ref.at[row], f_send.at[0], f_recv.at[0], row=other)
    copy.start()
    forward.append(copy)

    def ring(step, head):
        owner = lax.rem(me - step + C, C)
        piece = o_buf.at[head] if step == 0 else os_ref.at[owner, head]
        return remote(piece, os_ref.at[owner, head], o_send.at[step, head], o_recv.at[step, head], col=right)

    def one_head(head, carry):
        columns = pl.ds(pl.multiple_of(head * HEAD_DIM, HEAD_DIM), HEAD_DIM)
        for first in range(0, T, SEQ):
            for start in range(first, first + SEQ, bq):
                stop = start + bq
                scores = dot_nt(k_ref[first:stop, columns], q_ref[start:stop, columns]) * SCALE
                allowed = allowed_block(segk_ref[first:stop], segq_ref[:, start:stop], start - first)
                scores = jnp.where(allowed, scores, MASKED)
                peak = jnp.max(scores, axis=0, keepdims=True)
                exponent = jnp.exp(scores - peak)
                total = jnp.sum(exponent, axis=0, keepdims=True)
                weights = (exponent * (1.0 / total)).astype(BF)
                o_buf[head, start:stop] = dot_tn(v_ref[first:stop, columns], weights).T.astype(BF)
                log_ref[head, :, start:stop] = peak + jnp.log(total)
        ring(0, head).start()
        pltpu.make_async_copy(o_buf.at[head], os_ref.at[me, head], local.at[1 + head]).start()
        return carry

    lax.fori_loop(0, heads, one_head, 0)
    for step in range(1, C - 1):
        for head in range(heads):
            ring(step - 1, head).wait_recv()
            ring(step, head).start()
    for k in range(1, R // 2):
        spread[k - 1].wait_recv()
        block = w_ref.at[behind[k]]
        copy = remote(block, block, f_send.at[k], f_recv.at[k], row=other)
        copy.start()
        forward.append(copy)
    for head in range(heads):
        ring(C - 2, head).wait_recv()
        pltpu.make_async_copy(o_buf.at[head], os_ref.at[me, head], local.at[1 + head]).wait()
        for step in range(C - 1):
            ring(step, head).wait_send()
    for copy in forward:
        copy.wait_recv()
    for copy in spread + forward:
        copy.wait_send()
    mine.wait()


def attend(R, C, q, k, v, seg_column, seg_row, w_part):
    T, width = q.shape
    heads, half = width // HEAD_DIM, R // 2
    return pl.pallas_call(
        functools.partial(attend_kernel, R, C),
        in_specs=[VMEM_SPEC] * 5 + [ANY],
        out_specs=[ANY, VMEM_SPEC, ANY],
        out_shape=[
            struct((C, heads, T, HEAD_DIM), BF),
            struct((heads, 1, T), F32),
            struct((R,) + w_part.shape, BF),
        ],
        scratch_shapes=[
            pltpu.VMEM((heads, T, HEAD_DIM), BF),
            DMA((1 + heads,)),
            DMA((C - 1, heads)),
            DMA((C - 1, heads)),
            DMA((half,)),
            DMA((half,)),
            DMA((half,)),
            DMA((half,)),
        ],
        compiler_params=comm_params(1),
        cost_estimate=cost(7e10, 14 * MIB),
        name="attend",
    )(q, k, v, seg_column, seg_row, w_part)


class SumRing:
    def __init__(self, C, terms, held, send, recv):
        me, right, left = ring_places(C)
        self.C, self.terms, self.held, self.send, self.recv, self.right = C, terms, held, send, recv, right
        self.size = held.shape[1] // 2

    def part(self, ref, slot, half):
        return ref.at[slot, pl.ds(half * self.size, self.size), :]

    def copy(self, step, half):
        source = self.part(self.terms, 0, half) if step == 0 else self.part(self.held, step - 1, half)
        return remote(
            source, self.part(self.held, step, half), self.send.at[step, half], self.recv.at[step, half], col=self.right
        )

    def start(self):
        for half in range(2):
            self.copy(0, half).start()

    def pass_on(self, step):
        for half in range(2):
            self.copy(step - 1, half).wait_recv()
            add_into(self.part(self.held, step - 1, half), self.part(self.terms, step, half))
            self.copy(step, half).start()

    def arrived(self):
        for half in range(2):
            self.copy(self.C - 2, half).wait_recv()

    def sent(self):
        for step in range(self.C - 1):
            for half in range(2):
                self.copy(step, half).wait_send()


def add_into(held, terms):
    size = 64

    def body(i, carry):
        rows = pl.ds(pl.multiple_of(i * size, size), size)
        held[rows, :] = (held[rows, :].astype(F32) + terms[rows, :].astype(F32)).astype(BF)
        return carry

    lax.fori_loop(0, held.shape[0] // size, body, 0)


class RowSum:
    def __init__(self, R, own, twin, exchanged, arrived, semaphores):
        self.P = R // 4
        self.own, self.twin, self.exchanged, self.arrived = own, twin, exchanged, arrived
        self.x_send, self.x_recv, self.y_send, self.y_recv = semaphores
        self.width = arrived.shape[2]
        self.places = row_of(R)
        self.peers = row_peers(R)

    def part(self, ref, side):
        return ref.at[:, pl.ds(side * self.width, self.width)]

    def exchange(self, slot):
        return remote(
            self.twin(slot), self.exchanged.at[slot], self.x_send.at[slot], self.x_recv.at[slot], row=self.places(0, True)
        )

    def send(self, slot, side, index, target):
        return remote(
            self.part(self.own(slot), side), self.arrived.at[index], self.y_send.at[index], self.y_recv.at[index],
            row=self.places(target),
        )

    def left_one(self, dp):
        return self.send(2 * dp + 1, 0, dp, 1)

    def left_two(self, dp):
        return self.send(2 * dp, 0, self.P + dp - 1, 2 * dp)

    def right_one(self, dp, dq):
        return self.send(2 * dp + dq, 1, 2 * self.P - 1 + 2 * (dp - 1) + dq, 2 * dp)

    def right_two(self):
        return self.send(1, 1, 4 * self.P - 3, 1)

    def order(self):
        return (
            [2 * dp + 1 for dp in range(1, self.P)] + [1] + [2 * dp for dp in range(1, self.P)] + [0]
        )

    def relay(self, before=None):
        for slot in self.order():
            if before is not None:
                before(slot)
            self.exchange(slot).wait_recv()
            add_into(self.own(slot), self.exchanged.at[slot])
            dp, dq = divmod(slot, 2)
            if dq:
                self.left_one(dp).start()
            if dp:
                self.right_one(dp, dq).start()

    def relay_again(self):
        for dp in range(1, self.P):
            self.left_one(dp).wait_recv()
            add_into(self.part(self.own(2 * dp), 0), self.arrived.at[dp])
            self.left_two(dp).start()
        for dp in range(1, self.P):
            copy = self.right_one(dp, 1)
            copy.wait_recv()
            add_into(self.part(self.own(1), 1), self.arrived.at[2 * self.P - 1 + 2 * (dp - 1) + 1])
        self.right_two().start()

    def finish(self, write, size=64):
        P, width = self.P, self.width
        self.left_one(0).wait_recv()
        self.right_two().wait_recv()
        for dp in range(1, P):
            self.left_two(dp).wait_recv()
            self.right_one(dp, 0).wait_recv()
        lefts = [0] + [P + dp - 1 for dp in range(1, P)]
        rights = [4 * P - 3] + [2 * P - 1 + 2 * (dp - 1) for dp in range(1, P)]

        def body(i, carry):
            rows = pl.ds(pl.multiple_of(i * size, size), size)
            total = self.own(0)[rows, :].astype(F32)
            halves = []
            for side, places in enumerate((lefts, rights)):
                half = total[:, side * width : (side + 1) * width]
                for index in places:
                    half += self.arrived[index, rows, :].astype(F32)
                halves.append(half)
            write(rows, jnp.concatenate(halves, axis=1))
            return carry

        lax.fori_loop(0, self.exchanged.shape[1] // size, body, 0)
        for slot in range(2 * P):
            self.exchange(slot).wait_send()
        self.left_one(0).wait_send()
        self.right_two().wait_send()
        for dp in range(1, P):
            self.left_one(dp).wait_send()
            self.left_two(dp).wait_send()
            self.right_one(dp, 0).wait_send()
            self.right_one(dp, 1).wait_send()


def row_of(R):
    row = lax.axis_index("row")
    side, chip = lax.rem(row, 2), lax.div(row, 2)
    p, q = lax.div(chip, 2), lax.rem(chip, 2)

    def place(slot, twin=False):
        dp, dq = divmod(slot, 2)
        chip_there = 2 * lax.rem(p + dp, R // 4) + lax.rem(q + dq, 2)
        return 2 * chip_there + (1 - side if twin else side)

    return place


def row_peers(R):
    place = row_of(R)
    return [{"row": place(0, True)}, {"row": place(1)}] + [{"row": place(2 * dp)} for dp in range(1, R // 4)]


def row_sum_semaphores(R):
    return [DMA((R // 2,)), DMA((R // 2,)), DMA((R - 2,)), DMA((R - 2,))]


def row_sum_buffers(R, depth, columns):
    return [
        pltpu.VMEM((R // 2, depth, columns), BF),
        pltpu.VMEM((R - 2, depth, columns // 2), BF),
    ]


def held_row_sum(R, grad_hbm, own, exchanged, arrived, load, semaphores):
    place = row_of(R)
    sums = RowSum(R, lambda i: own.at[i], lambda i: grad_hbm.at[place(i, True)], exchanged, arrived, semaphores)
    loads = [pltpu.make_async_copy(grad_hbm.at[place(i)], own.at[i], load.at[i]) for i in range(R // 2)]
    return sums, loads


class LineGather:
    def __init__(self, C, source, whole, up, down):
        self.C, self.source, self.whole, self.up, self.down = C, source, whole, up, down
        self.me = lax.axis_index("col")

    def upward(self, step):
        owner = self.me - step
        piece = self.source if step == 0 else self.whole.at[owner]
        return remote(piece, self.whole.at[owner], self.up[0].at[step], self.up[1].at[step], col=self.me + 1)

    def downward(self, step):
        owner = self.me + step
        piece = self.source if step == 0 else self.whole.at[owner]
        return remote(piece, self.whole.at[owner], self.down[0].at[step], self.down[1].at[step], col=self.me - 1)

    def arrival(self, step, rises):
        sender = self.me - 1 if rises else self.me + 1
        send, recv = self.up if rises else self.down
        target = self.whole.at[sender - step if rises else sender + step]
        return remote(target, target, send.at[step], recv.at[step], col=sender)

    def event(self, step):
        me, last = self.me, self.C - 1
        if step:

            @pl.when(me >= step)
            def _():
                self.arrival(step - 1, True).wait_recv()

            @pl.when(me + step <= last)
            def _():
                self.arrival(step - 1, False).wait_recv()

        if step < last:

            @pl.when((me >= step) & (me < last))
            def _():
                self.upward(step).start()

            @pl.when((me + step <= last) & (me > 0))
            def _():
                self.downward(step).start()

    def finish(self):
        me, last = self.me, self.C - 1
        for step in range(last):

            @pl.when((me >= step) & (me < last))
            def _():
                self.upward(step).wait_send()

            @pl.when((me + step <= last) & (me > 0))
            def _():
                self.downward(step).wait_send()


class LineSum:
    def __init__(self, C, terms, rising, falling, up, down):
        self.C, self.terms, self.rising, self.falling, self.up, self.down = C, terms, rising, falling, up, down
        self.me = lax.axis_index("col")

    def upward(self, m, alone):
        source = self.terms.at[self.C - 1 - m] if alone else self.rising.at[m]
        return remote(source, self.rising.at[m], self.up[0].at[m], self.up[1].at[m], col=lax.rem(self.me + 1, self.C))

    def downward(self, m, alone):
        source = self.terms.at[m] if alone else self.falling.at[m]
        return remote(
            source, self.falling.at[m], self.down[0].at[m], self.down[1].at[m], col=lax.rem(self.me + self.C - 1, self.C)
        )

    def level(self, t):
        me, last = self.me, self.C - 1
        rise, fall = t - me, t - (last - me)
        if t < last:

            @pl.when(me == 0)
            def _():
                if t:
                    self.upward(t - 1, True).wait_send()
                self.upward(t, True).start()

            @pl.when(me == last)
            def _():
                if t:
                    self.downward(t - 1, True).wait_send()
                self.downward(t, True).start()

        if t:

            @pl.when((me > 0) & (rise >= 0))
            def _():
                self.upward(rise, False).wait_recv()
                if t < last:
                    add_into(self.rising.at[rise], self.terms.at[last - rise])
                    self.upward(rise, False).start()

            @pl.when((me < last) & (fall >= 0))
            def _():
                self.downward(fall, False).wait_recv()
                if t < last:
                    add_into(self.falling.at[fall], self.terms.at[fall])
                    self.downward(fall, False).start()

    def finish(self):
        me, last = self.me, self.C - 1

        @pl.when(me == 0)
        def _():
            self.upward(last - 1, True).wait_send()

        @pl.when(me == last)
        def _():
            self.downward(last - 1, True).wait_send()

        for m in range(last):

            @pl.when((me > 0) & (m < last - me))
            def _():
                self.upward(m, False).wait_send()

            @pl.when((me < last) & (m < me))
            def _():
                self.downward(m, False).wait_send()


def line_semaphores(C):
    return [DMA((C,)) for _ in range(4)]


def greet_line(C, others):
    me, last = lax.axis_index("col"), C - 1
    above, below = {"col": me + 1}, {"col": me - 1}

    @pl.when(me == 0)
    def _():
        greet([above] + others, 1 + len(others))

    @pl.when(me == last)
    def _():
        greet([below] + others, 1 + len(others))

    @pl.when((me > 0) & (me < last))
    def _():
        greet([above, below] + others, 2 + len(others))


def feed_kernel(
    R, C, os_hbm, w_hbm, xs_hbm, wg_hbm, wu_hbm, wd_hbm, dy_hbm,
    h_hbm, b_hbm, dg_hbm, du_hbm, dys_hbm, down_hbm, y_ref, grad_ref,
    big, hidden, slope, silu, b, gates, ups, terms, rising, falling, dys, h, exchanged, arrived,
    load, block_load, tile_load, store, h_load, w_send, w_recv, f_send, f_recv, *semaphores,
):
    me = lax.axis_index("col")
    row, ahead, behind, other = row_places(R)
    parts, heads, T = os_hbm.shape[0], os_hbm.shape[1], os_hbm.shape[2]
    D, F = wg_hbm.shape
    width, depth = D // C, D // R
    size, tiles, group = 256, 8, R // C
    bf = F // tiles
    up, down = semaphores[:2], semaphores[2:4]
    gather = LineGather(C, dy_hbm, dys, up, down)
    sums = LineSum(C, terms, rising, falling, semaphores[4:6], semaphores[6:8])
    place = row_of(R)
    row_sums = RowSum(
        R, lambda i: big.at[place(i), :, pl.ds(0, F)], lambda i: big.at[place(i, True), :, pl.ds(0, F)],
        exchanged, arrived, semaphores[8:],
    )

    def began(source, target, semaphore):
        copy = pltpu.make_async_copy(source, target, semaphore)
        copy.start()
        return copy

    def block_in(i):
        rows = pl.ds(i * size, size)
        copies = [
            pltpu.make_async_copy(
                os_hbm.at[j, n, rows, :], hidden.at[rows, pl.ds((j * heads + n) * HEAD_DIM, HEAD_DIM)], block_load.at[i, j * heads + n]
            )
            for j in range(parts)
            for n in range(heads)
        ]
        return copies + [
            pltpu.make_async_copy(
                xs_hbm.at[j, rows, :], slope.at[rows, pl.ds(j * width, width)], block_load.at[i, parts * heads + j]
            )
            for j in range(C)
        ]

    def tile_in(i):
        cut = pl.ds(i * bf, bf)
        return [
            pltpu.make_async_copy(wg_hbm.at[:, cut], gates.at[i % 2], tile_load.at[0, i % 2]),
            pltpu.make_async_copy(wu_hbm.at[:, cut], ups.at[i % 2], tile_load.at[1, i % 2]),
        ]

    blocks = [block_in(i) for i in range(T // size)]
    for copy in blocks[0]:
        copy.start()
    out_w = [
        began(w_hbm.at[:, j], big.at[:, :, pl.ds(j * width, width)], load.at[j]) for j in range(C)
    ]
    dy_mine = began(dy_hbm, dys.at[me], load.at[R])
    down_mine = began(wd_hbm, down_hbm.at[row], load.at[R + 1])
    for copies in blocks[1:] + [tile_in(0), tile_in(1)]:
        for copy in copies:
            copy.start()
    greet_line(C, [{"row": other}] + [{"row": ahead[k]} for k in range(1, R // 2)])
    gather.event(0)
    spread = [
        remote(wd_hbm, down_hbm.at[row], w_send.at[k], w_recv.at[k], row=ahead[k]) for k in range(1, R // 2)
    ]
    forward = [remote(wd_hbm, down_hbm.at[row], f_send.at[0], f_recv.at[0], row=other)]
    for copy in spread + forward:
        copy.start()

    stores = []
    mine = pl.ds(pl.multiple_of(me * width, width), width)
    for copy in out_w:
        copy.wait()
    for i in range(T // size):
        rows = pl.ds(i * size, size)
        for copy in blocks[i]:
            copy.wait()
        if i:
            stores[-1].wait()
        left = hidden[rows, :D]
        for j in range(C):
            columns = slice(j * width, (j + 1) * width)
            right = big[j * group : (j + 1) * group, :, :D].reshape(width, D)
            h[:, columns] = slope[rows, columns].astype(F32) + dot_nt(left, right)
        values = h[...]
        centre, inverse = norm_rows(values)
        b[rows, :] = ((values - centre) * inverse).astype(BF)
        stores.append(began(h, h_hbm.at[rows, :], store.at[0]))
    stores[-1].wait()
    b_out = began(b, b_hbm, store.at[1])
    h_back = [
        began(h_hbm.at[pl.ds(i * size, size), mine], h.at[:, pl.ds(i * width, width)], h_load.at[i])
        for i in range(T // size)
    ]
    for i in range(tiles):
        cut = slice(i * bf, (i + 1) * bf)
        for copy in tile_in(i):
            copy.wait()
        values = b[...]
        gate = dot_nn(values, gates[i % 2])
        upward = dot_nn(values, ups[i % 2])
        sigmoid = jax.nn.sigmoid(gate)
        silued = gate * sigmoid
        hidden[:, cut] = (silued * upward).astype(BF)
        slope[:, cut] = (upward * sigmoid * (1.0 + gate * (1.0 - sigmoid))).astype(BF)
        silu[:, cut] = silued.astype(BF)
        if i + 2 < tiles:
            for copy in tile_in(i + 2):
                copy.start()
        if i == 3:
            gather.event(1)
    for k in range(1, R // 2):
        spread[k - 1].wait_recv()
        block = down_hbm.at[behind[k]]
        copy = remote(block, block, f_send.at[k], f_recv.at[k], row=other)
        copy.start()
        forward.append(copy)
    for step in range(2, max(3, C - 1)):
        if step < C:
            gather.event(step)
    for copy in forward:
        copy.wait_recv()
    down_mine.wait()
    began(down_hbm, big.at[:, :, pl.ds(0, F)], load.at[0]).wait()
    half = lax.div(me, C // 2)

    def out_tile(k):
        j = (C - 1 - k) * (1 - half) + k * half
        right = big[pl.ds(j * group, group), :, :F].reshape(width, F)
        terms[j] = dot_nt(hidden[:, :F], right).astype(BF)

    out_tile(0)
    sums.level(0)
    for k in range(1, C):
        out_tile(k)
    for step in range(max(3, C - 1), C):
        gather.event(step)
    dy_mine.wait()
    b_out.wait()
    joined = [began(dys.at[j], b.at[:, pl.ds(j * width, width)], load.at[j]) for j in range(C)]
    saved = [began(dys, dys_hbm, store.at[1])]
    for copy in joined:
        copy.wait()
    sums.level(1)
    for i in range(tiles):
        cut = slice(i * bf, (i + 1) * bf)
        grad_hidden = dot_nn(b[...], big[:, :, cut].reshape(D, bf))
        slope[:, cut] = (grad_hidden * slope[:, cut].astype(F32)).astype(BF)
        silu[:, cut] = (grad_hidden * silu[:, cut].astype(F32)).astype(BF)
    saved.append(began(slope.at[:, pl.ds(0, F)], dg_hbm, store.at[2]))
    saved.append(began(silu.at[:, pl.ds(0, F)], du_hbm, store.at[3]))

    for slot in row_sums.order():
        chip = lax.div(place(slot), 2)
        product = dot_tn(dys[chip], hidden[:, :F]).astype(BF)
        for n in range(2):
            big[2 * chip + n, :, :F] = product[n * depth : (n + 1) * depth]
        row_sums.exchange(slot).start()
    row_sums.relay()
    for t in range(2, C - 1):
        sums.level(t)
    row_sums.relay_again()
    sums.level(C - 1)
    last = C - 1
    for copy in h_back:
        copy.wait()

    def result(more):
        for i in range(T // size):
            rows = pl.ds(i * size, size)
            total = h[:, i * width : (i + 1) * width] + terms[me, rows, :].astype(F32)
            for buffer, slot in more:
                total += buffer[slot, rows, :].astype(F32)
            y_ref[rows, :] = total.astype(BF)

    @pl.when(me == 0)
    def _():
        result([(falling, 0)])

    @pl.when(me == last)
    def _():
        result([(rising, 0)])

    @pl.when((me > 0) & (me < last))
    def _():
        result([(rising, last - me), (falling, me)])

    def write(part, values):
        grad_ref[:, part] = values.T.astype(BF)

    row_sums.finish(write, 128)
    sums.finish()
    gather.finish()
    for copy in spread + forward:
        copy.wait_send()
    for copy in saved:
        copy.wait()


def feed_forward(R, C, os, w_out, xs, w_gate, w_up, w_down, cotangent):
    heads, T = os.shape[1], os.shape[2]
    width = xs.shape[2]
    D, F = w_gate.shape
    most = max(D, F)
    flat = pltpu.VMEM((T, most), BF)
    return pl.pallas_call(
        functools.partial(feed_kernel, R, C),
        in_specs=[ANY] * 7,
        out_specs=[ANY] * 6 + [VMEM_SPEC] * 2,
        out_shape=[
            struct((T, D), F32),
            struct((T, D), BF),
            struct((T, F), BF),
            struct((T, F), BF),
            struct((C, T, width), BF),
            struct((R, D // R, F), BF),
            struct((T, width), BF),
            struct((F, D // R), BF),
        ],
        scratch_shapes=[
            pltpu.VMEM((R, D // R, most), BF),
            flat,
            flat,
            pltpu.VMEM((T, F), BF),
            pltpu.VMEM((T, D), BF),
            pltpu.VMEM((2, D, F // 8), BF),
            pltpu.VMEM((2, D, F // 8), BF),
            pltpu.VMEM((C, T, width), BF),
            pltpu.VMEM((C - 1, T, width), BF),
            pltpu.VMEM((C - 1, T, width), BF),
            pltpu.VMEM((C, T, width), BF),
            pltpu.VMEM((256, D), F32),
        ]
        + row_sum_buffers(R, D // R, F)
        + [
            DMA((R + 2,)),
            DMA((T // 256, C * heads + C)),
            DMA((2, 2)),
            DMA((4,)),
            DMA((T // 256,)),
            DMA((R // 2,)),
            DMA((R // 2,)),
            DMA((R // 2,)),
            DMA((R // 2,)),
        ]
        + line_semaphores(C)
        + line_semaphores(C)
        + row_sum_semaphores(R),
        compiler_params=comm_params(2, 63),
        cost_estimate=cost(1.2e11, 90 * MIB),
        name="feed_forward",
    )(os, w_out, xs, w_gate, w_up, w_down, cotangent)


def norm_terms_kernel(
    R, C, dg_hbm, du_hbm, wg_hbm, wu_hbm, b_hbm,
    sum_ref, up_hbm, gate_ref,
    dg, du, wg, wu, b, terms, held, stage, exchanged, arrived,
    load, tile_load, store, send, recv, *semaphores,
):
    me, right, left = ring_places(C)
    D, F = wg.shape
    T = dg.shape[0]
    rows = T // C
    width = D // C

    def fetch(source, target, semaphore):
        copy = pltpu.make_async_copy(source, target, semaphore)
        copy.start()
        return copy

    def chunk(s):
        return pl.ds(pl.multiple_of(lax.rem(me + 2 * C - 1 - s, C) * rows, rows), rows)

    grads_in = []
    for s in range(C):
        part = chunk(s)
        grads_in.append(
            (fetch(dg_hbm.at[part, :], dg.at[part, :], load.at[2 * s]), fetch(du_hbm.at[part, :], du.at[part, :], load.at[2 * s + 1]))
        )
        if s == 0:
            weights_in = []
            for n in range(C):
                cut = pl.ds(n * width, width)
                weights_in.append(
                    (fetch(wg_hbm.at[cut, :], wg.at[cut, :], tile_load.at[2 * n]), fetch(wu_hbm.at[cut, :], wu.at[cut, :], tile_load.at[2 * n + 1]))
                )
    b_in = fetch(b_hbm, b, load.at[2 * C])
    place, depth = row_of(R), D // R

    def block(places):
        return wu.at[pl.ds(pl.multiple_of(places * depth, depth), depth), :]

    sums = RowSum(R, lambda i: block(place(i)), lambda i: block(place(i, True)), exchanged, arrived, semaphores)
    greet([{"col": left}] + sums.peers, 1 + len(sums.peers))

    def term_tile(s, part, n):
        cut = pl.ds(pl.multiple_of(n * width, width), width)
        total = dot_nt(dg[part, :], wg[cut, :]) + dot_nt(du[part, :], wu[cut, :])
        terms[s, :, cut] = total.astype(BF)

    ring = SumRing(C, terms, held, send, recv)

    for s in range(C):
        part = chunk(s)
        for copy in grads_in[s]:
            copy.wait()
        if s == 0:
            for n in range(C):
                for copy in weights_in[n]:
                    copy.wait()
                term_tile(s, part, n)
            ring.start()
        else:

            def body(n, carry):
                term_tile(s, part, n)
                return carry

            lax.fori_loop(0, C, body, 0)
    b_in.wait()

    def stored(target, t, slot):
        cut = pl.ds(pl.multiple_of(t * width, width), width)
        return pltpu.make_async_copy(stage.at[slot], target.at[cut, :], store.at[slot])

    def product(right_ref, target):
        def body(t, carry):
            slot = lax.rem(t, 2)

            @pl.when(t >= 2)
            def _():
                stored(target, t, slot).wait()

            left_tile = b[:, pl.ds(pl.multiple_of(t * width, width), width)]
            stage[slot] = dot_tn(left_tile, right_ref[...]).astype(BF)
            stored(target, t, slot).start()
            return carry

        lax.fori_loop(0, C, body, 0)
        for slot in range(2):
            stored(target, slot, slot).wait()

    middle = max(1, (C - 1) // 2)
    for step in range(1, middle + 1):
        if step < C - 1:
            ring.pass_on(step)
    for slot in sums.order():
        cut = pl.ds(pl.multiple_of(lax.div(place(slot), 2) * 2 * depth, 2 * depth), 2 * depth)
        wu[cut, :] = dot_tn(b[:, cut], dg[...]).astype(BF)
        sums.exchange(slot).start()
    sums.relay()
    product(du, up_hbm)
    for step in range(middle + 1, C - 1):
        ring.pass_on(step)
    sums.relay_again()

    def write(part, values):
        gate_ref[part, :] = values.astype(BF)

    sums.finish(write)
    ring.arrived()
    sum_ref[...] = held[C - 2].astype(F32) + terms[C - 1].astype(F32)
    ring.sent()


def norm_terms(R, C, dg, du, w_gate, w_up, b):
    T, F = dg.shape
    D = w_gate.shape[0]
    rows, width = T // C, D // C
    return pl.pallas_call(
        functools.partial(norm_terms_kernel, R, C),
        in_specs=[ANY] * 5,
        out_specs=[VMEM_SPEC, ANY, VMEM_SPEC],
        out_shape=[struct((rows, D), F32), struct((D, F), BF), struct((D // R, F), BF)],
        scratch_shapes=[
            pltpu.VMEM((T, F), BF),
            pltpu.VMEM((T, F), BF),
            pltpu.VMEM((D, F), BF),
            pltpu.VMEM((D, F), BF),
            pltpu.VMEM((T, D), BF),
            pltpu.VMEM((C, rows, D), BF),
            pltpu.VMEM((C - 1, rows, D), BF),
            pltpu.VMEM((2, width, F), BF),
        ]
        + row_sum_buffers(R, D // R, F)
        + [
            DMA((2 * C + 1,)),
            DMA((2 * C,)),
            DMA((2,)),
            DMA((C - 1, 2)),
            DMA((C - 1, 2)),
        ]
        + row_sum_semaphores(R),
        compiler_params=comm_params(3, 63),
        cost_estimate=cost(9e10, 70 * MIB),
        name="norm_terms",
    )(dg, du, w_gate, w_up, b)


def attend_back_kernel(
    R, C, sum_ref, log_ref, segk_ref, segq_ref, cos_ref, sin_ref,
    q_hbm, k_hbm, v_hbm, h_hbm, dys_hbm, w_hbm, gate_hbm,
    dq_ref, dk_ref, dv_ref, gate_ref, dhs_hbm,
    h, dy, w, dh, out, q_ref, k_ref, v_ref, do_ref, dk_sum, dv_sum, own, exchanged, arrived,
    load, w_load, local, h_send, h_recv, o_send, o_recv, own_load, *semaphores,
):
    me, right, left = ring_places(C)
    rows, D = sum_ref.shape
    T, width = q_ref.shape
    heads, bq = width // HEAD_DIM, 256
    mine = pl.ds(pl.multiple_of(me * rows, rows), rows)
    first_in = [
        pltpu.make_async_copy(h_hbm.at[mine, :], h, load.at[0]),
        pltpu.make_async_copy(dys_hbm.at[:, mine, :], dy, load.at[1]),
    ]
    head_loads = [
        pltpu.make_async_copy(source, target, load.at[2 + i])
        for i, (source, target) in enumerate(((q_hbm, q_ref), (k_hbm, k_ref), (v_hbm, v_ref)))
    ]
    for copy in first_in:
        copy.start()
    order = [lax.rem(me + k, C) for k in range(1, C)] + [me]
    cuts = [pl.ds(pl.multiple_of(place * width, width), width) for place in order]
    loads = [pltpu.make_async_copy(w_hbm.at[:, order[k]], w.at[k], w_load.at[k]) for k in range(C)]
    sums, own_loads = held_row_sum(R, gate_hbm, own, exchanged, arrived, own_load, semaphores)
    for copy in loads + own_loads + head_loads:
        copy.start()
    greet([{"col": lax.rem(me + k, C)} for k in range(1, C)] + sums.peers, C - 1 + len(sums.peers))
    for slot in sums.order():
        sums.exchange(slot).start()
    for copy in first_in:
        copy.wait()
    grad = sum_ref[...]
    centre, inverse = norm_rows(h[...])
    normed = (h[...] - centre) * inverse
    first = jnp.mean(grad, axis=1, keepdims=True)
    second = jnp.mean(grad * normed, axis=1, keepdims=True)
    dh[...] = (beside(dy).astype(F32) + inverse * (grad - first - normed * second)).astype(BF)
    do_copies, dh_copies = [], []
    for k in range(C):
        loads[k].wait()
        out[k] = dot_nn(dh[...], w[k].reshape(D, width)).astype(BF)
        if k < C - 1:
            copy = remote(out.at[k], do_ref.at[mine, :], o_send.at[k], o_recv.at[k], col=order[k])
        else:
            copy = pltpu.make_async_copy(out.at[k], do_ref.at[mine, :], local.at[0])
        copy.start()
        do_copies.append(copy)
    sums.relay(lambda slot: own_loads[slot].wait())
    for copy in do_copies[:-1]:
        copy.wait_recv()
    do_copies[-1].wait()
    for k in range(C):
        if k < C - 1:
            copy = remote(dh.at[:, cuts[k]], dhs_hbm.at[mine, :], h_send.at[k], h_recv.at[k], col=order[k])
        else:
            copy = pltpu.make_async_copy(dh.at[:, cuts[k]], dhs_hbm.at[mine, :], local.at[1])
        copy.start()
        dh_copies.append(copy)
    for copy in head_loads:
        copy.wait()

    def one_head(head, carry):
        columns = pl.ds(pl.multiple_of(head * HEAD_DIM, HEAD_DIM), HEAD_DIM)
        dk_sum[...] = jnp.zeros_like(dk_sum)
        dv_sum[...] = jnp.zeros_like(dv_sum)
        for first in range(0, T, SEQ):
            for start in range(first, first + SEQ, bq):
                stop = start + bq
                keys = k_ref[first:stop, columns]
                queries = q_ref[start:stop, columns]
                grads = do_ref[start:stop, columns]
                scores = dot_nt(keys, queries) * SCALE
                allowed = allowed_block(segk_ref[first:stop], segq_ref[:, start:stop], start - first)
                scores = jnp.where(allowed, scores, MASKED)
                probs = jnp.exp(scores - log_ref[head, :, start:stop])
                dv_sum[first:stop] += dot_nn(probs.astype(BF), grads)
                grad_probs = dot_nt(v_ref[first:stop, columns], grads)
                inner = jnp.sum(probs * grad_probs, axis=0, keepdims=True)
                grad_scores = (probs * (grad_probs - inner)).astype(BF)
                dk_sum[first:stop] += dot_nn(grad_scores, queries)
                grad_query = dot_tn(keys, grad_scores).T * SCALE
                dq_ref[start:stop, columns] = turn(grad_query, cos_ref[start:stop], -sin_ref[start:stop]).astype(BF)
        dk_ref[:, columns] = turn(dk_sum[...] * SCALE, cos_ref[...], -sin_ref[...]).astype(BF)
        dv_ref[:, columns] = dv_sum[...].astype(BF)
        return carry

    lax.fori_loop(0, heads // 2, one_head, 0)
    sums.relay_again()
    lax.fori_loop(heads // 2, heads, one_head, 0)

    def write(part, values):
        gate_ref[part, :] = values.astype(BF)

    sums.finish(write)
    for copy in do_copies[:-1]:
        copy.wait_send()
    for copy in dh_copies:
        copy.wait()


def attend_back(R, total, log_total, seg_column, seg_row, cos_table, sin_table, q, k, v, h, dys, w_out, grad_gate):
    C, T, width = dys.shape
    rows, D = total.shape
    depth, columns = grad_gate.shape[1:]
    one = pltpu.VMEM((T, width), BF)
    return pl.pallas_call(
        functools.partial(attend_back_kernel, R, C),
        in_specs=[VMEM_SPEC] * 6 + [ANY] * 7,
        out_specs=[VMEM_SPEC] * 4 + [ANY],
        out_shape=[struct((T, width), BF)] * 3 + [struct((depth, columns), BF), struct((T, width), BF)],
        scratch_shapes=[
            pltpu.VMEM((rows, D), F32),
            pltpu.VMEM((C, rows, width), BF),
            pltpu.VMEM((C, R, D // R, width), BF),
            pltpu.VMEM((rows, D), BF),
            pltpu.VMEM((C, rows, width), BF),
            one,
            one,
            one,
            one,
            pltpu.VMEM((T, HEAD_DIM), F32),
            pltpu.VMEM((T, HEAD_DIM), F32),
            pltpu.VMEM((R // 2, depth, columns), BF),
        ]
        + row_sum_buffers(R, depth, columns)
        + [
            DMA((5,)),
            DMA((C,)),
            DMA((2,)),
            DMA((C - 1,)),
            DMA((C - 1,)),
            DMA((C - 1,)),
            DMA((C - 1,)),
            DMA((R // 2,)),
        ]
        + row_sum_semaphores(R),
        compiler_params=comm_params(5),
        cost_estimate=cost(5e10, 30 * MIB),
        name="attend_back",
    )(total, log_total, seg_column, seg_row, cos_table, sin_table, q, k, v, h, dys, w_out, grad_gate)


def input_terms_kernel(
    R, C, dq_ref, dk_ref, dv_ref, mu_hbm, r_hbm, w_hbm, a_hbm, x_hbm, dh_hbm, os_hbm,
    y_ref, gq_ref, gk_ref, gv_ref, out_ref,
    mu_ref, r_ref, w_ref, a_ref, x_ref, dh_ref, block, product, mine, by_column, by_row,
    terms, held, stats, stats_in, tiles, q_exchanged, q_arrived, o_tiles, o_exchanged, o_arrived,
    send, recv, s_send, s_recv, w_load, late_load, block_load, c_send, c_recv, r_send, r_recv, local, *semaphores,
):
    me, right, left = ring_places(C)
    T, width = dq_ref.shape
    D = width * C
    heads = (dq_ref, dk_ref, dv_ref)
    row = lax.axis_index("row")
    thin = width // R

    def cut_of(s):
        return pl.ds(pl.multiple_of(lax.rem(me + 2 * C - 1 - s, C) * width, width), width)

    def weight_in(s):
        return pltpu.make_async_copy(w_hbm.at[:, cut_of(s), :], w_ref.at[:, cut_of(s), :], w_load.at[s])

    for s in range(C):
        weight_in(s).start()
    late = [
        pltpu.make_async_copy(source, target, late_load.at[i])
        for i, (source, target) in enumerate(
            ((a_hbm, a_ref), (x_hbm, x_ref), (dh_hbm, dh_ref), (mu_hbm, mu_ref), (r_hbm, r_ref))
        )
    ]
    for copy in late:
        copy.start()
    depth = tiles.shape[2]
    side = lax.rem(lax.axis_index("row"), 2)
    q_sums = RowSum(
        R, lambda i: tiles.at[i, side], lambda i: tiles.at[i, 1 - side], q_exchanged, q_arrived, semaphores[:4]
    )
    o_sums = RowSum(
        R, lambda i: o_tiles.at[i, side], lambda i: o_tiles.at[i, 1 - side], o_exchanged, o_arrived, semaphores[4:]
    )

    def block_in(i):
        return [
            pltpu.make_async_copy(
                os_hbm.at[i, n], block.at[i % 2, :, pl.ds(n * HEAD_DIM, HEAD_DIM)], block_load.at[i % 2, n]
            )
            for n in range(os_hbm.shape[1])
        ]

    for copy in block_in(0) + block_in(1):
        copy.start()
    greet(
        [{"col": lax.rem(me + k, C)} for k in range(1, C)] + [{"row": lax.rem(row + k, R)} for k in range(1, R)],
        C + R - 2,
    )

    ring = SumRing(C, terms, held, send, recv)

    def compute(s):
        cut = cut_of(s)
        weight_in(s).wait()
        total = dot_nt(dq_ref[...], w_ref[0, cut, :])
        total += dot_nt(dk_ref[...], w_ref[1, cut, :])
        total += dot_nt(dv_ref[...], w_ref[2, cut, :])
        terms[s] = total.astype(BF)

    compute(0)
    ring.start()

    def body(s, carry):
        compute(s)
        return carry

    late[2].wait()
    for j in range(C):
        for copy in block_in(j):
            copy.wait()
        product[...] = dot_tn(block[j % 2], dh_ref[...]).astype(BF)
        for slot in range(R // 2):
            for place in range(2):
                rows = 2 * lax.div(o_sums.places(slot), 2) + place
                o_tiles[slot, place, j * thin : (j + 1) * thin] = product[pl.ds(pl.multiple_of(rows * thin, thin), thin), :]
        if j + 2 < C:
            for copy in block_in(j + 2):
                copy.start()
    for slot in o_sums.order():
        o_sums.exchange(slot).start()
    o_sums.relay()
    lax.fori_loop(1, C, body, 0)
    for i, copy in enumerate(late):
        if i != 2:
            copy.wait()
    for slot in q_sums.order():
        start = pl.multiple_of(lax.div(q_sums.places(slot), 2) * 2 * depth, 2 * depth)
        left_tile = a_ref[:, pl.ds(start, 2 * depth)]
        for i, right_side in enumerate(heads):
            product = dot_tn(left_tile, right_side[...]).astype(BF)
            tiles[slot, 0, :, i * width : (i + 1) * width] = product[:depth]
            tiles[slot, 1, :, i * width : (i + 1) * width] = product[depth:]
        q_sums.exchange(slot).start()
    o_sums.relay_again()
    ring.pass_on(1)
    q_sums.relay()

    def write_out(part, values):
        mine[part, :] = values.astype(BF)

    o_sums.finish(write_out)
    columns_out = []
    for k in range(1, C):
        place = lax.rem(me + k, C)
        rows = pl.ds(pl.multiple_of(place * thin, thin), thin)
        columns_out.append(remote(mine.at[rows, :], by_column.at[me], c_send.at[k - 1], c_recv.at[k - 1], col=place))
    stay = pltpu.make_async_copy(
        mine.at[pl.ds(pl.multiple_of(me * thin, thin), thin), :], by_column.at[me], local.at[0]
    )
    for copy in columns_out + [stay]:
        copy.start()
    size = 128

    def sum_rows(i, carry):
        rows = pl.ds(pl.multiple_of(i * size, size), size)
        lane = lax.broadcasted_iota(jnp.int32, (size, 128), 1)
        total = jnp.zeros((size, 1), F32)
        second = jnp.zeros((size, 1), F32)
        for s in range(C):
            grad = terms[s, rows, :].astype(F32)
            total += jnp.sum(grad, axis=1, keepdims=True)
            second += jnp.sum(grad * a_ref[rows, cut_of(s)].astype(F32), axis=1, keepdims=True)
        packed = jnp.where(lane == 0, total, jnp.where(lane == 1, second, 0.0))
        stats[:, rows] = packed.T[:8]
        return carry

    lax.fori_loop(0, T // size, sum_rows, 0)
    exchanges = [
        remote(stats, stats_in.at[k - 1], s_send.at[k - 1], s_recv.at[k - 1], col=lax.rem(me + k, C)) for k in range(1, C)
    ]
    for copy in exchanges:
        copy.start()
    for copy in columns_out:
        copy.wait_recv()
    stay.wait()

    def piece_of(place):
        return by_column.at[lax.div(place * C, R), :, pl.ds(pl.multiple_of(lax.rem(place, R // C) * depth, depth), depth)]

    rows_out = []
    for k in range(1, R):
        place = lax.rem(row + k, R)
        rows_out.append(remote(piece_of(place), by_row.at[row], r_send.at[k - 1], r_recv.at[k - 1], row=place))
    keep = pltpu.make_async_copy(piece_of(row), by_row.at[row], local.at[1])
    for copy in rows_out + [keep]:
        copy.start()
    for step in range(2, C - 1):
        ring.pass_on(step)
    q_sums.relay_again()
    for copy in rows_out:
        copy.wait_recv()
    keep.wait()
    for n in range(R):
        out_ref[n * thin : (n + 1) * thin, :] = by_row[n]

    def write_qkv(part, values):
        for i, target in enumerate((gq_ref, gk_ref, gv_ref)):
            target[part, :] = values[:, i * width : (i + 1) * width].astype(BF)

    q_sums.finish(write_qkv)
    for copy in exchanges:
        copy.wait_recv()
    ring.arrived()

    def last_rows(i, carry):
        rows = pl.ds(pl.multiple_of(i * size, size), size)
        both = stats[:, rows]
        for k in range(C - 1):
            both += stats_in[k, :, rows]
        columns = jnp.concatenate([both, jnp.zeros((120, size), F32)], axis=0).T * (1.0 / D)
        normed = (x_ref[rows, :].astype(F32) - mu_ref[rows, :]) * r_ref[rows, :]
        grad = held[C - 2, rows, :].astype(F32) + terms[C - 1, rows, :].astype(F32)
        grad = grad - columns[:, 0:1] - normed * columns[:, 1:2]
        y_ref[rows, :] = (dh_ref[rows, :].astype(F32) + r_ref[rows, :] * grad).astype(BF)
        return carry

    lax.fori_loop(0, T // size, last_rows, 0)
    for copy in exchanges + columns_out + rows_out:
        copy.wait_send()
    ring.sent()


def input_terms(R, C, dq, dk, dv, w_qkv, a, tokens, dh, mu, r, os):
    T, width = dq.shape
    D = w_qkv.shape[1]
    half, low = R // 2, D // R
    thin = width // R
    return pl.pallas_call(
        functools.partial(input_terms_kernel, R, C),
        in_specs=[VMEM_SPEC] * 3 + [ANY] * 7,
        out_specs=[VMEM_SPEC] * 5,
        out_shape=[struct((T, width), BF)]
        + [struct((low, width), BF)] * 3
        + [struct((width, low), BF)],
        scratch_shapes=[
            pltpu.VMEM((T, 1), F32),
            pltpu.VMEM((T, 1), F32),
            pltpu.VMEM((3, D, width), BF),
            pltpu.VMEM((T, D), BF),
            pltpu.VMEM((T, width), BF),
            pltpu.VMEM((T, width), BF),
            pltpu.VMEM((2, T, width), BF),
            pltpu.VMEM((width, width), BF),
            pltpu.VMEM((C * thin, width), BF),
            pltpu.VMEM((C, thin, width), BF),
            pltpu.VMEM((R, thin, low), BF),
            pltpu.VMEM((C, T, width), BF),
            pltpu.VMEM((C - 1, T, width), BF),
            pltpu.VMEM((8, T), F32),
            pltpu.VMEM((C - 1, 8, T), F32),
            pltpu.VMEM((half, 2, low, 3 * width), BF),
        ]
        + row_sum_buffers(R, low, 3 * width)
        + [pltpu.VMEM((half, 2, C * thin, width), BF)]
        + row_sum_buffers(R, C * thin, width)
        + [
            DMA((C - 1, 2)),
            DMA((C - 1, 2)),
            DMA((C - 1,)),
            DMA((C - 1,)),
            DMA((C,)),
            DMA((5,)),
            DMA((2, os.shape[1])),
            DMA((C - 1,)),
            DMA((C - 1,)),
            DMA((R - 1,)),
            DMA((R - 1,)),
            DMA((2,)),
        ]
        + row_sum_semaphores(R)
        + row_sum_semaphores(R),
        compiler_params=comm_params(6, 63),
        cost_estimate=cost(8e10, 20 * MIB),
        name="input_terms",
    )(dq, dk, dv, mu, r, w_qkv, a, tokens, dh, os)


def results_kernel(*refs):
    half = len(refs) // 2
    for source, target in zip(refs[:half], refs[half:]):
        target[...] = source[...].astype(target.dtype)


def results(*values):
    shapes = [struct(value.shape, BF if i < 2 else F32) for i, value in enumerate(values)]
    return pl.pallas_call(
        results_kernel,
        in_specs=[VMEM_SPEC] * len(values),
        out_specs=[VMEM_SPEC] * len(values),
        out_shape=shapes,
        compiler_params=params(),
        cost_estimate=cost(1e6, 16 * MIB),
        name="results",
    )(*values)


def on_device(R, C, tokens, cotangent, segments, w_query, w_key, w_value, w_out, w_gate, w_up, w_down):
    T, width = tokens.shape
    D = width * C
    gathered = lambda w: lax.all_gather(w, "row", axis=0, tiled=True)

    gate_w, up_w = gathered(w_gate), gathered(w_up)
    seg_row = segments.reshape(1, T)
    xs, w_qkv, cos_table, sin_table, seg_column, out_part, down_part = first_gather(
        R, C, seg_row, tokens, w_query, w_key, w_value, w_out, w_down
    )
    w_qkv = w_qkv.reshape(3, D, width)
    act_one, q, k, v, mu_one, r_one, out_part = norm_and_project(xs, w_qkv, cos_table, sin_table, out_part)
    os, log_total, out_w = attend(R, C, q, k, v, seg_column, seg_row, out_part)
    h_full, act_two, dg, du, dys, _, output, grad_down = feed_forward(
        R, C, os, out_w, xs, gate_w, up_w, down_part, cotangent
    )
    total, grad_up, grad_gate = norm_terms(R, C, dg, du, gate_w, up_w, act_two)
    grad_up = grad_up.reshape(R, D // R, -1)
    dq, dk, dv, grad_up, dh = attend_back(
        R, total, log_total, seg_column, seg_row, cos_table, sin_table, q, k, v, h_full, dys, out_w, grad_up
    )
    grad_tokens, grad_query, grad_key, grad_value, grad_out = input_terms(
        R, C, dq, dk, dv, w_qkv, act_one, tokens, dh, mu_one, r_one, os
    )
    return tuple(
        results(output, grad_tokens, grad_query, grad_key, grad_value, grad_out, grad_gate, grad_up, grad_down)
    )


def solution(mesh):
    here = P("row", "col")
    turned = P("col", "row")
    return jax.shard_map(
        functools.partial(on_device, mesh.shape["row"], mesh.shape["col"]),
        mesh=mesh,
        in_specs=(here, here, P("row"), here, here, here, turned, here, here, turned),
        out_specs=(here, here, here, here, here, turned, here, here, turned),
        check_vma=False,
    )
```

```python
import functools

import jax
import jax.numpy as jnp
from jax import lax
from jax.experimental import pallas as pl
from jax.experimental.pallas import tpu as pltpu
from jax.sharding import PartitionSpec as P

HEAD_DIM = 128
HALF = HEAD_DIM // 2
SEQ = 1024
EPSILON = 1e-05
MASKED = -1e30
SCALE = HEAD_DIM ** (-0.5)
BF = jnp.bfloat16
F32 = jnp.float32
MIB = 1 << 20
ANY = pl.BlockSpec(memory_space=pl.ANY)


def dot_nn(left, right):
    return jnp.dot(left, right, preferred_element_type=F32)


def dot_tn(left, right):
    return lax.dot_general(left, right, (((0,), (0,)), ((), ())), preferred_element_type=F32)


def dot_nt(left, right):
    return lax.dot_general(left, right, (((1,), (1,)), ((), ())), preferred_element_type=F32)


def struct(shape, dtype):
    return jax.ShapeDtypeStruct(shape, dtype)


def params(mib=60):
    return pltpu.CompilerParams(vmem_limit_bytes=mib * MIB)


def cost(flops, moved):
    return pl.CostEstimate(flops=int(flops), bytes_accessed=int(moved), transcendentals=0)


def turn(values, cos_table, sin_table):
    return values * cos_table + pltpu.roll(values, HALF, 1) * sin_table


MESH = pl.DeviceIdType.MESH
VMEM_SPEC = pl.BlockSpec(memory_space=pltpu.VMEM)
DMA = pltpu.SemaphoreType.DMA


def comm_params(number, mib=60):
    return pltpu.CompilerParams(vmem_limit_bytes=mib * MIB, collective_id=number, has_side_effects=True)


def remote(source, target, send, recv, **device):
    return pltpu.make_async_remote_copy(
        src_ref=source, dst_ref=target, send_sem=send, recv_sem=recv, device_id=device, device_id_type=MESH
    )


def greet(senders, targets):
    semaphore = pltpu.get_barrier_semaphore()
    for device in senders:
        pl.semaphore_signal(semaphore, inc=1, device_id=device, device_id_type=MESH)
    pl.semaphore_wait(semaphore, targets)


def ring_places(C):
    me = lax.axis_index("col")
    return me, lax.rem(me + 1, C), lax.rem(me + C - 1, C)


def row_places(R):
    row = lax.axis_index("row")
    ahead = [lax.rem(row + 2 * k, R) for k in range(R // 2)]
    behind = [lax.rem(row + R - 2 * k, R) for k in range(R // 2)]
    other = row + 1 - 2 * lax.rem(row, 2)
    return row, ahead, behind, other


class GatherRing:
    def __init__(self, C, source, whole, send, recv):
        me, right, left = ring_places(C)
        self.C = C
        size = source.shape[0] // 2
        self.copies = []
        for step in range(C - 1):
            owner = lax.rem(me - step + C, C)
            pair = []
            for half in range(2):
                rows = pl.ds(half * size, size)
                piece = source.at[rows, :] if step == 0 else whole.at[owner, rows, :]
                pair.append(
                    remote(piece, whole.at[owner, rows, :], send.at[step, half], recv.at[step, half], col=right)
                )
            self.copies.append(pair)

    def start(self):
        for copy in self.copies[0]:
            copy.start()

    def pass_on(self, step):
        for half in range(2):
            self.copies[step - 1][half].wait_recv()
            self.copies[step][half].start()

    def arrived(self):
        for copy in self.copies[-1]:
            copy.wait_recv()

    def sent(self):
        for pair in self.copies:
            for copy in pair:
                copy.wait_send()


def gather_kernel(
    R, C, segq_ref, rate_ref, wo_ref, wd_ref, x_ref, wq_ref, wk_ref, wv_ref,
    xs_ref, w_ref, cos_ref, sin_ref, segk_ref, wo_turned, wd_turned,
    local, x_send, x_recv, w_send, w_recv, f_send, f_recv,
):
    me, right, left = ring_places(C)
    row, ahead, behind, other = row_places(R)
    weights = (wq_ref, wk_ref, wv_ref)
    mine = [
        pltpu.make_async_copy(x_ref, xs_ref.at[me], local.at[0]),
    ] + [pltpu.make_async_copy(w, w_ref.at[i, row], local.at[1 + i]) for i, w in enumerate(weights)]
    for copy in mine:
        copy.start()
    greet(
        [{"col": left}, {"row": other}] + [{"row": r} for r in behind[1:]],
        1 + R // 2,
    )

    ring = GatherRing(C, x_ref, xs_ref, x_send, x_recv)
    ring.start()
    spread, forward = [], []
    for i, w in enumerate(weights):
        for k in range(1, R // 2):
            copy = remote(w, w_ref.at[i, row], w_send.at[i, k], w_recv.at[i, k], row=ahead[k])
            copy.start()
            spread.append(copy)
        copy = remote(w, w_ref.at[i, row], f_send.at[i, 0], f_recv.at[i, 0], row=other)
        copy.start()
        forward.append(copy)
    T = cos_ref.shape[0]
    size = 128

    def table_rows(i, carry):
        rows = pl.ds(pl.multiple_of(i * size, size), size)
        first = SEQ * lax.div(i * size, SEQ)
        here = jnp.broadcast_to(segq_ref[:, rows].astype(F32), (size, size)).T[:, :1]
        segk_ref[rows, :] = here.astype(jnp.int32)
        shape = (size, T)
        queries = lax.broadcasted_iota(jnp.int32, shape, 0) + i * size
        keys = lax.broadcasted_iota(jnp.int32, shape, 1)
        seen = (here == segq_ref[...].astype(F32)) & (keys <= queries) & (keys >= first)
        place = jnp.sum(jnp.where(seen, 1.0, 0.0), axis=1, keepdims=True) - 1.0
        angles = place * rate_ref[...]
        lane = lax.broadcasted_iota(jnp.int32, angles.shape, 1)
        sine = jnp.sin(angles)
        cos_ref[rows, :] = jnp.cos(angles)
        sin_ref[rows, :] = jnp.where(lane < HALF, -sine, sine)
        return carry

    lax.fori_loop(0, T // size, table_rows, 0)

    def turn_rows(source, target):
        def body(i, carry):
            cut = pl.ds(pl.multiple_of(i * size, size), size)
            target[:, cut] = source[cut, :].astype(F32).T.astype(BF)
            return carry

        lax.fori_loop(0, source.shape[0] // size, body, 0)

    turn_rows(wo_ref, wo_turned)
    turn_rows(wd_ref, wd_turned)
    for s in range(1, C - 1):
        ring.pass_on(s)
    for i in range(3):
        for k in range(1, R // 2):
            spread[i * (R // 2 - 1) + k - 1].wait_recv()
            block = w_ref.at[i, behind[k]]
            copy = remote(block, block, f_send.at[i, k], f_recv.at[i, k], row=other)
            copy.start()
            forward.append(copy)
    ring.arrived()
    for copy in forward:
        copy.wait_recv()
    ring.sent()
    for copy in spread + forward:
        copy.wait_send()
    for copy in mine:
        copy.wait()


def first_gather(R, C, seg_row, tokens, w_query, w_key, w_value, w_out, w_down):
    depth, width = w_query.shape
    T = tokens.shape[0]
    half = R // 2
    rate = 10000.0 ** (-(jnp.arange(HALF, dtype=F32) * 2.0 / HEAD_DIM))
    rate = jnp.concatenate([rate, rate]).reshape(1, HEAD_DIM)
    return pl.pallas_call(
        functools.partial(gather_kernel, R, C),
        in_specs=[VMEM_SPEC] * 4 + [ANY] * 4,
        out_specs=[ANY] * 2 + [VMEM_SPEC] * 5,
        out_shape=[
            struct((C,) + tokens.shape, BF),
            struct((3, R, depth, width), BF),
            struct((T, HEAD_DIM), F32),
            struct((T, HEAD_DIM), F32),
            struct((T, 1), jnp.int32),
            struct(w_out.shape[::-1], BF),
            struct(w_down.shape[::-1], BF),
        ],
        scratch_shapes=[
            DMA((4,)),
            DMA((C - 1, 2)),
            DMA((C - 1, 2)),
            DMA((3, half)),
            DMA((3, half)),
            DMA((3, half)),
            DMA((3, half)),
        ],
        compiler_params=comm_params(0),
        cost_estimate=cost(6e10, 14 * MIB),
        name="first_gather",
    )(seg_row, rate, w_out, w_down, tokens, w_query, w_key, w_value)


def norm_rows(x):
    centre = jnp.mean(x, axis=-1, keepdims=True)
    spread = jnp.mean(x * x, axis=-1, keepdims=True) - centre * centre
    inverse = lax.rsqrt(spread + EPSILON)
    return centre, inverse


def beside(ref):
    return jnp.concatenate([ref[j] for j in range(ref.shape[0])], axis=1)


def qkv_kernel(
    C, xs_ref, w_ref, cos_ref, sin_ref, wo_ref, a_ref, q_ref, k_ref, v_ref, mu_ref, r_ref, wos_ref, local, send, recv
):
    step, steps = pl.program_id(0), pl.num_programs(0)
    me, right, left = ring_places(C)
    ring = GatherRing(C, wo_ref, wos_ref, send, recv)
    mine = pltpu.make_async_copy(wo_ref, wos_ref.at[me], local.at[0])

    @pl.when(step == 0)
    def _():
        mine.start()
        greet([{"col": left}], 1)
        ring.start()

    @pl.when(step == steps // 2)
    def _():
        ring.pass_on(1)

    x = beside(xs_ref).astype(F32)
    centre, inverse = norm_rows(x)
    a = ((x - centre) * inverse).astype(BF)
    a_ref[...] = a
    mu_ref[...] = centre
    r_ref[...] = inverse
    cosine, sine = cos_ref[...], sin_ref[...]
    for index, out in enumerate((q_ref, k_ref, v_ref)):
        product = dot_nn(a, w_ref[index])
        if index == 2:
            out[...] = product.astype(BF)
            continue
        for start in range(0, out.shape[1], HEAD_DIM):
            part = product[:, start : start + HEAD_DIM]
            out[:, start : start + HEAD_DIM] = turn(part, cosine, sine).astype(BF)

    @pl.when(step == steps - 1)
    def _():
        for s in range(2, C - 1):
            ring.pass_on(s)
        ring.arrived()
        ring.sent()
        mine.wait()


def norm_and_project(xs, w_qkv, cos_table, sin_table, w_out):
    C, T, width = xs.shape
    D = width * C
    bt = 256
    rows = lambda n: pl.BlockSpec((bt, n), lambda i: (i, 0))
    return pl.pallas_call(
        functools.partial(qkv_kernel, C),
        grid=(T // bt,),
        in_specs=[
            pl.BlockSpec((C, bt, width), lambda i: (0, i, 0)),
            pl.BlockSpec(w_qkv.shape, lambda i: (0, 0, 0), pipeline_mode=pl.Buffered(1)),
            rows(HEAD_DIM),
            rows(HEAD_DIM),
            ANY,
        ],
        out_specs=[rows(D), rows(width), rows(width), rows(width), rows(1), rows(1), ANY],
        out_shape=[
            struct((T, D), BF),
            struct((T, width), BF),
            struct((T, width), BF),
            struct((T, width), BF),
            struct((T, 1), F32),
            struct((T, 1), F32),
            struct((C,) + w_out.shape, BF),
        ],
        scratch_shapes=[DMA((1,)), DMA((C - 1, 2)), DMA((C - 1, 2))],
        compiler_params=comm_params(7),
        cost_estimate=cost(2e10, 14 * MIB),
        name="norm_and_project",
    )(xs, w_qkv, cos_table, sin_table, w_out)


def allowed_block(seg_key, seg_query, first_query):
    shape = (seg_key.shape[0], seg_query.shape[1])
    keys = lax.broadcasted_iota(jnp.int32, shape, 0)
    queries = lax.broadcasted_iota(jnp.int32, shape, 1) + first_query
    return (seg_key == seg_query) & (keys <= queries)


def attend_kernel(
    R, C, q_ref, k_ref, v_ref, segk_ref, segq_ref, wos_ref, os_ref, log_ref, w_ref,
    o_buf, local, o_send, o_recv, w_send, w_recv, f_send, f_recv,
):
    me, right, left = ring_places(C)
    row, ahead, behind, other = row_places(R)
    T, width = q_ref.shape
    heads, bq = width // HEAD_DIM, 256
    greet([{"col": left}, {"row": other}] + [{"row": r} for r in behind[1:]], 1 + R // 2)
    mine = pltpu.make_async_copy(wos_ref, w_ref.at[row], local.at[0])
    mine.start()
    spread, forward = [], []
    for k in range(1, R // 2):
        copy = remote(wos_ref, w_ref.at[row], w_send.at[k], w_recv.at[k], row=ahead[k])
        copy.start()
        spread.append(copy)
    copy = remote(wos_ref, w_ref.at[row], f_send.at[0], f_recv.at[0], row=other)
    copy.start()
    forward.append(copy)

    def ring(step, head):
        owner = lax.rem(me - step + C, C)
        piece = o_buf.at[head] if step == 0 else os_ref.at[owner, head]
        return remote(piece, os_ref.at[owner, head], o_send.at[step, head], o_recv.at[step, head], col=right)

    def one_head(head, carry):
        columns = pl.ds(pl.multiple_of(head * HEAD_DIM, HEAD_DIM), HEAD_DIM)
        for first in range(0, T, SEQ):
            for start in range(first, first + SEQ, bq):
                stop = start + bq
                scores = dot_nt(k_ref[first:stop, columns], q_ref[start:stop, columns]) * SCALE
                allowed = allowed_block(segk_ref[first:stop], segq_ref[:, start:stop], start - first)
                scores = jnp.where(allowed, scores, MASKED)
                peak = jnp.max(scores, axis=0, keepdims=True)
                exponent = jnp.exp(scores - peak)
                total = jnp.sum(exponent, axis=0, keepdims=True)
                weights = (exponent * (1.0 / total)).astype(BF)
                o_buf[head, start:stop] = dot_tn(v_ref[first:stop, columns], weights).T.astype(BF)
                log_ref[head, :, start:stop] = peak + jnp.log(total)
        ring(0, head).start()
        pltpu.make_async_copy(o_buf.at[head], os_ref.at[me, head], local.at[1 + head]).start()
        return carry

    lax.fori_loop(0, heads, one_head, 0)
    for step in range(1, C - 1):
        for head in range(heads):
            ring(step - 1, head).wait_recv()
            ring(step, head).start()
    for k in range(1, R // 2):
        spread[k - 1].wait_recv()
        block = w_ref.at[behind[k]]
        copy = remote(block, block, f_send.at[k], f_recv.at[k], row=other)
        copy.start()
        forward.append(copy)
    for head in range(heads):
        ring(C - 2, head).wait_recv()
        pltpu.make_async_copy(o_buf.at[head], os_ref.at[me, head], local.at[1 + head]).wait()
        for step in range(C - 1):
            ring(step, head).wait_send()
    for copy in forward:
        copy.wait_recv()
    for copy in spread + forward:
        copy.wait_send()
    mine.wait()


def attend(R, C, q, k, v, seg_column, seg_row, w_part):
    T, width = q.shape
    heads, half = width // HEAD_DIM, R // 2
    return pl.pallas_call(
        functools.partial(attend_kernel, R, C),
        in_specs=[VMEM_SPEC] * 5 + [ANY],
        out_specs=[ANY, VMEM_SPEC, ANY],
        out_shape=[
            struct((C, heads, T, HEAD_DIM), BF),
            struct((heads, 1, T), F32),
            struct((R,) + w_part.shape, BF),
        ],
        scratch_shapes=[
            pltpu.VMEM((heads, T, HEAD_DIM), BF),
            DMA((1 + heads,)),
            DMA((C - 1, heads)),
            DMA((C - 1, heads)),
            DMA((half,)),
            DMA((half,)),
            DMA((half,)),
            DMA((half,)),
        ],
        compiler_params=comm_params(1),
        cost_estimate=cost(7e10, 14 * MIB),
        name="attend",
    )(q, k, v, seg_column, seg_row, w_part)


class SumRing:
    def __init__(self, C, terms, held, send, recv):
        me, right, left = ring_places(C)
        self.C, self.terms, self.held, self.send, self.recv, self.right = C, terms, held, send, recv, right

    def copy(self, step):
        source = self.terms.at[0] if step == 0 else self.held.at[step - 1]
        return remote(source, self.held.at[step], self.send.at[step], self.recv.at[step], col=self.right)

    def start(self):
        self.copy(0).start()

    def pass_on(self, step):
        self.copy(step - 1).wait_recv()
        add_into(self.held.at[step - 1], self.terms.at[step])
        self.copy(step).start()

    def arrived(self):
        self.copy(self.C - 2).wait_recv()

    def sent(self):
        for step in range(self.C - 1):
            self.copy(step).wait_send()


def add_into(held, terms):
    size = 64

    def body(i, carry):
        rows = pl.ds(pl.multiple_of(i * size, size), size)
        held[rows, :] = (held[rows, :].astype(F32) + terms[rows, :].astype(F32)).astype(BF)
        return carry

    lax.fori_loop(0, held.shape[0] // size, body, 0)


class RowSum:
    def __init__(self, R, own, twin, exchanged, arrived, semaphores):
        self.P = R // 4
        self.own, self.twin, self.exchanged, self.arrived = own, twin, exchanged, arrived
        self.x_send, self.x_recv, self.y_send, self.y_recv = semaphores
        self.width = arrived.shape[2]
        self.places = row_of(R)
        self.peers = row_peers(R)

    def part(self, ref, side):
        return ref.at[:, pl.ds(side * self.width, self.width)]

    def exchange(self, slot):
        return remote(
            self.twin(slot), self.exchanged.at[slot], self.x_send.at[slot], self.x_recv.at[slot], row=self.places(0, True)
        )

    def send(self, slot, side, index, target):
        return remote(
            self.part(self.own(slot), side), self.arrived.at[index], self.y_send.at[index], self.y_recv.at[index],
            row=self.places(target),
        )

    def left_one(self, dp):
        return self.send(2 * dp + 1, 0, dp, 1)

    def left_two(self, dp):
        return self.send(2 * dp, 0, self.P + dp - 1, 2 * dp)

    def right_one(self, dp, dq):
        return self.send(2 * dp + dq, 1, 2 * self.P - 1 + 2 * (dp - 1) + dq, 2 * dp)

    def right_two(self):
        return self.send(1, 1, 4 * self.P - 3, 1)

    def order(self):
        return (
            [2 * dp + 1 for dp in range(1, self.P)] + [1] + [2 * dp for dp in range(1, self.P)] + [0]
        )

    def relay_one(self, slot):
        self.exchange(slot).wait_recv()
        add_into(self.own(slot), self.exchanged.at[slot])
        dp, dq = divmod(slot, 2)
        if dq:
            self.left_one(dp).start()
        if dp:
            self.right_one(dp, dq).start()

    def relay(self, before=None):
        for slot in self.order():
            if before is not None:
                before(slot)
            self.relay_one(slot)

    def compute_and_relay(self, compute):
        slots = self.order()
        for i, slot in enumerate(slots):
            compute(slot)
            self.exchange(slot).start()
            if i:
                self.relay_one(slots[i - 1])
        self.relay_one(slots[-1])

    def relay_again(self):
        for dp in range(1, self.P):
            self.left_one(dp).wait_recv()
            add_into(self.part(self.own(2 * dp), 0), self.arrived.at[dp])
            self.left_two(dp).start()
        for dp in range(1, self.P):
            copy = self.right_one(dp, 1)
            copy.wait_recv()
            add_into(self.part(self.own(1), 1), self.arrived.at[2 * self.P - 1 + 2 * (dp - 1) + 1])
        self.right_two().start()

    def finish(self, write, size=64):
        P, width = self.P, self.width
        self.left_one(0).wait_recv()
        self.right_two().wait_recv()
        for dp in range(1, P):
            self.left_two(dp).wait_recv()
            self.right_one(dp, 0).wait_recv()
        lefts = [0] + [P + dp - 1 for dp in range(1, P)]
        rights = [4 * P - 3] + [2 * P - 1 + 2 * (dp - 1) for dp in range(1, P)]

        def body(i, carry):
            rows = pl.ds(pl.multiple_of(i * size, size), size)
            total = self.own(0)[rows, :].astype(F32)
            halves = []
            for side, places in enumerate((lefts, rights)):
                half = total[:, side * width : (side + 1) * width]
                for index in places:
                    half += self.arrived[index, rows, :].astype(F32)
                halves.append(half)
            write(rows, jnp.concatenate(halves, axis=1))
            return carry

        lax.fori_loop(0, self.exchanged.shape[1] // size, body, 0)
        for slot in range(2 * P):
            self.exchange(slot).wait_send()
        self.left_one(0).wait_send()
        self.right_two().wait_send()
        for dp in range(1, P):
            self.left_one(dp).wait_send()
            self.left_two(dp).wait_send()
            self.right_one(dp, 0).wait_send()
            self.right_one(dp, 1).wait_send()


def row_of(R):
    row = lax.axis_index("row")
    side, chip = lax.rem(row, 2), lax.div(row, 2)
    p, q = lax.div(chip, 2), lax.rem(chip, 2)

    def place(slot, twin=False):
        dp, dq = divmod(slot, 2)
        chip_there = 2 * lax.rem(p + dp, R // 4) + lax.rem(q + dq, 2)
        return 2 * chip_there + (1 - side if twin else side)

    return place


def row_peers(R):
    place = row_of(R)
    return [{"row": place(0, True)}, {"row": place(1)}] + [{"row": place(2 * dp)} for dp in range(1, R // 4)]


def row_sum_semaphores(R):
    return [DMA((R // 2,)), DMA((R // 2,)), DMA((R - 2,)), DMA((R - 2,))]


def row_sum_buffers(R, depth, columns):
    return [
        pltpu.VMEM((R // 2, depth, columns), BF),
        pltpu.VMEM((R - 2, depth, columns // 2), BF),
    ]


def held_row_sum(R, grad_hbm, own, exchanged, arrived, load, semaphores):
    place = row_of(R)
    sums = RowSum(R, lambda i: own.at[i], lambda i: grad_hbm.at[place(i, True)], exchanged, arrived, semaphores)
    loads = [pltpu.make_async_copy(grad_hbm.at[place(i)], own.at[i], load.at[i]) for i in range(R // 2)]
    return sums, loads


class LineGather:
    def __init__(self, C, source, whole, up, down):
        self.C, self.source, self.whole, self.up, self.down = C, source, whole, up, down
        self.me = lax.axis_index("col")

    def upward(self, step):
        owner = self.me - step
        piece = self.source if step == 0 else self.whole.at[owner]
        return remote(piece, self.whole.at[owner], self.up[0].at[step], self.up[1].at[step], col=self.me + 1)

    def downward(self, step):
        owner = self.me + step
        piece = self.source if step == 0 else self.whole.at[owner]
        return remote(piece, self.whole.at[owner], self.down[0].at[step], self.down[1].at[step], col=self.me - 1)

    def arrival(self, step, rises):
        sender = self.me - 1 if rises else self.me + 1
        send, recv = self.up if rises else self.down
        target = self.whole.at[sender - step if rises else sender + step]
        return remote(target, target, send.at[step], recv.at[step], col=sender)

    def event(self, step):
        me, last = self.me, self.C - 1
        if step:

            @pl.when(me >= step)
            def _():
                self.arrival(step - 1, True).wait_recv()

            @pl.when(me + step <= last)
            def _():
                self.arrival(step - 1, False).wait_recv()

        if step < last:

            @pl.when((me >= step) & (me < last))
            def _():
                self.upward(step).start()

            @pl.when((me + step <= last) & (me > 0))
            def _():
                self.downward(step).start()

    def finish(self):
        me, last = self.me, self.C - 1
        for step in range(last):

            @pl.when((me >= step) & (me < last))
            def _():
                self.upward(step).wait_send()

            @pl.when((me + step <= last) & (me > 0))
            def _():
                self.downward(step).wait_send()


class LineSum:
    def __init__(self, C, terms, rising, falling, up, down):
        self.C, self.terms, self.rising, self.falling, self.up, self.down = C, terms, rising, falling, up, down
        self.me = lax.axis_index("col")

    def upward(self, m, alone):
        source = self.terms.at[self.C - 1 - m] if alone else self.rising.at[m]
        return remote(source, self.rising.at[m], self.up[0].at[m], self.up[1].at[m], col=lax.rem(self.me + 1, self.C))

    def downward(self, m, alone):
        source = self.terms.at[m] if alone else self.falling.at[m]
        return remote(
            source, self.falling.at[m], self.down[0].at[m], self.down[1].at[m], col=lax.rem(self.me + self.C - 1, self.C)
        )

    def level(self, t):
        me, last = self.me, self.C - 1
        rise, fall = t - me, t - (last - me)
        if t < last:

            @pl.when(me == 0)
            def _():
                if t:
                    self.upward(t - 1, True).wait_send()
                self.upward(t, True).start()

            @pl.when(me == last)
            def _():
                if t:
                    self.downward(t - 1, True).wait_send()
                self.downward(t, True).start()

        if t:

            @pl.when((me > 0) & (rise >= 0))
            def _():
                self.upward(rise, False).wait_recv()
                if t < last:
                    add_into(self.rising.at[rise], self.terms.at[last - rise])
                    self.upward(rise, False).start()

            @pl.when((me < last) & (fall >= 0))
            def _():
                self.downward(fall, False).wait_recv()
                if t < last:
                    add_into(self.falling.at[fall], self.terms.at[fall])
                    self.downward(fall, False).start()

    def finish(self):
        me, last = self.me, self.C - 1

        @pl.when(me == 0)
        def _():
            self.upward(last - 1, True).wait_send()

        @pl.when(me == last)
        def _():
            self.downward(last - 1, True).wait_send()

        for m in range(last):

            @pl.when((me > 0) & (m < last - me))
            def _():
                self.upward(m, False).wait_send()

            @pl.when((me < last) & (m < me))
            def _():
                self.downward(m, False).wait_send()


def line_semaphores(C):
    return [DMA((C,)) for _ in range(4)]


def greet_line(C, others):
    me, last = lax.axis_index("col"), C - 1
    above, below = {"col": me + 1}, {"col": me - 1}

    @pl.when(me == 0)
    def _():
        greet([above] + others, 1 + len(others))

    @pl.when(me == last)
    def _():
        greet([below] + others, 1 + len(others))

    @pl.when((me > 0) & (me < last))
    def _():
        greet([above, below] + others, 2 + len(others))


def feed_kernel(
    R, C, os_hbm, w_hbm, xs_hbm, wg_hbm, wu_hbm, wd_hbm, dy_hbm,
    h_hbm, b_hbm, dg_hbm, du_hbm, dys_hbm, down_hbm, y_ref, grad_ref,
    big, hidden, slope, silu, b, gates, ups, terms, rising, falling, dys, h, exchanged, arrived,
    load, block_load, tile_load, store, h_load, w_send, w_recv, f_send, f_recv, *semaphores,
):
    me = lax.axis_index("col")
    row, ahead, behind, other = row_places(R)
    parts, heads, T = os_hbm.shape[0], os_hbm.shape[1], os_hbm.shape[2]
    D, F = wg_hbm.shape
    width, depth = D // C, D // R
    size, tiles, group = 256, 8, R // C
    bf = F // tiles
    up, down = semaphores[:2], semaphores[2:4]
    gather = LineGather(C, dy_hbm, dys, up, down)
    sums = LineSum(C, terms, rising, falling, semaphores[4:6], semaphores[6:8])
    place = row_of(R)
    row_sums = RowSum(
        R, lambda i: big.at[place(i), :, pl.ds(0, F)], lambda i: big.at[place(i, True), :, pl.ds(0, F)],
        exchanged, arrived, semaphores[8:],
    )

    def began(source, target, semaphore):
        copy = pltpu.make_async_copy(source, target, semaphore)
        copy.start()
        return copy

    def block_in(i):
        rows = pl.ds(i * size, size)
        copies = [
            pltpu.make_async_copy(
                os_hbm.at[j, n, rows, :], hidden.at[rows, pl.ds((j * heads + n) * HEAD_DIM, HEAD_DIM)], block_load.at[i, j * heads + n]
            )
            for j in range(parts)
            for n in range(heads)
        ]
        return copies + [
            pltpu.make_async_copy(
                xs_hbm.at[j, rows, :], slope.at[rows, pl.ds(j * width, width)], block_load.at[i, parts * heads + j]
            )
            for j in range(C)
        ]

    def tile_in(i):
        cut = pl.ds(i * bf, bf)
        return [
            pltpu.make_async_copy(wg_hbm.at[:, cut], gates.at[i % 2], tile_load.at[0, i % 2]),
            pltpu.make_async_copy(wu_hbm.at[:, cut], ups.at[i % 2], tile_load.at[1, i % 2]),
        ]

    blocks = [block_in(i) for i in range(T // size)]
    for copy in blocks[0]:
        copy.start()
    out_w = [
        began(w_hbm.at[:, j], big.at[:, :, pl.ds(j * width, width)], load.at[j]) for j in range(C)
    ]
    dy_mine = began(dy_hbm, dys.at[me], load.at[R])
    down_mine = began(wd_hbm, down_hbm.at[row], load.at[R + 1])
    for copies in blocks[1:] + [tile_in(0), tile_in(1)]:
        for copy in copies:
            copy.start()
    greet_line(C, [{"row": other}] + [{"row": ahead[k]} for k in range(1, R // 2)])
    gather.event(0)
    spread = [
        remote(wd_hbm, down_hbm.at[row], w_send.at[k], w_recv.at[k], row=ahead[k]) for k in range(1, R // 2)
    ]
    forward = [remote(wd_hbm, down_hbm.at[row], f_send.at[0], f_recv.at[0], row=other)]
    for copy in spread + forward:
        copy.start()

    stores = []
    mine = pl.ds(pl.multiple_of(me * width, width), width)
    for copy in out_w:
        copy.wait()
    for i in range(T // size):
        rows = pl.ds(i * size, size)
        for copy in blocks[i]:
            copy.wait()
        if i:
            stores[-1].wait()
        left = hidden[rows, :D]
        for j in range(C):
            columns = slice(j * width, (j + 1) * width)
            right = big[j * group : (j + 1) * group, :, :D].reshape(width, D)
            h[:, columns] = slope[rows, columns].astype(F32) + dot_nt(left, right)
        values = h[...]
        centre, inverse = norm_rows(values)
        b[rows, :] = ((values - centre) * inverse).astype(BF)
        stores.append(began(h, h_hbm.at[rows, :], store.at[0]))
    stores[-1].wait()
    b_out = began(b, b_hbm, store.at[1])
    h_back = [
        began(h_hbm.at[pl.ds(i * size, size), mine], h.at[:, pl.ds(i * width, width)], h_load.at[i])
        for i in range(T // size)
    ]
    for i in range(tiles):
        cut = slice(i * bf, (i + 1) * bf)
        for copy in tile_in(i):
            copy.wait()
        values = b[...]
        gate = dot_nn(values, gates[i % 2])
        upward = dot_nn(values, ups[i % 2])
        sigmoid = jax.nn.sigmoid(gate)
        silued = gate * sigmoid
        hidden[:, cut] = (silued * upward).astype(BF)
        slope[:, cut] = (upward * sigmoid * (1.0 + gate * (1.0 - sigmoid))).astype(BF)
        silu[:, cut] = silued.astype(BF)
        if i + 2 < tiles:
            for copy in tile_in(i + 2):
                copy.start()
        if i == 3:
            gather.event(1)
    for k in range(1, R // 2):
        spread[k - 1].wait_recv()
        block = down_hbm.at[behind[k]]
        copy = remote(block, block, f_send.at[k], f_recv.at[k], row=other)
        copy.start()
        forward.append(copy)
    for step in range(2, max(3, C - 1)):
        if step < C:
            gather.event(step)
    for copy in forward:
        copy.wait_recv()
    down_mine.wait()
    began(down_hbm, big.at[:, :, pl.ds(0, F)], load.at[0]).wait()
    half = lax.div(me, C // 2)

    def out_tile(k):
        j = (C - 1 - k) * (1 - half) + k * half
        right = big[pl.ds(j * group, group), :, :F].reshape(width, F)
        terms[j] = dot_nt(hidden[:, :F], right).astype(BF)

    out_tile(0)
    sums.level(0)
    for k in range(1, C):
        out_tile(k)
    for step in range(max(3, C - 1), C):
        gather.event(step)
    dy_mine.wait()
    b_out.wait()
    joined = [began(dys.at[j], b.at[:, pl.ds(j * width, width)], load.at[j]) for j in range(C)]
    saved = [began(dys, dys_hbm, store.at[1])]
    for copy in joined:
        copy.wait()
    sums.level(1)
    for i in range(tiles):
        cut = slice(i * bf, (i + 1) * bf)
        grad_hidden = dot_nn(b[...], big[:, :, cut].reshape(D, bf))
        slope[:, cut] = (grad_hidden * slope[:, cut].astype(F32)).astype(BF)
        silu[:, cut] = (grad_hidden * silu[:, cut].astype(F32)).astype(BF)
    saved.append(began(slope.at[:, pl.ds(0, F)], dg_hbm, store.at[2]))
    saved.append(began(silu.at[:, pl.ds(0, F)], du_hbm, store.at[3]))


    def down_tile(slot):
        chip = lax.div(place(slot), 2)
        product = dot_tn(dys[chip], hidden[:, :F]).astype(BF)
        for n in range(2):
            big[2 * chip + n, :, :F] = product[n * depth : (n + 1) * depth]

    row_sums.compute_and_relay(down_tile)
    for t in range(2, C - 1):
        sums.level(t)
    row_sums.relay_again()
    sums.level(C - 1)
    last = C - 1
    for copy in h_back:
        copy.wait()

    def result(more):
        for i in range(T // size):
            rows = pl.ds(i * size, size)
            total = h[:, i * width : (i + 1) * width] + terms[me, rows, :].astype(F32)
            for buffer, slot in more:
                total += buffer[slot, rows, :].astype(F32)
            y_ref[rows, :] = total.astype(BF)

    @pl.when(me == 0)
    def _():
        result([(falling, 0)])

    @pl.when(me == last)
    def _():
        result([(rising, 0)])

    @pl.when((me > 0) & (me < last))
    def _():
        result([(rising, last - me), (falling, me)])

    def write(part, values):
        grad_ref[:, part] = values.T.astype(BF)

    row_sums.finish(write, 128)
    sums.finish()
    gather.finish()
    for copy in spread + forward:
        copy.wait_send()
    for copy in saved:
        copy.wait()


def feed_forward(R, C, os, w_out, xs, w_gate, w_up, w_down, cotangent):
    heads, T = os.shape[1], os.shape[2]
    width = xs.shape[2]
    D, F = w_gate.shape
    most = max(D, F)
    flat = pltpu.VMEM((T, most), BF)
    return pl.pallas_call(
        functools.partial(feed_kernel, R, C),
        in_specs=[ANY] * 7,
        out_specs=[ANY] * 6 + [VMEM_SPEC] * 2,
        out_shape=[
            struct((T, D), F32),
            struct((T, D), BF),
            struct((T, F), BF),
            struct((T, F), BF),
            struct((C, T, width), BF),
            struct((R, D // R, F), BF),
            struct((T, width), BF),
            struct((F, D // R), BF),
        ],
        scratch_shapes=[
            pltpu.VMEM((R, D // R, most), BF),
            flat,
            flat,
            pltpu.VMEM((T, F), BF),
            pltpu.VMEM((T, D), BF),
            pltpu.VMEM((2, D, F // 8), BF),
            pltpu.VMEM((2, D, F // 8), BF),
            pltpu.VMEM((C, T, width), BF),
            pltpu.VMEM((C - 1, T, width), BF),
            pltpu.VMEM((C - 1, T, width), BF),
            pltpu.VMEM((C, T, width), BF),
            pltpu.VMEM((256, D), F32),
        ]
        + row_sum_buffers(R, D // R, F)
        + [
            DMA((R + 2,)),
            DMA((T // 256, C * heads + C)),
            DMA((2, 2)),
            DMA((4,)),
            DMA((T // 256,)),
            DMA((R // 2,)),
            DMA((R // 2,)),
            DMA((R // 2,)),
            DMA((R // 2,)),
        ]
        + line_semaphores(C)
        + line_semaphores(C)
        + row_sum_semaphores(R),
        compiler_params=comm_params(2, 63),
        cost_estimate=cost(1.2e11, 90 * MIB),
        name="feed_forward",
    )(os, w_out, xs, w_gate, w_up, w_down, cotangent)


def norm_terms_kernel(
    R, C, dg_hbm, du_hbm, wg_hbm, wu_hbm, b_hbm,
    sum_ref, up_hbm, gate_ref,
    dg, du, wg, wu, b, terms, held, stage, exchanged, arrived,
    load, tile_load, store, send, recv, *semaphores,
):
    me, right, left = ring_places(C)
    D, F = wg.shape
    T = dg.shape[0]
    rows = T // C
    width = D // C

    def fetch(source, target, semaphore):
        copy = pltpu.make_async_copy(source, target, semaphore)
        copy.start()
        return copy

    def chunk(s):
        return pl.ds(pl.multiple_of(lax.rem(me + 2 * C - 1 - s, C) * rows, rows), rows)

    grads_in = []
    for s in range(C):
        part = chunk(s)
        grads_in.append(
            (fetch(dg_hbm.at[part, :], dg.at[part, :], load.at[2 * s]), fetch(du_hbm.at[part, :], du.at[part, :], load.at[2 * s + 1]))
        )
        if s == 0:
            weights_in = []
            for n in range(C):
                cut = pl.ds(n * width, width)
                weights_in.append(
                    (fetch(wg_hbm.at[cut, :], wg.at[cut, :], tile_load.at[2 * n]), fetch(wu_hbm.at[cut, :], wu.at[cut, :], tile_load.at[2 * n + 1]))
                )
    b_in = fetch(b_hbm, b, load.at[2 * C])
    place, depth = row_of(R), D // R

    def block(places):
        return wu.at[pl.ds(pl.multiple_of(places * depth, depth), depth), :]

    sums = RowSum(R, lambda i: block(place(i)), lambda i: block(place(i, True)), exchanged, arrived, semaphores)
    greet([{"col": left}] + sums.peers, 1 + len(sums.peers))

    def term_tile(s, part, n):
        cut = pl.ds(pl.multiple_of(n * width, width), width)
        total = dot_nt(dg[part, :], wg[cut, :]) + dot_nt(du[part, :], wu[cut, :])
        terms[s, :, cut] = total.astype(BF)

    ring = SumRing(C, terms, held, send, recv)

    for s in range(C):
        part = chunk(s)
        for copy in grads_in[s]:
            copy.wait()
        if s == 0:
            for n in range(C):
                for copy in weights_in[n]:
                    copy.wait()
                term_tile(s, part, n)
            ring.start()
        else:

            def body(n, carry):
                term_tile(s, part, n)
                return carry

            lax.fori_loop(0, C, body, 0)
    b_in.wait()

    def stored(target, t, slot):
        cut = pl.ds(pl.multiple_of(t * width, width), width)
        return pltpu.make_async_copy(stage.at[slot], target.at[cut, :], store.at[slot])

    def product(right_ref, target):
        def body(t, carry):
            slot = lax.rem(t, 2)

            @pl.when(t >= 2)
            def _():
                stored(target, t, slot).wait()

            left_tile = b[:, pl.ds(pl.multiple_of(t * width, width), width)]
            stage[slot] = dot_tn(left_tile, right_ref[...]).astype(BF)
            stored(target, t, slot).start()
            return carry

        lax.fori_loop(0, C, body, 0)
        for slot in range(2):
            stored(target, slot, slot).wait()

    middle = max(1, (C - 1) // 2)
    for step in range(1, middle + 1):
        if step < C - 1:
            ring.pass_on(step)

    def gate_tile(slot):
        cut = pl.ds(pl.multiple_of(lax.div(place(slot), 2) * 2 * depth, 2 * depth), 2 * depth)
        wu[cut, :] = dot_tn(b[:, cut], dg[...]).astype(BF)

    sums.compute_and_relay(gate_tile)
    product(du, up_hbm)
    for step in range(middle + 1, C - 1):
        ring.pass_on(step)
    sums.relay_again()

    def write(part, values):
        gate_ref[part, :] = values.astype(BF)

    sums.finish(write)
    ring.arrived()
    sum_ref[...] = held[C - 2].astype(F32) + terms[C - 1].astype(F32)
    ring.sent()


def norm_terms(R, C, dg, du, w_gate, w_up, b):
    T, F = dg.shape
    D = w_gate.shape[0]
    rows, width = T // C, D // C
    return pl.pallas_call(
        functools.partial(norm_terms_kernel, R, C),
        in_specs=[ANY] * 5,
        out_specs=[VMEM_SPEC, ANY, VMEM_SPEC],
        out_shape=[struct((rows, D), F32), struct((D, F), BF), struct((D // R, F), BF)],
        scratch_shapes=[
            pltpu.VMEM((T, F), BF),
            pltpu.VMEM((T, F), BF),
            pltpu.VMEM((D, F), BF),
            pltpu.VMEM((D, F), BF),
            pltpu.VMEM((T, D), BF),
            pltpu.VMEM((C, rows, D), BF),
            pltpu.VMEM((C - 1, rows, D), BF),
            pltpu.VMEM((2, width, F), BF),
        ]
        + row_sum_buffers(R, D // R, F)
        + [
            DMA((2 * C + 1,)),
            DMA((2 * C,)),
            DMA((2,)),
            DMA((C - 1,)),
            DMA((C - 1,)),
        ]
        + row_sum_semaphores(R),
        compiler_params=comm_params(3, 63),
        cost_estimate=cost(9e10, 70 * MIB),
        name="norm_terms",
    )(dg, du, w_gate, w_up, b)


def attend_back_kernel(
    R, C, sum_ref, log_ref, segk_ref, segq_ref, cos_ref, sin_ref,
    q_hbm, k_hbm, v_hbm, h_hbm, dys_hbm, w_hbm, gate_hbm,
    dq_ref, dk_ref, dv_ref, gate_ref, dhs_hbm,
    h, dy, w, dh, out, q_ref, k_ref, v_ref, do_ref, dk_sum, dv_sum, own, exchanged, arrived,
    load, w_load, local, h_send, h_recv, o_send, o_recv, own_load, *semaphores,
):
    me, right, left = ring_places(C)
    rows, D = sum_ref.shape
    T, width = q_ref.shape
    heads, bq = width // HEAD_DIM, 256
    mine = pl.ds(pl.multiple_of(me * rows, rows), rows)
    first_in = [
        pltpu.make_async_copy(h_hbm.at[mine, :], h, load.at[0]),
        pltpu.make_async_copy(dys_hbm.at[:, mine, :], dy, load.at[1]),
    ]
    head_loads = [
        pltpu.make_async_copy(source, target, load.at[2 + i])
        for i, (source, target) in enumerate(((q_hbm, q_ref), (k_hbm, k_ref), (v_hbm, v_ref)))
    ]
    for copy in first_in:
        copy.start()
    order = [lax.rem(me + k, C) for k in range(1, C)] + [me]
    cuts = [pl.ds(pl.multiple_of(place * width, width), width) for place in order]
    loads = [pltpu.make_async_copy(w_hbm.at[:, order[k]], w.at[k], w_load.at[k]) for k in range(C)]
    sums, own_loads = held_row_sum(R, gate_hbm, own, exchanged, arrived, own_load, semaphores)
    for copy in loads + own_loads + head_loads:
        copy.start()
    greet([{"col": lax.rem(me + k, C)} for k in range(1, C)] + sums.peers, C - 1 + len(sums.peers))
    for slot in sums.order():
        sums.exchange(slot).start()
    for copy in first_in:
        copy.wait()
    grad = sum_ref[...]
    centre, inverse = norm_rows(h[...])
    normed = (h[...] - centre) * inverse
    first = jnp.mean(grad, axis=1, keepdims=True)
    second = jnp.mean(grad * normed, axis=1, keepdims=True)
    dh[...] = (beside(dy).astype(F32) + inverse * (grad - first - normed * second)).astype(BF)
    do_copies, dh_copies = [], []
    for k in range(C):
        loads[k].wait()
        out[k] = dot_nn(dh[...], w[k].reshape(D, width)).astype(BF)
        if k < C - 1:
            copy = remote(out.at[k], do_ref.at[mine, :], o_send.at[k], o_recv.at[k], col=order[k])
        else:
            copy = pltpu.make_async_copy(out.at[k], do_ref.at[mine, :], local.at[0])
        copy.start()
        do_copies.append(copy)
    sums.relay(lambda slot: own_loads[slot].wait())
    for copy in do_copies[:-1]:
        copy.wait_recv()
    do_copies[-1].wait()
    for k in range(C):
        if k < C - 1:
            copy = remote(dh.at[:, cuts[k]], dhs_hbm.at[mine, :], h_send.at[k], h_recv.at[k], col=order[k])
        else:
            copy = pltpu.make_async_copy(dh.at[:, cuts[k]], dhs_hbm.at[mine, :], local.at[1])
        copy.start()
        dh_copies.append(copy)
    for copy in head_loads:
        copy.wait()

    def one_head(head, carry):
        columns = pl.ds(pl.multiple_of(head * HEAD_DIM, HEAD_DIM), HEAD_DIM)
        dk_sum[...] = jnp.zeros_like(dk_sum)
        dv_sum[...] = jnp.zeros_like(dv_sum)
        for first in range(0, T, SEQ):
            for start in range(first, first + SEQ, bq):
                stop = start + bq
                keys = k_ref[first:stop, columns]
                queries = q_ref[start:stop, columns]
                grads = do_ref[start:stop, columns]
                scores = dot_nt(keys, queries) * SCALE
                allowed = allowed_block(segk_ref[first:stop], segq_ref[:, start:stop], start - first)
                scores = jnp.where(allowed, scores, MASKED)
                probs = jnp.exp(scores - log_ref[head, :, start:stop])
                dv_sum[first:stop] += dot_nn(probs.astype(BF), grads)
                grad_probs = dot_nt(v_ref[first:stop, columns], grads)
                inner = jnp.sum(probs * grad_probs, axis=0, keepdims=True)
                grad_scores = (probs * (grad_probs - inner)).astype(BF)
                dk_sum[first:stop] += dot_nn(grad_scores, queries)
                grad_query = dot_tn(keys, grad_scores).T * SCALE
                dq_ref[start:stop, columns] = turn(grad_query, cos_ref[start:stop], -sin_ref[start:stop]).astype(BF)
        dk_ref[:, columns] = turn(dk_sum[...] * SCALE, cos_ref[...], -sin_ref[...]).astype(BF)
        dv_ref[:, columns] = dv_sum[...].astype(BF)
        return carry

    lax.fori_loop(0, heads // 2, one_head, 0)
    sums.relay_again()
    lax.fori_loop(heads // 2, heads, one_head, 0)

    def write(part, values):
        gate_ref[part, :] = values.astype(BF)

    sums.finish(write)
    for copy in do_copies[:-1]:
        copy.wait_send()
    for copy in dh_copies:
        copy.wait()


def attend_back(R, total, log_total, seg_column, seg_row, cos_table, sin_table, q, k, v, h, dys, w_out, grad_gate):
    C, T, width = dys.shape
    rows, D = total.shape
    depth, columns = grad_gate.shape[1:]
    one = pltpu.VMEM((T, width), BF)
    return pl.pallas_call(
        functools.partial(attend_back_kernel, R, C),
        in_specs=[VMEM_SPEC] * 6 + [ANY] * 7,
        out_specs=[VMEM_SPEC] * 4 + [ANY],
        out_shape=[struct((T, width), BF)] * 3 + [struct((depth, columns), BF), struct((T, width), BF)],
        scratch_shapes=[
            pltpu.VMEM((rows, D), F32),
            pltpu.VMEM((C, rows, width), BF),
            pltpu.VMEM((C, R, D // R, width), BF),
            pltpu.VMEM((rows, D), BF),
            pltpu.VMEM((C, rows, width), BF),
            one,
            one,
            one,
            one,
            pltpu.VMEM((T, HEAD_DIM), F32),
            pltpu.VMEM((T, HEAD_DIM), F32),
            pltpu.VMEM((R // 2, depth, columns), BF),
        ]
        + row_sum_buffers(R, depth, columns)
        + [
            DMA((5,)),
            DMA((C,)),
            DMA((2,)),
            DMA((C - 1,)),
            DMA((C - 1,)),
            DMA((C - 1,)),
            DMA((C - 1,)),
            DMA((R // 2,)),
        ]
        + row_sum_semaphores(R),
        compiler_params=comm_params(5),
        cost_estimate=cost(5e10, 30 * MIB),
        name="attend_back",
    )(total, log_total, seg_column, seg_row, cos_table, sin_table, q, k, v, h, dys, w_out, grad_gate)


def input_terms_kernel(
    R, C, dq_ref, dk_ref, dv_ref, mu_hbm, r_hbm, w_hbm, a_hbm, x_hbm, dh_hbm, os_hbm,
    y_ref, gq_ref, gk_ref, gv_ref, out_ref,
    mu_ref, r_ref, w_ref, a_ref, x_ref, dh_ref, block, product, mine, by_column, by_row,
    terms, held, stats, stats_in, tiles, q_exchanged, q_arrived, o_tiles, o_exchanged, o_arrived,
    send, recv, s_send, s_recv, w_load, late_load, block_load, c_send, c_recv, r_send, r_recv, local, *semaphores,
):
    me, right, left = ring_places(C)
    T, width = dq_ref.shape
    D = width * C
    heads = (dq_ref, dk_ref, dv_ref)
    row = lax.axis_index("row")
    thin = width // R

    def cut_of(s):
        return pl.ds(pl.multiple_of(lax.rem(me + 2 * C - 1 - s, C) * width, width), width)

    def weight_in(s):
        return pltpu.make_async_copy(w_hbm.at[:, cut_of(s), :], w_ref.at[:, cut_of(s), :], w_load.at[s])

    for s in range(C):
        weight_in(s).start()
    late = [
        pltpu.make_async_copy(source, target, late_load.at[i])
        for i, (source, target) in enumerate(
            ((a_hbm, a_ref), (x_hbm, x_ref), (dh_hbm, dh_ref), (mu_hbm, mu_ref), (r_hbm, r_ref))
        )
    ]
    for copy in late:
        copy.start()
    depth = tiles.shape[2]
    side = lax.rem(lax.axis_index("row"), 2)
    q_sums = RowSum(
        R, lambda i: tiles.at[i, side], lambda i: tiles.at[i, 1 - side], q_exchanged, q_arrived, semaphores[:4]
    )
    o_sums = RowSum(
        R, lambda i: o_tiles.at[i, side], lambda i: o_tiles.at[i, 1 - side], o_exchanged, o_arrived, semaphores[4:]
    )

    def block_in(i):
        return [
            pltpu.make_async_copy(
                os_hbm.at[i, n], block.at[i % 2, :, pl.ds(n * HEAD_DIM, HEAD_DIM)], block_load.at[i % 2, n]
            )
            for n in range(os_hbm.shape[1])
        ]

    for copy in block_in(0) + block_in(1):
        copy.start()
    greet(
        [{"col": lax.rem(me + k, C)} for k in range(1, C)] + [{"row": lax.rem(row + k, R)} for k in range(1, R)],
        C + R - 2,
    )

    ring = SumRing(C, terms, held, send, recv)

    def compute(s):
        cut = cut_of(s)
        weight_in(s).wait()
        total = dot_nt(dq_ref[...], w_ref[0, cut, :])
        total += dot_nt(dk_ref[...], w_ref[1, cut, :])
        total += dot_nt(dv_ref[...], w_ref[2, cut, :])
        terms[s] = total.astype(BF)

    compute(0)
    ring.start()

    def body(s, carry):
        compute(s)
        return carry

    late[2].wait()
    for j in range(C):
        for copy in block_in(j):
            copy.wait()
        product[...] = dot_tn(block[j % 2], dh_ref[...]).astype(BF)
        for slot in range(R // 2):
            for place in range(2):
                rows = 2 * lax.div(o_sums.places(slot), 2) + place
                o_tiles[slot, place, j * thin : (j + 1) * thin] = product[pl.ds(pl.multiple_of(rows * thin, thin), thin), :]
        if j + 2 < C:
            for copy in block_in(j + 2):
                copy.start()
    for slot in o_sums.order():
        o_sums.exchange(slot).start()
    o_sums.relay()
    lax.fori_loop(1, C, body, 0)
    for i, copy in enumerate(late):
        if i != 2:
            copy.wait()

    def qkv_tile(slot):
        start = pl.multiple_of(lax.div(q_sums.places(slot), 2) * 2 * depth, 2 * depth)
        left_tile = a_ref[:, pl.ds(start, 2 * depth)]
        for i, right_side in enumerate(heads):
            product = dot_tn(left_tile, right_side[...]).astype(BF)
            tiles[slot, 0, :, i * width : (i + 1) * width] = product[:depth]
            tiles[slot, 1, :, i * width : (i + 1) * width] = product[depth:]

    q_sums.compute_and_relay(qkv_tile)
    o_sums.relay_again()
    ring.pass_on(1)

    def write_out(part, values):
        mine[part, :] = values.astype(BF)

    o_sums.finish(write_out)
    columns_out = []
    for k in range(1, C):
        place = lax.rem(me + k, C)
        rows = pl.ds(pl.multiple_of(place * thin, thin), thin)
        columns_out.append(remote(mine.at[rows, :], by_column.at[me], c_send.at[k - 1], c_recv.at[k - 1], col=place))
    stay = pltpu.make_async_copy(
        mine.at[pl.ds(pl.multiple_of(me * thin, thin), thin), :], by_column.at[me], local.at[0]
    )
    for copy in columns_out + [stay]:
        copy.start()
    size = 128

    def sum_rows(i, carry):
        rows = pl.ds(pl.multiple_of(i * size, size), size)
        lane = lax.broadcasted_iota(jnp.int32, (size, 128), 1)
        total = jnp.zeros((size, 1), F32)
        second = jnp.zeros((size, 1), F32)
        for s in range(C):
            grad = terms[s, rows, :].astype(F32)
            total += jnp.sum(grad, axis=1, keepdims=True)
            second += jnp.sum(grad * a_ref[rows, cut_of(s)].astype(F32), axis=1, keepdims=True)
        packed = jnp.where(lane == 0, total, jnp.where(lane == 1, second, 0.0))
        stats[:, rows] = packed.T[:8]
        return carry

    lax.fori_loop(0, T // size, sum_rows, 0)
    exchanges = [
        remote(stats, stats_in.at[k - 1], s_send.at[k - 1], s_recv.at[k - 1], col=lax.rem(me + k, C)) for k in range(1, C)
    ]
    for copy in exchanges:
        copy.start()
    for step in range(2, C - 1):
        ring.pass_on(step)
    for copy in columns_out:
        copy.wait_recv()
    stay.wait()

    def piece_of(place):
        return by_column.at[lax.div(place * C, R), :, pl.ds(pl.multiple_of(lax.rem(place, R // C) * depth, depth), depth)]

    rows_out = []
    for k in range(1, R):
        place = lax.rem(row + k, R)
        rows_out.append(remote(piece_of(place), by_row.at[row], r_send.at[k - 1], r_recv.at[k - 1], row=place))
    keep = pltpu.make_async_copy(piece_of(row), by_row.at[row], local.at[1])
    for copy in rows_out + [keep]:
        copy.start()
    q_sums.relay_again()
    for copy in rows_out:
        copy.wait_recv()
    keep.wait()
    for n in range(R):
        out_ref[n * thin : (n + 1) * thin, :] = by_row[n]

    def write_qkv(part, values):
        for i, target in enumerate((gq_ref, gk_ref, gv_ref)):
            target[part, :] = values[:, i * width : (i + 1) * width].astype(BF)

    q_sums.finish(write_qkv)
    for copy in exchanges:
        copy.wait_recv()
    ring.arrived()

    def last_rows(i, carry):
        rows = pl.ds(pl.multiple_of(i * size, size), size)
        both = stats[:, rows]
        for k in range(C - 1):
            both += stats_in[k, :, rows]
        columns = jnp.concatenate([both, jnp.zeros((120, size), F32)], axis=0).T * (1.0 / D)
        normed = (x_ref[rows, :].astype(F32) - mu_ref[rows, :]) * r_ref[rows, :]
        grad = held[C - 2, rows, :].astype(F32) + terms[C - 1, rows, :].astype(F32)
        grad = grad - columns[:, 0:1] - normed * columns[:, 1:2]
        y_ref[rows, :] = (dh_ref[rows, :].astype(F32) + r_ref[rows, :] * grad).astype(BF)
        return carry

    lax.fori_loop(0, T // size, last_rows, 0)
    for copy in exchanges + columns_out + rows_out:
        copy.wait_send()
    ring.sent()


def input_terms(R, C, dq, dk, dv, w_qkv, a, tokens, dh, mu, r, os):
    T, width = dq.shape
    D = w_qkv.shape[1]
    half, low = R // 2, D // R
    thin = width // R
    return pl.pallas_call(
        functools.partial(input_terms_kernel, R, C),
        in_specs=[VMEM_SPEC] * 3 + [ANY] * 7,
        out_specs=[VMEM_SPEC] * 5,
        out_shape=[struct((T, width), BF)]
        + [struct((low, width), BF)] * 3
        + [struct((width, low), BF)],
        scratch_shapes=[
            pltpu.VMEM((T, 1), F32),
            pltpu.VMEM((T, 1), F32),
            pltpu.VMEM((3, D, width), BF),
            pltpu.VMEM((T, D), BF),
            pltpu.VMEM((T, width), BF),
            pltpu.VMEM((T, width), BF),
            pltpu.VMEM((2, T, width), BF),
            pltpu.VMEM((width, width), BF),
            pltpu.VMEM((C * thin, width), BF),
            pltpu.VMEM((C, thin, width), BF),
            pltpu.VMEM((R, thin, low), BF),
            pltpu.VMEM((C, T, width), BF),
            pltpu.VMEM((C - 1, T, width), BF),
            pltpu.VMEM((8, T), F32),
            pltpu.VMEM((C - 1, 8, T), F32),
            pltpu.VMEM((half, 2, low, 3 * width), BF),
        ]
        + row_sum_buffers(R, low, 3 * width)
        + [pltpu.VMEM((half, 2, C * thin, width), BF)]
        + row_sum_buffers(R, C * thin, width)
        + [
            DMA((C - 1,)),
            DMA((C - 1,)),
            DMA((C - 1,)),
            DMA((C - 1,)),
            DMA((C,)),
            DMA((5,)),
            DMA((2, os.shape[1])),
            DMA((C - 1,)),
            DMA((C - 1,)),
            DMA((R - 1,)),
            DMA((R - 1,)),
            DMA((2,)),
        ]
        + row_sum_semaphores(R)
        + row_sum_semaphores(R),
        compiler_params=comm_params(6, 63),
        cost_estimate=cost(8e10, 20 * MIB),
        name="input_terms",
    )(dq, dk, dv, mu, r, w_qkv, a, tokens, dh, os)


def results_kernel(*refs):
    half = len(refs) // 2
    for source, target in zip(refs[:half], refs[half:]):
        target[...] = source[...].astype(target.dtype)


def results(*values):
    shapes = [struct(value.shape, BF if i < 2 else F32) for i, value in enumerate(values)]
    return pl.pallas_call(
        results_kernel,
        in_specs=[VMEM_SPEC] * len(values),
        out_specs=[VMEM_SPEC] * len(values),
        out_shape=shapes,
        compiler_params=params(),
        cost_estimate=cost(1e6, 16 * MIB),
        name="results",
    )(*values)


def on_device(R, C, tokens, cotangent, segments, w_query, w_key, w_value, w_out, w_gate, w_up, w_down):
    T, width = tokens.shape
    D = width * C
    gathered = lambda w: lax.all_gather(w, "row", axis=0, tiled=True)

    gate_w, up_w = gathered(w_gate), gathered(w_up)
    seg_row = segments.reshape(1, T)
    xs, w_qkv, cos_table, sin_table, seg_column, out_part, down_part = first_gather(
        R, C, seg_row, tokens, w_query, w_key, w_value, w_out, w_down
    )
    w_qkv = w_qkv.reshape(3, D, width)
    act_one, q, k, v, mu_one, r_one, out_part = norm_and_project(xs, w_qkv, cos_table, sin_table, out_part)
    os, log_total, out_w = attend(R, C, q, k, v, seg_column, seg_row, out_part)
    h_full, act_two, dg, du, dys, _, output, grad_down = feed_forward(
        R, C, os, out_w, xs, gate_w, up_w, down_part, cotangent
    )
    total, grad_up, grad_gate = norm_terms(R, C, dg, du, gate_w, up_w, act_two)
    grad_up = grad_up.reshape(R, D // R, -1)
    dq, dk, dv, grad_up, dh = attend_back(
        R, total, log_total, seg_column, seg_row, cos_table, sin_table, q, k, v, h_full, dys, out_w, grad_up
    )
    grad_tokens, grad_query, grad_key, grad_value, grad_out = input_terms(
        R, C, dq, dk, dv, w_qkv, act_one, tokens, dh, mu_one, r_one, os
    )
    return tuple(
        results(output, grad_tokens, grad_query, grad_key, grad_value, grad_out, grad_gate, grad_up, grad_down)
    )


def solution(mesh):
    here = P("row", "col")
    turned = P("col", "row")
    return jax.shard_map(
        functools.partial(on_device, mesh.shape["row"], mesh.shape["col"]),
        mesh=mesh,
        in_specs=(here, here, P("row"), here, here, here, turned, here, here, turned),
        out_specs=(here, here, here, here, here, turned, here, here, turned),
        check_vma=False,
    )
```

```python
import functools

import jax
import jax.numpy as jnp
from jax import lax
from jax.experimental import pallas as pl
from jax.experimental.pallas import tpu as pltpu
from jax.sharding import PartitionSpec as P

HEAD_DIM = 128
HALF = HEAD_DIM // 2
SEQ = 1024
EPSILON = 1e-05
MASKED = -1e30
SCALE = HEAD_DIM ** (-0.5)
BF = jnp.bfloat16
F32 = jnp.float32
MIB = 1 << 20
ANY = pl.BlockSpec(memory_space=pl.ANY)


def dot_nn(left, right):
    return jnp.dot(left, right, preferred_element_type=F32)


def dot_tn(left, right):
    return lax.dot_general(left, right, (((0,), (0,)), ((), ())), preferred_element_type=F32)


def dot_nt(left, right):
    return lax.dot_general(left, right, (((1,), (1,)), ((), ())), preferred_element_type=F32)


def struct(shape, dtype):
    return jax.ShapeDtypeStruct(shape, dtype)


def params(mib=60):
    return pltpu.CompilerParams(vmem_limit_bytes=mib * MIB)


def cost(flops, moved):
    return pl.CostEstimate(flops=int(flops), bytes_accessed=int(moved), transcendentals=0)


def turn(values, cos_table, sin_table):
    return values * cos_table + pltpu.roll(values, HALF, 1) * sin_table


MESH = pl.DeviceIdType.MESH
VMEM_SPEC = pl.BlockSpec(memory_space=pltpu.VMEM)
DMA = pltpu.SemaphoreType.DMA


def comm_params(number, mib=60):
    return pltpu.CompilerParams(vmem_limit_bytes=mib * MIB, collective_id=number, has_side_effects=True)


def remote(source, target, send, recv, **device):
    return pltpu.make_async_remote_copy(
        src_ref=source, dst_ref=target, send_sem=send, recv_sem=recv, device_id=device, device_id_type=MESH
    )


def greet(senders, targets):
    semaphore = pltpu.get_barrier_semaphore()
    for device in senders:
        pl.semaphore_signal(semaphore, inc=1, device_id=device, device_id_type=MESH)
    pl.semaphore_wait(semaphore, targets)


def ring_places(C):
    me = lax.axis_index("col")
    return me, lax.rem(me + 1, C), lax.rem(me + C - 1, C)


def row_places(R):
    row = lax.axis_index("row")
    ahead = [lax.rem(row + 2 * k, R) for k in range(R // 2)]
    behind = [lax.rem(row + R - 2 * k, R) for k in range(R // 2)]
    other = row + 1 - 2 * lax.rem(row, 2)
    return row, ahead, behind, other


class GatherRing:
    def __init__(self, C, source, whole, send, recv):
        me, right, left = ring_places(C)
        self.C = C
        size = source.shape[0] // 2
        self.copies = []
        for step in range(C - 1):
            owner = lax.rem(me - step + C, C)
            pair = []
            for half in range(2):
                rows = pl.ds(half * size, size)
                piece = source.at[rows, :] if step == 0 else whole.at[owner, rows, :]
                pair.append(
                    remote(piece, whole.at[owner, rows, :], send.at[step, half], recv.at[step, half], col=right)
                )
            self.copies.append(pair)

    def start(self):
        for copy in self.copies[0]:
            copy.start()

    def pass_on(self, step):
        for half in range(2):
            self.copies[step - 1][half].wait_recv()
            self.copies[step][half].start()

    def arrived(self):
        for copy in self.copies[-1]:
            copy.wait_recv()

    def sent(self):
        for pair in self.copies:
            for copy in pair:
                copy.wait_send()


def gather_kernel(
    R, C, segq_ref, rate_ref, wo_ref, wd_ref, x_ref, wq_ref, wk_ref, wv_ref,
    xs_ref, w_ref, cos_ref, sin_ref, segk_ref, wo_turned, wd_turned,
    local, x_send, x_recv, w_send, w_recv, f_send, f_recv,
):
    me, right, left = ring_places(C)
    row, ahead, behind, other = row_places(R)
    weights = (wq_ref, wk_ref, wv_ref)
    mine = [
        pltpu.make_async_copy(x_ref, xs_ref.at[me], local.at[0]),
    ] + [pltpu.make_async_copy(w, w_ref.at[i, row], local.at[1 + i]) for i, w in enumerate(weights)]
    for copy in mine:
        copy.start()
    greet(
        [{"col": left}, {"row": other}] + [{"row": r} for r in behind[1:]],
        1 + R // 2,
    )

    ring = GatherRing(C, x_ref, xs_ref, x_send, x_recv)
    ring.start()
    spread, forward = [], []
    for i, w in enumerate(weights):
        for k in range(1, R // 2):
            copy = remote(w, w_ref.at[i, row], w_send.at[i, k], w_recv.at[i, k], row=ahead[k])
            copy.start()
            spread.append(copy)
        copy = remote(w, w_ref.at[i, row], f_send.at[i, 0], f_recv.at[i, 0], row=other)
        copy.start()
        forward.append(copy)
    T = cos_ref.shape[0]
    size = 128

    def table_rows(i, carry):
        rows = pl.ds(pl.multiple_of(i * size, size), size)
        first = SEQ * lax.div(i * size, SEQ)
        here = jnp.broadcast_to(segq_ref[:, rows].astype(F32), (size, size)).T[:, :1]
        segk_ref[rows, :] = here.astype(jnp.int32)
        shape = (size, T)
        queries = lax.broadcasted_iota(jnp.int32, shape, 0) + i * size
        keys = lax.broadcasted_iota(jnp.int32, shape, 1)
        seen = (here == segq_ref[...].astype(F32)) & (keys <= queries) & (keys >= first)
        place = jnp.sum(jnp.where(seen, 1.0, 0.0), axis=1, keepdims=True) - 1.0
        angles = place * rate_ref[...]
        lane = lax.broadcasted_iota(jnp.int32, angles.shape, 1)
        sine = jnp.sin(angles)
        cos_ref[rows, :] = jnp.cos(angles)
        sin_ref[rows, :] = jnp.where(lane < HALF, -sine, sine)
        return carry

    lax.fori_loop(0, T // size, table_rows, 0)

    def turn_rows(source, target):
        def body(i, carry):
            cut = pl.ds(pl.multiple_of(i * size, size), size)
            target[:, cut] = source[cut, :].astype(F32).T.astype(BF)
            return carry

        lax.fori_loop(0, source.shape[0] // size, body, 0)

    turn_rows(wo_ref, wo_turned)
    turn_rows(wd_ref, wd_turned)
    for s in range(1, C - 1):
        ring.pass_on(s)
    for i in range(3):
        for k in range(1, R // 2):
            spread[i * (R // 2 - 1) + k - 1].wait_recv()
            block = w_ref.at[i, behind[k]]
            copy = remote(block, block, f_send.at[i, k], f_recv.at[i, k], row=other)
            copy.start()
            forward.append(copy)
    ring.arrived()
    for copy in forward:
        copy.wait_recv()
    ring.sent()
    for copy in spread + forward:
        copy.wait_send()
    for copy in mine:
        copy.wait()


def first_gather(R, C, seg_row, tokens, w_query, w_key, w_value, w_out, w_down):
    depth, width = w_query.shape
    T = tokens.shape[0]
    half = R // 2
    rate = 10000.0 ** (-(jnp.arange(HALF, dtype=F32) * 2.0 / HEAD_DIM))
    rate = jnp.concatenate([rate, rate]).reshape(1, HEAD_DIM)
    return pl.pallas_call(
        functools.partial(gather_kernel, R, C),
        in_specs=[VMEM_SPEC] * 4 + [ANY] * 4,
        out_specs=[ANY] * 2 + [VMEM_SPEC] * 5,
        out_shape=[
            struct((C,) + tokens.shape, BF),
            struct((3, R, depth, width), BF),
            struct((T, HEAD_DIM), F32),
            struct((T, HEAD_DIM), F32),
            struct((T, 1), jnp.int32),
            struct(w_out.shape[::-1], BF),
            struct(w_down.shape[::-1], BF),
        ],
        scratch_shapes=[
            DMA((4,)),
            DMA((C - 1, 2)),
            DMA((C - 1, 2)),
            DMA((3, half)),
            DMA((3, half)),
            DMA((3, half)),
            DMA((3, half)),
        ],
        compiler_params=comm_params(0),
        cost_estimate=cost(6e10, 14 * MIB),
        name="first_gather",
    )(seg_row, rate, w_out, w_down, tokens, w_query, w_key, w_value)


def norm_rows(x):
    centre = jnp.mean(x, axis=-1, keepdims=True)
    spread = jnp.mean(x * x, axis=-1, keepdims=True) - centre * centre
    inverse = lax.rsqrt(spread + EPSILON)
    return centre, inverse


def beside(ref):
    return jnp.concatenate([ref[j] for j in range(ref.shape[0])], axis=1)


def qkv_kernel(
    C, xs_ref, w_ref, cos_ref, sin_ref, wo_ref, a_ref, q_ref, k_ref, v_ref, mu_ref, r_ref, wos_ref, local, send, recv
):
    step, steps = pl.program_id(0), pl.num_programs(0)
    me, right, left = ring_places(C)
    ring = GatherRing(C, wo_ref, wos_ref, send, recv)
    mine = pltpu.make_async_copy(wo_ref, wos_ref.at[me], local.at[0])

    @pl.when(step == 0)
    def _():
        mine.start()
        greet([{"col": left}], 1)
        ring.start()

    @pl.when(step == steps // 2)
    def _():
        ring.pass_on(1)

    x = beside(xs_ref).astype(F32)
    centre, inverse = norm_rows(x)
    a = ((x - centre) * inverse).astype(BF)
    a_ref[...] = a
    mu_ref[...] = centre
    r_ref[...] = inverse
    cosine, sine = cos_ref[...], sin_ref[...]
    for index, out in enumerate((q_ref, k_ref, v_ref)):
        product = dot_nn(a, w_ref[index])
        if index == 2:
            out[...] = product.astype(BF)
            continue
        for start in range(0, out.shape[1], HEAD_DIM):
            part = product[:, start : start + HEAD_DIM]
            out[:, start : start + HEAD_DIM] = turn(part, cosine, sine).astype(BF)

    @pl.when(step == steps - 1)
    def _():
        for s in range(2, C - 1):
            ring.pass_on(s)
        ring.arrived()
        ring.sent()
        mine.wait()


def norm_and_project(xs, w_qkv, cos_table, sin_table, w_out):
    C, T, width = xs.shape
    D = width * C
    bt = 256
    rows = lambda n: pl.BlockSpec((bt, n), lambda i: (i, 0))
    return pl.pallas_call(
        functools.partial(qkv_kernel, C),
        grid=(T // bt,),
        in_specs=[
            pl.BlockSpec((C, bt, width), lambda i: (0, i, 0)),
            pl.BlockSpec(w_qkv.shape, lambda i: (0, 0, 0), pipeline_mode=pl.Buffered(1)),
            rows(HEAD_DIM),
            rows(HEAD_DIM),
            ANY,
        ],
        out_specs=[rows(D), rows(width), rows(width), rows(width), rows(1), rows(1), ANY],
        out_shape=[
            struct((T, D), BF),
            struct((T, width), BF),
            struct((T, width), BF),
            struct((T, width), BF),
            struct((T, 1), F32),
            struct((T, 1), F32),
            struct((C,) + w_out.shape, BF),
        ],
        scratch_shapes=[DMA((1,)), DMA((C - 1, 2)), DMA((C - 1, 2))],
        compiler_params=comm_params(7),
        cost_estimate=cost(2e10, 14 * MIB),
        name="norm_and_project",
    )(xs, w_qkv, cos_table, sin_table, w_out)


def allowed_block(seg_key, seg_query, first_query):
    shape = (seg_key.shape[0], seg_query.shape[1])
    keys = lax.broadcasted_iota(jnp.int32, shape, 0)
    queries = lax.broadcasted_iota(jnp.int32, shape, 1) + first_query
    return (seg_key == seg_query) & (keys <= queries)


def attend_kernel(
    R, C, q_ref, k_ref, v_ref, segk_ref, segq_ref, wos_ref, os_ref, log_ref, w_ref,
    o_buf, local, o_send, o_recv, w_send, w_recv, f_send, f_recv,
):
    me, right, left = ring_places(C)
    row, ahead, behind, other = row_places(R)
    T, width = q_ref.shape
    heads, bq = width // HEAD_DIM, 256
    greet([{"col": left}, {"row": other}] + [{"row": r} for r in behind[1:]], 1 + R // 2)
    mine = pltpu.make_async_copy(wos_ref, w_ref.at[row], local.at[0])
    mine.start()
    spread, forward = [], []
    for k in range(1, R // 2):
        copy = remote(wos_ref, w_ref.at[row], w_send.at[k], w_recv.at[k], row=ahead[k])
        copy.start()
        spread.append(copy)
    copy = remote(wos_ref, w_ref.at[row], f_send.at[0], f_recv.at[0], row=other)
    copy.start()
    forward.append(copy)

    def ring(step, head):
        owner = lax.rem(me - step + C, C)
        piece = o_buf.at[head] if step == 0 else os_ref.at[owner, head]
        return remote(piece, os_ref.at[owner, head], o_send.at[step, head], o_recv.at[step, head], col=right)

    def one_head(head, carry):
        columns = pl.ds(pl.multiple_of(head * HEAD_DIM, HEAD_DIM), HEAD_DIM)
        for first in range(0, T, SEQ):
            for start in range(first, first + SEQ, bq):
                stop = start + bq
                scores = dot_nt(k_ref[first:stop, columns], q_ref[start:stop, columns]) * SCALE
                allowed = allowed_block(segk_ref[first:stop], segq_ref[:, start:stop], start - first)
                scores = jnp.where(allowed, scores, MASKED)
                peak = jnp.max(scores, axis=0, keepdims=True)
                exponent = jnp.exp(scores - peak)
                total = jnp.sum(exponent, axis=0, keepdims=True)
                weights = (exponent * (1.0 / total)).astype(BF)
                o_buf[head, start:stop] = dot_tn(v_ref[first:stop, columns], weights).T.astype(BF)
                log_ref[head, :, start:stop] = peak + jnp.log(total)
        ring(0, head).start()
        pltpu.make_async_copy(o_buf.at[head], os_ref.at[me, head], local.at[1 + head]).start()
        return carry

    lax.fori_loop(0, heads, one_head, 0)
    for step in range(1, C - 1):
        for head in range(heads):
            ring(step - 1, head).wait_recv()
            ring(step, head).start()
    for k in range(1, R // 2):
        spread[k - 1].wait_recv()
        block = w_ref.at[behind[k]]
        copy = remote(block, block, f_send.at[k], f_recv.at[k], row=other)
        copy.start()
        forward.append(copy)
    for head in range(heads):
        ring(C - 2, head).wait_recv()
        pltpu.make_async_copy(o_buf.at[head], os_ref.at[me, head], local.at[1 + head]).wait()
        for step in range(C - 1):
            ring(step, head).wait_send()
    for copy in forward:
        copy.wait_recv()
    for copy in spread + forward:
        copy.wait_send()
    mine.wait()


def attend(R, C, q, k, v, seg_column, seg_row, w_part):
    T, width = q.shape
    heads, half = width // HEAD_DIM, R // 2
    return pl.pallas_call(
        functools.partial(attend_kernel, R, C),
        in_specs=[VMEM_SPEC] * 5 + [ANY],
        out_specs=[ANY, VMEM_SPEC, ANY],
        out_shape=[
            struct((C, heads, T, HEAD_DIM), BF),
            struct((heads, 1, T), F32),
            struct((R,) + w_part.shape, BF),
        ],
        scratch_shapes=[
            pltpu.VMEM((heads, T, HEAD_DIM), BF),
            DMA((1 + heads,)),
            DMA((C - 1, heads)),
            DMA((C - 1, heads)),
            DMA((half,)),
            DMA((half,)),
            DMA((half,)),
            DMA((half,)),
        ],
        compiler_params=comm_params(1),
        cost_estimate=cost(7e10, 14 * MIB),
        name="attend",
    )(q, k, v, seg_column, seg_row, w_part)


class SumRing:
    def __init__(self, C, terms, held, send, recv):
        me, right, left = ring_places(C)
        self.C, self.terms, self.held, self.send, self.recv, self.right = C, terms, held, send, recv, right

    def copy(self, step):
        source = self.terms.at[0] if step == 0 else self.held.at[step - 1]
        return remote(source, self.held.at[step], self.send.at[step], self.recv.at[step], col=self.right)

    def start(self):
        self.copy(0).start()

    def pass_on(self, step):
        self.copy(step - 1).wait_recv()
        add_into(self.held.at[step - 1], self.terms.at[step])
        self.copy(step).start()

    def arrived(self):
        self.copy(self.C - 2).wait_recv()

    def sent(self):
        for step in range(self.C - 1):
            self.copy(step).wait_send()


def add_into(held, terms):
    size = 64

    def body(i, carry):
        rows = pl.ds(pl.multiple_of(i * size, size), size)
        held[rows, :] = (held[rows, :].astype(F32) + terms[rows, :].astype(F32)).astype(BF)
        return carry

    lax.fori_loop(0, held.shape[0] // size, body, 0)


class RowSum:
    def __init__(self, R, own, twin, exchanged, arrived, semaphores):
        self.P = R // 4
        self.own, self.twin, self.exchanged, self.arrived = own, twin, exchanged, arrived
        self.x_send, self.x_recv, self.y_send, self.y_recv = semaphores
        self.width = arrived.shape[2]
        self.places = row_of(R)
        self.peers = row_peers(R)

    def part(self, ref, side):
        return ref.at[:, pl.ds(side * self.width, self.width)]

    def exchange(self, slot):
        return remote(
            self.twin(slot), self.exchanged.at[slot], self.x_send.at[slot], self.x_recv.at[slot], row=self.places(0, True)
        )

    def send(self, slot, side, index, target):
        return remote(
            self.part(self.own(slot), side), self.arrived.at[index], self.y_send.at[index], self.y_recv.at[index],
            row=self.places(target),
        )

    def left_one(self, dp):
        return self.send(2 * dp + 1, 0, dp, 1)

    def left_two(self, dp):
        return self.send(2 * dp, 0, self.P + dp - 1, 2 * dp)

    def right_one(self, dp, dq):
        return self.send(2 * dp + dq, 1, 2 * self.P - 1 + 2 * (dp - 1) + dq, 2 * dp)

    def right_two(self):
        return self.send(1, 1, 4 * self.P - 3, 1)

    def order(self):
        return (
            [2 * dp + 1 for dp in range(1, self.P)] + [1] + [2 * dp for dp in range(1, self.P)] + [0]
        )

    def relay_one(self, slot):
        self.exchange(slot).wait_recv()
        add_into(self.own(slot), self.exchanged.at[slot])
        dp, dq = divmod(slot, 2)
        if dq:
            self.left_one(dp).start()
        if dp:
            self.right_one(dp, dq).start()

    def relay(self, before=None):
        for slot in self.order():
            if before is not None:
                before(slot)
            self.relay_one(slot)

    def compute_and_relay(self, compute):
        slots = self.order()
        for i, slot in enumerate(slots):
            compute(slot)
            self.exchange(slot).start()
            if i:
                self.relay_one(slots[i - 1])
        self.relay_one(slots[-1])

    def relay_again(self):
        for dp in range(1, self.P):
            self.left_one(dp).wait_recv()
            add_into(self.part(self.own(2 * dp), 0), self.arrived.at[dp])
            self.left_two(dp).start()
        for dp in range(1, self.P):
            copy = self.right_one(dp, 1)
            copy.wait_recv()
            add_into(self.part(self.own(1), 1), self.arrived.at[2 * self.P - 1 + 2 * (dp - 1) + 1])
        self.right_two().start()

    def finish(self, write, size=64):
        P, width = self.P, self.width
        self.left_one(0).wait_recv()
        self.right_two().wait_recv()
        for dp in range(1, P):
            self.left_two(dp).wait_recv()
            self.right_one(dp, 0).wait_recv()
        lefts = [0] + [P + dp - 1 for dp in range(1, P)]
        rights = [4 * P - 3] + [2 * P - 1 + 2 * (dp - 1) for dp in range(1, P)]

        def body(i, carry):
            rows = pl.ds(pl.multiple_of(i * size, size), size)
            total = self.own(0)[rows, :].astype(F32)
            halves = []
            for side, places in enumerate((lefts, rights)):
                half = total[:, side * width : (side + 1) * width]
                for index in places:
                    half += self.arrived[index, rows, :].astype(F32)
                halves.append(half)
            write(rows, jnp.concatenate(halves, axis=1))
            return carry

        lax.fori_loop(0, self.exchanged.shape[1] // size, body, 0)
        for slot in range(2 * P):
            self.exchange(slot).wait_send()
        self.left_one(0).wait_send()
        self.right_two().wait_send()
        for dp in range(1, P):
            self.left_one(dp).wait_send()
            self.left_two(dp).wait_send()
            self.right_one(dp, 0).wait_send()
            self.right_one(dp, 1).wait_send()


def row_of(R):
    row = lax.axis_index("row")
    side, chip = lax.rem(row, 2), lax.div(row, 2)
    p, q = lax.div(chip, 2), lax.rem(chip, 2)

    def place(slot, twin=False):
        dp, dq = divmod(slot, 2)
        chip_there = 2 * lax.rem(p + dp, R // 4) + lax.rem(q + dq, 2)
        return 2 * chip_there + (1 - side if twin else side)

    return place


def row_peers(R):
    place = row_of(R)
    return [{"row": place(0, True)}, {"row": place(1)}] + [{"row": place(2 * dp)} for dp in range(1, R // 4)]


def row_sum_semaphores(R):
    return [DMA((R // 2,)), DMA((R // 2,)), DMA((R - 2,)), DMA((R - 2,))]


def row_sum_buffers(R, depth, columns):
    return [
        pltpu.VMEM((R // 2, depth, columns), BF),
        pltpu.VMEM((R - 2, depth, columns // 2), BF),
    ]


def held_row_sum(R, grad_hbm, own, exchanged, arrived, load, semaphores):
    place = row_of(R)
    sums = RowSum(R, lambda i: own.at[i], lambda i: grad_hbm.at[place(i, True)], exchanged, arrived, semaphores)
    loads = [pltpu.make_async_copy(grad_hbm.at[place(i)], own.at[i], load.at[i]) for i in range(R // 2)]
    return sums, loads


class LineGather:
    def __init__(self, C, source, whole, up, down):
        self.C, self.source, self.whole, self.up, self.down = C, source, whole, up, down
        self.me = lax.axis_index("col")

    def upward(self, step):
        owner = self.me - step
        piece = self.source if step == 0 else self.whole.at[owner]
        return remote(piece, self.whole.at[owner], self.up[0].at[step], self.up[1].at[step], col=self.me + 1)

    def downward(self, step):
        owner = self.me + step
        piece = self.source if step == 0 else self.whole.at[owner]
        return remote(piece, self.whole.at[owner], self.down[0].at[step], self.down[1].at[step], col=self.me - 1)

    def arrival(self, step, rises):
        sender = self.me - 1 if rises else self.me + 1
        send, recv = self.up if rises else self.down
        target = self.whole.at[sender - step if rises else sender + step]
        return remote(target, target, send.at[step], recv.at[step], col=sender)

    def event(self, step):
        me, last = self.me, self.C - 1
        if step:

            @pl.when(me >= step)
            def _():
                self.arrival(step - 1, True).wait_recv()

            @pl.when(me + step <= last)
            def _():
                self.arrival(step - 1, False).wait_recv()

        if step < last:

            @pl.when((me >= step) & (me < last))
            def _():
                self.upward(step).start()

            @pl.when((me + step <= last) & (me > 0))
            def _():
                self.downward(step).start()

    def finish(self):
        me, last = self.me, self.C - 1
        for step in range(last):

            @pl.when((me >= step) & (me < last))
            def _():
                self.upward(step).wait_send()

            @pl.when((me + step <= last) & (me > 0))
            def _():
                self.downward(step).wait_send()


class LineSum:
    def __init__(self, C, terms, rising, falling, up, down):
        self.C, self.terms, self.rising, self.falling, self.up, self.down = C, terms, rising, falling, up, down
        self.me = lax.axis_index("col")

    def upward(self, m, alone):
        source = self.terms.at[self.C - 1 - m] if alone else self.rising.at[m]
        return remote(source, self.rising.at[m], self.up[0].at[m], self.up[1].at[m], col=lax.rem(self.me + 1, self.C))

    def downward(self, m, alone):
        source = self.terms.at[m] if alone else self.falling.at[m]
        return remote(
            source, self.falling.at[m], self.down[0].at[m], self.down[1].at[m], col=lax.rem(self.me + self.C - 1, self.C)
        )

    def level(self, t):
        me, last = self.me, self.C - 1
        rise, fall = t - me, t - (last - me)
        if t < last:

            @pl.when(me == 0)
            def _():
                if t:
                    self.upward(t - 1, True).wait_send()
                self.upward(t, True).start()

            @pl.when(me == last)
            def _():
                if t:
                    self.downward(t - 1, True).wait_send()
                self.downward(t, True).start()

        if t:

            @pl.when((me > 0) & (rise >= 0))
            def _():
                self.upward(rise, False).wait_recv()
                if t < last:
                    add_into(self.rising.at[rise], self.terms.at[last - rise])
                    self.upward(rise, False).start()

            @pl.when((me < last) & (fall >= 0))
            def _():
                self.downward(fall, False).wait_recv()
                if t < last:
                    add_into(self.falling.at[fall], self.terms.at[fall])
                    self.downward(fall, False).start()

    def finish(self):
        me, last = self.me, self.C - 1

        @pl.when(me == 0)
        def _():
            self.upward(last - 1, True).wait_send()

        @pl.when(me == last)
        def _():
            self.downward(last - 1, True).wait_send()

        for m in range(last):

            @pl.when((me > 0) & (m < last - me))
            def _():
                self.upward(m, False).wait_send()

            @pl.when((me < last) & (m < me))
            def _():
                self.downward(m, False).wait_send()


def line_semaphores(C):
    return [DMA((C,)) for _ in range(4)]


def greet_line(C, others):
    me, last = lax.axis_index("col"), C - 1
    above, below = {"col": me + 1}, {"col": me - 1}

    @pl.when(me == 0)
    def _():
        greet([above] + others, 1 + len(others))

    @pl.when(me == last)
    def _():
        greet([below] + others, 1 + len(others))

    @pl.when((me > 0) & (me < last))
    def _():
        greet([above, below] + others, 2 + len(others))


def feed_kernel(
    R, C, os_hbm, w_hbm, xs_hbm, wg_hbm, wu_hbm, wd_hbm, dy_hbm,
    h_hbm, b_hbm, dg_hbm, du_hbm, dys_hbm, down_hbm, y_ref, grad_ref,
    big, hidden, slope, silu, b, gates, ups, terms, rising, falling, dys, h, exchanged, arrived,
    load, block_load, tile_load, store, h_load, w_send, w_recv, f_send, f_recv, *semaphores,
):
    me = lax.axis_index("col")
    row, ahead, behind, other = row_places(R)
    parts, heads, T = os_hbm.shape[0], os_hbm.shape[1], os_hbm.shape[2]
    D, F = wg_hbm.shape
    width, depth = D // C, D // R
    size, tiles, group = 256, 8, R // C
    bf = F // tiles
    up, down = semaphores[:2], semaphores[2:4]
    gather = LineGather(C, dy_hbm, dys, up, down)
    sums = LineSum(C, terms, rising, falling, semaphores[4:6], semaphores[6:8])
    place = row_of(R)
    row_sums = RowSum(
        R, lambda i: big.at[place(i), :, pl.ds(0, F)], lambda i: big.at[place(i, True), :, pl.ds(0, F)],
        exchanged, arrived, semaphores[8:],
    )

    def began(source, target, semaphore):
        copy = pltpu.make_async_copy(source, target, semaphore)
        copy.start()
        return copy

    def block_in(i):
        rows = pl.ds(i * size, size)
        copies = [
            pltpu.make_async_copy(
                os_hbm.at[j, n, rows, :], hidden.at[rows, pl.ds((j * heads + n) * HEAD_DIM, HEAD_DIM)], block_load.at[i, j * heads + n]
            )
            for j in range(parts)
            for n in range(heads)
        ]
        return copies + [
            pltpu.make_async_copy(
                xs_hbm.at[j, rows, :], slope.at[rows, pl.ds(j * width, width)], block_load.at[i, parts * heads + j]
            )
            for j in range(C)
        ]

    def tile_in(i):
        cut = pl.ds(i * bf, bf)
        return [
            pltpu.make_async_copy(wg_hbm.at[:, cut], gates.at[i % 2], tile_load.at[0, i % 2]),
            pltpu.make_async_copy(wu_hbm.at[:, cut], ups.at[i % 2], tile_load.at[1, i % 2]),
        ]

    blocks = [block_in(i) for i in range(T // size)]
    for copy in blocks[0]:
        copy.start()
    out_w = [
        began(w_hbm.at[:, j], big.at[:, :, pl.ds(j * width, width)], load.at[j]) for j in range(C)
    ]
    dy_mine = began(dy_hbm, dys.at[me], load.at[R])
    down_mine = began(wd_hbm, down_hbm.at[row], load.at[R + 1])
    for copies in blocks[1:] + [tile_in(0), tile_in(1)]:
        for copy in copies:
            copy.start()
    greet_line(C, [{"row": other}] + [{"row": ahead[k]} for k in range(1, R // 2)])
    gather.event(0)
    spread = [
        remote(wd_hbm, down_hbm.at[row], w_send.at[k], w_recv.at[k], row=ahead[k]) for k in range(1, R // 2)
    ]
    forward = [remote(wd_hbm, down_hbm.at[row], f_send.at[0], f_recv.at[0], row=other)]
    for copy in spread + forward:
        copy.start()

    stores = []
    mine = pl.ds(pl.multiple_of(me * width, width), width)
    for copy in out_w:
        copy.wait()
    for i in range(T // size):
        rows = pl.ds(i * size, size)
        for copy in blocks[i]:
            copy.wait()
        if i:
            stores[-1].wait()
        left = hidden[rows, :D]
        for j in range(C):
            columns = slice(j * width, (j + 1) * width)
            right = big[j * group : (j + 1) * group, :, :D].reshape(width, D)
            h[:, columns] = slope[rows, columns].astype(F32) + dot_nt(left, right)
        values = h[...]
        centre, inverse = norm_rows(values)
        b[rows, :] = ((values - centre) * inverse).astype(BF)
        stores.append(began(h, h_hbm.at[rows, :], store.at[0]))
    stores[-1].wait()
    b_out = began(b, b_hbm, store.at[1])
    h_back = [
        began(h_hbm.at[pl.ds(i * size, size), mine], h.at[:, pl.ds(i * width, width)], h_load.at[i])
        for i in range(T // size)
    ]
    for i in range(tiles):
        cut = slice(i * bf, (i + 1) * bf)
        for copy in tile_in(i):
            copy.wait()
        values = b[...]
        gate = dot_nn(values, gates[i % 2])
        upward = dot_nn(values, ups[i % 2])
        sigmoid = jax.nn.sigmoid(gate)
        silued = gate * sigmoid
        hidden[:, cut] = (silued * upward).astype(BF)
        slope[:, cut] = (upward * sigmoid * (1.0 + gate * (1.0 - sigmoid))).astype(BF)
        silu[:, cut] = silued.astype(BF)
        if i + 2 < tiles:
            for copy in tile_in(i + 2):
                copy.start()
        if i == 3:
            gather.event(1)
    for k in range(1, R // 2):
        spread[k - 1].wait_recv()
        block = down_hbm.at[behind[k]]
        copy = remote(block, block, f_send.at[k], f_recv.at[k], row=other)
        copy.start()
        forward.append(copy)
    for step in range(2, max(3, C - 1)):
        if step < C:
            gather.event(step)
    for copy in forward:
        copy.wait_recv()
    down_mine.wait()
    began(down_hbm, big.at[:, :, pl.ds(0, F)], load.at[0]).wait()
    half = lax.div(me, C // 2)

    def out_tile(k):
        j = (C - 1 - k) * (1 - half) + k * half
        right = big[pl.ds(j * group, group), :, :F].reshape(width, F)
        terms[j] = dot_nt(hidden[:, :F], right).astype(BF)

    out_tile(0)
    sums.level(0)
    for k in range(1, C):
        out_tile(k)
    for step in range(max(3, C - 1), C):
        gather.event(step)
    dy_mine.wait()
    b_out.wait()
    joined = [began(dys.at[j], b.at[:, pl.ds(j * width, width)], load.at[j]) for j in range(C)]
    saved = [began(dys, dys_hbm, store.at[1])]
    for copy in joined:
        copy.wait()
    sums.level(1)
    for i in range(tiles):
        cut = slice(i * bf, (i + 1) * bf)
        grad_hidden = dot_nn(b[...], big[:, :, cut].reshape(D, bf))
        slope[:, cut] = (grad_hidden * slope[:, cut].astype(F32)).astype(BF)
        silu[:, cut] = (grad_hidden * silu[:, cut].astype(F32)).astype(BF)
    saved.append(began(slope.at[:, pl.ds(0, F)], dg_hbm, store.at[2]))
    saved.append(began(silu.at[:, pl.ds(0, F)], du_hbm, store.at[3]))


    def down_tile(slot):
        chip = lax.div(place(slot), 2)
        product = dot_tn(dys[chip], hidden[:, :F]).astype(BF)
        for n in range(2):
            big[2 * chip + n, :, :F] = product[n * depth : (n + 1) * depth]

    row_sums.compute_and_relay(down_tile)
    for t in range(2, C - 1):
        sums.level(t)
    row_sums.relay_again()
    sums.level(C - 1)
    last = C - 1
    for copy in h_back:
        copy.wait()

    def result(more):
        for i in range(T // size):
            rows = pl.ds(i * size, size)
            total = h[:, i * width : (i + 1) * width] + terms[me, rows, :].astype(F32)
            for buffer, slot in more:
                total += buffer[slot, rows, :].astype(F32)
            y_ref[rows, :] = total.astype(BF)

    @pl.when(me == 0)
    def _():
        result([(falling, 0)])

    @pl.when(me == last)
    def _():
        result([(rising, 0)])

    @pl.when((me > 0) & (me < last))
    def _():
        result([(rising, last - me), (falling, me)])

    def write(part, values):
        grad_ref[:, part] = values.T.astype(BF)

    row_sums.finish(write, 128)
    sums.finish()
    gather.finish()
    for copy in spread + forward:
        copy.wait_send()
    for copy in saved:
        copy.wait()


def feed_forward(R, C, os, w_out, xs, w_gate, w_up, w_down, cotangent):
    heads, T = os.shape[1], os.shape[2]
    width = xs.shape[2]
    D, F = w_gate.shape
    most = max(D, F)
    flat = pltpu.VMEM((T, most), BF)
    return pl.pallas_call(
        functools.partial(feed_kernel, R, C),
        in_specs=[ANY] * 7,
        out_specs=[ANY] * 6 + [VMEM_SPEC] * 2,
        out_shape=[
            struct((T, D), F32),
            struct((T, D), BF),
            struct((T, F), BF),
            struct((T, F), BF),
            struct((C, T, width), BF),
            struct((R, D // R, F), BF),
            struct((T, width), BF),
            struct((F, D // R), BF),
        ],
        scratch_shapes=[
            pltpu.VMEM((R, D // R, most), BF),
            flat,
            flat,
            pltpu.VMEM((T, F), BF),
            pltpu.VMEM((T, D), BF),
            pltpu.VMEM((2, D, F // 8), BF),
            pltpu.VMEM((2, D, F // 8), BF),
            pltpu.VMEM((C, T, width), BF),
            pltpu.VMEM((C - 1, T, width), BF),
            pltpu.VMEM((C - 1, T, width), BF),
            pltpu.VMEM((C, T, width), BF),
            pltpu.VMEM((256, D), F32),
        ]
        + row_sum_buffers(R, D // R, F)
        + [
            DMA((R + 2,)),
            DMA((T // 256, C * heads + C)),
            DMA((2, 2)),
            DMA((4,)),
            DMA((T // 256,)),
            DMA((R // 2,)),
            DMA((R // 2,)),
            DMA((R // 2,)),
            DMA((R // 2,)),
        ]
        + line_semaphores(C)
        + line_semaphores(C)
        + row_sum_semaphores(R),
        compiler_params=comm_params(2, 63),
        cost_estimate=cost(1.2e11, 90 * MIB),
        name="feed_forward",
    )(os, w_out, xs, w_gate, w_up, w_down, cotangent)


def norm_terms_kernel(
    R, C, dg_hbm, du_hbm, wg_hbm, wu_hbm, b_hbm,
    sum_ref, up_hbm, gate_ref,
    dg, du, wg, wu, b, terms, held, stage, exchanged, arrived,
    load, tile_load, store, send, recv, *semaphores,
):
    me, right, left = ring_places(C)
    D, F = wg.shape
    T = dg.shape[0]
    rows = T // C
    width = D // C

    def fetch(source, target, semaphore):
        copy = pltpu.make_async_copy(source, target, semaphore)
        copy.start()
        return copy

    def chunk(s):
        return pl.ds(pl.multiple_of(lax.rem(me + 2 * C - 1 - s, C) * rows, rows), rows)

    grads_in = []
    for s in range(C):
        part = chunk(s)
        grads_in.append(
            (fetch(dg_hbm.at[part, :], dg.at[part, :], load.at[2 * s]), fetch(du_hbm.at[part, :], du.at[part, :], load.at[2 * s + 1]))
        )
        if s == 0:
            weights_in = []
            for n in range(C):
                cut = pl.ds(n * width, width)
                weights_in.append(
                    (fetch(wg_hbm.at[cut, :], wg.at[cut, :], tile_load.at[2 * n]), fetch(wu_hbm.at[cut, :], wu.at[cut, :], tile_load.at[2 * n + 1]))
                )
    b_in = fetch(b_hbm, b, load.at[2 * C])
    place, depth = row_of(R), D // R

    def block(places):
        return wu.at[pl.ds(pl.multiple_of(places * depth, depth), depth), :]

    sums = RowSum(R, lambda i: block(place(i)), lambda i: block(place(i, True)), exchanged, arrived, semaphores)
    greet([{"col": left}] + sums.peers, 1 + len(sums.peers))

    def term_tile(s, part, n):
        cut = pl.ds(pl.multiple_of(n * width, width), width)
        total = dot_nt(dg[part, :], wg[cut, :]) + dot_nt(du[part, :], wu[cut, :])
        terms[s, :, cut] = total.astype(BF)

    ring = SumRing(C, terms, held, send, recv)

    for s in range(C):
        part = chunk(s)
        for copy in grads_in[s]:
            copy.wait()
        if s == 0:
            for n in range(C):
                for copy in weights_in[n]:
                    copy.wait()
                term_tile(s, part, n)
            ring.start()
        else:

            def body(n, carry):
                term_tile(s, part, n)
                return carry

            lax.fori_loop(0, C, body, 0)
    b_in.wait()

    def stored(target, t, slot):
        cut = pl.ds(pl.multiple_of(t * width, width), width)
        return pltpu.make_async_copy(stage.at[slot], target.at[cut, :], store.at[slot])

    def product(right_ref, target):
        def body(t, carry):
            slot = lax.rem(t, 2)

            @pl.when(t >= 2)
            def _():
                stored(target, t, slot).wait()

            left_tile = b[:, pl.ds(pl.multiple_of(t * width, width), width)]
            stage[slot] = dot_tn(left_tile, right_ref[...]).astype(BF)
            stored(target, t, slot).start()
            return carry

        lax.fori_loop(0, C, body, 0)
        for slot in range(2):
            stored(target, slot, slot).wait()

    middle = max(1, (C - 1) // 2)
    for step in range(1, middle + 1):
        if step < C - 1:
            ring.pass_on(step)

    def gate_tile(slot):
        cut = pl.ds(pl.multiple_of(lax.div(place(slot), 2) * 2 * depth, 2 * depth), 2 * depth)
        wu[cut, :] = dot_tn(b[:, cut], dg[...]).astype(BF)

    sums.compute_and_relay(gate_tile)
    product(du, up_hbm)
    for step in range(middle + 1, C - 1):
        ring.pass_on(step)
    sums.relay_again()

    def write(part, values):
        gate_ref[part, :] = values.astype(BF)

    sums.finish(write)
    ring.arrived()
    sum_ref[...] = held[C - 2].astype(F32) + terms[C - 1].astype(F32)
    ring.sent()


def norm_terms(R, C, dg, du, w_gate, w_up, b):
    T, F = dg.shape
    D = w_gate.shape[0]
    rows, width = T // C, D // C
    return pl.pallas_call(
        functools.partial(norm_terms_kernel, R, C),
        in_specs=[ANY] * 5,
        out_specs=[VMEM_SPEC, ANY, VMEM_SPEC],
        out_shape=[struct((rows, D), F32), struct((D, F), BF), struct((D // R, F), BF)],
        scratch_shapes=[
            pltpu.VMEM((T, F), BF),
            pltpu.VMEM((T, F), BF),
            pltpu.VMEM((D, F), BF),
            pltpu.VMEM((D, F), BF),
            pltpu.VMEM((T, D), BF),
            pltpu.VMEM((C, rows, D), BF),
            pltpu.VMEM((C - 1, rows, D), BF),
            pltpu.VMEM((2, width, F), BF),
        ]
        + row_sum_buffers(R, D // R, F)
        + [
            DMA((2 * C + 1,)),
            DMA((2 * C,)),
            DMA((2,)),
            DMA((C - 1,)),
            DMA((C - 1,)),
        ]
        + row_sum_semaphores(R),
        compiler_params=comm_params(3, 63),
        cost_estimate=cost(9e10, 70 * MIB),
        name="norm_terms",
    )(dg, du, w_gate, w_up, b)


def attend_back_kernel(
    R, C, sum_ref, log_ref, segk_ref, segq_ref, cos_ref, sin_ref,
    q_hbm, k_hbm, v_hbm, h_hbm, dys_hbm, w_hbm, gate_hbm,
    dq_ref, dk_ref, dv_ref, gate_ref, dhs_hbm,
    h, dy, w, dh, out, q_ref, k_ref, v_ref, do_ref, dk_sum, dv_sum, own, exchanged, arrived,
    load, w_load, local, h_send, h_recv, o_send, o_recv, own_load, *semaphores,
):
    me, right, left = ring_places(C)
    rows, D = sum_ref.shape
    T, width = q_ref.shape
    heads, bq = width // HEAD_DIM, 256
    mine = pl.ds(pl.multiple_of(me * rows, rows), rows)
    first_in = [
        pltpu.make_async_copy(h_hbm.at[mine, :], h, load.at[0]),
        pltpu.make_async_copy(dys_hbm.at[:, mine, :], dy, load.at[1]),
    ]
    head_loads = [
        pltpu.make_async_copy(source, target, load.at[2 + i])
        for i, (source, target) in enumerate(((q_hbm, q_ref), (k_hbm, k_ref), (v_hbm, v_ref)))
    ]
    for copy in first_in:
        copy.start()
    order = [lax.rem(me + k, C) for k in range(1, C)] + [me]
    cuts = [pl.ds(pl.multiple_of(place * width, width), width) for place in order]
    loads = [pltpu.make_async_copy(w_hbm.at[:, order[k]], w.at[k], w_load.at[k]) for k in range(C)]
    sums, own_loads = held_row_sum(R, gate_hbm, own, exchanged, arrived, own_load, semaphores)
    for copy in loads + own_loads + head_loads:
        copy.start()
    greet([{"col": lax.rem(me + k, C)} for k in range(1, C)] + sums.peers, C - 1 + len(sums.peers))
    for slot in sums.order():
        sums.exchange(slot).start()
    for copy in first_in:
        copy.wait()
    grad = sum_ref[...]
    centre, inverse = norm_rows(h[...])
    normed = (h[...] - centre) * inverse
    first = jnp.mean(grad, axis=1, keepdims=True)
    second = jnp.mean(grad * normed, axis=1, keepdims=True)
    dh[...] = (beside(dy).astype(F32) + inverse * (grad - first - normed * second)).astype(BF)
    do_copies, dh_copies = [], []
    for k in range(C):
        loads[k].wait()
        out[k] = dot_nn(dh[...], w[k].reshape(D, width)).astype(BF)
        if k < C - 1:
            copy = remote(out.at[k], do_ref.at[mine, :], o_send.at[k], o_recv.at[k], col=order[k])
        else:
            copy = pltpu.make_async_copy(out.at[k], do_ref.at[mine, :], local.at[0])
        copy.start()
        do_copies.append(copy)
    sums.relay(lambda slot: own_loads[slot].wait())
    for copy in do_copies[:-1]:
        copy.wait_recv()
    do_copies[-1].wait()
    for k in range(C):
        if k < C - 1:
            copy = remote(dh.at[:, cuts[k]], dhs_hbm.at[mine, :], h_send.at[k], h_recv.at[k], col=order[k])
        else:
            copy = pltpu.make_async_copy(dh.at[:, cuts[k]], dhs_hbm.at[mine, :], local.at[1])
        copy.start()
        dh_copies.append(copy)
    for copy in head_loads:
        copy.wait()

    def one_head(head, carry):
        columns = pl.ds(pl.multiple_of(head * HEAD_DIM, HEAD_DIM), HEAD_DIM)
        dk_sum[...] = jnp.zeros_like(dk_sum)
        dv_sum[...] = jnp.zeros_like(dv_sum)
        for first in range(0, T, SEQ):
            for start in range(first, first + SEQ, bq):
                stop = start + bq
                keys = k_ref[first:stop, columns]
                queries = q_ref[start:stop, columns]
                grads = do_ref[start:stop, columns]
                scores = dot_nt(keys, queries) * SCALE
                allowed = allowed_block(segk_ref[first:stop], segq_ref[:, start:stop], start - first)
                scores = jnp.where(allowed, scores, MASKED)
                probs = jnp.exp(scores - log_ref[head, :, start:stop])
                dv_sum[first:stop] += dot_nn(probs.astype(BF), grads)
                grad_probs = dot_nt(v_ref[first:stop, columns], grads)
                inner = jnp.sum(probs * grad_probs, axis=0, keepdims=True)
                grad_scores = (probs * (grad_probs - inner)).astype(BF)
                dk_sum[first:stop] += dot_nn(grad_scores, queries)
                grad_query = dot_tn(keys, grad_scores).T * SCALE
                dq_ref[start:stop, columns] = turn(grad_query, cos_ref[start:stop], -sin_ref[start:stop]).astype(BF)
        dk_ref[:, columns] = turn(dk_sum[...] * SCALE, cos_ref[...], -sin_ref[...]).astype(BF)
        dv_ref[:, columns] = dv_sum[...].astype(BF)
        return carry

    lax.fori_loop(0, heads // 2, one_head, 0)
    sums.relay_again()
    lax.fori_loop(heads // 2, heads, one_head, 0)

    def write(part, values):
        gate_ref[part, :] = values.astype(BF)

    sums.finish(write)
    for copy in do_copies[:-1]:
        copy.wait_send()
    for copy in dh_copies:
        copy.wait()


def attend_back(R, total, log_total, seg_column, seg_row, cos_table, sin_table, q, k, v, h, dys, w_out, grad_gate):
    C, T, width = dys.shape
    rows, D = total.shape
    depth, columns = grad_gate.shape[1:]
    one = pltpu.VMEM((T, width), BF)
    return pl.pallas_call(
        functools.partial(attend_back_kernel, R, C),
        in_specs=[VMEM_SPEC] * 6 + [ANY] * 7,
        out_specs=[VMEM_SPEC] * 4 + [ANY],
        out_shape=[struct((T, width), BF)] * 3 + [struct((depth, columns), BF), struct((T, width), BF)],
        scratch_shapes=[
            pltpu.VMEM((rows, D), F32),
            pltpu.VMEM((C, rows, width), BF),
            pltpu.VMEM((C, R, D // R, width), BF),
            pltpu.VMEM((rows, D), BF),
            pltpu.VMEM((C, rows, width), BF),
            one,
            one,
            one,
            one,
            pltpu.VMEM((T, HEAD_DIM), F32),
            pltpu.VMEM((T, HEAD_DIM), F32),
            pltpu.VMEM((R // 2, depth, columns), BF),
        ]
        + row_sum_buffers(R, depth, columns)
        + [
            DMA((5,)),
            DMA((C,)),
            DMA((2,)),
            DMA((C - 1,)),
            DMA((C - 1,)),
            DMA((C - 1,)),
            DMA((C - 1,)),
            DMA((R // 2,)),
        ]
        + row_sum_semaphores(R),
        compiler_params=comm_params(5),
        cost_estimate=cost(5e10, 30 * MIB),
        name="attend_back",
    )(total, log_total, seg_column, seg_row, cos_table, sin_table, q, k, v, h, dys, w_out, grad_gate)


def input_terms_kernel(
    R, C, dq_ref, dk_ref, dv_ref, mu_hbm, r_hbm, w_hbm, a_hbm, x_hbm, dh_hbm, os_hbm,
    y_ref, gq_ref, gk_ref, gv_ref, out_ref,
    mu_ref, r_ref, w_ref, a_ref, x_ref, dh_ref, block, product, mine, by_column, by_row,
    terms, rising, falling, stats, stats_in, tiles, q_exchanged, q_arrived, o_tiles, o_exchanged, o_arrived,
    s_send, s_recv, w_load, late_load, block_load, c_send, c_recv, r_send, r_recv, local, *semaphores,
):
    me, right, left = ring_places(C)
    T, width = dq_ref.shape
    D = width * C
    heads = (dq_ref, dk_ref, dv_ref)
    row = lax.axis_index("row")
    thin = width // R

    upper = lax.div(me, C // 2)

    def column_of(s):
        return (C - 1 - s) * (1 - upper) + s * upper

    def cut_of(s):
        return pl.ds(pl.multiple_of(column_of(s) * width, width), width)

    def weight_in(s):
        return pltpu.make_async_copy(w_hbm.at[:, cut_of(s), :], w_ref.at[:, cut_of(s), :], w_load.at[s])

    for s in range(C):
        weight_in(s).start()
    late = [
        pltpu.make_async_copy(source, target, late_load.at[i])
        for i, (source, target) in enumerate(
            ((a_hbm, a_ref), (x_hbm, x_ref), (dh_hbm, dh_ref), (mu_hbm, mu_ref), (r_hbm, r_ref))
        )
    ]
    for copy in late:
        copy.start()
    depth = tiles.shape[2]
    side = lax.rem(lax.axis_index("row"), 2)
    q_sums = RowSum(
        R, lambda i: tiles.at[i, side], lambda i: tiles.at[i, 1 - side], q_exchanged, q_arrived, semaphores[:4]
    )
    o_sums = RowSum(
        R, lambda i: o_tiles.at[i, side], lambda i: o_tiles.at[i, 1 - side], o_exchanged, o_arrived, semaphores[4:8]
    )

    def block_in(i):
        return [
            pltpu.make_async_copy(
                os_hbm.at[i, n], block.at[i % 2, :, pl.ds(n * HEAD_DIM, HEAD_DIM)], block_load.at[i % 2, n]
            )
            for n in range(os_hbm.shape[1])
        ]

    for copy in block_in(0) + block_in(1):
        copy.start()
    greet(
        [{"col": lax.rem(me + k, C)} for k in range(1, C)] + [{"row": lax.rem(row + k, R)} for k in range(1, R)],
        C + R - 2,
    )

    line = LineSum(C, terms, rising, falling, semaphores[8:10], semaphores[10:])

    def compute(s):
        cut = cut_of(s)
        weight_in(s).wait()
        total = dot_nt(dq_ref[...], w_ref[0, cut, :])
        total += dot_nt(dk_ref[...], w_ref[1, cut, :])
        total += dot_nt(dv_ref[...], w_ref[2, cut, :])
        terms[column_of(s)] = total.astype(BF)

    compute(0)
    line.level(0)

    def body(s, carry):
        compute(s)
        return carry

    late[2].wait()
    for j in range(C):
        for copy in block_in(j):
            copy.wait()
        product[...] = dot_tn(block[j % 2], dh_ref[...]).astype(BF)
        for slot in range(R // 2):
            for place in range(2):
                rows = 2 * lax.div(o_sums.places(slot), 2) + place
                o_tiles[slot, place, j * thin : (j + 1) * thin] = product[pl.ds(pl.multiple_of(rows * thin, thin), thin), :]
        if j + 2 < C:
            for copy in block_in(j + 2):
                copy.start()
    for slot in o_sums.order():
        o_sums.exchange(slot).start()
    o_sums.relay()
    lax.fori_loop(1, C, body, 0)
    for i, copy in enumerate(late):
        if i != 2:
            copy.wait()

    def qkv_tile(slot):
        start = pl.multiple_of(lax.div(q_sums.places(slot), 2) * 2 * depth, 2 * depth)
        left_tile = a_ref[:, pl.ds(start, 2 * depth)]
        for i, right_side in enumerate(heads):
            product = dot_tn(left_tile, right_side[...]).astype(BF)
            tiles[slot, 0, :, i * width : (i + 1) * width] = product[:depth]
            tiles[slot, 1, :, i * width : (i + 1) * width] = product[depth:]

    q_sums.compute_and_relay(qkv_tile)
    o_sums.relay_again()
    line.level(1)

    def write_out(part, values):
        mine[part, :] = values.astype(BF)

    o_sums.finish(write_out)
    columns_out = []
    for k in range(1, C):
        place = lax.rem(me + k, C)
        rows = pl.ds(pl.multiple_of(place * thin, thin), thin)
        columns_out.append(remote(mine.at[rows, :], by_column.at[me], c_send.at[k - 1], c_recv.at[k - 1], col=place))
    stay = pltpu.make_async_copy(
        mine.at[pl.ds(pl.multiple_of(me * thin, thin), thin), :], by_column.at[me], local.at[0]
    )
    for copy in columns_out + [stay]:
        copy.start()
    size = 128

    def sum_rows(i, carry):
        rows = pl.ds(pl.multiple_of(i * size, size), size)
        lane = lax.broadcasted_iota(jnp.int32, (size, 128), 1)
        total = jnp.zeros((size, 1), F32)
        second = jnp.zeros((size, 1), F32)
        for s in range(C):
            grad = terms[s, rows, :].astype(F32)
            total += jnp.sum(grad, axis=1, keepdims=True)
            second += jnp.sum(grad * a_ref[rows, s * width : (s + 1) * width].astype(F32), axis=1, keepdims=True)
        packed = jnp.where(lane == 0, total, jnp.where(lane == 1, second, 0.0))
        stats[:, rows] = packed.T[:8]
        return carry

    lax.fori_loop(0, T // size, sum_rows, 0)
    exchanges = [
        remote(stats, stats_in.at[k - 1], s_send.at[k - 1], s_recv.at[k - 1], col=lax.rem(me + k, C)) for k in range(1, C)
    ]
    for copy in exchanges:
        copy.start()
    for step in range(2, C - 1):
        line.level(step)
    for copy in columns_out:
        copy.wait_recv()
    stay.wait()

    def piece_of(place):
        return by_column.at[lax.div(place * C, R), :, pl.ds(pl.multiple_of(lax.rem(place, R // C) * depth, depth), depth)]

    rows_out = []
    for k in range(1, R):
        place = lax.rem(row + k, R)
        rows_out.append(remote(piece_of(place), by_row.at[row], r_send.at[k - 1], r_recv.at[k - 1], row=place))
    keep = pltpu.make_async_copy(piece_of(row), by_row.at[row], local.at[1])
    for copy in rows_out + [keep]:
        copy.start()
    q_sums.relay_again()
    for copy in rows_out:
        copy.wait_recv()
    keep.wait()
    for n in range(R):
        out_ref[n * thin : (n + 1) * thin, :] = by_row[n]

    def write_qkv(part, values):
        for i, target in enumerate((gq_ref, gk_ref, gv_ref)):
            target[part, :] = values[:, i * width : (i + 1) * width].astype(BF)

    q_sums.finish(write_qkv)
    for copy in exchanges:
        copy.wait_recv()
    line.level(C - 1)

    def last_rows(more):
        def body(i, carry):
            rows = pl.ds(pl.multiple_of(i * size, size), size)
            both = stats[:, rows]
            for k in range(C - 1):
                both += stats_in[k, :, rows]
            columns = jnp.concatenate([both, jnp.zeros((120, size), F32)], axis=0).T * (1.0 / D)
            normed = (x_ref[rows, :].astype(F32) - mu_ref[rows, :]) * r_ref[rows, :]
            grad = terms[me, rows, :].astype(F32)
            for buffer, slot in more:
                grad += buffer[slot, rows, :].astype(F32)
            grad = grad - columns[:, 0:1] - normed * columns[:, 1:2]
            y_ref[rows, :] = (dh_ref[rows, :].astype(F32) + r_ref[rows, :] * grad).astype(BF)
            return carry

        lax.fori_loop(0, T // size, body, 0)

    @pl.when(me == 0)
    def _():
        last_rows([(falling, 0)])

    @pl.when(me == C - 1)
    def _():
        last_rows([(rising, 0)])

    @pl.when((me > 0) & (me < C - 1))
    def _():
        last_rows([(rising, C - 1 - me), (falling, me)])

    for copy in exchanges + columns_out + rows_out:
        copy.wait_send()
    line.finish()


def input_terms(R, C, dq, dk, dv, w_qkv, a, tokens, dh, mu, r, os):
    T, width = dq.shape
    D = w_qkv.shape[1]
    half, low = R // 2, D // R
    thin = width // R
    return pl.pallas_call(
        functools.partial(input_terms_kernel, R, C),
        in_specs=[VMEM_SPEC] * 3 + [ANY] * 7,
        out_specs=[VMEM_SPEC] * 5,
        out_shape=[struct((T, width), BF)]
        + [struct((low, width), BF)] * 3
        + [struct((width, low), BF)],
        scratch_shapes=[
            pltpu.VMEM((T, 1), F32),
            pltpu.VMEM((T, 1), F32),
            pltpu.VMEM((3, D, width), BF),
            pltpu.VMEM((T, D), BF),
            pltpu.VMEM((T, width), BF),
            pltpu.VMEM((T, width), BF),
            pltpu.VMEM((2, T, width), BF),
            pltpu.VMEM((width, width), BF),
            pltpu.VMEM((C * thin, width), BF),
            pltpu.VMEM((C, thin, width), BF),
            pltpu.VMEM((R, thin, low), BF),
            pltpu.VMEM((C, T, width), BF),
            pltpu.VMEM((C - 1, T, width), BF),
            pltpu.VMEM((C - 1, T, width), BF),
            pltpu.VMEM((8, T), F32),
            pltpu.VMEM((C - 1, 8, T), F32),
            pltpu.VMEM((half, 2, low, 3 * width), BF),
        ]
        + row_sum_buffers(R, low, 3 * width)
        + [pltpu.VMEM((half, 2, C * thin, width), BF)]
        + row_sum_buffers(R, C * thin, width)
        + [
            DMA((C - 1,)),
            DMA((C - 1,)),
            DMA((C,)),
            DMA((5,)),
            DMA((2, os.shape[1])),
            DMA((C - 1,)),
            DMA((C - 1,)),
            DMA((R - 1,)),
            DMA((R - 1,)),
            DMA((2,)),
        ]
        + row_sum_semaphores(R)
        + row_sum_semaphores(R)
        + line_semaphores(C),
        compiler_params=comm_params(6, 63),
        cost_estimate=cost(8e10, 20 * MIB),
        name="input_terms",
    )(dq, dk, dv, mu, r, w_qkv, a, tokens, dh, os)


def results_kernel(*refs):
    half = len(refs) // 2
    for source, target in zip(refs[:half], refs[half:]):
        target[...] = source[...].astype(target.dtype)


def results(*values):
    shapes = [struct(value.shape, BF if i < 2 else F32) for i, value in enumerate(values)]
    return pl.pallas_call(
        results_kernel,
        in_specs=[VMEM_SPEC] * len(values),
        out_specs=[VMEM_SPEC] * len(values),
        out_shape=shapes,
        compiler_params=params(),
        cost_estimate=cost(1e6, 16 * MIB),
        name="results",
    )(*values)


def on_device(R, C, tokens, cotangent, segments, w_query, w_key, w_value, w_out, w_gate, w_up, w_down):
    T, width = tokens.shape
    D = width * C
    gathered = lambda w: lax.all_gather(w, "row", axis=0, tiled=True)

    gate_w, up_w = gathered(w_gate), gathered(w_up)
    seg_row = segments.reshape(1, T)
    xs, w_qkv, cos_table, sin_table, seg_column, out_part, down_part = first_gather(
        R, C, seg_row, tokens, w_query, w_key, w_value, w_out, w_down
    )
    w_qkv = w_qkv.reshape(3, D, width)
    act_one, q, k, v, mu_one, r_one, out_part = norm_and_project(xs, w_qkv, cos_table, sin_table, out_part)
    os, log_total, out_w = attend(R, C, q, k, v, seg_column, seg_row, out_part)
    h_full, act_two, dg, du, dys, _, output, grad_down = feed_forward(
        R, C, os, out_w, xs, gate_w, up_w, down_part, cotangent
    )
    total, grad_up, grad_gate = norm_terms(R, C, dg, du, gate_w, up_w, act_two)
    grad_up = grad_up.reshape(R, D // R, -1)
    dq, dk, dv, grad_up, dh = attend_back(
        R, total, log_total, seg_column, seg_row, cos_table, sin_table, q, k, v, h_full, dys, out_w, grad_up
    )
    grad_tokens, grad_query, grad_key, grad_value, grad_out = input_terms(
        R, C, dq, dk, dv, w_qkv, act_one, tokens, dh, mu_one, r_one, os
    )
    return tuple(
        results(output, grad_tokens, grad_query, grad_key, grad_value, grad_out, grad_gate, grad_up, grad_down)
    )


def solution(mesh):
    here = P("row", "col")
    turned = P("col", "row")
    return jax.shard_map(
        functools.partial(on_device, mesh.shape["row"], mesh.shape["col"]),
        mesh=mesh,
        in_specs=(here, here, P("row"), here, here, here, turned, here, here, turned),
        out_specs=(here, here, here, here, here, turned, here, here, turned),
        check_vma=False,
    )
```
